32 devices in a mesh: group: 4 (over z), tile: 8 (over y, x, core).
Axes of the slice: x: 2, y: 2, z: 4, core: 2. Of those that a mesh axis runs over, the one named last changes fastest.
Arguments:
- potential: float32 [64, 8192], P('group', 'tile'), may hold values from -6 to 6
- species_inputs: bfloat16 [7, 64, 8192], P(None, 'group', 'tile'), may hold values from -6 to 6
- diffusion: float32 [4, 8192], P(None, 'tile'), may hold values from 0.02 to 0.2
- neighbours: int32 [4, 8192], P(None, 'tile'), may hold values from 0 to 1535, as said below
- sunlit_column_index: int32 [4, 8, 256], P('group', 'tile'), may hold values from 0 to 255, each once within a row
- day_count: int32 [4, 8], P('group', 'tile'), may hold values from 0 to 256, as said below
- zenith: bfloat16 [4, 8, 256], P('group', 'tile'), may hold values from 0.099609375 to 1
- lw_first: bfloat16 [8, 64], replicated, may hold values from -2 to 2
- lw_bias: float32 [64], replicated, may hold values from -3 to 3
- lw_second: bfloat16 [64, 64], replicated, may hold values from -0.75 to 0.75
- lw_depth: bfloat16 [64, 256], replicated, may hold values from -0.75 to 0.75
- lw_fraction: bfloat16 [64, 256], replicated, may hold values from -0.75 to 0.75
- sw_first: bfloat16 [8, 64], replicated, may hold values from -2 to 2
- sw_bias: float32 [64], replicated, may hold values from -3 to 3
- sw_second: bfloat16 [64, 64], replicated, may hold values from -0.75 to 0.75
- sw_depth: bfloat16 [64, 224], replicated, may hold values from -0.75 to 0.75
- solar_flux: float32 [224], replicated, may hold values from 0.5 to 2
Outputs:
- evolved: float32 [64, 8192], P('group', 'tile')
The draws below stay inside these ranges and needn't reach their ends.
Inputs may be any that keep to these rules, and one draw needn't show every extreme that they name: neighbours[k, c] - 256 - (c mod 1024) is a nonzero offset between -256 and 256. `sunlit_column_index`: each list [g, t, :] is a permutation of 0 .. 255. day_count[g, 2 i] + day_count[g, 2 i + 1] = 256 for every g and i.
All inputs are finite; a program needn't handle non-finite values.
Results may differ from the reference program's by a relative error of at most 0.0003.
Values may be sent and summed in bfloat16 or wider, within the bound.
No kernel may reach another device: no remote copies, remote signals or barrier semaphores. Data moves between devices by JAX's collectives and lax.ppermute only.
A program may use at most 128 MiB of HBM per device.

```python
import math
from functools import partial
import jax
import jax.numpy as jnp
from jax import lax

LEV = 64
COL_DEV = 256
GAS = 7
HID = 64
GPT = 256
SWG = 224
NB = 4
HW = 256
FIN = 8
TILE_COLS = 1024
NCOL = 8192
N_GROUP = 4
N_TILE = 8


def draw_neighbours(key, part):
    reaches = jax.random.randint(jax.random.fold_in(key, 101), (NB, NCOL), 1, HW + 1)
    sign_of = jax.random.randint(jax.random.fold_in(key, 102), (NB, NCOL), 0, 2) * 2 - 1
    column = jnp.arange(NCOL, dtype=jnp.int32)
    within = column % TILE_COLS
    offset_all = reaches * sign_of
    opening_line = jnp.arange(NB, dtype=jnp.int32)[:, None] == 0
    offset_all = jnp.where(opening_line & (within[None, :] == 0), -HW, offset_all)
    offset_all = jnp.where(opening_line & (within[None, :] == TILE_COLS - 1), HW, offset_all)
    return (within[None, :] + HW + offset_all).astype(jnp.int32)


def draw_day_count(key, part):
    evens = jax.random.randint(jax.random.fold_in(key, 201), (N_GROUP, N_TILE // 2), 0, COL_DEV + 1)
    chosen = jax.random.randint(jax.random.fold_in(key, 202), (N_GROUP, 1), 0, N_TILE // 2)
    extreme = jax.random.randint(jax.random.fold_in(key, 203), (N_GROUP, 1), 0, 2) * COL_DEV
    pair_ids = jnp.arange(N_TILE // 2, dtype=jnp.int32)[None, :]
    evens = jnp.where(pair_ids == chosen, extreme, evens)
    odds = COL_DEV - evens
    return jnp.stack([evens, odds], axis=2).reshape(N_GROUP, N_TILE).astype(jnp.int32)


def level_of(stream_key, dims, cuts, least, high):
    loudness = 1.0
    for axis_at, shards_of in cuts:
        heights = jax.random.uniform(jax.random.fold_in(jax.random.fold_in(stream_key, 6), axis_at), (shards_of,), jnp.float32, least / len(cuts), high / len(cuts))
        loudness = loudness * jnp.repeat(jnp.exp(heights), dims[axis_at] // shards_of).reshape((-1,) + (1,) * (len(dims) - 1 - axis_at))
    return loudness


def gaussian(key, extent, width, reach, shards=(), held_as=jnp.bfloat16):
    drawn = width * jax.random.normal(key, extent, jnp.float32)
    if shards:
        drawn = drawn * level_of(key, extent, shards, -0.22, 0.18)
    return jnp.clip(drawn, -reach, reach).astype(held_as)


def setup_inputs(seed: int = 0) -> dict:
    streams_of = jax.random.split(jax.random.key(seed), 18)
    potential = gaussian(streams_of[0], (LEV, NCOL), 1.0, 6.0, ((0, 4), (1, 8)), jnp.float32)
    species_inputs = gaussian(streams_of[1], (GAS, LEV, NCOL), 1.0, 6.0, ((1, 4), (2, 8)))
    diffusion = jnp.clip(jnp.exp(math.log(0.2) - 2.3025851 * jax.random.uniform(streams_of[2], (NB, NCOL), jnp.float32) ** level_of(streams_of[2], (NB, NCOL), ((1, 8),), -0.2, 0.2)), 0.02, 0.2)
    neighbours = draw_neighbours(jax.random.fold_in(streams_of[17], 71), 0)
    sunlit_column_index = jax.vmap(lambda own: jax.random.permutation(own, COL_DEV))(jax.random.split(streams_of[4], N_GROUP * N_TILE)).reshape((N_GROUP, N_TILE, COL_DEV)).astype(jnp.int32)
    day_count = draw_day_count(jax.random.fold_in(streams_of[17], 71), 0)
    zenith = jnp.clip(0.099609375 + 0.9003906 * jax.random.uniform(streams_of[6], (N_GROUP, N_TILE, COL_DEV), jnp.float32) ** level_of(streams_of[6], (N_GROUP, N_TILE, COL_DEV), ((0, 4), (1, 8)), -0.2, 0.2), 0.099609375, 1.0).astype(jnp.bfloat16)
    lw_first = gaussian(streams_of[7], (FIN, HID), FIN ** -0.5, 2.0)
    lw_bias = gaussian(streams_of[8], (HID,), 0.5, 3.0, (), jnp.float32)
    lw_second = gaussian(streams_of[9], (HID, HID), HID ** -0.5, 0.75)
    lw_depth = gaussian(streams_of[10], (HID, GPT), HID ** -0.5, 0.75)
    lw_fraction = gaussian(streams_of[11], (HID, GPT), HID ** -0.5, 0.75)
    sw_first = gaussian(streams_of[12], (FIN, HID), FIN ** -0.5, 2.0)
    sw_bias = gaussian(streams_of[13], (HID,), 0.5, 3.0, (), jnp.float32)
    sw_second = gaussian(streams_of[14], (HID, HID), HID ** -0.5, 0.75)
    sw_depth = gaussian(streams_of[15], (HID, SWG), HID ** -0.5, 0.75)
    solar_flux = jnp.clip(jnp.exp(jax.random.uniform(streams_of[16], (SWG,), jnp.float32, math.log(0.5), math.log(2.0))), 0.5, 2.0)
    return {"potential": potential, "species_inputs": species_inputs, "diffusion": diffusion, "neighbours": neighbours, "sunlit_column_index": sunlit_column_index, "day_count": day_count, "zenith": zenith, "lw_first": lw_first, "lw_bias": lw_bias, "lw_second": lw_second, "lw_depth": lw_depth, "lw_fraction": lw_fraction, "sw_first": sw_first, "sw_bias": sw_bias, "sw_second": sw_second, "sw_depth": sw_depth, "solar_flux": solar_flux}


depth_scale = 0.1
heat_scale = 12.0


def tendency(field, neighbours, diffusion):
    tile_cols = COL_DEV * N_GROUP
    grand_profile_tally = tile_cols * N_TILE
    column = jnp.arange(grand_profile_tally, dtype=jnp.int32)
    anchor = column - column % tile_cols
    outcome_state = jnp.zeros_like(field)
    for branch in range(NB):
        target = ((anchor + neighbours[branch] - HW) % grand_profile_tally).astype(jnp.int32)
        outcome_state = outcome_state + diffusion[branch] * (field[:, target] - field)
    return outcome_state


def hidden_layers(inputs, w_first, bias, w_second):
    flat_in = inputs.reshape(inputs.shape[0], -1)
    layer_one = jax.nn.silu(jnp.dot(w_first.T, flat_in, preferred_element_type=jnp.float32) + bias[:, None]).astype(jnp.bfloat16)
    return jax.nn.silu(jnp.dot(w_second.T, layer_one, preferred_element_type=jnp.float32)).astype(jnp.bfloat16)


def longwave(inputs, weights):
    w_first, bias, w_second, w_depth, w_fraction = weights
    vertical_levels, col_count = inputs.shape[1], inputs.shape[2]
    hidden = hidden_layers(inputs, w_first, bias, w_second)
    depth = depth_scale * jax.nn.softplus(jnp.dot(w_depth.T, hidden, preferred_element_type=jnp.float32)).reshape(-1, vertical_levels, col_count)
    fraction = jax.nn.softplus(jnp.dot(w_fraction.T, hidden, preferred_element_type=jnp.float32)).reshape(-1, vertical_levels, col_count)
    above = jnp.cumsum(depth, axis=1) - depth
    planck = jnp.exp(0.25 * inputs[0].astype(jnp.float32))
    emitted = jnp.sum(fraction * (1.0 - jnp.exp(-depth)) * jnp.exp(-above), axis=0)
    return -(heat_scale / depth.shape[0]) * planck * emitted


def shortwave(inputs, cosine, weights):
    w_first, bias, w_second, w_depth, solar_flux = weights
    vertical_levels, col_count = inputs.shape[1], inputs.shape[2]
    hidden = hidden_layers(inputs, w_first, bias, w_second)
    depth = depth_scale * jax.nn.softplus(jnp.dot(w_depth.T, hidden, preferred_element_type=jnp.float32)).reshape(-1, vertical_levels, col_count)
    above = jnp.cumsum(depth, axis=1) - depth
    slant = 1.0 / cosine
    beam = solar_flux[:, None, None] * cosine * jnp.exp(-above * slant) * (1.0 - jnp.exp(-depth * slant))
    return (heat_scale / depth.shape[0]) * jnp.sum(beam, axis=0)


def blockwise(kernel, inputs, cosine, weights):
    span_cols = inputs.shape[2]
    block_cols = 128 if span_cols % 128 == 0 else span_cols

    def one_block(begin_at):
        part_in = lax.dynamic_slice_in_dim(inputs, begin_at, block_cols, 2)
        if cosine is None:
            return kernel(part_in, weights)
        return kernel(part_in, lax.dynamic_slice_in_dim(cosine, begin_at, block_cols, 0), weights)

    starts = jnp.arange(span_cols // block_cols, dtype=jnp.int32) * block_cols
    stacked = lax.map(one_block, starts)
    return jnp.transpose(stacked, (1, 0, 2)).reshape(stacked.shape[1], span_cols)


def reference(potential, species_inputs, diffusion, neighbours, sunlit_column_index, day_count, zenith, lw_first, lw_bias, lw_second, lw_depth, lw_fraction, sw_first, sw_bias, sw_second, sw_depth, solar_flux):
    update = partial(tendency, neighbours=neighbours, diffusion=diffusion)
    first = potential + update(potential)
    second = 0.75 * potential + 0.25 * (first + update(first))
    tertile_portion = potential / 3.0 + (2.0 / 3.0) * (second + update(second))
    features = jnp.concatenate([tertile_portion.astype(jnp.bfloat16)[None], species_inputs], axis=0)
    layout = features.reshape(GAS + 1, LEV, N_TILE, N_GROUP, COL_DEV)
    slots = jnp.arange(COL_DEV, dtype=jnp.int32)
    long_weights = (lw_first, lw_bias, lw_second, lw_depth, lw_fraction)
    short_weights = (sw_first, sw_bias, sw_second, sw_depth, solar_flux)

    def portion_each_processor(number):
        tile_no = number // N_GROUP
        group_no = number % N_GROUP
        block = lax.dynamic_index_in_dim(layout, tile_no, 2, keepdims=False)
        block = lax.dynamic_index_in_dim(block, group_no, 2, keepdims=False)
        cosine = zenith[group_no, tile_no].astype(jnp.float32)
        listed = (sunlit_column_index[group_no, tile_no][:, None] == slots[None, :]) & (slots[:, None] < day_count[group_no, tile_no])
        daylit = jnp.sum(listed.astype(jnp.float32), axis=0)
        longwave_heating_rate = blockwise(longwave, block, None, long_weights)
        short_heat = blockwise(shortwave, block, cosine, short_weights)
        return longwave_heating_rate + short_heat * daylit

    heats = lax.map(portion_each_processor, jnp.arange(N_TILE * N_GROUP, dtype=jnp.int32))
    heating = jnp.transpose(heats.reshape(N_TILE, N_GROUP, LEV, COL_DEV), (2, 0, 1, 3)).reshape(LEV, -1)
    return tertile_portion + update(tertile_portion) + heating
```

```python
import functools
import math

import jax
import jax.numpy as jnp
from jax import lax
from jax.experimental import pallas as pl
from jax.experimental.pallas import tpu as pltpu
from jax.sharding import PartitionSpec as P

HW = 256
LANES = 128
SUBS = 8
STEP_LEVELS = SUBS // 2

depth_scale = 0.1
heat_scale = 12.0
LOG2E = 1.4426950408889634

F32 = jnp.float32
BF16 = jnp.bfloat16
VMEM = pl.BlockSpec(memory_space=pltpu.VMEM)
SMEM = pl.BlockSpec(memory_space=pltpu.SMEM)
PARAMS = pltpu.CompilerParams(vmem_limit_bytes=48 * 1024 * 1024)


def call(body, outs, ins, scratch=(), flops=0, trans=0, specs=None):
    return pl.pallas_call(
        body,
        out_shape=outs,
        in_specs=specs or [SMEM if a.size == 1 else VMEM for a in ins],
        out_specs=[VMEM for _ in outs],
        scratch_shapes=list(scratch),
        compiler_params=PARAMS,
        cost_estimate=pl.CostEstimate(
            flops=flops,
            transcendentals=trans,
            bytes_accessed=sum(a.size * a.dtype.itemsize for a in list(ins) + list(outs)),
        ),
    )(*ins)


def shaped(shape, dtype):
    return jax.ShapeDtypeStruct(shape, dtype)


def iota(shape, dim):
    return lax.broadcasted_iota(jnp.int32, shape, dim)


def mm(a, b):
    return jnp.dot(a, b, preferred_element_type=F32)


def lane_take(x, idx):
    return jnp.take_along_axis(x, idx, axis=1, mode="promise_in_bounds")


def diffused(src, src_at, table, weight, within, at):
    reach = HW // LANES
    wide = 2 * reach + 1
    rows = src.shape[0]
    groups = range(0, rows, SUBS)
    base = at - src_at
    middle = [src[r : r + SUBS, base : base + LANES] for r in groups]
    total = [jnp.zeros_like(m) for m in middle]
    for k in range(table.shape[0]):
        place = jnp.broadcast_to(table[k : k + 1, within : within + LANES], (SUBS, LANES)) - within
        lane = place & (LANES - 1)
        which = place >> (LANES.bit_length() - 1)
        factor = jnp.broadcast_to(weight[k : k + 1, within : within + LANES], (SUBS, LANES))
        tests = [which == w for w in range(1, wide)]
        for n, r in enumerate(groups):
            near = None
            for w in range(wide):
                lo = base + (w - reach) * LANES
                got = lane_take(src[r : r + SUBS, lo : lo + LANES], lane)
                near = got if w == 0 else jnp.where(tests[w - 1], got, near)
            total[n] = total[n] + factor * (near - middle[n])
    return [(r, m, m + t) for r, m, t in zip(groups, middle, total)]


def sections_body(
    n_group, me, left, own, right, nl, n0, nr, dl, d0, dr, third_out, *rest
):
    pieces, (frame, first, second) = rest[:n_group], rest[n_group:]
    tile = own.shape[1]
    cols = tile // n_group
    frame[:, 0:tile] = left[...]
    frame[:, tile : 2 * tile] = own[...]
    frame[:, 2 * tile :] = right[...]
    tables, weights = (nl, n0, nr), (dl, d0, dr)

    def run(src, src_at, halo, put):
        for at in range(tile - halo, 2 * tile + halo, LANES):
            t = at // tile
            for r, _, value in diffused(src, src_at, tables[t], weights[t], at - t * tile, at):
                put(r, at, value)

    def put_first(r, at, value):
        first[r : r + SUBS, at : at + LANES] = value

    def put_second(r, at, value):
        start = frame[r : r + SUBS, at : at + LANES]
        second[r : r + SUBS, at : at + LANES] = 0.75 * start + 0.25 * value

    def put_third(r, at, value):
        start = frame[r : r + SUBS, at : at + LANES]
        lo = at - tile + HW
        third_out[r : r + SUBS, lo : lo + LANES] = start / 3.0 + (2.0 / 3.0) * value

    run(frame, 0, 3 * HW, put_first)
    run(first, 0, 2 * HW, put_second)
    run(second, 0, HW, put_third)
    mine = me[0]
    for s in range(n_group):
        goal = lax.rem(mine + s, n_group)
        lo = pl.multiple_of(HW + goal * cols, LANES)
        pieces[s][...] = third_out[:, pl.ds(lo, cols)].astype(BF16)


def closing_body(third, table, weight, out):
    tile = out.shape[1]
    for at in range(0, tile, LANES):
        for r, _, value in diffused(third, -HW, table, weight, at, at):
            out[r : r + SUBS, at : at + LANES] = value


def gas_cut_body(n_group, me, species, *outs):
    cols = outs[0].shape[2]
    for s in range(1, n_group):
        goal = lax.rem(me[0] + s, n_group)
        outs[s - 1][...] = species[:, :, pl.ds(pl.multiple_of(goal * cols, LANES), cols)]


def one_hots(listing, count):
    cols = listing.shape[-1]
    half = cols // 2
    label = iota((cols, half), 0)
    slot = iota((cols, half), 1)
    first = jnp.broadcast_to(listing[0, :, 0:half], (cols, half))
    last = jnp.broadcast_to(listing[0, :, half:cols], (cols, half))
    kept = jnp.where((first == label) & (slot < count), 1.0, 0.0)
    sent = jnp.where((last == label) & (slot + half < count), 1.0, 0.0)
    return first == label, last == label, kept.astype(BF16), sent.astype(BF16)


def gas_join_body(
    n_group, me, count, species, *rest
):
    arrived, rest = rest[: n_group - 1], rest[n_group - 1 :]
    listing, zenith, packed, outgoing, kept_x, kept_cos, slot_of, spread = rest
    gases, slab, _ = species.shape
    cols = packed.shape[2]
    half = cols // 2
    spread[...] = jnp.zeros_like(spread)
    for s in range(n_group):
        source = lax.rem(me[0] + n_group - s, n_group)
        for lo in range(0, cols, LANES):
            for f in range(gases):
                if s == 0:
                    at = pl.multiple_of(me[0] * cols + lo, LANES)
                    value = species[f, :, pl.ds(at, LANES)]
                else:
                    value = arrived[s - 1][f, :, lo : lo + LANES]
                spread[(f + 1) * slab : (f + 2) * slab, :] = value.astype(F32)
            for l in range(slab):
                packed[source * slab + l, :, lo : lo + LANES] = spread[pl.ds(l, SUBS, stride=slab), :]
    hit_first, hit_last, kept, sent = one_hots(listing, count[0, 0])
    levels = packed.shape[0]
    flat = packed[...].reshape(levels * SUBS, cols).astype(BF16)
    outgoing[0 : levels * SUBS, :] = mm(flat, sent).astype(BF16)
    kept_x[...] = mm(flat, kept)
    cosine = jnp.broadcast_to(zenith[0].astype(F32), (2 * SUBS, cols)).astype(BF16)
    outgoing[levels * SUBS :, :] = mm(cosine, sent).astype(BF16)
    kept_cos[...] = mm(cosine, kept)[0:SUBS]
    hits = jnp.concatenate([hit_first, hit_last], axis=1)
    hits = jnp.where(hits, 1.0, 0.0).astype(BF16)
    numbers = iota((2 * SUBS, cols), 1).astype(F32).astype(BF16)
    found = lax.dot_general(
        numbers, hits, (((1,), (1,)), ((), ())), preferred_element_type=F32
    )
    slot_of[...] = found[0:SUBS].astype(jnp.int32)


def warm_join_body(n_group, me, count, *rest):
    pieces, (listing, warm, outgoing, kept_warm) = rest[:n_group], rest[n_group:]
    slab = pieces[0].shape[0]
    for s in range(n_group):
        source = lax.rem(me[0] + n_group - s, n_group)
        lo = pl.multiple_of(source * slab, SUBS)
        warm[pl.ds(lo, slab), :] = pieces[s][...].astype(F32)
    _, _, kept, sent = one_hots(listing, count[0, 0])
    flat = warm[...].astype(BF16)
    outgoing[...] = mm(flat, sent).astype(BF16)
    kept_warm[...] = mm(flat, kept)


def softplus(z):
    return jnp.maximum(z, jnp.log(1.0 + jnp.exp(jnp.minimum(z, 80.0))))


def sweep(x_at, warm_at, first, bias, second, heads, gpts, rate, both, buffers, levels):
    hid_a, hid_b, z_a, z_b, trans, parts = buffers
    steps = levels // STEP_LEVELS
    top = iota((SUBS, LANES), 0) == 0

    def hidden(pair, odd, out):
        pair = jnp.minimum(pair, steps // 2 - 1)
        warm = warm_at(pl.multiple_of(pair * SUBS, SUBS))
        tiles = []
        for i in range(odd * STEP_LEVELS, (odd + 1) * STEP_LEVELS):
            row = jnp.broadcast_to(warm[i : i + 1], (SUBS, LANES))
            tiles.append(jnp.where(top, row, x_at(pair * SUBS + i)))
        x = jnp.concatenate(tiles, axis=1).astype(BF16)
        v = mm(first[...], x) + bias[...]
        one = (v + v * jnp.tanh(v)).astype(BF16)
        v = mm(second[...], one)
        out[...] = (v + v * jnp.tanh(v)).astype(BF16)

    def optics(hid, out):
        out[...] = mm(heads[...], hid[...])

    def consume(t, z):
        total = [None] * STEP_LEVELS
        for lo in range(0, gpts, SUBS):
            carry = trans[lo : lo + SUBS, :]
            for i in range(STEP_LEVELS):
                at = i * LANES
                depth = softplus(z[lo : lo + SUBS, at : at + LANES])
                following = carry * jnp.exp2(depth * rate)
                drop = carry - following
                if both:
                    drop = drop * softplus(z[gpts + lo : gpts + lo + SUBS, at : at + LANES])
                total[i] = drop if total[i] is None else total[i] + drop
                carry = following
            trans[lo : lo + SUBS, :] = carry
        for i in range(STEP_LEVELS):
            at = pl.multiple_of((t * STEP_LEVELS + i) * SUBS, SUBS)
            parts[pl.ds(at, SUBS), :] = total[i]

    hidden(0, 0, hid_a)
    optics(hid_a, z_a)
    hidden(0, 1, hid_b)

    def two(i, _):
        t = 2 * i
        consume(t, z_a)
        optics(hid_b, z_b)
        hidden(i + 1, 0, hid_a)
        consume(t + 1, z_b)
        optics(hid_a, z_a)
        hidden(i + 1, 1, hid_b)
        return 0

    lax.fori_loop(0, steps // 2, two, 0)
    emitted = parts[pl.ds(0, levels, stride=SUBS), :]
    for s in range(1, SUBS):
        emitted = emitted + parts[pl.ds(s, levels, stride=SUBS), :]
    return emitted


def sweep_scratch(hid, rows, gpts, levels):
    wide = STEP_LEVELS * LANES
    return [
        pltpu.VMEM((hid, wide), BF16),
        pltpu.VMEM((hid, wide), BF16),
        pltpu.VMEM((rows, wide), F32),
        pltpu.VMEM((rows, wide), F32),
        pltpu.VMEM((gpts, LANES), F32),
        pltpu.VMEM((levels * SUBS, LANES), F32),
    ]


def longwave_part(lo, packed, warm, first, bias, second, heads, buffers):
    gpts = heads.shape[0] // 2
    levels = packed.shape[0]
    buffers[4][...] = jnp.ones_like(buffers[4])
    emitted = sweep(
        lambda l: packed[l, :, lo : lo + LANES],
        lambda l: warm[pl.ds(l, SUBS), lo : lo + LANES],
        first, bias, second, heads, gpts, -depth_scale * LOG2E, True, buffers, levels,
    )
    planck = jnp.exp(0.25 * warm[:, lo : lo + LANES])
    return -(heat_scale / gpts) * planck * emitted


def longwave_body(packed, warm, first, bias, second, heads, out, *buffers):
    out[...] = longwave_part(0, packed, warm, first, bias, second, heads, buffers)


def shortwave_body(
    count, kept_x, kept_warm, kept_cos, in_x, in_warm, first, bias, second, heads, flux, out,
    work_x, work_warm, *buffers
):
    levels = kept_warm.shape[0]
    half = kept_warm.shape[1]
    gpts = heads.shape[0]
    slot = iota((half, half), 1) - count[0, 0]
    placed = jnp.where(slot == iota((half, half), 0), 1.0, 0.0).astype(BF16)
    cells = levels * SUBS
    work_x[...] = kept_x[...] + mm(in_x[0:cells, :], placed)
    work_warm[...] = kept_warm[...] + mm(in_warm[...], placed)
    cosine = kept_cos[...] + mm(in_x[cells:, :], placed)[0:SUBS]
    cosine = jnp.where(cosine > 0.0, cosine, 1.0)
    buffers[4][...] = jnp.broadcast_to(flux[...], buffers[4].shape)
    emitted = sweep(
        lambda l: work_x[pl.ds(pl.multiple_of(l * SUBS, SUBS), SUBS), :],
        lambda l: work_warm[pl.ds(l, SUBS), :],
        first, bias, second, heads, gpts, (-depth_scale * LOG2E) / cosine, False, buffers, levels,
    )
    out[...] = (heat_scale / gpts) * cosine[0:1] * emitted


def finish_body(
    n_group, me, count, packed, warm, first, bias, second, heads, long_first, work, partner, slot_of,
    *rest
):
    pieces, heat, buffers = rest[:n_group], rest[n_group], rest[n_group + 1 :]
    levels, cols = heat.shape
    half = cols // 2
    slab = pieces[0].shape[0]
    sunlit = count[0, 0]
    long_last = longwave_part(half, packed, warm, first, bias, second, heads, buffers)
    for lo, long in ((0, long_first[...]), (half, long_last)):
        slot = slot_of[:, lo : lo + half]
        here = slot < half
        place = jnp.where(here, slot, slot + half - sunlit) & (half - 1)
        lit = slot < sunlit
        for r in range(0, levels, SUBS):
            near = lane_take(work[r : r + SUBS, :], place)
            far = lane_take(partner[r : r + SUBS, :], place)
            short = jnp.where(lit, jnp.where(here, near, far), 0.0)
            heat[r : r + SUBS, lo : lo + half] = long[r : r + SUBS] + short
    for s in range(n_group):
        goal = lax.rem(me[0] + s, n_group)
        pieces[s][...] = heat[pl.ds(pl.multiple_of(goal * slab, SUBS), slab), :]


def add_body(n_group, me, closed, *rest):
    pieces, out = rest[:n_group], rest[n_group]
    cols = pieces[0].shape[1]
    for s in range(n_group):
        source = lax.rem(me[0] + n_group - s, n_group)
        at = pl.ds(pl.multiple_of(source * cols, LANES), cols)
        out[:, at] = closed[:, at] + pieces[s][...]


def per_device(
    potential, species, diffusion, neighbours, listing, day_count, zenith,
    lw_first, lw_bias, lw_second, lw_depth, lw_fraction,
    sw_first, sw_bias, sw_second, sw_depth, solar_flux,
):
    n_group = lax.axis_size("group")
    n_tile = lax.axis_size("tile")
    me = lax.axis_index("group").astype(jnp.int32).reshape(1)
    slab, tile = potential.shape
    gases = species.shape[0]
    cols = tile // n_group
    half = cols // 2
    levels = slab * n_group

    def turned(value, by):
        return lax.ppermute(value, "tile", [(i, (i + by) % n_tile) for i in range(n_tile)])

    def along(value, by):
        return lax.ppermute(value, "group", [(i, (i + by) % n_group) for i in range(n_group)])

    def paired(value):
        return lax.ppermute(value, "tile", [(i, i ^ 1) for i in range(n_tile)])

    framing = (potential, neighbours, diffusion)
    left = [turned(a, 1) for a in framing]
    right = [turned(a, -1) for a in framing]

    cuts = call(
        functools.partial(gas_cut_body, n_group),
        [shaped((gases, slab, cols), BF16)] * (n_group - 1),
        [me, species],
    )
    arrived = [along(c, s + 1) for s, c in enumerate(cuts)]

    lw_one = (0.5 * lw_first).T
    lw_two = (0.5 * lw_second).T
    lw_heads = jnp.concatenate([lw_depth, lw_fraction], axis=1).T
    lw_shift = (0.5 * lw_bias)[:, None]
    sw_one = (0.5 * sw_first).T
    sw_two = (0.5 * sw_second).T
    sw_heads = sw_depth.T
    sw_shift = (0.5 * sw_bias)[:, None]
    flux = solar_flux[:, None]
    hid = lw_first.shape[1]
    long_weights = [lw_one, lw_shift, lw_two, lw_heads]
    short_weights = [sw_one, sw_shift, sw_two, sw_heads, flux]

    third, *warm_cuts = call(
        functools.partial(sections_body, n_group),
        [shaped((slab, tile + 2 * HW), F32)] + [shaped((slab, cols), BF16)] * n_group,
        [me, left[0], potential, right[0], left[1], neighbours, right[1], left[2], diffusion, right[2]],
        [pltpu.VMEM((slab, 3 * tile), F32)] * 3,
        flops=10_000_000,
    )
    warm_pieces = [warm_cuts[0]] + [along(c, s + 1) for s, c in enumerate(warm_cuts[1:])]

    packed, out_x, kept_x, kept_cos, slot_of = call(
        functools.partial(gas_join_body, n_group),
        [
            shaped((levels, SUBS, cols), F32),
            shaped((levels * SUBS + 2 * SUBS, half), BF16),
            shaped((levels * SUBS, half), F32),
            shaped((SUBS, half), F32),
            shaped((SUBS, cols), jnp.int32),
        ],
        [me, day_count, species, *arrived, listing, zenith],
        [pltpu.VMEM((SUBS * slab, LANES), F32)],
    )
    in_x = paired(out_x)

    (closed,) = call(
        closing_body, [shaped((slab, tile), F32)], [third, neighbours, diffusion], flops=2_000_000
    )

    warm, out_warm, kept_warm = call(
        functools.partial(warm_join_body, n_group),
        [
            shaped((levels, cols), F32),
            shaped((levels, half), BF16),
            shaped((levels, half), F32),
        ],
        [me, day_count, *warm_pieces, listing],
    )
    in_warm = paired(out_warm)

    lw_rows = lw_heads.shape[0]
    lw_scratch = sweep_scratch(hid, lw_rows, lw_rows // 2, levels)
    lw_cells = levels * half
    (long_first,) = call(
        longwave_body,
        [shaped((levels, half), F32)],
        [packed, warm, *long_weights],
        lw_scratch,
        flops=2 * lw_cells * hid * lw_rows,
        trans=5 * lw_cells * lw_rows // 2,
    )
    sw_rows = sw_heads.shape[0]
    (work,) = call(
        shortwave_body,
        [shaped((levels, half), F32)],
        [day_count, kept_x, kept_warm, kept_cos, in_x, in_warm, *short_weights],
        [pltpu.VMEM((levels * SUBS, half), F32), pltpu.VMEM((levels, half), F32)]
        + sweep_scratch(hid, sw_rows, sw_rows, levels),
        flops=2 * lw_cells * hid * sw_rows,
        trans=3 * lw_cells * sw_rows,
    )
    partner = paired(work)
    heat_cuts = call(
        functools.partial(finish_body, n_group),
        [shaped((slab, cols), F32)] * n_group,
        [me, day_count, packed, warm, *long_weights, long_first, work, partner, slot_of],
        [pltpu.VMEM((levels, cols), F32)] + lw_scratch,
        flops=2 * lw_cells * hid * lw_rows,
        trans=5 * lw_cells * lw_rows // 2,
    )
    heat_pieces = [heat_cuts[0]] + [along(c, s + 1) for s, c in enumerate(heat_cuts[1:])]
    (evolved,) = call(
        functools.partial(add_body, n_group),
        [shaped((slab, tile), F32)],
        [me, closed, *heat_pieces],
    )
    return evolved


def solution(mesh):
    return jax.shard_map(
        per_device,
        mesh=mesh,
        in_specs=(
            P("group", "tile"),
            P(None, "group", "tile"),
            P(None, "tile"),
            P(None, "tile"),
            P("group", "tile", None),
            P("group", "tile"),
            P("group", "tile", None),
            *([P()] * 10),
        ),
        out_specs=P("group", "tile"),
        check_vma=False,
    )
```

```python
import functools
import math

import jax
import jax.numpy as jnp
from jax import lax
from jax.experimental import pallas as pl
from jax.experimental.pallas import tpu as pltpu
from jax.sharding import PartitionSpec as P

HW = 256
LANES = 128
SUBS = 8
STEP_LEVELS = SUBS // 2
TILE = 2 * LANES

depth_scale = 0.1
heat_scale = 12.0
LOG2E = 1.4426950408889634

F32 = jnp.float32
BF16 = jnp.bfloat16
VMEM = pl.BlockSpec(memory_space=pltpu.VMEM)
SMEM = pl.BlockSpec(memory_space=pltpu.SMEM)
PARAMS = pltpu.CompilerParams(vmem_limit_bytes=48 * 1024 * 1024)


def call(body, outs, ins, scratch=(), flops=0, trans=0, specs=None):
    return pl.pallas_call(
        body,
        out_shape=outs,
        in_specs=specs or [SMEM if a.size == 1 else VMEM for a in ins],
        out_specs=[VMEM for _ in outs],
        scratch_shapes=list(scratch),
        compiler_params=PARAMS,
        cost_estimate=pl.CostEstimate(
            flops=flops,
            transcendentals=trans,
            bytes_accessed=sum(a.size * a.dtype.itemsize for a in list(ins) + list(outs)),
        ),
    )(*ins)


def shaped(shape, dtype):
    return jax.ShapeDtypeStruct(shape, dtype)


def iota(shape, dim):
    return lax.broadcasted_iota(jnp.int32, shape, dim)


def mm(a, b):
    return jnp.dot(a, b, preferred_element_type=F32)


def lane_take(x, idx):
    return jnp.take_along_axis(x, idx, axis=1, mode="promise_in_bounds")


def diffused(src, src_at, table, weight, within, at):
    reach = HW // LANES
    wide = 2 * reach + 1
    rows = src.shape[0]
    groups = range(0, rows, SUBS)
    base = at - src_at
    middle = [src[r : r + SUBS, base : base + LANES] for r in groups]
    total = [jnp.zeros_like(m) for m in middle]
    for k in range(table.shape[0]):
        place = jnp.broadcast_to(table[k : k + 1, within : within + LANES], (SUBS, LANES)) - within
        lane = place & (LANES - 1)
        which = place >> (LANES.bit_length() - 1)
        factor = jnp.broadcast_to(weight[k : k + 1, within : within + LANES], (SUBS, LANES))
        tests = [which == w for w in range(1, wide)]
        for n, r in enumerate(groups):
            near = None
            for w in range(wide):
                lo = base + (w - reach) * LANES
                got = lane_take(src[r : r + SUBS, lo : lo + LANES], lane)
                near = got if w == 0 else jnp.where(tests[w - 1], got, near)
            total[n] = total[n] + factor * (near - middle[n])
    return [(r, m, m + t) for r, m, t in zip(groups, middle, total)]


def sections_body(n_group, me, left, own, right, table, weight, third_out, *rest):
    pieces, (frame, first, second, tables, weights) = rest[:n_group], rest[n_group:]
    slab, tile = own.shape
    near = table.shape[0]
    cols = tile // n_group
    for t, packed in ((0, left), (2, right)):
        at = slice(t * tile, (t + 1) * tile)
        frame[:, at] = packed[0:slab, :]
        tables[t] = packed[slab : slab + near, :].astype(jnp.int32)
        weights[t] = packed[slab + near : slab + 2 * near, :]
    frame[:, tile : 2 * tile] = own[...]
    tables[1] = table[...]
    weights[1] = weight[...]

    def run(src, src_at, halo, put):
        for at in range(tile - halo, 2 * tile + halo, LANES):
            t = at // tile
            for r, _, value in diffused(src, src_at, tables.at[t], weights.at[t], at - t * tile, at):
                put(r, at, value)

    def put_first(r, at, value):
        first[r : r + SUBS, at : at + LANES] = value

    def put_second(r, at, value):
        start = frame[r : r + SUBS, at : at + LANES]
        second[r : r + SUBS, at : at + LANES] = 0.75 * start + 0.25 * value

    def put_third(r, at, value):
        start = frame[r : r + SUBS, at : at + LANES]
        lo = at - tile + HW
        third_out[r : r + SUBS, lo : lo + LANES] = start / 3.0 + (2.0 / 3.0) * value

    run(frame, 0, 3 * HW, put_first)
    run(first, 0, 2 * HW, put_second)
    run(second, 0, HW, put_third)
    mine = me[0]
    for s in range(n_group):
        goal = lax.rem(mine + s, n_group)
        lo = pl.multiple_of(HW + goal * cols, LANES)
        pieces[s][...] = third_out[:, pl.ds(lo, cols)].astype(BF16)


def closing_body(third, table, weight, out):
    tile = out.shape[1]
    for at in range(0, tile, LANES):
        for r, _, value in diffused(third, -HW, table, weight, at, at):
            out[r : r + SUBS, at : at + LANES] = value


def one_hots(listing, count):
    cols = listing.shape[-1]
    half = cols // 2
    label = iota((cols, half), 0)
    slot = iota((cols, half), 1)
    first = jnp.broadcast_to(listing[0, :, 0:half], (cols, half))
    last = jnp.broadcast_to(listing[0, :, half:cols], (cols, half))
    kept = jnp.where((first == label) & (slot < count), 1.0, 0.0)
    sent = jnp.where((last == label) & (slot + half < count), 1.0, 0.0)
    return first == label, last == label, kept.astype(BF16), sent.astype(BF16)


def gas_join_body(
    me, count, gathered, listing, zenith, packed, outgoing, kept_x, kept_cos, slot_of, spread
):
    n_group, gases, slab, _ = gathered.shape
    cols = packed.shape[2]
    half = cols // 2
    spread[...] = jnp.zeros_like(spread)
    for s in range(n_group):
        for lo in range(0, cols, LANES):
            at = pl.multiple_of(me[0] * cols + lo, LANES)
            for f in range(gases):
                value = gathered[s, f, :, pl.ds(at, LANES)]
                spread[(f + 1) * slab : (f + 2) * slab, :] = value.astype(F32)
            for l in range(slab):
                packed[s * slab + l, :, lo : lo + LANES] = spread[pl.ds(l, SUBS, stride=slab), :]
    hit_first, hit_last, kept, sent = one_hots(listing, count[0, 0])
    levels = packed.shape[0]
    flat = packed[...].reshape(levels * SUBS, cols).astype(BF16)
    outgoing[0 : levels * SUBS, :] = mm(flat, sent).astype(BF16)
    kept_x[...] = mm(flat, kept)
    cosine = jnp.broadcast_to(zenith[0].astype(F32), (2 * SUBS, cols)).astype(BF16)
    outgoing[levels * SUBS :, :] = mm(cosine, sent).astype(BF16)
    kept_cos[...] = mm(cosine, kept)[0:SUBS]
    hits = jnp.concatenate([hit_first, hit_last], axis=1)
    hits = jnp.where(hits, 1.0, 0.0).astype(BF16)
    numbers = iota((2 * SUBS, cols), 1).astype(F32).astype(BF16)
    found = lax.dot_general(
        numbers, hits, (((1,), (1,)), ((), ())), preferred_element_type=F32
    )
    slot_of[...] = found[0:SUBS].astype(jnp.int32)


def warm_join_body(n_group, me, count, *rest):
    pieces, (listing, warm, outgoing, kept_warm) = rest[:n_group], rest[n_group:]
    slab = pieces[0].shape[0]
    for s in range(n_group):
        source = lax.rem(me[0] + n_group - s, n_group)
        lo = pl.multiple_of(source * slab, SUBS)
        warm[pl.ds(lo, slab), :] = pieces[s][...].astype(F32)
    _, _, kept, sent = one_hots(listing, count[0, 0])
    flat = warm[...].astype(BF16)
    outgoing[...] = mm(flat, sent).astype(BF16)
    kept_warm[...] = mm(flat, kept)


def softplus(z):
    return jnp.maximum(z, jnp.log(1.0 + jnp.exp(jnp.minimum(z, 80.0))))


def sweep(x_at, warm_at, first, bias, second, heads, gpts, rate, both, buffers, levels):
    one_a, one_b, hid_a, hid_b, z_a, z_b, trans, parts = buffers
    steps = levels // STEP_LEVELS
    top = iota((SUBS, LANES), 0) == 0
    wide = STEP_LEVELS * LANES
    rows = heads.shape[0]
    row_cut = rows // (4 if both else 2)

    def first_tasks(pair, odd, out):
        pair = jnp.minimum(pair, steps // 2 - 1)

        def task(lo):
            warm = warm_at(pl.multiple_of(pair * SUBS, SUBS))
            tiles = []
            for at in range(lo, lo + TILE, LANES):
                i = odd * STEP_LEVELS + at // LANES
                row = jnp.broadcast_to(warm[i : i + 1], (SUBS, LANES))
                tiles.append(jnp.where(top, row, x_at(pair * SUBS + i)))
            x = jnp.concatenate(tiles, axis=1).astype(BF16)
            v = mm(first[...], x) + bias[...]
            out[:, lo : lo + TILE] = (v + v * jnp.tanh(v)).astype(BF16)

        return [functools.partial(task, lo) for lo in range(0, wide, TILE)]

    def second_tasks(one, out):
        def task(lo):
            v = mm(second[...], one[:, lo : lo + TILE])
            out[:, lo : lo + TILE] = (v + v * jnp.tanh(v)).astype(BF16)

        return [functools.partial(task, lo) for lo in range(0, wide, TILE)]

    def optics_tasks(hid, out):
        def task(lo, r):
            out[r : r + row_cut, lo : lo + TILE] = mm(heads[r : r + row_cut, :], hid[:, lo : lo + TILE])

        return [
            functools.partial(task, lo, r)
            for lo in range(0, wide, TILE)
            for r in range(0, rows, row_cut)
        ]

    def consume_tasks(t, z, total):
        def task(lo):
            carry = trans[lo : lo + SUBS, :]
            for i in range(STEP_LEVELS):
                at = i * LANES
                depth = softplus(z[lo : lo + SUBS, at : at + LANES])
                following = carry * jnp.exp2(depth * rate)
                drop = carry - following
                if both:
                    drop = drop * softplus(z[gpts + lo : gpts + lo + SUBS, at : at + LANES])
                total[i] = drop if total[i] is None else total[i] + drop
                carry = following
            trans[lo : lo + SUBS, :] = carry

        return [functools.partial(task, lo) for lo in range(0, gpts, SUBS)]

    def woven(main, side):
        done = 0
        for n, task in enumerate(main):
            while done < len(side) and done * len(main) <= n * len(side):
                side[done]()
                done += 1
            task()
        for task in side[done:]:
            task()

    def plain(tasks):
        for task in tasks:
            task()

    def step(t, pair, odd, z, z_next, hid_next, hid_later, one_later, one_last):
        total = [None] * STEP_LEVELS
        side = (
            optics_tasks(hid_next, z_next)
            + second_tasks(one_later, hid_later)
            + first_tasks(pair, odd, one_last)
        )
        woven(consume_tasks(t, z, total), side)
        for i in range(STEP_LEVELS):
            at = pl.multiple_of((t * STEP_LEVELS + i) * SUBS, SUBS)
            parts[pl.ds(at, SUBS), :] = total[i]

    plain(first_tasks(0, 0, one_a))
    plain(second_tasks(one_a, hid_a))
    plain(first_tasks(0, 1, one_b))
    plain(optics_tasks(hid_a, z_a))
    plain(second_tasks(one_b, hid_b))
    plain(first_tasks(1, 0, one_a))

    def two(i, _):
        step(2 * i, i + 1, 1, z_a, z_b, hid_b, hid_a, one_a, one_b)
        step(2 * i + 1, i + 2, 0, z_b, z_a, hid_a, hid_b, one_b, one_a)
        return 0

    lax.fori_loop(0, steps // 2, two, 0)
    emitted = parts[pl.ds(0, levels, stride=SUBS), :]
    for s in range(1, SUBS):
        emitted = emitted + parts[pl.ds(s, levels, stride=SUBS), :]
    return emitted


def sweep_scratch(hid, rows, gpts, levels):
    wide = STEP_LEVELS * LANES
    return [
        pltpu.VMEM((hid, wide), BF16),
        pltpu.VMEM((hid, wide), BF16),
        pltpu.VMEM((hid, wide), BF16),
        pltpu.VMEM((hid, wide), BF16),
        pltpu.VMEM((rows, wide), F32),
        pltpu.VMEM((rows, wide), F32),
        pltpu.VMEM((gpts, LANES), F32),
        pltpu.VMEM((levels * SUBS, LANES), F32),
    ]


def longwave_part(lo, packed, warm, first, bias, second, heads, buffers):
    gpts = heads.shape[0] // 2
    levels = packed.shape[0]
    buffers[6][...] = jnp.ones_like(buffers[6])
    emitted = sweep(
        lambda l: packed[l, :, lo : lo + LANES],
        lambda l: warm[pl.ds(l, SUBS), lo : lo + LANES],
        first, bias, second, heads, gpts, -depth_scale * LOG2E, True, buffers, levels,
    )
    planck = jnp.exp(0.25 * warm[:, lo : lo + LANES])
    return -(heat_scale / gpts) * planck * emitted


def longwave_body(packed, warm, first, bias, second, heads, out, *buffers):
    out[...] = longwave_part(0, packed, warm, first, bias, second, heads, buffers)


def shortwave_body(
    count, kept_x, kept_warm, kept_cos, in_x, in_warm, first, bias, second, heads, flux, out,
    work_x, work_warm, *buffers
):
    levels = kept_warm.shape[0]
    half = kept_warm.shape[1]
    gpts = heads.shape[0]
    slot = iota((half, half), 1) - count[0, 0]
    placed = jnp.where(slot == iota((half, half), 0), 1.0, 0.0).astype(BF16)
    cells = levels * SUBS
    work_x[...] = kept_x[...] + mm(in_x[0:cells, :], placed)
    work_warm[...] = kept_warm[...] + mm(in_warm[...], placed)
    cosine = kept_cos[...] + mm(in_x[cells:, :], placed)[0:SUBS]
    cosine = jnp.where(cosine > 0.0, cosine, 1.0)
    buffers[6][...] = jnp.broadcast_to(flux[...], buffers[6].shape)
    emitted = sweep(
        lambda l: work_x[pl.ds(pl.multiple_of(l * SUBS, SUBS), SUBS), :],
        lambda l: work_warm[pl.ds(l, SUBS), :],
        first, bias, second, heads, gpts, (-depth_scale * LOG2E) / cosine, False, buffers, levels,
    )
    out[...] = (heat_scale / gpts) * cosine[0:1] * emitted


def finish_body(
    n_group, me, count, packed, warm, first, bias, second, heads, long_first, work, partner, slot_of,
    *rest
):
    pieces, heat, buffers = rest[:n_group], rest[n_group], rest[n_group + 1 :]
    levels, cols = heat.shape
    half = cols // 2
    slab = pieces[0].shape[0]
    sunlit = count[0, 0]
    long_last = longwave_part(half, packed, warm, first, bias, second, heads, buffers)
    for lo, long in ((0, long_first[...]), (half, long_last)):
        slot = slot_of[:, lo : lo + half]
        here = slot < half
        place = jnp.where(here, slot, slot + half - sunlit) & (half - 1)
        lit = slot < sunlit
        for r in range(0, levels, SUBS):
            near = lane_take(work[r : r + SUBS, :], place)
            far = lane_take(partner[r : r + SUBS, :], place)
            short = jnp.where(lit, jnp.where(here, near, far), 0.0)
            heat[r : r + SUBS, lo : lo + half] = long[r : r + SUBS] + short
    for s in range(n_group):
        goal = lax.rem(me[0] + s, n_group)
        pieces[s][...] = heat[pl.ds(pl.multiple_of(goal * slab, SUBS), slab), :]


def add_body(n_group, me, closed, *rest):
    pieces, out = rest[:n_group], rest[n_group]
    cols = pieces[0].shape[1]
    for s in range(n_group):
        source = lax.rem(me[0] + n_group - s, n_group)
        at = pl.ds(pl.multiple_of(source * cols, LANES), cols)
        out[:, at] = closed[:, at] + pieces[s][...]


def per_device(
    potential, species, diffusion, neighbours, listing, day_count, zenith,
    lw_first, lw_bias, lw_second, lw_depth, lw_fraction,
    sw_first, sw_bias, sw_second, sw_depth, solar_flux,
):
    n_group = lax.axis_size("group")
    n_tile = lax.axis_size("tile")
    me = lax.axis_index("group").astype(jnp.int32).reshape(1)
    slab, tile = potential.shape
    cols = tile // n_group
    half = cols // 2
    levels = slab * n_group

    def turned(value, by):
        return lax.ppermute(value, "tile", [(i, (i + by) % n_tile) for i in range(n_tile)])

    def along(value, by):
        return lax.ppermute(value, "group", [(i, (i + by) % n_group) for i in range(n_group)])

    def paired(value):
        return lax.ppermute(value, "tile", [(i, i ^ 1) for i in range(n_tile)])

    framing = jnp.concatenate([potential, neighbours.astype(F32), diffusion], axis=0)
    left = turned(framing, 1)
    right = turned(framing, -1)
    gathered = lax.all_gather(species, "group")

    lw_one = (0.5 * lw_first).T
    lw_two = (0.5 * lw_second).T
    lw_heads = jnp.concatenate([lw_depth, lw_fraction], axis=1).T
    lw_shift = (0.5 * lw_bias)[:, None]
    sw_one = (0.5 * sw_first).T
    sw_two = (0.5 * sw_second).T
    sw_heads = sw_depth.T
    sw_shift = (0.5 * sw_bias)[:, None]
    flux = solar_flux[:, None]
    hid = lw_first.shape[1]
    long_weights = [lw_one, lw_shift, lw_two, lw_heads]
    short_weights = [sw_one, sw_shift, sw_two, sw_heads, flux]

    third, *warm_cuts = call(
        functools.partial(sections_body, n_group),
        [shaped((slab, tile + 2 * HW), F32)] + [shaped((slab, cols), BF16)] * n_group,
        [me, left, potential, right, neighbours, diffusion],
        [pltpu.VMEM((slab, 3 * tile), F32)] * 3
        + [pltpu.VMEM((3, *neighbours.shape), jnp.int32), pltpu.VMEM((3, *diffusion.shape), F32)],
        flops=10_000_000,
    )
    warm_pieces = [warm_cuts[0]] + [along(c, s + 1) for s, c in enumerate(warm_cuts[1:])]

    packed, out_x, kept_x, kept_cos, slot_of = call(
        gas_join_body,
        [
            shaped((levels, SUBS, cols), F32),
            shaped((levels * SUBS + 2 * SUBS, half), BF16),
            shaped((levels * SUBS, half), F32),
            shaped((SUBS, half), F32),
            shaped((SUBS, cols), jnp.int32),
        ],
        [me, day_count, gathered, listing, zenith],
        [pltpu.VMEM((SUBS * slab, LANES), F32)],
    )
    in_x = paired(out_x)

    (closed,) = call(
        closing_body, [shaped((slab, tile), F32)], [third, neighbours, diffusion], flops=2_000_000
    )

    warm, out_warm, kept_warm = call(
        functools.partial(warm_join_body, n_group),
        [
            shaped((levels, cols), F32),
            shaped((levels, half), BF16),
            shaped((levels, half), F32),
        ],
        [me, day_count, *warm_pieces, listing],
    )
    in_warm = paired(out_warm)

    lw_rows = lw_heads.shape[0]
    lw_scratch = sweep_scratch(hid, lw_rows, lw_rows // 2, levels)
    lw_cells = levels * half
    (long_first,) = call(
        longwave_body,
        [shaped((levels, half), F32)],
        [packed, warm, *long_weights],
        lw_scratch,
        flops=2 * lw_cells * hid * lw_rows,
        trans=5 * lw_cells * lw_rows // 2,
    )
    sw_rows = sw_heads.shape[0]
    (work,) = call(
        shortwave_body,
        [shaped((levels, half), F32)],
        [day_count, kept_x, kept_warm, kept_cos, in_x, in_warm, *short_weights],
        [pltpu.VMEM((levels * SUBS, half), F32), pltpu.VMEM((levels, half), F32)]
        + sweep_scratch(hid, sw_rows, sw_rows, levels),
        flops=2 * lw_cells * hid * sw_rows,
        trans=3 * lw_cells * sw_rows,
    )
    partner = paired(work)
    heat_cuts = call(
        functools.partial(finish_body, n_group),
        [shaped((slab, cols), F32)] * n_group,
        [me, day_count, packed, warm, *long_weights, long_first, work, partner, slot_of],
        [pltpu.VMEM((levels, cols), F32)] + lw_scratch,
        flops=2 * lw_cells * hid * lw_rows,
        trans=5 * lw_cells * lw_rows // 2,
    )
    heat_pieces = [heat_cuts[0]] + [along(c, s + 1) for s, c in enumerate(heat_cuts[1:])]
    (evolved,) = call(
        functools.partial(add_body, n_group),
        [shaped((slab, tile), F32)],
        [me, closed, *heat_pieces],
    )
    return evolved


def solution(mesh):
    return jax.shard_map(
        per_device,
        mesh=mesh,
        in_specs=(
            P("group", "tile"),
            P(None, "group", "tile"),
            P(None, "tile"),
            P(None, "tile"),
            P("group", "tile", None),
            P("group", "tile"),
            P("group", "tile", None),
            *([P()] * 10),
        ),
        out_specs=P("group", "tile"),
        check_vma=False,
    )
```

```python
import functools
import math

import jax
import jax.numpy as jnp
from jax import lax
from jax.experimental import pallas as pl
from jax.experimental.pallas import tpu as pltpu
from jax.sharding import PartitionSpec as P

HW = 256
LANES = 128
SUBS = 8
STEP_LEVELS = SUBS // 2

depth_scale = 0.1
heat_scale = 12.0
LOG2E = 1.4426950408889634

F32 = jnp.float32
BF16 = jnp.bfloat16
VMEM = pl.BlockSpec(memory_space=pltpu.VMEM)
SMEM = pl.BlockSpec(memory_space=pltpu.SMEM)
PARAMS = pltpu.CompilerParams(vmem_limit_bytes=48 * 1024 * 1024)


def call(body, outs, ins, scratch=(), flops=0, trans=0, after=None):
    in_specs = [SMEM if a.size == 1 else VMEM for a in ins]
    if after is not None:
        whole, ins = body, [after, *ins]
        in_specs = [pl.BlockSpec(memory_space=pl.ANY), *in_specs]

        def body(_, *refs):
            whole(*refs)

    return pl.pallas_call(
        body,
        out_shape=outs,
        in_specs=in_specs,
        out_specs=[VMEM for _ in outs],
        scratch_shapes=list(scratch),
        compiler_params=PARAMS,
        cost_estimate=pl.CostEstimate(
            flops=flops,
            transcendentals=trans,
            bytes_accessed=sum(a.size * a.dtype.itemsize for a in list(ins) + list(outs)),
        ),
    )(*ins)


def shaped(shape, dtype):
    return jax.ShapeDtypeStruct(shape, dtype)


def iota(shape, dim):
    return lax.broadcasted_iota(jnp.int32, shape, dim)


def mm(a, b):
    return jnp.dot(a, b, preferred_element_type=F32)


def lane_take(x, idx):
    return jnp.take_along_axis(x, idx, axis=1, mode="promise_in_bounds")


def diffused(src, src_at, table, weight, within, at):
    reach = HW // LANES
    wide = 2 * reach + 1
    rows = src.shape[0]
    groups = range(0, rows, SUBS)
    base = at - src_at
    middle = [src[r : r + SUBS, base : base + LANES] for r in groups]
    total = [jnp.zeros_like(m) for m in middle]
    for k in range(table.shape[0]):
        place = jnp.broadcast_to(table[k : k + 1, within : within + LANES], (SUBS, LANES)) - within
        lane = place & (LANES - 1)
        which = place >> (LANES.bit_length() - 1)
        factor = jnp.broadcast_to(weight[k : k + 1, within : within + LANES], (SUBS, LANES))
        tests = [which == w for w in range(1, wide)]
        for n, r in enumerate(groups):
            near = None
            for w in range(wide):
                lo = base + (w - reach) * LANES
                got = lane_take(src[r : r + SUBS, lo : lo + LANES], lane)
                near = got if w == 0 else jnp.where(tests[w - 1], got, near)
            total[n] = total[n] + factor * (near - middle[n])
    return [(r, m, m + t) for r, m, t in zip(groups, middle, total)]


def pack_body(own, table, weight, out):
    slab = own.shape[0]
    near = table.shape[0]
    out[0:slab, :] = own[...]
    out[slab : slab + near, :] = table[...].astype(F32)
    out[slab + near :, :] = weight[...]


def sections_body(
    me, place, outer, inner, own, table, weight, third_out, leaving, staying,
    frame, first, second, tables, weights,
):
    slab, tile = own.shape
    near = table.shape[0]
    cols = leaving.shape[2]
    odd = place[0] & 1
    for side, packed in ((odd, outer), (1 - odd, inner)):
        at = pl.ds(pl.multiple_of(side * (2 * tile), LANES), tile)
        frame[:, at] = packed[0:slab, :]
        tables[side * 2] = packed[slab : slab + near, :].astype(jnp.int32)
        weights[side * 2] = packed[slab + near : slab + 2 * near, :]
    frame[:, tile : 2 * tile] = own[...]
    tables[1] = table[...]
    weights[1] = weight[...]

    def run(src, src_at, halo, put):
        for at in range(tile - halo, 2 * tile + halo, LANES):
            t = at // tile
            for r, _, value in diffused(src, src_at, tables.at[t], weights.at[t], at - t * tile, at):
                put(r, at, value)

    def put_first(r, at, value):
        first[r : r + SUBS, at : at + LANES] = value

    def put_second(r, at, value):
        start = frame[r : r + SUBS, at : at + LANES]
        second[r : r + SUBS, at : at + LANES] = 0.75 * start + 0.25 * value

    def put_third(r, at, value):
        start = frame[r : r + SUBS, at : at + LANES]
        lo = at - tile + HW
        third_out[r : r + SUBS, lo : lo + LANES] = start / 3.0 + (2.0 / 3.0) * value

    run(frame, 0, 3 * HW, put_first)
    run(first, 0, 2 * HW, put_second)
    run(second, 0, HW, put_third)
    for out, bits in ((leaving, (1, 3)), (staying, (0, 2))):
        for n, bit in enumerate(bits):
            lo = pl.multiple_of(HW + (me[0] ^ bit) * cols, LANES)
            out[n] = third_out[:, pl.ds(lo, cols)].astype(BF16)


def closing_body(third, table, weight, out):
    tile = out.shape[1]
    for at in range(0, tile, LANES):
        for r, _, value in diffused(third, -HW, table, weight, at, at):
            out[r : r + SUBS, at : at + LANES] = value


def gas_cut_body(me, species, leaving):
    cols = leaving.shape[3]
    for n, bit in enumerate((2, 3)):
        leaving[n] = species[:, :, pl.ds(pl.multiple_of((me[0] ^ bit) * cols, LANES), cols)]


def gas_turn_body(me, species, arrived, passing):
    cols = passing.shape[3]
    passing[0] = species[:, :, pl.ds(pl.multiple_of((me[0] ^ 1) * cols, LANES), cols)]
    passing[1] = arrived[1]


def turned_over(matrix):
    return matrix.astype(F32).T


def weights_body(
    w1, b1, w2, wd, wf, v1, c1, v2, vd, flux,
    w1_out, b1_out, w2_out, heads_out, v1_out, c1_out, v2_out, vd_out, flux_out,
):
    for weight, out in ((w1, w1_out), (w2, w2_out), (v1, v1_out), (v2, v2_out)):
        out[...] = (0.5 * turned_over(weight[...])).astype(BF16)
    gpts = wd.shape[1]
    heads_out[0:gpts, :] = turned_over(wd[...]).astype(BF16)
    heads_out[gpts:, :] = turned_over(wf[...]).astype(BF16)
    vd_out[...] = turned_over(vd[...]).astype(BF16)
    for row, out, scale in ((b1, b1_out, 0.5), (c1, c1_out, 0.5), (flux, flux_out, 1.0)):
        out[...] = scale * jnp.broadcast_to(row[...], (LANES, row.shape[1])).T


def turn_body(staying, arrived, passing):
    passing[0] = staying[1]
    passing[1] = arrived[1]


def one_hots(listing, count):
    cols = listing.shape[-1]
    half = cols // 2
    label = iota((cols, half), 0)
    slot = iota((cols, half), 1)
    first = jnp.broadcast_to(listing[0, :, 0:half], (cols, half))
    last = jnp.broadcast_to(listing[0, :, half:cols], (cols, half))
    kept = jnp.where((first == label) & (slot < count), 1.0, 0.0)
    sent = jnp.where((last == label) & (slot + half < count), 1.0, 0.0)
    return first == label, last == label, kept.astype(BF16), sent.astype(BF16)


def gas_join_body(
    me, count, species, near, far, listing, zenith,
    packed, outgoing, kept_x, kept_cos, slot_of, spread,
):
    gases, slab, _ = species.shape
    cols = packed.shape[2]
    half = cols // 2
    spread[...] = jnp.zeros_like(spread)
    for bit in range(4):
        source = me[0] ^ bit
        for lo in range(0, cols, LANES):
            for f in range(gases):
                if bit == 0:
                    value = species[f, :, pl.ds(pl.multiple_of(me[0] * cols + lo, LANES), LANES)]
                elif bit == 2:
                    value = near[0, f, :, lo : lo + LANES]
                else:
                    value = far[bit // 2, f, :, lo : lo + LANES]
                spread[(f + 1) * slab : (f + 2) * slab, :] = value.astype(F32)
            for l in range(slab):
                packed[source * slab + l, :, lo : lo + LANES] = spread[pl.ds(l, SUBS, stride=slab), :]
    hit_first, hit_last, kept, sent = one_hots(listing, count[0, 0])
    levels = packed.shape[0]
    flat = packed[...].reshape(levels * SUBS, cols).astype(BF16)
    outgoing[0 : levels * SUBS, :] = mm(flat, sent).astype(BF16)
    kept_x[...] = mm(flat, kept)
    cosine = jnp.broadcast_to(zenith[0].astype(F32), (2 * SUBS, cols)).astype(BF16)
    outgoing[levels * SUBS :, :] = mm(cosine, sent).astype(BF16)
    kept_cos[...] = mm(cosine, kept)[0:SUBS]
    hits = jnp.concatenate([hit_first, hit_last], axis=1)
    hits = jnp.where(hits, 1.0, 0.0).astype(BF16)
    numbers = iota((2 * SUBS, cols), 1).astype(F32).astype(BF16)
    found = lax.dot_general(
        numbers, hits, (((1,), (1,)), ((), ())), preferred_element_type=F32
    )
    slot_of[...] = found[0:SUBS].astype(jnp.int32)


def sources(me, staying, near, far):
    return ((me, staying[0]), (me ^ 1, near[0]), (me ^ 2, far[0]), (me ^ 3, far[1]))


def warm_join_body(me, count, staying, near, far, listing, warm, outgoing, kept_warm):
    slab = staying.shape[1]
    for source, piece in sources(me[0], staying, near, far):
        warm[pl.ds(pl.multiple_of(source * slab, SUBS), slab), :] = piece.astype(F32)
    _, _, kept, sent = one_hots(listing, count[0, 0])
    flat = warm[...].astype(BF16)
    outgoing[...] = mm(flat, sent).astype(BF16)
    kept_warm[...] = mm(flat, kept)


def softplus(z):
    return jnp.maximum(z, jnp.log(1.0 + jnp.exp(jnp.minimum(z, 80.0))))


def sweep(x_at, warm_at, first, bias, second, heads, gpts, rate, both, buffers, levels):
    one_a, one_b, hid_a, hid_b, z_a, z_b, trans, parts = buffers
    steps = levels // STEP_LEVELS
    top = iota((SUBS, LANES), 0) == 0
    wide = STEP_LEVELS * LANES
    rows = heads.shape[0]
    row_cut = rows // (8 if both else 4)
    units = first.shape[0]
    unit_cut = units // 2

    def first_tasks(pair, odd, out):
        pair = jnp.minimum(pair, steps // 2 - 1)

        def task(r):
            warm = warm_at(pl.multiple_of(pair * SUBS, SUBS))
            tiles = []
            for i in range(odd * STEP_LEVELS, (odd + 1) * STEP_LEVELS):
                row = jnp.broadcast_to(warm[i : i + 1], (SUBS, LANES))
                tiles.append(jnp.where(top, row, x_at(pair * SUBS + i)))
            x = jnp.concatenate(tiles, axis=1).astype(BF16)
            v = mm(first[r : r + unit_cut, :], x)
            shift = bias[r : r + unit_cut, :]
            v = v + jnp.concatenate([shift] * STEP_LEVELS, axis=1)
            out[r : r + unit_cut, :] = (v + v * jnp.tanh(v)).astype(BF16)

        return [functools.partial(task, r) for r in range(0, units, unit_cut)]

    def second_tasks(one, out):
        def task(r):
            v = mm(second[r : r + unit_cut, :], one[...])
            out[r : r + unit_cut, :] = (v + v * jnp.tanh(v)).astype(BF16)

        return [functools.partial(task, r) for r in range(0, units, unit_cut)]

    def optics_tasks(hid, out):
        def task(r):
            out[r : r + row_cut, :] = mm(heads[r : r + row_cut, :], hid[...])

        return [functools.partial(task, r) for r in range(0, rows, row_cut)]

    def consume_tasks(t, z, total):
        def task(lo):
            carry = trans[lo : lo + SUBS, :]
            for i in range(STEP_LEVELS):
                at = i * LANES
                depth = softplus(z[lo : lo + SUBS, at : at + LANES])
                following = carry * jnp.exp2(depth * rate)
                drop = carry - following
                if both:
                    drop = drop * softplus(z[gpts + lo : gpts + lo + SUBS, at : at + LANES])
                total[i] = drop if total[i] is None else total[i] + drop
                carry = following
            trans[lo : lo + SUBS, :] = carry

        return [functools.partial(task, lo) for lo in range(0, gpts, SUBS)]

    def woven(main, side):
        done = 0
        for n, task in enumerate(main):
            while done < len(side) and done * len(main) <= n * len(side):
                side[done]()
                done += 1
            task()
        for task in side[done:]:
            task()

    def plain(tasks):
        for task in tasks:
            task()

    def step(t, pair, odd, z, z_next, hid_next, hid_later, one_later, one_last):
        total = [None] * STEP_LEVELS
        side = (
            optics_tasks(hid_next, z_next)
            + second_tasks(one_later, hid_later)
            + first_tasks(pair, odd, one_last)
        )
        woven(consume_tasks(t, z, total), side)
        for i in range(STEP_LEVELS):
            at = pl.multiple_of((t * STEP_LEVELS + i) * SUBS, SUBS)
            parts[pl.ds(at, SUBS), :] = total[i]

    plain(first_tasks(0, 0, one_a))
    plain(second_tasks(one_a, hid_a))
    plain(first_tasks(0, 1, one_b))
    plain(optics_tasks(hid_a, z_a))
    plain(second_tasks(one_b, hid_b))
    plain(first_tasks(1, 0, one_a))

    def two(i, _):
        step(2 * i, i + 1, 1, z_a, z_b, hid_b, hid_a, one_a, one_b)
        step(2 * i + 1, i + 2, 0, z_b, z_a, hid_a, hid_b, one_b, one_a)
        return 0

    lax.fori_loop(0, steps // 2, two, 0)
    emitted = parts[pl.ds(0, levels, stride=SUBS), :]
    for s in range(1, SUBS):
        emitted = emitted + parts[pl.ds(s, levels, stride=SUBS), :]
    return emitted


def sweep_scratch(hid, rows, gpts, levels):
    wide = STEP_LEVELS * LANES
    return [
        pltpu.VMEM((hid, wide), BF16),
        pltpu.VMEM((hid, wide), BF16),
        pltpu.VMEM((hid, wide), BF16),
        pltpu.VMEM((hid, wide), BF16),
        pltpu.VMEM((rows, wide), F32),
        pltpu.VMEM((rows, wide), F32),
        pltpu.VMEM((gpts, LANES), F32),
        pltpu.VMEM((levels * SUBS, LANES), F32),
    ]


def longwave_part(lo, packed, warm, first, bias, second, heads, buffers):
    gpts = heads.shape[0] // 2
    levels = packed.shape[0]
    buffers[6][...] = jnp.ones_like(buffers[6])
    emitted = sweep(
        lambda l: packed[l, :, lo : lo + LANES],
        lambda l: warm[pl.ds(l, SUBS), lo : lo + LANES],
        first, bias, second, heads, gpts, -depth_scale * LOG2E, True, buffers, levels,
    )
    planck = jnp.exp(0.25 * warm[:, lo : lo + LANES])
    return -(heat_scale / gpts) * planck * emitted


def longwave_body(packed, warm, first, bias, second, heads, out, *buffers):
    out[...] = longwave_part(0, packed, warm, first, bias, second, heads, buffers)


def shortwave_body(
    count, kept_x, kept_warm, kept_cos, in_x, in_warm, first, bias, second, heads, flux, out,
    work_x, work_warm, *buffers
):
    levels = kept_warm.shape[0]
    half = kept_warm.shape[1]
    gpts = heads.shape[0]
    slot = iota((half, half), 1) - count[0, 0]
    placed = jnp.where(slot == iota((half, half), 0), 1.0, 0.0).astype(BF16)
    cells = levels * SUBS
    work_x[...] = kept_x[...] + mm(in_x[0:cells, :], placed)
    work_warm[...] = kept_warm[...] + mm(in_warm[...], placed)
    cosine = kept_cos[...] + mm(in_x[cells:, :], placed)[0:SUBS]
    cosine = jnp.where(cosine > 0.0, cosine, 1.0)
    buffers[6][...] = flux[...]
    emitted = sweep(
        lambda l: work_x[pl.ds(pl.multiple_of(l * SUBS, SUBS), SUBS), :],
        lambda l: work_warm[pl.ds(l, SUBS), :],
        first, bias, second, heads, gpts, (-depth_scale * LOG2E) / cosine, False, buffers, levels,
    )
    out[...] = (heat_scale / gpts) * cosine[0:1] * emitted


def finish_body(
    me, count, packed, warm, first, bias, second, heads, long_first, work, partner, slot_of,
    leaving, staying, heat, *buffers
):
    levels, cols = heat.shape
    half = cols // 2
    slab = leaving.shape[1]
    sunlit = count[0, 0]
    long_last = longwave_part(half, packed, warm, first, bias, second, heads, buffers)
    for lo, long in ((0, long_first[...]), (half, long_last)):
        slot = slot_of[:, lo : lo + half]
        here = slot < half
        place = jnp.where(here, slot, slot + half - sunlit) & (half - 1)
        lit = slot < sunlit
        for r in range(0, levels, SUBS):
            near = lane_take(work[r : r + SUBS, :], place)
            far = lane_take(partner[r : r + SUBS, :], place)
            short = jnp.where(lit, jnp.where(here, near, far), 0.0)
            heat[r : r + SUBS, lo : lo + half] = long[r : r + SUBS] + short
    for out, bits in ((leaving, (1, 3)), (staying, (0, 2))):
        for n, bit in enumerate(bits):
            out[n] = heat[pl.ds(pl.multiple_of((me[0] ^ bit) * slab, SUBS), slab), :]


def add_body(me, closed, staying, near, far, out):
    cols = staying.shape[2]
    for source, piece in sources(me[0], staying, near, far):
        at = pl.ds(pl.multiple_of(source * cols, LANES), cols)
        out[:, at] = closed[:, at] + piece


def per_device(
    potential, species, diffusion, neighbours, listing, day_count, zenith,
    lw_first, lw_bias, lw_second, lw_depth, lw_fraction,
    sw_first, sw_bias, sw_second, sw_depth, solar_flux,
):
    n_group = lax.axis_size("group")
    n_tile = lax.axis_size("tile")
    assert n_group == 4 and n_tile % 2 == 0
    me = lax.axis_index("group").astype(jnp.int32).reshape(1)
    place = lax.axis_index("tile").astype(jnp.int32).reshape(1)
    slab, tile = potential.shape
    gases = species.shape[0]
    cols = tile // n_group
    half = cols // 2
    levels = slab * n_group
    hid = lw_first.shape[1]
    lw_gpts = lw_depth.shape[1]
    sw_gpts = sw_depth.shape[1]

    def outward(value):
        across = [(i, (i + 1 if i % 2 else i - 1) % n_tile) for i in range(n_tile)]
        return lax.ppermute(value, "tile", across)

    def paired(value):
        return lax.ppermute(value, "tile", [(i, i ^ 1) for i in range(n_tile)])

    def swapped(value, bit):
        return lax.ppermute(value, "group", [(i, i ^ bit) for i in range(n_group)])

    near = neighbours.shape[0]
    (framing,) = call(
        pack_body,
        [shaped((slab + 2 * near, tile), F32)],
        [potential, neighbours, diffusion],
    )
    outer = outward(framing)
    inner = paired(framing)

    gas_pair = shaped((2, gases, slab, cols), BF16)
    (gas_leaving,) = call(gas_cut_body, [gas_pair], [me, species], after=inner)
    gas_near = swapped(gas_leaving, 2)

    warm_pair = shaped((2, slab, cols), BF16)
    third, warm_leaving, warm_staying = call(
        sections_body,
        [shaped((slab, tile + 2 * HW), F32), warm_pair, warm_pair],
        [me, place, outer, inner, potential, neighbours, diffusion],
        [pltpu.VMEM((slab, 3 * tile), F32)] * 3
        + [pltpu.VMEM((3, *neighbours.shape), jnp.int32), pltpu.VMEM((3, *diffusion.shape), F32)],
        flops=10_000_000,
    )
    warm_near = swapped(warm_leaving, 1)
    (gas_passing,) = call(gas_turn_body, [gas_pair], [me, species, gas_near], after=warm_leaving)
    gas_far = swapped(gas_passing, 1)
    (warm_passing,) = call(turn_body, [warm_pair], [warm_staying, warm_near])
    warm_far = swapped(warm_passing, 2)

    lw_one, lw_shift, lw_two, lw_heads, sw_one, sw_shift, sw_two, sw_heads, flux = call(
        weights_body,
        [
            shaped(lw_first.shape[::-1], BF16),
            shaped((hid, LANES), F32),
            shaped(lw_second.shape[::-1], BF16),
            shaped((2 * lw_gpts, hid), BF16),
            shaped(sw_first.shape[::-1], BF16),
            shaped((hid, LANES), F32),
            shaped(sw_second.shape[::-1], BF16),
            shaped((sw_gpts, hid), BF16),
            shaped((sw_gpts, LANES), F32),
        ],
        [
            lw_first, lw_bias[None], lw_second, lw_depth, lw_fraction,
            sw_first, sw_bias[None], sw_second, sw_depth, solar_flux[None],
        ],
        after=warm_passing,
    )
    long_weights = [lw_one, lw_shift, lw_two, lw_heads]
    short_weights = [sw_one, sw_shift, sw_two, sw_heads, flux]

    packed, out_x, kept_x, kept_cos, slot_of = call(
        gas_join_body,
        [
            shaped((levels, SUBS, cols), F32),
            shaped((levels * SUBS + 2 * SUBS, half), BF16),
            shaped((levels * SUBS, half), F32),
            shaped((SUBS, half), F32),
            shaped((SUBS, cols), jnp.int32),
        ],
        [me, day_count, species, gas_near, gas_far, listing, zenith],
        [pltpu.VMEM((SUBS * slab, LANES), F32)],
    )
    in_x = paired(out_x)

    (closed,) = call(
        closing_body, [shaped((slab, tile), F32)], [third, neighbours, diffusion], flops=2_000_000
    )

    warm, out_warm, kept_warm = call(
        warm_join_body,
        [
            shaped((levels, cols), F32),
            shaped((levels, half), BF16),
            shaped((levels, half), F32),
        ],
        [me, day_count, warm_staying, warm_near, warm_far, listing],
    )
    in_warm = paired(out_warm)

    lw_rows = lw_heads.shape[0]
    lw_scratch = sweep_scratch(hid, lw_rows, lw_rows // 2, levels)
    lw_cells = levels * half
    (long_first,) = call(
        longwave_body,
        [shaped((levels, half), F32)],
        [packed, warm, *long_weights],
        lw_scratch,
        flops=2 * lw_cells * hid * lw_rows,
        trans=5 * lw_cells * lw_rows // 2,
    )
    sw_rows = sw_heads.shape[0]
    (work,) = call(
        shortwave_body,
        [shaped((levels, half), F32)],
        [day_count, kept_x, kept_warm, kept_cos, in_x, in_warm, *short_weights],
        [pltpu.VMEM((levels * SUBS, half), F32), pltpu.VMEM((levels, half), F32)]
        + sweep_scratch(hid, sw_rows, sw_rows, levels),
        flops=2 * lw_cells * hid * sw_rows,
        trans=3 * lw_cells * sw_rows,
    )
    partner = paired(work)
    heat_pair = shaped((2, slab, cols), F32)
    heat_leaving, heat_staying = call(
        finish_body,
        [heat_pair, heat_pair],
        [me, day_count, packed, warm, *long_weights, long_first, work, partner, slot_of],
        [pltpu.VMEM((levels, cols), F32)] + lw_scratch,
        flops=2 * lw_cells * hid * lw_rows,
        trans=5 * lw_cells * lw_rows // 2,
    )
    heat_near = swapped(heat_leaving, 1)
    (heat_passing,) = call(turn_body, [heat_pair], [heat_staying, heat_near])
    heat_far = swapped(heat_passing, 2)
    (evolved,) = call(
        add_body,
        [shaped((slab, tile), F32)],
        [me, closed, heat_staying, heat_near, heat_far],
    )
    return evolved


def solution(mesh):
    return jax.shard_map(
        per_device,
        mesh=mesh,
        in_specs=(
            P("group", "tile"),
            P(None, "group", "tile"),
            P(None, "tile"),
            P(None, "tile"),
            P("group", "tile", None),
            P("group", "tile"),
            P("group", "tile", None),
            *([P()] * 10),
        ),
        out_specs=P("group", "tile"),
        check_vma=False,
    )
```

```python
import functools
import math

import jax
import jax.numpy as jnp
from jax import lax
from jax.experimental import pallas as pl
from jax.experimental.pallas import tpu as pltpu
from jax.sharding import PartitionSpec as P

HW = 256
LANES = 128
SUBS = 8
STEP_LEVELS = SUBS // 2

depth_scale = 0.1
heat_scale = 12.0
LOG2E = 1.4426950408889634
LN2 = 0.6931471805599453

F32 = jnp.float32
BF16 = jnp.bfloat16
VMEM = pl.BlockSpec(memory_space=pltpu.VMEM)
ANY = pl.BlockSpec(memory_space=pl.ANY)
SMEM = pl.BlockSpec(memory_space=pltpu.SMEM)
PARAMS = pltpu.CompilerParams(vmem_limit_bytes=48 * 1024 * 1024)


def call(body, outs, ins, scratch=(), flops=0, trans=0, after=None, where=VMEM):
    in_specs = [SMEM if a.size == 1 else where for a in ins]
    if after is not None:
        whole, ins = body, [after, *ins]
        in_specs = [ANY, *in_specs]

        def body(_, *refs):
            whole(*refs)

    return pl.pallas_call(
        body,
        out_shape=outs,
        in_specs=in_specs,
        out_specs=[VMEM for _ in outs],
        scratch_shapes=list(scratch),
        compiler_params=PARAMS,
        cost_estimate=pl.CostEstimate(
            flops=flops,
            transcendentals=trans,
            bytes_accessed=sum(a.size * a.dtype.itemsize for a in list(ins) + list(outs)),
        ),
    )(*ins)


def shaped(shape, dtype):
    return jax.ShapeDtypeStruct(shape, dtype)


def iota(shape, dim):
    return lax.broadcasted_iota(jnp.int32, shape, dim)


def mm(a, b):
    return jnp.dot(a, b, preferred_element_type=F32)


def lane_take(x, idx):
    return jnp.take_along_axis(x, idx, axis=1, mode="promise_in_bounds")


def diffused(src, src_at, table, weight, within, at):
    reach = HW // LANES
    wide = 2 * reach + 1
    rows = src.shape[0]
    groups = range(0, rows, SUBS)
    base = at - src_at
    middle = [src[r : r + SUBS, base : base + LANES] for r in groups]
    total = [jnp.zeros_like(m) for m in middle]
    for k in range(table.shape[0]):
        place = jnp.broadcast_to(table[k : k + 1, within : within + LANES], (SUBS, LANES)) - within
        lane = place & (LANES - 1)
        which = place >> (LANES.bit_length() - 1)
        factor = jnp.broadcast_to(weight[k : k + 1, within : within + LANES], (SUBS, LANES))
        tests = [which == w for w in range(1, wide)]
        for n, r in enumerate(groups):
            near = None
            for w in range(wide):
                lo = base + (w - reach) * LANES
                got = lane_take(src[r : r + SUBS, lo : lo + LANES], lane)
                near = got if w == 0 else jnp.where(tests[w - 1], got, near)
            total[n] = total[n] + factor * (near - middle[n])
    return [(r, m, m + t) for r, m, t in zip(groups, middle, total)]


def pack_body(own, table, weight, out, table_here, weight_here, sems):
    slab = own.shape[0]
    near = table.shape[0]
    moves = [
        pltpu.make_async_copy(own, out.at[0:slab], sems.at[0]),
        pltpu.make_async_copy(table, table_here, sems.at[1]),
        pltpu.make_async_copy(weight, weight_here, sems.at[2]),
    ]
    for move in moves:
        move.start()
    for move in moves:
        move.wait()
    out[slab : slab + near, :] = table_here[...].astype(F32)
    out[slab + near :, :] = weight_here[...]


def sections_body(
    me, place, outer, inner, own, table, weight, third_out, *rest
):
    pieces, (frame, first, second, tables, weights) = rest[:-5], rest[-5:]
    slab, tile = own.shape
    near = table.shape[0]
    cols = tile // len(pieces)
    odd = place[0] & 1
    for side, packed in ((odd, outer), (1 - odd, inner)):
        at = pl.ds(pl.multiple_of(side * (2 * tile), LANES), tile)
        frame[:, at] = packed[0:slab, :]
        tables[side * 2] = packed[slab : slab + near, :].astype(jnp.int32)
        weights[side * 2] = packed[slab + near : slab + 2 * near, :]
    frame[:, tile : 2 * tile] = own[...]
    tables[1] = table[...]
    weights[1] = weight[...]

    def run(src, src_at, halo, put):
        for at in range(tile - halo, 2 * tile + halo, LANES):
            t = at // tile
            for r, _, value in diffused(src, src_at, tables.at[t], weights.at[t], at - t * tile, at):
                put(r, at, value)

    def put_first(r, at, value):
        first[r : r + SUBS, at : at + LANES] = value

    def put_second(r, at, value):
        start = frame[r : r + SUBS, at : at + LANES]
        second[r : r + SUBS, at : at + LANES] = 0.75 * start + 0.25 * value

    def put_third(r, at, value):
        start = frame[r : r + SUBS, at : at + LANES]
        lo = at - tile + HW
        third_out[r : r + SUBS, lo : lo + LANES] = start / 3.0 + (2.0 / 3.0) * value

    run(frame, 0, 3 * HW, put_first)
    run(first, 0, 2 * HW, put_second)
    run(second, 0, HW, put_third)
    for bit, out in enumerate(pieces):
        lo = pl.multiple_of(HW + (me[0] ^ bit) * cols, LANES)
        out[...] = third_out[:, pl.ds(lo, cols)].astype(BF16)


def closing_body(third, table, weight, out):
    tile = out.shape[1]
    for at in range(0, tile, LANES):
        for r, _, value in diffused(third, -HW, table, weight, at, at):
            out[r : r + SUBS, at : at + LANES] = value


def gas_cut_body(me, species, *pieces):
    cols = pieces[0].shape[2]
    for bit, out in enumerate(pieces, 1):
        out[...] = species[:, :, pl.ds(pl.multiple_of((me[0] ^ bit) * cols, LANES), cols)]


def turned_over(matrix):
    return matrix.astype(F32).T


def weights_body(
    w1, b1, w2, wd, wf, v1, c1, v2, vd, flux,
    w1_out, b1_out, w2_out, heads_out, scaled_out, v1_out, c1_out, v2_out, vd_out, flux_out,
):
    for weight, out in ((w1, w1_out), (w2, w2_out), (v1, v1_out), (v2, v2_out)):
        out[...] = (0.5 * turned_over(weight[...])).astype(BF16)
    gpts = wd.shape[1]
    heads_out[0:gpts, :] = turned_over(wd[...]).astype(BF16)
    heads_out[gpts:, :] = turned_over(wf[...]).astype(BF16)
    scaled = LOG2E * heads_out[...].astype(F32)
    high = scaled.astype(BF16)
    hid = wd.shape[0]
    scaled_out[:, 0:hid] = high
    scaled_out[:, hid:] = (scaled - high.astype(F32)).astype(BF16)
    vd_out[...] = turned_over(vd[...]).astype(BF16)
    for row, out, scale in ((b1, b1_out, 0.5), (c1, c1_out, 0.5), (flux, flux_out, 1.0)):
        out[...] = scale * jnp.broadcast_to(row[...], (LANES, row.shape[1])).T


def one_hots(listing, count):
    cols = listing.shape[-1]
    half = cols // 2
    label = iota((cols, half), 0)
    slot = iota((cols, half), 1)
    first = jnp.broadcast_to(listing[0, :, 0:half], (cols, half))
    last = jnp.broadcast_to(listing[0, :, half:cols], (cols, half))
    kept = jnp.where((first == label) & (slot < count), 1.0, 0.0)
    sent = jnp.where((last == label) & (slot + half < count), 1.0, 0.0)
    return first == label, last == label, kept.astype(BF16), sent.astype(BF16)


def gas_join_body(
    me, count, species, *rest
):
    arrived, rest = rest[:-8], rest[-8:]
    listing, zenith, packed, outgoing, kept_x, kept_cos, slot_of, spread = rest
    gases, slab, _ = species.shape
    cols = packed.shape[2]
    half = cols // 2
    spread[...] = jnp.zeros_like(spread)
    for bit in range(len(arrived) + 1):
        source = me[0] ^ bit
        for lo in range(0, cols, LANES):
            for f in range(gases):
                if bit == 0:
                    value = species[f, :, pl.ds(pl.multiple_of(me[0] * cols + lo, LANES), LANES)]
                else:
                    value = arrived[bit - 1][f, :, lo : lo + LANES]
                spread[(f + 1) * slab : (f + 2) * slab, :] = value.astype(F32)
            for l in range(slab):
                packed[source * slab + l, :, lo : lo + LANES] = spread[pl.ds(l, SUBS, stride=slab), :]
    hit_first, hit_last, kept, sent = one_hots(listing, count[0, 0])
    levels = packed.shape[0]
    flat = packed[...].reshape(levels * SUBS, cols).astype(BF16)
    outgoing[0 : levels * SUBS, :] = mm(flat, sent).astype(BF16)
    kept_x[...] = mm(flat, kept)
    cosine = jnp.broadcast_to(zenith[0].astype(F32), (2 * SUBS, cols)).astype(BF16)
    outgoing[levels * SUBS :, :] = mm(cosine, sent).astype(BF16)
    kept_cos[...] = mm(cosine, kept)[0:SUBS]
    hits = jnp.concatenate([hit_first, hit_last], axis=1)
    hits = jnp.where(hits, 1.0, 0.0).astype(BF16)
    numbers = iota((2 * SUBS, cols), 1).astype(F32).astype(BF16)
    found = lax.dot_general(
        numbers, hits, (((1,), (1,)), ((), ())), preferred_element_type=F32
    )
    slot_of[...] = found[0:SUBS].astype(jnp.int32)


def warm_join_body(me, count, *rest):
    pieces, (listing, warm, outgoing, kept_warm) = rest[:-4], rest[-4:]
    slab = pieces[0].shape[0]
    for bit, piece in enumerate(pieces):
        at = pl.multiple_of((me[0] ^ bit) * slab, SUBS)
        warm[pl.ds(at, slab), :] = piece[...].astype(F32)
    _, _, kept, sent = one_hots(listing, count[0, 0])
    flat = warm[...].astype(BF16)
    outgoing[...] = mm(flat, sent).astype(BF16)
    kept_warm[...] = mm(flat, kept)


def softplus(z):
    return jnp.maximum(z, jnp.log(1.0 + jnp.exp(jnp.minimum(z, 80.0))))


def softplus_of_scaled(z):
    power = jnp.exp2(jnp.minimum(z.astype(BF16), 120.0))
    return jnp.maximum(z * LN2, jnp.log(1.0 + power.astype(F32)))


def sweep(x_at, warm_at, first, bias, second, heads, gpts, rate, both, buffers, levels, scaled):
    one_a, one_b, hid_a, hid_b, z_a, z_b, trans, parts = buffers
    steps = levels // STEP_LEVELS
    top = iota((SUBS, LANES), 0) == 0
    wide = STEP_LEVELS * LANES
    rows = heads.shape[0]
    row_cut = rows // (8 if both else 4) if scaled else rows
    col_cut = wide if scaled else wide // 2
    plus = softplus_of_scaled if scaled else softplus
    chunk = 2 * SUBS if scaled else SUBS
    units = first.shape[0]
    unit_cut = units // 2

    def first_tasks(pair, odd, out):
        pair = jnp.minimum(pair, steps // 2 - 1)

        def task(r):
            warm = warm_at(pl.multiple_of(pair * SUBS, SUBS))
            tiles = []
            for i in range(odd * STEP_LEVELS, (odd + 1) * STEP_LEVELS):
                row = jnp.broadcast_to(warm[i : i + 1], (SUBS, LANES))
                tiles.append(jnp.where(top, row, x_at(pair * SUBS + i)))
            x = jnp.concatenate(tiles, axis=1).astype(BF16)
            v = mm(first[r : r + unit_cut, :], x)
            shift = bias[r : r + unit_cut, :]
            v = v + jnp.concatenate([shift] * STEP_LEVELS, axis=1)
            out[r : r + unit_cut, :] = (v + v * jnp.tanh(v)).astype(BF16)

        return [functools.partial(task, r) for r in range(0, units, unit_cut)]

    def second_tasks(one, out):
        def task(r):
            v = mm(second[r : r + unit_cut, :], one[...])
            value = (v + v * jnp.tanh(v)).astype(BF16)
            for at in range(0, out.shape[0], units):
                out[at + r : at + r + unit_cut, :] = value

        return [functools.partial(task, r) for r in range(0, units, unit_cut)]

    def optics_tasks(hid, out):
        def task(lo, r):
            at = slice(lo, lo + col_cut)
            out[r : r + row_cut, at] = mm(heads[r : r + row_cut, :], hid[:, at])

        return [
            functools.partial(task, lo, r)
            for lo in range(0, wide, col_cut)
            for r in range(0, rows, row_cut)
        ]

    def consume_tasks(t, z, total):
        def task(lo):
            carry = trans[lo : lo + chunk, :]
            for i in range(STEP_LEVELS):
                at = i * LANES
                depth = plus(z[lo : lo + chunk, at : at + LANES])
                following = carry * jnp.exp2(depth * rate)
                drop = carry - following
                if both:
                    drop = drop * plus(z[gpts + lo : gpts + lo + chunk, at : at + LANES])
                for r in range(0, chunk, SUBS):
                    part = drop[r : r + SUBS]
                    total[i] = part if total[i] is None else total[i] + part
                carry = following
            trans[lo : lo + chunk, :] = carry

        return [functools.partial(task, lo) for lo in range(0, gpts, chunk)]

    def woven(main, side):
        done = 0
        for n, task in enumerate(main):
            while done < len(side) and done * len(main) <= n * len(side):
                side[done]()
                done += 1
            task()
        for task in side[done:]:
            task()

    def plain(tasks):
        for task in tasks:
            task()

    def step(t, pair, odd, z, z_next, hid_next, hid_later, one_later, one_last):
        total = [None] * STEP_LEVELS
        side = (
            optics_tasks(hid_next, z_next)
            + second_tasks(one_later, hid_later)
            + first_tasks(pair, odd, one_last)
        )
        woven(consume_tasks(t, z, total), side)
        for i in range(STEP_LEVELS):
            at = pl.multiple_of((t * STEP_LEVELS + i) * SUBS, SUBS)
            parts[pl.ds(at, SUBS), :] = total[i]

    plain(first_tasks(0, 0, one_a))
    plain(second_tasks(one_a, hid_a))
    plain(first_tasks(0, 1, one_b))
    plain(optics_tasks(hid_a, z_a))
    plain(second_tasks(one_b, hid_b))
    plain(first_tasks(1, 0, one_a))

    def two(i, _):
        step(2 * i, i + 1, 1, z_a, z_b, hid_b, hid_a, one_a, one_b)
        step(2 * i + 1, i + 2, 0, z_b, z_a, hid_a, hid_b, one_b, one_a)
        return 0

    lax.fori_loop(0, steps // 2, two, 0)
    emitted = parts[pl.ds(0, levels, stride=SUBS), :]
    for s in range(1, SUBS):
        emitted = emitted + parts[pl.ds(s, levels, stride=SUBS), :]
    return emitted


def sweep_scratch(hid, depth, rows, gpts, levels):
    wide = STEP_LEVELS * LANES
    return [
        pltpu.VMEM((hid, wide), BF16),
        pltpu.VMEM((hid, wide), BF16),
        pltpu.VMEM((depth, wide), BF16),
        pltpu.VMEM((depth, wide), BF16),
        pltpu.VMEM((rows, wide), F32),
        pltpu.VMEM((rows, wide), F32),
        pltpu.VMEM((gpts, LANES), F32),
        pltpu.VMEM((levels * SUBS, LANES), F32),
    ]


def longwave_part(lo, packed, warm, first, bias, second, heads, buffers, scaled):
    gpts = heads.shape[0] // 2
    levels = packed.shape[0]
    buffers[6][...] = jnp.ones_like(buffers[6])
    emitted = sweep(
        lambda l: packed[l, :, lo : lo + LANES],
        lambda l: warm[pl.ds(l, SUBS), lo : lo + LANES],
        first, bias, second, heads, gpts, -depth_scale * LOG2E, True, buffers, levels, scaled,
    )
    planck = jnp.exp(0.25 * warm[:, lo : lo + LANES])
    return -(heat_scale / gpts) * planck * emitted


def longwave_body(packed, warm, first, bias, second, heads, out, *buffers):
    out[...] = longwave_part(0, packed, warm, first, bias, second, heads, buffers, True)


def shortwave_body(
    count, kept_x, kept_warm, kept_cos, in_x, in_warm, first, bias, second, heads, flux, out,
    work_x, work_warm, *buffers
):
    levels = kept_warm.shape[0]
    half = kept_warm.shape[1]
    gpts = heads.shape[0]
    slot = iota((half, half), 1) - count[0, 0]
    placed = jnp.where(slot == iota((half, half), 0), 1.0, 0.0).astype(BF16)
    cells = levels * SUBS
    work_x[...] = kept_x[...] + mm(in_x[0:cells, :], placed)
    work_warm[...] = kept_warm[...] + mm(in_warm[...], placed)
    cosine = kept_cos[...] + mm(in_x[cells:, :], placed)[0:SUBS]
    cosine = jnp.where(cosine > 0.0, cosine, 1.0)
    buffers[6][...] = flux[...]
    emitted = sweep(
        lambda l: work_x[pl.ds(pl.multiple_of(l * SUBS, SUBS), SUBS), :],
        lambda l: work_warm[pl.ds(l, SUBS), :],
        first, bias, second, heads, gpts, (-depth_scale * LOG2E) / cosine, False, buffers, levels, False,
    )
    out[...] = (heat_scale / gpts) * cosine[0:1] * emitted


def finish_body(
    n_group, me, count, packed, warm, first, bias, second, heads, long_first, work, partner, slot_of,
    *rest
):
    pieces, heat, buffers = rest[:n_group], rest[n_group], rest[n_group + 1 :]
    levels, cols = heat.shape
    half = cols // 2
    slab = pieces[0].shape[0]
    sunlit = count[0, 0]
    long_last = longwave_part(half, packed, warm, first, bias, second, heads, buffers, False)
    for lo, long in ((0, long_first[...]), (half, long_last)):
        slot = slot_of[:, lo : lo + half]
        here = slot < half
        place = jnp.where(here, slot, slot + half - sunlit) & (half - 1)
        lit = slot < sunlit
        for r in range(0, levels, SUBS):
            near = lane_take(work[r : r + SUBS, :], place)
            far = lane_take(partner[r : r + SUBS, :], place)
            short = jnp.where(lit, jnp.where(here, near, far), 0.0)
            heat[r : r + SUBS, lo : lo + half] = long[r : r + SUBS] + short
    for bit, out in enumerate(pieces):
        out[...] = heat[pl.ds(pl.multiple_of((me[0] ^ bit) * slab, SUBS), slab), :]


def add_body(me, closed, *rest):
    pieces, out = rest[:-1], rest[-1]
    cols = pieces[0].shape[1]
    for bit, piece in enumerate(pieces):
        at = pl.ds(pl.multiple_of((me[0] ^ bit) * cols, LANES), cols)
        out[:, at] = closed[:, at] + piece[...]


def per_device(
    potential, species, diffusion, neighbours, listing, day_count, zenith,
    lw_first, lw_bias, lw_second, lw_depth, lw_fraction,
    sw_first, sw_bias, sw_second, sw_depth, solar_flux,
):
    n_group = lax.axis_size("group")
    n_tile = lax.axis_size("tile")
    assert n_group & (n_group - 1) == 0 and n_tile % 2 == 0
    me = lax.axis_index("group").astype(jnp.int32).reshape(1)
    place = lax.axis_index("tile").astype(jnp.int32).reshape(1)
    slab, tile = potential.shape
    gases = species.shape[0]
    cols = tile // n_group
    half = cols // 2
    levels = slab * n_group
    hid = lw_first.shape[1]
    lw_gpts = lw_depth.shape[1]
    sw_gpts = sw_depth.shape[1]

    def outward(value):
        across = [(i, (i + 1 if i % 2 else i - 1) % n_tile) for i in range(n_tile)]
        return lax.ppermute(value, "tile", across)

    def paired(value):
        return lax.ppermute(value, "tile", [(i, i ^ 1) for i in range(n_tile)])

    def swapped(value, bit):
        return lax.ppermute(value, "group", [(i, i ^ bit) for i in range(n_group)])

    near = neighbours.shape[0]
    (framing,) = call(
        pack_body,
        [shaped((slab + 2 * near, tile), F32)],
        [potential, neighbours, diffusion],
        [
            pltpu.VMEM(neighbours.shape, jnp.int32),
            pltpu.VMEM(diffusion.shape, F32),
            pltpu.SemaphoreType.DMA((3,)),
        ],
        where=ANY,
    )
    outer = outward(framing)
    inner = paired(framing)

    gas_cuts = call(
        gas_cut_body, [shaped((gases, slab, cols), BF16)] * (n_group - 1), [me, species], after=framing
    )
    gas_arrived = [swapped(c, bit) for bit, c in enumerate(gas_cuts, 1)]

    third, *warm_cuts = call(
        sections_body,
        [shaped((slab, tile + 2 * HW), F32)] + [shaped((slab, cols), BF16)] * n_group,
        [me, place, outer, inner, potential, neighbours, diffusion],
        [pltpu.VMEM((slab, 3 * tile), F32)] * 3
        + [pltpu.VMEM((3, *neighbours.shape), jnp.int32), pltpu.VMEM((3, *diffusion.shape), F32)],
        flops=10_000_000,
    )
    warm_pieces = [warm_cuts[0]] + [swapped(c, bit) for bit, c in enumerate(warm_cuts[1:], 1)]

    lw_one, lw_shift, lw_two, lw_heads, lw_scaled, sw_one, sw_shift, sw_two, sw_heads, flux = call(
        weights_body,
        [
            shaped(lw_first.shape[::-1], BF16),
            shaped((hid, LANES), F32),
            shaped(lw_second.shape[::-1], BF16),
            shaped((2 * lw_gpts, hid), BF16),
            shaped((2 * lw_gpts, 2 * hid), BF16),
            shaped(sw_first.shape[::-1], BF16),
            shaped((hid, LANES), F32),
            shaped(sw_second.shape[::-1], BF16),
            shaped((sw_gpts, hid), BF16),
            shaped((sw_gpts, LANES), F32),
        ],
        [
            lw_first, lw_bias[None], lw_second, lw_depth, lw_fraction,
            sw_first, sw_bias[None], sw_second, sw_depth, solar_flux[None],
        ],
        after=third,
    )
    long_weights = [lw_one, lw_shift, lw_two, lw_heads]
    scaled_weights = [lw_one, lw_shift, lw_two, lw_scaled]
    short_weights = [sw_one, sw_shift, sw_two, sw_heads, flux]

    packed, out_x, kept_x, kept_cos, slot_of = call(
        gas_join_body,
        [
            shaped((levels, SUBS, cols), F32),
            shaped((levels * SUBS + 2 * SUBS, half), BF16),
            shaped((levels * SUBS, half), F32),
            shaped((SUBS, half), F32),
            shaped((SUBS, cols), jnp.int32),
        ],
        [me, day_count, species, *gas_arrived, listing, zenith],
        [pltpu.VMEM((SUBS * slab, LANES), F32)],
        after=third,
    )
    in_x = paired(out_x)

    (closed,) = call(
        closing_body, [shaped((slab, tile), F32)], [third, neighbours, diffusion], flops=2_000_000
    )

    warm, out_warm, kept_warm = call(
        warm_join_body,
        [
            shaped((levels, cols), F32),
            shaped((levels, half), BF16),
            shaped((levels, half), F32),
        ],
        [me, day_count, *warm_pieces, listing],
    )
    in_warm = paired(out_warm)

    lw_rows = lw_heads.shape[0]
    lw_scratch = sweep_scratch(hid, hid, lw_rows, lw_rows // 2, levels)
    lw_cells = levels * half
    (long_first,) = call(
        longwave_body,
        [shaped((levels, half), F32)],
        [packed, warm, *scaled_weights],
        sweep_scratch(hid, 2 * hid, lw_rows, lw_rows // 2, levels),
        flops=2 * lw_cells * hid * lw_rows,
        trans=5 * lw_cells * lw_rows // 2,
    )
    sw_rows = sw_heads.shape[0]
    (work,) = call(
        shortwave_body,
        [shaped((levels, half), F32)],
        [day_count, kept_x, kept_warm, kept_cos, in_x, in_warm, *short_weights],
        [pltpu.VMEM((levels * SUBS, half), F32), pltpu.VMEM((levels, half), F32)]
        + sweep_scratch(hid, hid, sw_rows, sw_rows, levels),
        flops=2 * lw_cells * hid * sw_rows,
        trans=3 * lw_cells * sw_rows,
    )
    partner = paired(work)
    heat_cuts = call(
        functools.partial(finish_body, n_group),
        [shaped((slab, cols), F32)] * n_group,
        [me, day_count, packed, warm, *long_weights, long_first, work, partner, slot_of],
        [pltpu.VMEM((levels, cols), F32)] + lw_scratch,
        flops=2 * lw_cells * hid * lw_rows,
        trans=5 * lw_cells * lw_rows // 2,
    )
    heat_pieces = [heat_cuts[0]] + [swapped(c, bit) for bit, c in enumerate(heat_cuts[1:], 1)]
    (evolved,) = call(add_body, [shaped((slab, tile), F32)], [me, closed, *heat_pieces])
    return evolved


def solution(mesh):
    return jax.shard_map(
        per_device,
        mesh=mesh,
        in_specs=(
            P("group", "tile"),
            P(None, "group", "tile"),
            P(None, "tile"),
            P(None, "tile"),
            P("group", "tile", None),
            P("group", "tile"),
            P("group", "tile", None),
            *([P()] * 10),
        ),
        out_specs=P("group", "tile"),
        check_vma=False,
    )
```

```python
import functools
import math

import jax
import jax.numpy as jnp
from jax import lax
from jax.experimental import pallas as pl
from jax.experimental.pallas import tpu as pltpu
from jax.sharding import PartitionSpec as P

HW = 256
LANES = 128
SUBS = 8
STEP_LEVELS = SUBS // 2

depth_scale = 0.1
heat_scale = 12.0
LOG2E = 1.4426950408889634
LN2 = 0.6931471805599453
SAFE = 120.0

F32 = jnp.float32
BF16 = jnp.bfloat16
VMEM = pl.BlockSpec(memory_space=pltpu.VMEM)
ANY = pl.BlockSpec(memory_space=pl.ANY)
HBM = pl.BlockSpec(memory_space=pltpu.HBM)
SMEM = pl.BlockSpec(memory_space=pltpu.SMEM)
PARAMS = pltpu.CompilerParams(vmem_limit_bytes=48 * 1024 * 1024)


def call(body, outs, ins, scratch=(), flops=0, trans=0, after=None, where=VMEM):
    in_specs = [SMEM if a.size == 1 else where for a in ins]
    if after is not None:
        whole, ins = body, [after, *ins]
        in_specs = [ANY, *in_specs]

        def body(_, *refs):
            whole(*refs)

    return pl.pallas_call(
        body,
        out_shape=outs,
        in_specs=in_specs,
        out_specs=[VMEM for _ in outs],
        scratch_shapes=list(scratch),
        compiler_params=PARAMS,
        cost_estimate=pl.CostEstimate(
            flops=flops,
            transcendentals=trans,
            bytes_accessed=sum(a.size * a.dtype.itemsize for a in list(ins) + list(outs)),
        ),
    )(*ins)


def shaped(shape, dtype):
    return jax.ShapeDtypeStruct(shape, dtype)


def iota(shape, dim):
    return lax.broadcasted_iota(jnp.int32, shape, dim)


def mm(a, b):
    return jnp.dot(a, b, preferred_element_type=F32)


def lane_take(x, idx):
    return jnp.take_along_axis(x, idx, axis=1, mode="promise_in_bounds")


def diffused(src, src_at, table, weight, within, at):
    reach = HW // LANES
    wide = 2 * reach + 1
    rows = src.shape[0]
    groups = range(0, rows, SUBS)
    base = at - src_at
    middle = [src[r : r + SUBS, base : base + LANES] for r in groups]
    total = [jnp.zeros_like(m) for m in middle]
    for k in range(table.shape[0]):
        place = jnp.broadcast_to(table[k : k + 1, within : within + LANES], (SUBS, LANES)) - within
        lane = place & (LANES - 1)
        which = place >> (LANES.bit_length() - 1)
        factor = jnp.broadcast_to(weight[k : k + 1, within : within + LANES], (SUBS, LANES))
        tests = [which == w for w in range(1, wide)]
        for n, r in enumerate(groups):
            near = None
            for w in range(wide):
                lo = base + (w - reach) * LANES
                got = lane_take(src[r : r + SUBS, lo : lo + LANES], lane)
                near = got if w == 0 else jnp.where(tests[w - 1], got, near)
            total[n] = total[n] + factor * (near - middle[n])
    return [(r, m, m + t) for r, m, t in zip(groups, middle, total)]


def pack_body(me, own, table, weight, species, out, *rest):
    pieces, (table_here, weight_here, sems) = rest[:-3], rest[-3:]
    slab = own.shape[0]
    near = table.shape[0]
    cols = pieces[0].shape[2]
    moves = [
        pltpu.make_async_copy(own, out.at[0:slab], sems.at[0]),
        pltpu.make_async_copy(table, table_here, sems.at[1]),
        pltpu.make_async_copy(weight, weight_here, sems.at[2]),
    ]
    for bit, piece in enumerate(pieces):
        at = pl.ds(pl.multiple_of((me[0] ^ bit) * cols, LANES), cols)
        moves.append(pltpu.make_async_copy(species.at[:, :, at], piece, sems.at[3 + bit]))
    for move in moves:
        move.start()
    for move in moves:
        move.wait()
    out[slab : slab + near, :] = table_here[...].astype(F32)
    out[slab + near :, :] = weight_here[...]


def sections_body(
    me, place, outer, inner, own, table, weight, third_out, *rest
):
    pieces, (frame, first, second, tables, weights) = rest[:-5], rest[-5:]
    slab, tile = own.shape
    near = table.shape[0]
    cols = tile // len(pieces)
    odd = place[0] & 1
    for side, packed in ((odd, outer), (1 - odd, inner)):
        at = pl.ds(pl.multiple_of(side * (2 * tile), LANES), tile)
        frame[:, at] = packed[0:slab, :]
        tables[side * 2] = packed[slab : slab + near, :].astype(jnp.int32)
        weights[side * 2] = packed[slab + near : slab + 2 * near, :]
    frame[:, tile : 2 * tile] = own[...]
    tables[1] = table[...]
    weights[1] = weight[...]

    def run(src, src_at, halo, put):
        for at in range(tile - halo, 2 * tile + halo, LANES):
            t = at // tile
            for r, _, value in diffused(src, src_at, tables.at[t], weights.at[t], at - t * tile, at):
                put(r, at, value)

    def put_first(r, at, value):
        first[r : r + SUBS, at : at + LANES] = value

    def put_second(r, at, value):
        start = frame[r : r + SUBS, at : at + LANES]
        second[r : r + SUBS, at : at + LANES] = 0.75 * start + 0.25 * value

    def put_third(r, at, value):
        start = frame[r : r + SUBS, at : at + LANES]
        lo = at - tile + HW
        third_out[r : r + SUBS, lo : lo + LANES] = start / 3.0 + (2.0 / 3.0) * value

    run(frame, 0, 3 * HW, put_first)
    run(first, 0, 2 * HW, put_second)
    run(second, 0, HW, put_third)
    for bit, out in enumerate(pieces):
        lo = pl.multiple_of(HW + (me[0] ^ bit) * cols, LANES)
        out[...] = third_out[:, pl.ds(lo, cols)].astype(BF16)


def closing_body(third, table, weight, out):
    tile = out.shape[1]
    for at in range(0, tile, LANES):
        for r, _, value in diffused(third, -HW, table, weight, at, at):
            out[r : r + SUBS, at : at + LANES] = value


def turned_over(matrix):
    return matrix.astype(F32).T


def head_parts(weight, out, at):
    hid, gpts = weight.shape
    scaled = LOG2E * turned_over(weight[...])
    high = scaled.astype(BF16)
    out[at : at + gpts, 0:hid] = high
    out[at : at + gpts, hid:] = (scaled - high.astype(F32)).astype(BF16)


def reach_of(heads):
    rows, depth = heads.shape
    sums = mm(jnp.abs(heads[...]), jnp.ones((depth, LANES), BF16))
    return jnp.max(sums.reshape(rows // SUBS, SUBS, LANES), axis=0)


def prepare_body(
    count, listing, zenith, w1, b1, w2, wd, wf, v1, c1, v2, vd, flux,
    kept_out, sent_out, kept_cos, sent_cos, slot_of,
    w1_out, b1_out, w2_out, heads_out, reach_out, v1_out, c1_out, v2_out, vd_out, vreach_out, flux_out,
):
    for weight, out in ((w1, w1_out), (w2, w2_out), (v1, v1_out), (v2, v2_out)):
        out[...] = (0.5 * turned_over(weight[...])).astype(BF16)
    head_parts(wd, heads_out, 0)
    head_parts(wf, heads_out, wd.shape[1])
    head_parts(vd, vd_out, 0)
    reach_out[...] = reach_of(heads_out)
    vreach_out[...] = reach_of(vd_out)
    for row, out, scale in ((b1, b1_out, 0.5), (c1, c1_out, 0.5), (flux, flux_out, 1.0)):
        out[...] = scale * jnp.broadcast_to(row[...], (LANES, row.shape[1])).T
    cols = listing.shape[-1]
    half = cols // 2
    sunlit = count[0, 0]
    label = iota((cols, half), 0)
    slot = iota((cols, half), 1)
    first = jnp.broadcast_to(listing[0, :, 0:half], (cols, half)) == label
    last = jnp.broadcast_to(listing[0, :, half:cols], (cols, half)) == label
    kept = jnp.where(first & (slot < sunlit), 1.0, 0.0).astype(BF16)
    sent = jnp.where(last & (slot + half < sunlit), 1.0, 0.0).astype(BF16)
    kept_out[...] = kept
    sent_out[...] = sent
    cosine = jnp.broadcast_to(zenith[0].astype(F32), (2 * SUBS, cols)).astype(BF16)
    sent_cos[...] = mm(cosine, sent).astype(BF16)
    kept_cos[...] = mm(cosine, kept)[0:SUBS]
    hits = jnp.where(jnp.concatenate([first, last], axis=1), 1.0, 0.0).astype(BF16)
    numbers = iota((2 * SUBS, cols), 1).astype(F32).astype(BF16)
    found = lax.dot_general(numbers, hits, (((1,), (1,)), ((), ())), preferred_element_type=F32)
    slot_of[...] = found[0:SUBS].astype(jnp.int32)


def join_body(n_group, me, *rest):
    gases, warms = rest[:n_group], rest[n_group : 2 * n_group]
    kept, sent, sent_cos, packed, outgoing, kept_x, spread = rest[2 * n_group :]
    slab = warms[0].shape[0]
    for bit, (gas, warm) in enumerate(zip(gases, warms)):
        source = me[0] ^ bit
        for h in range(packed.shape[0]):
            at = slice(h * LANES, (h + 1) * LANES)
            spread[0:slab, :] = warm[:, at].astype(F32)
            for f in range(gas.shape[0]):
                spread[(f + 1) * slab : (f + 2) * slab, :] = gas[f, :, at].astype(F32)
            for l in range(slab):
                row = pl.multiple_of((source * slab + l) * SUBS, SUBS)
                packed[h, pl.ds(row, SUBS), :] = spread[pl.ds(l, SUBS, stride=slab), :]
    cells = packed.shape[1]
    first, last = packed[0].astype(BF16), packed[1].astype(BF16)
    outgoing[0:cells, :] = (mm(first, sent[0:LANES]) + mm(last, sent[LANES:])).astype(BF16)
    outgoing[cells:, :] = sent_cos[...]
    kept_x[...] = mm(first, kept[0:LANES]) + mm(last, kept[LANES:])


def softplus(z, guarded):
    if not guarded:
        return jnp.log(1.0 + jnp.exp2(z))
    return jnp.maximum(z * LN2, jnp.log(1.0 + jnp.exp2(jnp.minimum(z, SAFE))))


def sweep(x, first, bias, second, heads, reach, start, gpts, rate, both, buffers):
    one_a, one_b, hid_a, hid_b, z_a, z_b, trans, parts, peak = buffers
    levels = x.shape[0] // SUBS
    steps = levels // STEP_LEVELS
    wide = STEP_LEVELS * LANES
    rows = heads.shape[0]
    col_cut = wide // 2
    units = first.shape[0]
    unit_cut = units // 2

    def first_tasks(t, out):
        def task(r):
            row = jnp.minimum(t, steps - 1) * (STEP_LEVELS * SUBS)
            tiles = [
                x[pl.ds(pl.multiple_of(row + i * SUBS, SUBS), SUBS), :] for i in range(STEP_LEVELS)
            ]
            v = mm(first[r : r + unit_cut, :], jnp.concatenate(tiles, axis=1).astype(BF16))
            v = v + jnp.concatenate([bias[r : r + unit_cut, :]] * STEP_LEVELS, axis=1)
            out[r : r + unit_cut, :] = (v + v * jnp.tanh(v)).astype(BF16)

        return [functools.partial(task, r) for r in range(0, units, unit_cut)]

    def second_tasks(one, out):
        def task(r):
            v = mm(second[r : r + unit_cut, :], one[...])
            value = (v + v * jnp.tanh(v)).astype(BF16)
            out[r : r + unit_cut, :] = value
            out[units + r : units + r + unit_cut, :] = value
            most = peak[...]
            for i in range(0, unit_cut, 2 * SUBS):
                for at in range(0, wide, LANES):
                    most = jnp.maximum(most, value[i : i + 2 * SUBS, at : at + LANES])
            peak[...] = most

        return [functools.partial(task, r) for r in range(0, units, unit_cut)]

    def optics_tasks(hid, out):
        def task(lo):
            at = slice(lo, lo + col_cut)
            out[:, at] = mm(heads[...], hid[:, at])

        return [functools.partial(task, lo) for lo in range(0, wide, col_cut)]

    def consume_tasks(z, total, guarded):
        def task(lo):
            carry = trans[lo : lo + SUBS, :]
            for i in range(STEP_LEVELS):
                at = slice(i * LANES, (i + 1) * LANES)
                following = carry * jnp.exp2(softplus(z[lo : lo + SUBS, at], guarded) * rate)
                term = following
                if both:
                    share = softplus(z[gpts + lo : gpts + lo + SUBS, at], guarded)
                    term = (carry - following) * share
                total[i] = term if total[i] is None else total[i] + term
                carry = following
            trans[lo : lo + SUBS, :] = carry

        return [functools.partial(task, lo) for lo in range(0, gpts, SUBS)]

    def woven(main, side):
        done = 0
        for n, task in enumerate(main):
            while done < len(side) and done * len(main) <= n * len(side):
                side[done]()
                done += 1
            task()
        for task in side[done:]:
            task()

    def plain(tasks):
        for task in tasks:
            task()

    def run(guarded):
        trans[...] = start
        if not both:
            parts[0:SUBS, :] = jnp.sum(start.reshape(gpts // SUBS, SUBS, LANES), axis=0)

        def step(t, z, z_next, hid_next, hid_later, one_later, one_last):
            total = [None] * STEP_LEVELS
            side = (
                optics_tasks(hid_next, z_next)
                + second_tasks(one_later, hid_later)
                + first_tasks(t + 3, one_last)
            )
            woven(consume_tasks(z, total, guarded), side)
            for i in range(STEP_LEVELS):
                at = pl.multiple_of((t * STEP_LEVELS + i + 1) * SUBS, SUBS)
                parts[pl.ds(at, SUBS), :] = total[i]

        def two(i, _):
            step(2 * i, z_a, z_b, hid_b, hid_a, one_a, one_b)
            step(2 * i + 1, z_b, z_a, hid_a, hid_b, one_b, one_a)
            return 0

        plain(first_tasks(0, one_a))
        plain(second_tasks(one_a, hid_a))
        plain(first_tasks(1, one_b))
        plain(optics_tasks(hid_a, z_a))
        plain(second_tasks(one_b, hid_b))
        plain(first_tasks(2, one_a))
        lax.fori_loop(0, steps // 2, two, 0)

    peak[...] = jnp.ones_like(peak)
    run(False)

    @pl.when(jnp.max(peak[...].astype(F32)) * jnp.max(reach[...]) > SAFE)
    def _():
        run(True)

    emitted = None
    for s in range(SUBS):
        part = parts[pl.ds(s + SUBS, levels, stride=SUBS), :]
        if not both:
            part = parts[pl.ds(s, levels, stride=SUBS), :] - part
        emitted = part if emitted is None else emitted + part
    return emitted


def sweep_scratch(hid, rows, gpts, levels):
    wide = STEP_LEVELS * LANES
    return [
        pltpu.VMEM((hid, wide), BF16),
        pltpu.VMEM((hid, wide), BF16),
        pltpu.VMEM((2 * hid, wide), BF16),
        pltpu.VMEM((2 * hid, wide), BF16),
        pltpu.VMEM((rows, wide), F32),
        pltpu.VMEM((rows, wide), F32),
        pltpu.VMEM((gpts, LANES), F32),
        pltpu.VMEM(((levels + 1) * SUBS, LANES), F32),
        pltpu.VMEM((2 * SUBS, LANES), BF16),
    ]


def longwave_body(which, packed, first, bias, second, heads, reach, out, *buffers):
    gpts = heads.shape[0] // 2
    levels = out.shape[0]
    x = packed.at[which]
    emitted = sweep(
        x, first, bias, second, heads, reach, jnp.ones((gpts, LANES), F32), gpts,
        -depth_scale * LOG2E, True, buffers,
    )
    planck = jnp.exp(0.25 * x[pl.ds(0, levels, stride=SUBS), :])
    out[...] = -(heat_scale / gpts) * planck * emitted


def shortwave_body(
    count, kept_x, kept_cos, in_x, first, bias, second, heads, reach, flux, out, work_x, *buffers
):
    cells, half = kept_x.shape
    gpts = heads.shape[0]
    slot = iota((half, half), 1) - count[0, 0]
    placed = jnp.where(slot == iota((half, half), 0), 1.0, 0.0).astype(BF16)
    work_x[...] = kept_x[...] + mm(in_x[0:cells, :], placed)
    cosine = kept_cos[...] + mm(in_x[cells:, :], placed)[0:SUBS]
    cosine = jnp.where(cosine > 0.0, cosine, 1.0)
    emitted = sweep(
        work_x, first, bias, second, heads, reach, flux[...], gpts,
        (-depth_scale * LOG2E) / cosine, False, buffers,
    )
    out[...] = (heat_scale / gpts) * cosine[0:1] * emitted


def finish_body(me, count, long_first, long_last, work, partner, slot_of, *rest):
    pieces, heat = rest[:-1], rest[-1]
    levels, cols = heat.shape
    half = cols // 2
    slab = pieces[0].shape[0]
    sunlit = count[0, 0]
    for lo, long in ((0, long_first), (half, long_last)):
        slot = slot_of[:, lo : lo + half]
        here = slot < half
        place = jnp.where(here, slot, slot + half - sunlit) & (half - 1)
        lit = slot < sunlit
        for r in range(0, levels, SUBS):
            near = lane_take(work[r : r + SUBS, :], place)
            far = lane_take(partner[r : r + SUBS, :], place)
            short = jnp.where(lit, jnp.where(here, near, far), 0.0)
            heat[r : r + SUBS, lo : lo + half] = long[r : r + SUBS, :] + short
    for bit, out in enumerate(pieces):
        out[...] = heat[pl.ds(pl.multiple_of((me[0] ^ bit) * slab, SUBS), slab), :]


def add_body(me, closed, *rest):
    pieces, out = rest[:-1], rest[-1]
    cols = pieces[0].shape[1]
    for bit, piece in enumerate(pieces):
        at = pl.ds(pl.multiple_of((me[0] ^ bit) * cols, LANES), cols)
        out[:, at] = closed[:, at] + piece[...]


def per_device(
    potential, species, diffusion, neighbours, listing, day_count, zenith,
    lw_first, lw_bias, lw_second, lw_depth, lw_fraction,
    sw_first, sw_bias, sw_second, sw_depth, solar_flux,
):
    n_group = lax.axis_size("group")
    n_tile = lax.axis_size("tile")
    assert n_group & (n_group - 1) == 0 and n_tile % 2 == 0
    me = lax.axis_index("group").astype(jnp.int32).reshape(1)
    place = lax.axis_index("tile").astype(jnp.int32).reshape(1)
    slab, tile = potential.shape
    gases = species.shape[0]
    cols = tile // n_group
    half = cols // 2
    levels = slab * n_group
    hid = lw_first.shape[1]
    lw_gpts = lw_depth.shape[1]
    sw_gpts = sw_depth.shape[1]

    def outward(value):
        across = [(i, (i + 1 if i % 2 else i - 1) % n_tile) for i in range(n_tile)]
        return lax.ppermute(value, "tile", across)

    def paired(value):
        return lax.ppermute(value, "tile", [(i, i ^ 1) for i in range(n_tile)])

    def swapped(value, bit):
        return lax.ppermute(value, "group", [(i, i ^ bit) for i in range(n_group)])

    def exchanged(pieces):
        bits = range(n_group - 1, 0, -1)
        moved = {bit: swapped(pieces[bit], bit) for bit in bits}
        return [pieces[0], *(moved[bit] for bit in range(1, n_group))]

    near = neighbours.shape[0]
    framing, *gas_cuts = call(
        pack_body,
        [shaped((slab + 2 * near, tile), F32)] + [shaped((gases, slab, cols), BF16)] * n_group,
        [me, potential, neighbours, diffusion, species],
        [
            pltpu.VMEM(neighbours.shape, jnp.int32),
            pltpu.VMEM(diffusion.shape, F32),
            pltpu.SemaphoreType.DMA((3 + n_group,)),
        ],
        where=HBM,
    )
    outer = outward(framing)
    inner = paired(framing)
    gas_pieces = exchanged(gas_cuts)

    (
        kept, sent, kept_cos, sent_cos, slot_of,
        lw_one, lw_shift, lw_two, lw_heads, lw_reach,
        sw_one, sw_shift, sw_two, sw_heads, sw_reach, flux,
    ) = call(
        prepare_body,
        [
            shaped((cols, half), BF16),
            shaped((cols, half), BF16),
            shaped((SUBS, half), F32),
            shaped((2 * SUBS, half), BF16),
            shaped((SUBS, cols), jnp.int32),
            shaped(lw_first.shape[::-1], BF16),
            shaped((hid, LANES), F32),
            shaped(lw_second.shape[::-1], BF16),
            shaped((2 * lw_gpts, 2 * hid), BF16),
            shaped((SUBS, LANES), F32),
            shaped(sw_first.shape[::-1], BF16),
            shaped((hid, LANES), F32),
            shaped(sw_second.shape[::-1], BF16),
            shaped((sw_gpts, 2 * hid), BF16),
            shaped((SUBS, LANES), F32),
            shaped((sw_gpts, LANES), F32),
        ],
        [
            day_count, listing, zenith,
            lw_first, lw_bias[None], lw_second, lw_depth, lw_fraction,
            sw_first, sw_bias[None], sw_second, sw_depth, solar_flux[None],
        ],
        after=framing,
    )

    third, *warm_cuts = call(
        sections_body,
        [shaped((slab, tile + 2 * HW), F32)] + [shaped((slab, cols), BF16)] * n_group,
        [me, place, outer, inner, potential, neighbours, diffusion],
        [pltpu.VMEM((slab, 3 * tile), F32)] * 3
        + [pltpu.VMEM((3, *neighbours.shape), jnp.int32), pltpu.VMEM((3, *diffusion.shape), F32)],
        flops=10_000_000,
    )
    warm_pieces = exchanged(warm_cuts)
    (closed,) = call(
        closing_body, [shaped((slab, tile), F32)], [third, neighbours, diffusion], flops=2_000_000
    )

    cells = levels * SUBS
    packed, out_x, kept_x = call(
        functools.partial(join_body, n_group),
        [
            shaped((cols // LANES, cells, LANES), F32),
            shaped((cells + 2 * SUBS, half), BF16),
            shaped((cells, half), F32),
        ],
        [me, *gas_pieces, *warm_pieces, kept, sent, sent_cos],
        [pltpu.VMEM((SUBS * slab, LANES), F32)],
    )
    in_x = paired(out_x)

    def longwave(which):
        (heat,) = call(
            functools.partial(longwave_body, which),
            [shaped((levels, half), F32)],
            [packed, lw_one, lw_shift, lw_two, lw_heads, lw_reach],
            sweep_scratch(hid, 2 * lw_gpts, lw_gpts, levels),
            flops=4 * levels * half * hid * lw_gpts,
            trans=5 * levels * half * lw_gpts,
            after=work if which else None,
        )
        return heat

    long_first = longwave(0)
    (work,) = call(
        shortwave_body,
        [shaped((levels, half), F32)],
        [day_count, kept_x, kept_cos, in_x, sw_one, sw_shift, sw_two, sw_heads, sw_reach, flux],
        [pltpu.VMEM((cells, half), F32)] + sweep_scratch(hid, sw_gpts, sw_gpts, levels),
        flops=2 * levels * half * hid * sw_gpts,
        trans=3 * levels * half * sw_gpts,
        after=long_first,
    )
    partner = paired(work)
    long_last = longwave(1)
    heat_cuts = call(
        finish_body,
        [shaped((slab, cols), F32)] * n_group,
        [me, day_count, long_first, long_last, work, partner, slot_of],
        [pltpu.VMEM((levels, cols), F32)],
    )
    heat_pieces = exchanged(heat_cuts)
    (evolved,) = call(add_body, [shaped((slab, tile), F32)], [me, closed, *heat_pieces])
    return evolved


def solution(mesh):
    return jax.shard_map(
        per_device,
        mesh=mesh,
        in_specs=(
            P("group", "tile"),
            P(None, "group", "tile"),
            P(None, "tile"),
            P(None, "tile"),
            P("group", "tile", None),
            P("group", "tile"),
            P("group", "tile", None),
            *([P()] * 10),
        ),
        out_specs=P("group", "tile"),
        check_vma=False,
    )
```

```python
import functools
import math

import jax
import jax.numpy as jnp
from jax import lax
from jax.experimental import pallas as pl
from jax.experimental.pallas import tpu as pltpu
from jax.sharding import PartitionSpec as P

HW = 256
LANES = 128
SUBS = 8
STEP_LEVELS = SUBS // 2

depth_scale = 0.1
heat_scale = 12.0
LOG2E = 1.4426950408889634
LN2 = 0.6931471805599453
SAFE = 120.0

F32 = jnp.float32
BF16 = jnp.bfloat16
VMEM = pl.BlockSpec(memory_space=pltpu.VMEM)
ANY = pl.BlockSpec(memory_space=pl.ANY)
HBM = pl.BlockSpec(memory_space=pltpu.HBM)
SMEM = pl.BlockSpec(memory_space=pltpu.SMEM)
PARAMS = pltpu.CompilerParams(vmem_limit_bytes=48 * 1024 * 1024)


def call(body, outs, ins, scratch=(), flops=0, trans=0, after=None, where=VMEM):
    in_specs = [SMEM if a.size == 1 else where for a in ins]
    if after is not None:
        whole, ins = body, [after, *ins]
        in_specs = [ANY, *in_specs]

        def body(_, *refs):
            whole(*refs)

    return pl.pallas_call(
        body,
        out_shape=outs,
        in_specs=in_specs,
        out_specs=[VMEM for _ in outs],
        scratch_shapes=list(scratch),
        compiler_params=PARAMS,
        cost_estimate=pl.CostEstimate(
            flops=flops,
            transcendentals=trans,
            bytes_accessed=sum(a.size * a.dtype.itemsize for a in list(ins) + list(outs)),
        ),
    )(*ins)


def shaped(shape, dtype):
    return jax.ShapeDtypeStruct(shape, dtype)


def iota(shape, dim):
    return lax.broadcasted_iota(jnp.int32, shape, dim)


def mm(a, b):
    return jnp.dot(a, b, preferred_element_type=F32)


def far_first(n):
    return [0, *range(n - 1, 0, -1)]


def partners(me, pieces):
    return [(me[0] ^ bit, piece) for bit, piece in zip(far_first(len(pieces)), pieces)]


def lane_take(x, idx):
    return jnp.take_along_axis(x, idx, axis=1, mode="promise_in_bounds")


def diffused(src, src_at, table, weight, within, at):
    reach = HW // LANES
    wide = 2 * reach + 1
    rows = src.shape[0]
    groups = range(0, rows, SUBS)
    base = at - src_at
    middle = [src[r : r + SUBS, base : base + LANES] for r in groups]
    total = [jnp.zeros_like(m) for m in middle]
    for k in range(table.shape[0]):
        place = jnp.broadcast_to(table[k : k + 1, within : within + LANES], (SUBS, LANES)) - within
        lane = place & (LANES - 1)
        which = place >> (LANES.bit_length() - 1)
        factor = jnp.broadcast_to(weight[k : k + 1, within : within + LANES], (SUBS, LANES))
        tests = [which == w for w in range(1, wide)]
        for n, r in enumerate(groups):
            near = None
            for w in range(wide):
                lo = base + (w - reach) * LANES
                got = lane_take(src[r : r + SUBS, lo : lo + LANES], lane)
                near = got if w == 0 else jnp.where(tests[w - 1], got, near)
            total[n] = total[n] + factor * (near - middle[n])
    return [(r, m, m + t) for r, m, t in zip(groups, middle, total)]


def pack_body(me, own, table, weight, species, out, *rest):
    pieces, (table_here, weight_here, sems) = rest[:-3], rest[-3:]
    slab = own.shape[0]
    near = table.shape[0]
    cols = pieces[0].shape[2]
    moves = [
        pltpu.make_async_copy(own, out.at[0:slab], sems.at[0]),
        pltpu.make_async_copy(table, table_here, sems.at[1]),
        pltpu.make_async_copy(weight, weight_here, sems.at[2]),
    ]
    for source, piece in partners(me, pieces):
        at = pl.ds(pl.multiple_of(source * cols, LANES), cols)
        moves.append(pltpu.make_async_copy(species.at[:, :, at], piece, sems.at[len(moves)]))
    for move in moves:
        move.start()
    for move in moves:
        move.wait()
    out[slab : slab + near, :] = table_here[...].astype(F32)
    out[slab + near :, :] = weight_here[...]


def sections_body(
    me, place, outer, inner, own, table, weight, third_out, *rest
):
    pieces, (frame, first, second, tables, weights) = rest[:-5], rest[-5:]
    slab, tile = own.shape
    near = table.shape[0]
    cols = tile // len(pieces)
    odd = place[0] & 1
    for side, packed in ((odd, outer), (1 - odd, inner)):
        at = pl.ds(pl.multiple_of(side * (2 * tile), LANES), tile)
        frame[:, at] = packed[0:slab, :]
        tables[side * 2] = packed[slab : slab + near, :].astype(jnp.int32)
        weights[side * 2] = packed[slab + near : slab + 2 * near, :]
    frame[:, tile : 2 * tile] = own[...]
    tables[1] = table[...]
    weights[1] = weight[...]

    def run(src, src_at, halo, put):
        for at in range(tile - halo, 2 * tile + halo, LANES):
            t = at // tile
            for r, _, value in diffused(src, src_at, tables.at[t], weights.at[t], at - t * tile, at):
                put(r, at, value)

    def put_first(r, at, value):
        first[r : r + SUBS, at : at + LANES] = value

    def put_second(r, at, value):
        start = frame[r : r + SUBS, at : at + LANES]
        second[r : r + SUBS, at : at + LANES] = 0.75 * start + 0.25 * value

    def put_third(r, at, value):
        start = frame[r : r + SUBS, at : at + LANES]
        lo = at - tile + HW
        third_out[r : r + SUBS, lo : lo + LANES] = start / 3.0 + (2.0 / 3.0) * value

    run(frame, 0, 3 * HW, put_first)
    run(first, 0, 2 * HW, put_second)
    run(second, 0, HW, put_third)
    for goal, out in partners(me, pieces):
        lo = pl.multiple_of(HW + goal * cols, LANES)
        out[...] = third_out[:, pl.ds(lo, cols)].astype(BF16)


def closing_body(third, table, weight, out):
    tile = out.shape[1]
    for at in range(0, tile, LANES):
        for r, _, value in diffused(third, -HW, table, weight, at, at):
            out[r : r + SUBS, at : at + LANES] = value


def turned_over(matrix):
    return matrix.astype(F32).T


def head_parts(weight, out, at):
    hid, gpts = weight.shape
    scaled = LOG2E * turned_over(weight[...])
    high = scaled.astype(BF16)
    out[at : at + gpts, 0:hid] = high
    out[at : at + gpts, hid:] = (scaled - high.astype(F32)).astype(BF16)


def reach_of(heads):
    rows, depth = heads.shape
    sums = mm(jnp.abs(heads[...]), jnp.ones((depth, LANES), BF16))
    return jnp.max(sums.reshape(rows // SUBS, SUBS, LANES), axis=0)


def prepare_body(
    count, listing, zenith, w1, b1, w2, wd, wf, v1, c1, v2, vd, flux,
    kept_out, sent_out, kept_cos, sent_cos, slot_of,
    w1_out, b1_out, w2_out, heads_out, reach_out, v1_out, c1_out, v2_out, vd_out, vreach_out, flux_out,
):
    for weight, out in ((w1, w1_out), (w2, w2_out), (v1, v1_out), (v2, v2_out)):
        out[...] = (0.5 * turned_over(weight[...])).astype(BF16)
    head_parts(wd, heads_out, 0)
    head_parts(wf, heads_out, wd.shape[1])
    head_parts(vd, vd_out, 0)
    reach_out[...] = reach_of(heads_out)
    vreach_out[...] = reach_of(vd_out)
    for row, out, scale in ((b1, b1_out, 0.5), (c1, c1_out, 0.5), (flux, flux_out, 1.0)):
        out[...] = scale * jnp.broadcast_to(row[...], (LANES, row.shape[1])).T
    cols = listing.shape[-1]
    half = cols // 2
    sunlit = count[0, 0]
    label = iota((cols, half), 0)
    slot = iota((cols, half), 1)
    first = jnp.broadcast_to(listing[0, :, 0:half], (cols, half)) == label
    last = jnp.broadcast_to(listing[0, :, half:cols], (cols, half)) == label
    kept = jnp.where(first & (slot < sunlit), 1.0, 0.0).astype(BF16)
    sent = jnp.where(last & (slot + half < sunlit), 1.0, 0.0).astype(BF16)
    kept_out[...] = kept
    sent_out[...] = sent
    cosine = jnp.broadcast_to(zenith[0].astype(F32), (2 * SUBS, cols)).astype(BF16)
    sent_cos[...] = mm(cosine, sent).astype(BF16)
    kept_cos[...] = mm(cosine, kept)[0:SUBS]
    hits = jnp.where(jnp.concatenate([first, last], axis=1), 1.0, 0.0).astype(BF16)
    numbers = iota((2 * SUBS, cols), 1).astype(F32).astype(BF16)
    found = lax.dot_general(numbers, hits, (((1,), (1,)), ((), ())), preferred_element_type=F32)
    slot_of[...] = found[0:SUBS].astype(jnp.int32)


def join_body(n_group, me, *rest):
    gases, warms = rest[:n_group], rest[n_group : 2 * n_group]
    kept, sent, sent_cos, packed, outgoing, kept_x, spread = rest[2 * n_group :]
    slab = warms[0].shape[0]
    for (source, gas), warm in zip(partners(me, gases), warms):
        for h in range(packed.shape[0]):
            at = slice(h * LANES, (h + 1) * LANES)
            spread[0:slab, :] = warm[:, at].astype(F32)
            for f in range(gas.shape[0]):
                spread[(f + 1) * slab : (f + 2) * slab, :] = gas[f, :, at].astype(F32)
            for l in range(slab):
                row = pl.multiple_of((source * slab + l) * SUBS, SUBS)
                packed[h, pl.ds(row, SUBS), :] = spread[pl.ds(l, SUBS, stride=slab), :]
    cells = packed.shape[1]
    first, last = packed[0].astype(BF16), packed[1].astype(BF16)
    outgoing[0:cells, :] = (mm(first, sent[0:LANES]) + mm(last, sent[LANES:])).astype(BF16)
    outgoing[cells:, :] = sent_cos[...]
    kept_x[...] = mm(first, kept[0:LANES]) + mm(last, kept[LANES:])


def softplus(z, guarded):
    if not guarded:
        return jnp.log(1.0 + jnp.exp2(z))
    return jnp.maximum(z * LN2, jnp.log(1.0 + jnp.exp2(jnp.minimum(z, SAFE))))


def sweep(x, first, bias, second, heads, reach, start, gpts, rate, both, buffers, form):
    one_a, one_b, hid_a, hid_b, z_a, z_b, trans, parts, peak = buffers
    levels = x.shape[0] // SUBS
    steps = levels // STEP_LEVELS
    wide = STEP_LEVELS * LANES
    rows = heads.shape[0]
    col_cut = wide // 2
    chunk = {0: SUBS, 1: 4 * SUBS, 2: 8 * SUBS}[form]
    units = first.shape[0]
    unit_cut = units // 2

    def first_tasks(t, out):
        def task(r):
            row = jnp.minimum(t, steps - 1) * (STEP_LEVELS * SUBS)
            tiles = [
                x[pl.ds(pl.multiple_of(row + i * SUBS, SUBS), SUBS), :] for i in range(STEP_LEVELS)
            ]
            v = mm(first[r : r + unit_cut, :], jnp.concatenate(tiles, axis=1).astype(BF16))
            v = v + jnp.concatenate([bias[r : r + unit_cut, :]] * STEP_LEVELS, axis=1)
            out[r : r + unit_cut, :] = (v + v * jnp.tanh(v)).astype(BF16)

        return [functools.partial(task, r) for r in range(0, units, unit_cut)]

    def second_tasks(one, out):
        def task(r):
            v = mm(second[r : r + unit_cut, :], one[...])
            value = (v + v * jnp.tanh(v)).astype(BF16)
            out[r : r + unit_cut, :] = value
            out[units + r : units + r + unit_cut, :] = value
            most = peak[...]
            for i in range(0, unit_cut, 2 * SUBS):
                for at in range(0, wide, LANES):
                    most = jnp.maximum(most, value[i : i + 2 * SUBS, at : at + LANES])
            peak[...] = most

        return [functools.partial(task, r) for r in range(0, units, unit_cut)]

    def optics_tasks(hid, out):
        def task(lo):
            at = slice(lo, lo + col_cut)
            out[:, at] = mm(heads[...], hid[:, at])

        return [functools.partial(task, lo) for lo in range(0, wide, col_cut)]

    def consume_tasks(z, total, guarded):
        def product(lo):
            if form == 2:
                return mm(heads[lo : lo + chunk, :], z[...])
            return z[lo : lo + chunk, :]

        def task(lo):
            carry = trans[lo : lo + chunk, :]
            depth = product(lo)
            share = product(gpts + lo) if both else None
            for i in range(STEP_LEVELS):
                at = slice(i * LANES, (i + 1) * LANES)
                following = carry * jnp.exp2(softplus(depth[:, at], guarded) * rate)
                term = following
                if both:
                    term = (carry - following) * softplus(share[:, at], guarded)
                for r in range(0, chunk, SUBS):
                    part = term[r : r + SUBS]
                    total[i] = part if total[i] is None else total[i] + part
                carry = following
            trans[lo : lo + chunk, :] = carry

        return [functools.partial(task, lo) for lo in range(0, gpts, chunk)]

    def woven(main, side):
        done = 0
        for n, task in enumerate(main):
            while done < len(side) and done * len(main) <= n * len(side):
                side[done]()
                done += 1
            task()
        for task in side[done:]:
            task()

    def plain(tasks):
        for task in tasks:
            task()

    def run(guarded):
        trans[...] = start
        if not both:
            parts[0:SUBS, :] = jnp.sum(start.reshape(gpts // SUBS, SUBS, LANES), axis=0)

        def step(t, z, z_next, hid_next, hid_later, one_later, one_last):
            total = [None] * STEP_LEVELS
            side = second_tasks(one_later, hid_later) + first_tasks(t + (2 if form == 2 else 3), one_last)
            if form == 2:
                woven(consume_tasks(z, total, guarded), side)
            elif form == 1:
                plain(optics_tasks(hid_next, z_next) + side + consume_tasks(z, total, guarded))
            else:
                woven(consume_tasks(z, total, guarded), optics_tasks(hid_next, z_next) + side)
            for i in range(STEP_LEVELS):
                at = pl.multiple_of((t * STEP_LEVELS + i + 1) * SUBS, SUBS)
                parts[pl.ds(at, SUBS), :] = total[i]

        def two(i, _):
            if form == 2:
                step(2 * i, hid_a, None, None, hid_b, one_b, one_a)
                step(2 * i + 1, hid_b, None, None, hid_a, one_a, one_b)
            else:
                step(2 * i, z_a, z_b, hid_b, hid_a, one_a, one_b)
                step(2 * i + 1, z_b, z_a, hid_a, hid_b, one_b, one_a)
            return 0

        plain(first_tasks(0, one_a))
        plain(second_tasks(one_a, hid_a))
        plain(first_tasks(1, one_b))
        if form != 2:
            plain(optics_tasks(hid_a, z_a))
            plain(second_tasks(one_b, hid_b))
            plain(first_tasks(2, one_a))
        lax.fori_loop(0, steps // 2, two, 0)

    peak[...] = jnp.ones_like(peak)
    run(False)

    @pl.when(jnp.max(peak[...].astype(F32)) * jnp.max(reach[...]) > SAFE)
    def _():
        run(True)

    emitted = None
    for s in range(SUBS):
        part = parts[pl.ds(s + SUBS, levels, stride=SUBS), :]
        if not both:
            part = parts[pl.ds(s, levels, stride=SUBS), :] - part
        emitted = part if emitted is None else emitted + part
    return emitted


def sweep_scratch(hid, rows, gpts, levels):
    wide = STEP_LEVELS * LANES
    return [
        pltpu.VMEM((hid, wide), BF16),
        pltpu.VMEM((hid, wide), BF16),
        pltpu.VMEM((2 * hid, wide), BF16),
        pltpu.VMEM((2 * hid, wide), BF16),
        pltpu.VMEM((rows, wide), F32),
        pltpu.VMEM((rows, wide), F32),
        pltpu.VMEM((gpts, LANES), F32),
        pltpu.VMEM(((levels + 1) * SUBS, LANES), F32),
        pltpu.VMEM((2 * SUBS, LANES), BF16),
    ]


def longwave_body(which, packed, first, bias, second, heads, reach, out, *buffers):
    gpts = heads.shape[0] // 2
    levels = out.shape[0]
    x = packed.at[which]
    emitted = sweep(
        x, first, bias, second, heads, reach, jnp.ones((gpts, LANES), F32), gpts,
        -depth_scale * LOG2E, True, buffers, 1 + which,
    )
    planck = jnp.exp(0.25 * x[pl.ds(0, levels, stride=SUBS), :])
    out[...] = -(heat_scale / gpts) * planck * emitted


def shortwave_body(
    count, kept_x, kept_cos, in_x, first, bias, second, heads, reach, flux, out, work_x, *buffers
):
    cells, half = kept_x.shape
    gpts = heads.shape[0]
    slot = iota((half, half), 1) - count[0, 0]
    placed = jnp.where(slot == iota((half, half), 0), 1.0, 0.0).astype(BF16)
    work_x[...] = kept_x[...] + mm(in_x[0:cells, :], placed)
    cosine = kept_cos[...] + mm(in_x[cells:, :], placed)[0:SUBS]
    cosine = jnp.where(cosine > 0.0, cosine, 1.0)
    emitted = sweep(
        work_x, first, bias, second, heads, reach, flux[...], gpts,
        (-depth_scale * LOG2E) / cosine, False, buffers, 0,
    )
    out[...] = (heat_scale / gpts) * cosine[0:1] * emitted


def finish_body(me, count, long_first, long_last, work, partner, slot_of, *rest):
    pieces, heat = rest[:-1], rest[-1]
    levels, cols = heat.shape
    half = cols // 2
    slab = pieces[0].shape[0]
    sunlit = count[0, 0]
    for lo, long in ((0, long_first), (half, long_last)):
        slot = slot_of[:, lo : lo + half]
        here = slot < half
        place = jnp.where(here, slot, slot + half - sunlit) & (half - 1)
        lit = slot < sunlit
        for r in range(0, levels, SUBS):
            near = lane_take(work[r : r + SUBS, :], place)
            far = lane_take(partner[r : r + SUBS, :], place)
            short = jnp.where(lit, jnp.where(here, near, far), 0.0)
            heat[r : r + SUBS, lo : lo + half] = long[r : r + SUBS, :] + short
    for goal, out in partners(me, pieces):
        out[...] = heat[pl.ds(pl.multiple_of(goal * slab, SUBS), slab), :]


def add_body(me, closed, *rest):
    pieces, out = rest[:-1], rest[-1]
    cols = pieces[0].shape[1]
    for source, piece in partners(me, pieces):
        at = pl.ds(pl.multiple_of(source * cols, LANES), cols)
        out[:, at] = closed[:, at] + piece[...]


def per_device(
    potential, species, diffusion, neighbours, listing, day_count, zenith,
    lw_first, lw_bias, lw_second, lw_depth, lw_fraction,
    sw_first, sw_bias, sw_second, sw_depth, solar_flux,
):
    n_group = lax.axis_size("group")
    n_tile = lax.axis_size("tile")
    assert n_group & (n_group - 1) == 0 and n_tile % 2 == 0
    me = lax.axis_index("group").astype(jnp.int32).reshape(1)
    place = lax.axis_index("tile").astype(jnp.int32).reshape(1)
    slab, tile = potential.shape
    gases = species.shape[0]
    cols = tile // n_group
    half = cols // 2
    levels = slab * n_group
    hid = lw_first.shape[1]
    lw_gpts = lw_depth.shape[1]
    sw_gpts = sw_depth.shape[1]

    def outward(value):
        across = [(i, (i + 1 if i % 2 else i - 1) % n_tile) for i in range(n_tile)]
        return lax.ppermute(value, "tile", across)

    def paired(value):
        return lax.ppermute(value, "tile", [(i, i ^ 1) for i in range(n_tile)])

    def swapped(value, bit):
        return lax.ppermute(value, "group", [(i, i ^ bit) for i in range(n_group)])

    def exchanged(pieces):
        return [swapped(p, bit) if bit else p for bit, p in zip(far_first(n_group), pieces)]

    near = neighbours.shape[0]
    raw = (potential, neighbours, diffusion, species)
    framing, *gas_cuts = call(
        pack_body,
        [shaped((slab + 2 * near, tile), F32)] + [shaped((gases, slab, cols), BF16)] * n_group,
        [me, *(pltpu.with_memory_space_constraint(a, pltpu.HBM) for a in raw)],
        [
            pltpu.VMEM(neighbours.shape, jnp.int32),
            pltpu.VMEM(diffusion.shape, F32),
            pltpu.SemaphoreType.DMA((3 + n_group,)),
        ],
        where=HBM,
    )
    inner = paired(framing)
    outer = outward(framing)
    gas_pieces = exchanged(gas_cuts)

    (
        kept, sent, kept_cos, sent_cos, slot_of,
        lw_one, lw_shift, lw_two, lw_heads, lw_reach,
        sw_one, sw_shift, sw_two, sw_heads, sw_reach, flux,
    ) = call(
        prepare_body,
        [
            shaped((cols, half), BF16),
            shaped((cols, half), BF16),
            shaped((SUBS, half), F32),
            shaped((2 * SUBS, half), BF16),
            shaped((SUBS, cols), jnp.int32),
            shaped(lw_first.shape[::-1], BF16),
            shaped((hid, LANES), F32),
            shaped(lw_second.shape[::-1], BF16),
            shaped((2 * lw_gpts, 2 * hid), BF16),
            shaped((SUBS, LANES), F32),
            shaped(sw_first.shape[::-1], BF16),
            shaped((hid, LANES), F32),
            shaped(sw_second.shape[::-1], BF16),
            shaped((sw_gpts, 2 * hid), BF16),
            shaped((SUBS, LANES), F32),
            shaped((sw_gpts, LANES), F32),
        ],
        [
            day_count, listing, zenith,
            lw_first, lw_bias[None], lw_second, lw_depth, lw_fraction,
            sw_first, sw_bias[None], sw_second, sw_depth, solar_flux[None],
        ],
        after=framing,
    )

    third, *warm_cuts = call(
        sections_body,
        [shaped((slab, tile + 2 * HW), F32)] + [shaped((slab, cols), BF16)] * n_group,
        [me, place, outer, inner, potential, neighbours, diffusion],
        [pltpu.VMEM((slab, 3 * tile), F32)] * 3
        + [pltpu.VMEM((3, *neighbours.shape), jnp.int32), pltpu.VMEM((3, *diffusion.shape), F32)],
        flops=10_000_000,
    )
    warm_pieces = exchanged(warm_cuts)
    (closed,) = call(
        closing_body, [shaped((slab, tile), F32)], [third, neighbours, diffusion], flops=2_000_000
    )

    cells = levels * SUBS
    packed, out_x, kept_x = call(
        functools.partial(join_body, n_group),
        [
            shaped((cols // LANES, cells, LANES), F32),
            shaped((cells + 2 * SUBS, half), BF16),
            shaped((cells, half), F32),
        ],
        [me, *gas_pieces, *warm_pieces, kept, sent, sent_cos],
        [pltpu.VMEM((SUBS * slab, LANES), F32)],
    )
    in_x = paired(out_x)

    def longwave(which):
        (heat,) = call(
            functools.partial(longwave_body, which),
            [shaped((levels, half), F32)],
            [packed, lw_one, lw_shift, lw_two, lw_heads, lw_reach],
            sweep_scratch(hid, 2 * lw_gpts, lw_gpts, levels),
            flops=4 * levels * half * hid * lw_gpts,
            trans=5 * levels * half * lw_gpts,
            after=work if which else None,
        )
        return heat

    long_first = longwave(0)
    (work,) = call(
        shortwave_body,
        [shaped((levels, half), F32)],
        [day_count, kept_x, kept_cos, in_x, sw_one, sw_shift, sw_two, sw_heads, sw_reach, flux],
        [pltpu.VMEM((cells, half), F32)] + sweep_scratch(hid, sw_gpts, sw_gpts, levels),
        flops=2 * levels * half * hid * sw_gpts,
        trans=3 * levels * half * sw_gpts,
        after=long_first,
    )
    partner = paired(work)
    long_last = longwave(1)
    heat_cuts = call(
        finish_body,
        [shaped((slab, cols), F32)] * n_group,
        [me, day_count, long_first, long_last, work, partner, slot_of],
        [pltpu.VMEM((levels, cols), F32)],
    )
    heat_pieces = exchanged(heat_cuts)
    (evolved,) = call(add_body, [shaped((slab, tile), F32)], [me, closed, *heat_pieces])
    return evolved


def solution(mesh):
    return jax.shard_map(
        per_device,
        mesh=mesh,
        in_specs=(
            P("group", "tile"),
            P(None, "group", "tile"),
            P(None, "tile"),
            P(None, "tile"),
            P("group", "tile", None),
            P("group", "tile"),
            P("group", "tile", None),
            *([P()] * 10),
        ),
        out_specs=P("group", "tile"),
        check_vma=False,
    )
```

```python
import functools
import math

import jax
import jax.numpy as jnp
from jax import lax
from jax.experimental import pallas as pl
from jax.experimental.pallas import tpu as pltpu
from jax.sharding import PartitionSpec as P

HW = 256
LANES = 128
SUBS = 8
STEP_LEVELS = SUBS // 2

depth_scale = 0.1
heat_scale = 12.0
LOG2E = 1.4426950408889634
LN2 = 0.6931471805599453
SAFE = 120.0

F32 = jnp.float32
BF16 = jnp.bfloat16
VMEM = pl.BlockSpec(memory_space=pltpu.VMEM)
ANY = pl.BlockSpec(memory_space=pl.ANY)
HBM = pl.BlockSpec(memory_space=pltpu.HBM)
SMEM = pl.BlockSpec(memory_space=pltpu.SMEM)
PARAMS = pltpu.CompilerParams(vmem_limit_bytes=48 * 1024 * 1024)


def call(body, outs, ins, scratch=(), flops=0, trans=0, after=None, where=VMEM):
    in_specs = [SMEM if a.size == 1 else where for a in ins]
    if after is not None:
        whole, ins = body, [after, *ins]
        in_specs = [ANY, *in_specs]

        def body(_, *refs):
            whole(*refs)

    return pl.pallas_call(
        body,
        out_shape=outs,
        in_specs=in_specs,
        out_specs=[VMEM for _ in outs],
        scratch_shapes=list(scratch),
        compiler_params=PARAMS,
        cost_estimate=pl.CostEstimate(
            flops=flops,
            transcendentals=trans,
            bytes_accessed=sum(a.size * a.dtype.itemsize for a in list(ins) + list(outs)),
        ),
    )(*ins)


def shaped(shape, dtype):
    return jax.ShapeDtypeStruct(shape, dtype)


def iota(shape, dim):
    return lax.broadcasted_iota(jnp.int32, shape, dim)


def mm(a, b):
    return jnp.dot(a, b, preferred_element_type=F32)


def far_first(n):
    return [0, *range(n - 1, 0, -1)]


def partners(me, pieces):
    return [(me[0] ^ bit, piece) for bit, piece in zip(far_first(len(pieces)), pieces)]


def lane_take(x, idx):
    return jnp.take_along_axis(x, idx, axis=1, mode="promise_in_bounds")


def diffused(src, src_at, table, weight, within, at):
    reach = HW // LANES
    wide = 2 * reach + 1
    rows = src.shape[0]
    groups = range(0, rows, SUBS)
    base = at - src_at
    middle = [src[r : r + SUBS, base : base + LANES] for r in groups]
    total = [jnp.zeros_like(m) for m in middle]
    for k in range(table.shape[0]):
        place = jnp.broadcast_to(table[k : k + 1, within : within + LANES], (SUBS, LANES)) - within
        lane = place & (LANES - 1)
        which = place >> (LANES.bit_length() - 1)
        factor = jnp.broadcast_to(weight[k : k + 1, within : within + LANES], (SUBS, LANES))
        tests = [which == w for w in range(1, wide)]
        for n, r in enumerate(groups):
            near = None
            for w in range(wide):
                lo = base + (w - reach) * LANES
                got = lane_take(src[r : r + SUBS, lo : lo + LANES], lane)
                near = got if w == 0 else jnp.where(tests[w - 1], got, near)
            total[n] = total[n] + factor * (near - middle[n])
    return [(r, m, m + t) for r, m, t in zip(groups, middle, total)]


def pack_body(me, own, table, weight, species, out, *rest):
    pieces, (table_here, weight_here, sems) = rest[:-3], rest[-3:]
    slab = own.shape[0]
    near = table.shape[0]
    cols = pieces[0].shape[2]
    moves = [
        pltpu.make_async_copy(own, out.at[0:slab], sems.at[0]),
        pltpu.make_async_copy(table, table_here, sems.at[1]),
        pltpu.make_async_copy(weight, weight_here, sems.at[2]),
    ]
    for source, piece in partners(me, pieces):
        at = pl.ds(pl.multiple_of(source * cols, LANES), cols)
        moves.append(pltpu.make_async_copy(species.at[:, :, at], piece, sems.at[len(moves)]))
    for move in moves:
        move.start()
    for move in moves:
        move.wait()
    out[slab : slab + near, :] = table_here[...].astype(F32)
    out[slab + near :, :] = weight_here[...]


def sections_body(
    me, place, outer, inner, own, table, weight, third_out, *rest
):
    pieces, (frame, first, second, tables, weights) = rest[:-5], rest[-5:]
    slab, tile = own.shape
    near = table.shape[0]
    cols = tile // len(pieces)
    odd = place[0] & 1
    for side, packed in ((odd, outer), (1 - odd, inner)):
        at = pl.ds(pl.multiple_of(side * (2 * tile), LANES), tile)
        frame[:, at] = packed[0:slab, :]
        tables[side * 2] = packed[slab : slab + near, :].astype(jnp.int32)
        weights[side * 2] = packed[slab + near : slab + 2 * near, :]
    frame[:, tile : 2 * tile] = own[...]
    tables[1] = table[...]
    weights[1] = weight[...]

    def run(src, src_at, halo, put):
        for at in range(tile - halo, 2 * tile + halo, LANES):
            t = at // tile
            for r, _, value in diffused(src, src_at, tables.at[t], weights.at[t], at - t * tile, at):
                put(r, at, value)

    def put_first(r, at, value):
        first[r : r + SUBS, at : at + LANES] = value

    def put_second(r, at, value):
        start = frame[r : r + SUBS, at : at + LANES]
        second[r : r + SUBS, at : at + LANES] = 0.75 * start + 0.25 * value

    def put_third(r, at, value):
        start = frame[r : r + SUBS, at : at + LANES]
        lo = at - tile + HW
        third_out[r : r + SUBS, lo : lo + LANES] = start / 3.0 + (2.0 / 3.0) * value

    run(frame, 0, 3 * HW, put_first)
    run(first, 0, 2 * HW, put_second)
    run(second, 0, HW, put_third)
    for goal, out in partners(me, pieces):
        lo = pl.multiple_of(HW + goal * cols, LANES)
        out[...] = third_out[:, pl.ds(lo, cols)].astype(BF16)


def closing_body(third, table, weight, out):
    tile = out.shape[1]
    for at in range(0, tile, LANES):
        for r, _, value in diffused(third, -HW, table, weight, at, at):
            out[r : r + SUBS, at : at + LANES] = value


def turned_over(matrix):
    return matrix.astype(F32).T


def head_parts(weight, out, at):
    hid, gpts = weight.shape
    scaled = LOG2E * turned_over(weight[...])
    high = scaled.astype(BF16)
    out[at : at + gpts, 0:hid] = high
    out[at : at + gpts, hid:] = (scaled - high.astype(F32)).astype(BF16)


def reach_of(heads):
    rows, depth = heads.shape
    sums = mm(jnp.abs(heads[...]), jnp.ones((depth, LANES), BF16))
    return jnp.max(sums.reshape(rows // SUBS, SUBS, LANES), axis=0)


def prepare_body(
    count, listing, zenith, w1, b1, w2, wd, wf, v1, c1, v2, vd, flux,
    kept_out, sent_out, kept_cos, sent_cos, slot_of,
    w1_out, b1_out, w2_out, heads_out, reach_out, v1_out, c1_out, v2_out, vd_out, vreach_out, flux_out,
):
    for weight, out in ((w1, w1_out), (w2, w2_out), (v1, v1_out), (v2, v2_out)):
        out[...] = (0.5 * turned_over(weight[...])).astype(BF16)
    head_parts(wd, heads_out, 0)
    head_parts(wf, heads_out, wd.shape[1])
    head_parts(vd, vd_out, 0)
    reach_out[...] = reach_of(heads_out)
    vreach_out[...] = reach_of(vd_out)
    for row, out, scale in ((b1, b1_out, 0.5), (c1, c1_out, 0.5), (flux, flux_out, 1.0)):
        out[...] = scale * jnp.broadcast_to(row[...], (LANES, row.shape[1])).T
    cols = listing.shape[-1]
    half = cols // 2
    sunlit = count[0, 0]
    label = iota((cols, half), 0)
    slot = iota((cols, half), 1)
    first = jnp.broadcast_to(listing[0, :, 0:half], (cols, half)) == label
    last = jnp.broadcast_to(listing[0, :, half:cols], (cols, half)) == label
    kept = jnp.where(first & (slot < sunlit), 1.0, 0.0).astype(BF16)
    sent = jnp.where(last & (slot + half < sunlit), 1.0, 0.0).astype(BF16)
    kept_out[...] = kept
    sent_out[...] = sent
    cosine = jnp.broadcast_to(zenith[0].astype(F32), (2 * SUBS, cols)).astype(BF16)
    sent_cos[...] = mm(cosine, sent).astype(BF16)
    kept_cos[...] = mm(cosine, kept)[0:SUBS]
    hits = jnp.where(jnp.concatenate([first, last], axis=1), 1.0, 0.0).astype(BF16)
    numbers = iota((2 * SUBS, cols), 1).astype(F32).astype(BF16)
    found = lax.dot_general(numbers, hits, (((1,), (1,)), ((), ())), preferred_element_type=F32)
    slot_of[...] = found[0:SUBS].astype(jnp.int32)


def join_body(n_group, me, *rest):
    gases, warms = rest[:n_group], rest[n_group : 2 * n_group]
    kept, sent, sent_cos, packed, outgoing, kept_x, spread = rest[2 * n_group :]
    slab = warms[0].shape[0]
    for (source, gas), warm in zip(partners(me, gases), warms):
        for h in range(packed.shape[0]):
            at = slice(h * LANES, (h + 1) * LANES)
            spread[0:slab, :] = warm[:, at].astype(F32)
            for f in range(gas.shape[0]):
                spread[(f + 1) * slab : (f + 2) * slab, :] = gas[f, :, at].astype(F32)
            for l in range(slab):
                row = pl.multiple_of((source * slab + l) * SUBS, SUBS)
                packed[h, pl.ds(row, SUBS), :] = spread[pl.ds(l, SUBS, stride=slab), :]
    cells = packed.shape[1]
    first, last = packed[0].astype(BF16), packed[1].astype(BF16)
    outgoing[0:cells, :] = (mm(first, sent[0:LANES]) + mm(last, sent[LANES:])).astype(BF16)
    outgoing[cells:, :] = sent_cos[...]
    kept_x[...] = mm(first, kept[0:LANES]) + mm(last, kept[LANES:])


def softplus(z, guarded):
    if not guarded:
        return jnp.log(1.0 + jnp.exp2(z))
    return jnp.maximum(z * LN2, jnp.log(1.0 + jnp.exp2(jnp.minimum(z, SAFE))))


def silu_of_half(v, form):
    if form == 1:
        return ((v + v) * pl.reciprocal(1.0 + jnp.exp2(v * (-2.0 * LOG2E)), approx=True)).astype(BF16)
    if form == 2:
        half = v.astype(BF16)
        return half + half * jnp.tanh(half)
    return (v + v * jnp.tanh(v)).astype(BF16)


def sweep(x, first, bias, second, heads, reach, start, gpts, rate, both, buffers, form):
    one_a, one_b, hid_a, hid_b, z_a, z_b, trans, parts, peak = buffers
    levels = x.shape[0] // SUBS
    steps = levels // STEP_LEVELS
    wide = STEP_LEVELS * LANES
    rows = heads.shape[0]
    col_cut = wide // 2
    chunk = SUBS
    units = first.shape[0]
    unit_cut = units // 2

    def first_tasks(t, out):
        def task(r):
            row = jnp.minimum(t, steps - 1) * (STEP_LEVELS * SUBS)
            tiles = [
                x[pl.ds(pl.multiple_of(row + i * SUBS, SUBS), SUBS), :] for i in range(STEP_LEVELS)
            ]
            v = mm(first[r : r + unit_cut, :], jnp.concatenate(tiles, axis=1).astype(BF16))
            v = v + jnp.concatenate([bias[r : r + unit_cut, :]] * STEP_LEVELS, axis=1)
            out[r : r + unit_cut, :] = silu_of_half(v, form)

        return [functools.partial(task, r) for r in range(0, units, unit_cut)]

    def second_tasks(one, out):
        def task(r):
            v = mm(second[r : r + unit_cut, :], one[...])
            value = silu_of_half(v, form)
            out[r : r + unit_cut, :] = value
            out[units + r : units + r + unit_cut, :] = value
            most = peak[...]
            for i in range(0, unit_cut, 2 * SUBS):
                for at in range(0, wide, LANES):
                    most = jnp.maximum(most, value[i : i + 2 * SUBS, at : at + LANES])
            peak[...] = most

        return [functools.partial(task, r) for r in range(0, units, unit_cut)]

    def optics_tasks(hid, out):
        def task(lo):
            at = slice(lo, lo + col_cut)
            out[:, at] = mm(heads[...], hid[:, at])

        return [functools.partial(task, lo) for lo in range(0, wide, col_cut)]

    def consume_tasks(z, total, guarded):
        def product(lo):
            return z[lo : lo + chunk, :]

        def task(lo):
            carry = trans[lo : lo + chunk, :]
            depth = product(lo)
            share = product(gpts + lo) if both else None
            for i in range(STEP_LEVELS):
                at = slice(i * LANES, (i + 1) * LANES)
                following = carry * jnp.exp2(softplus(depth[:, at], guarded) * rate)
                term = following
                if both:
                    term = (carry - following) * softplus(share[:, at], guarded)
                for r in range(0, chunk, SUBS):
                    part = term[r : r + SUBS]
                    total[i] = part if total[i] is None else total[i] + part
                carry = following
            trans[lo : lo + chunk, :] = carry

        return [functools.partial(task, lo) for lo in range(0, gpts, chunk)]

    def woven(main, side):
        done = 0
        for n, task in enumerate(main):
            while done < len(side) and done * len(main) <= n * len(side):
                side[done]()
                done += 1
            task()
        for task in side[done:]:
            task()

    def plain(tasks):
        for task in tasks:
            task()

    def run(guarded):
        trans[...] = start
        if not both:
            parts[0:SUBS, :] = jnp.sum(start.reshape(gpts // SUBS, SUBS, LANES), axis=0)

        def step(t, z, z_next, hid_next, hid_later, one_later, one_last):
            total = [None] * STEP_LEVELS
            side = second_tasks(one_later, hid_later) + first_tasks(t + 3, one_last)
            woven(consume_tasks(z, total, guarded), optics_tasks(hid_next, z_next) + side)
            for i in range(STEP_LEVELS):
                at = pl.multiple_of((t * STEP_LEVELS + i + 1) * SUBS, SUBS)
                parts[pl.ds(at, SUBS), :] = total[i]

        def two(i, _):
            step(2 * i, z_a, z_b, hid_b, hid_a, one_a, one_b)
            step(2 * i + 1, z_b, z_a, hid_a, hid_b, one_b, one_a)
            return 0

        plain(first_tasks(0, one_a))
        plain(second_tasks(one_a, hid_a))
        plain(first_tasks(1, one_b))
        plain(optics_tasks(hid_a, z_a))
        plain(second_tasks(one_b, hid_b))
        plain(first_tasks(2, one_a))
        lax.fori_loop(0, steps // 2, two, 0)

    peak[...] = jnp.ones_like(peak)
    run(False)

    @pl.when(jnp.max(peak[...].astype(F32)) * jnp.max(reach[...]) > SAFE)
    def _():
        run(True)

    emitted = None
    for s in range(SUBS):
        part = parts[pl.ds(s + SUBS, levels, stride=SUBS), :]
        if not both:
            part = parts[pl.ds(s, levels, stride=SUBS), :] - part
        emitted = part if emitted is None else emitted + part
    return emitted


def sweep_scratch(hid, rows, gpts, levels):
    wide = STEP_LEVELS * LANES
    return [
        pltpu.VMEM((hid, wide), BF16),
        pltpu.VMEM((hid, wide), BF16),
        pltpu.VMEM((2 * hid, wide), BF16),
        pltpu.VMEM((2 * hid, wide), BF16),
        pltpu.VMEM((rows, wide), F32),
        pltpu.VMEM((rows, wide), F32),
        pltpu.VMEM((gpts, LANES), F32),
        pltpu.VMEM(((levels + 1) * SUBS, LANES), F32),
        pltpu.VMEM((2 * SUBS, LANES), BF16),
    ]


def longwave_body(which, packed, first, bias, second, heads, reach, out, *buffers):
    gpts = heads.shape[0] // 2
    levels = out.shape[0]
    x = packed.at[which]
    emitted = sweep(
        x, first, bias, second, heads, reach, jnp.ones((gpts, LANES), F32), gpts,
        -depth_scale * LOG2E, True, buffers, 1 + which,
    )
    planck = jnp.exp(0.25 * x[pl.ds(0, levels, stride=SUBS), :])
    out[...] = -(heat_scale / gpts) * planck * emitted


def shortwave_body(
    count, kept_x, kept_cos, in_x, first, bias, second, heads, reach, flux, out, work_x, *buffers
):
    cells, half = kept_x.shape
    gpts = heads.shape[0]
    slot = iota((half, half), 1) - count[0, 0]
    placed = jnp.where(slot == iota((half, half), 0), 1.0, 0.0).astype(BF16)
    work_x[...] = kept_x[...] + mm(in_x[0:cells, :], placed)
    cosine = kept_cos[...] + mm(in_x[cells:, :], placed)[0:SUBS]
    cosine = jnp.where(cosine > 0.0, cosine, 1.0)
    emitted = sweep(
        work_x, first, bias, second, heads, reach, flux[...], gpts,
        (-depth_scale * LOG2E) / cosine, False, buffers, 0,
    )
    out[...] = (heat_scale / gpts) * cosine[0:1] * emitted


def finish_body(me, count, long_first, long_last, work, partner, slot_of, *rest):
    pieces, heat = rest[:-1], rest[-1]
    levels, cols = heat.shape
    half = cols // 2
    slab = pieces[0].shape[0]
    sunlit = count[0, 0]
    for lo, long in ((0, long_first), (half, long_last)):
        slot = slot_of[:, lo : lo + half]
        here = slot < half
        place = jnp.where(here, slot, slot + half - sunlit) & (half - 1)
        lit = slot < sunlit
        for r in range(0, levels, SUBS):
            near = lane_take(work[r : r + SUBS, :], place)
            far = lane_take(partner[r : r + SUBS, :], place)
            short = jnp.where(lit, jnp.where(here, near, far), 0.0)
            heat[r : r + SUBS, lo : lo + half] = long[r : r + SUBS, :] + short
    for goal, out in partners(me, pieces):
        out[...] = heat[pl.ds(pl.multiple_of(goal * slab, SUBS), slab), :]


def add_body(me, closed, *rest):
    pieces, out = rest[:-1], rest[-1]
    cols = pieces[0].shape[1]
    for source, piece in partners(me, pieces):
        at = pl.ds(pl.multiple_of(source * cols, LANES), cols)
        out[:, at] = closed[:, at] + piece[...]


def per_device(
    potential, species, diffusion, neighbours, listing, day_count, zenith,
    lw_first, lw_bias, lw_second, lw_depth, lw_fraction,
    sw_first, sw_bias, sw_second, sw_depth, solar_flux,
):
    n_group = lax.axis_size("group")
    n_tile = lax.axis_size("tile")
    assert n_group & (n_group - 1) == 0 and n_tile % 2 == 0
    me = lax.axis_index("group").astype(jnp.int32).reshape(1)
    place = lax.axis_index("tile").astype(jnp.int32).reshape(1)
    slab, tile = potential.shape
    gases = species.shape[0]
    cols = tile // n_group
    half = cols // 2
    levels = slab * n_group
    hid = lw_first.shape[1]
    lw_gpts = lw_depth.shape[1]
    sw_gpts = sw_depth.shape[1]

    def outward(value):
        across = [(i, (i + 1 if i % 2 else i - 1) % n_tile) for i in range(n_tile)]
        return lax.ppermute(value, "tile", across)

    def paired(value):
        return lax.ppermute(value, "tile", [(i, i ^ 1) for i in range(n_tile)])

    def swapped(value, bit):
        return lax.ppermute(value, "group", [(i, i ^ bit) for i in range(n_group)])

    def exchanged(pieces):
        return [swapped(p, bit) if bit else p for bit, p in zip(far_first(n_group), pieces)]

    near = neighbours.shape[0]
    raw = (potential, neighbours, diffusion, species)
    framing, *gas_cuts = call(
        pack_body,
        [shaped((slab + 2 * near, tile), F32)] + [shaped((gases, slab, cols), BF16)] * n_group,
        [me, *(pltpu.with_memory_space_constraint(a, pltpu.HBM) for a in raw)],
        [
            pltpu.VMEM(neighbours.shape, jnp.int32),
            pltpu.VMEM(diffusion.shape, F32),
            pltpu.SemaphoreType.DMA((3 + n_group,)),
        ],
        where=HBM,
    )
    inner = paired(framing)
    outer = outward(framing)
    gas_pieces = exchanged(gas_cuts)

    (
        kept, sent, kept_cos, sent_cos, slot_of,
        lw_one, lw_shift, lw_two, lw_heads, lw_reach,
        sw_one, sw_shift, sw_two, sw_heads, sw_reach, flux,
    ) = call(
        prepare_body,
        [
            shaped((cols, half), BF16),
            shaped((cols, half), BF16),
            shaped((SUBS, half), F32),
            shaped((2 * SUBS, half), BF16),
            shaped((SUBS, cols), jnp.int32),
            shaped(lw_first.shape[::-1], BF16),
            shaped((hid, LANES), F32),
            shaped(lw_second.shape[::-1], BF16),
            shaped((2 * lw_gpts, 2 * hid), BF16),
            shaped((SUBS, LANES), F32),
            shaped(sw_first.shape[::-1], BF16),
            shaped((hid, LANES), F32),
            shaped(sw_second.shape[::-1], BF16),
            shaped((sw_gpts, 2 * hid), BF16),
            shaped((SUBS, LANES), F32),
            shaped((sw_gpts, LANES), F32),
        ],
        [
            day_count, listing, zenith,
            lw_first, lw_bias[None], lw_second, lw_depth, lw_fraction,
            sw_first, sw_bias[None], sw_second, sw_depth, solar_flux[None],
        ],
        after=framing,
    )

    third, *warm_cuts = call(
        sections_body,
        [shaped((slab, tile + 2 * HW), F32)] + [shaped((slab, cols), BF16)] * n_group,
        [me, place, outer, inner, potential, neighbours, diffusion],
        [pltpu.VMEM((slab, 3 * tile), F32)] * 3
        + [pltpu.VMEM((3, *neighbours.shape), jnp.int32), pltpu.VMEM((3, *diffusion.shape), F32)],
        flops=10_000_000,
    )
    warm_pieces = exchanged(warm_cuts)
    (closed,) = call(
        closing_body, [shaped((slab, tile), F32)], [third, neighbours, diffusion], flops=2_000_000
    )

    cells = levels * SUBS
    packed, out_x, kept_x = call(
        functools.partial(join_body, n_group),
        [
            shaped((cols // LANES, cells, LANES), F32),
            shaped((cells + 2 * SUBS, half), BF16),
            shaped((cells, half), F32),
        ],
        [me, *gas_pieces, *warm_pieces, kept, sent, sent_cos],
        [pltpu.VMEM((SUBS * slab, LANES), F32)],
    )
    in_x = paired(out_x)

    def longwave(which):
        (heat,) = call(
            functools.partial(longwave_body, which),
            [shaped((levels, half), F32)],
            [packed, lw_one, lw_shift, lw_two, lw_heads, lw_reach],
            sweep_scratch(hid, 2 * lw_gpts, lw_gpts, levels),
            flops=4 * levels * half * hid * lw_gpts,
            trans=5 * levels * half * lw_gpts,
            after=work if which else None,
        )
        return heat

    long_first = longwave(0)
    (work,) = call(
        shortwave_body,
        [shaped((levels, half), F32)],
        [day_count, kept_x, kept_cos, in_x, sw_one, sw_shift, sw_two, sw_heads, sw_reach, flux],
        [pltpu.VMEM((cells, half), F32)] + sweep_scratch(hid, sw_gpts, sw_gpts, levels),
        flops=2 * levels * half * hid * sw_gpts,
        trans=3 * levels * half * sw_gpts,
        after=long_first,
    )
    partner = paired(work)
    long_last = longwave(1)
    heat_cuts = call(
        finish_body,
        [shaped((slab, cols), F32)] * n_group,
        [me, day_count, long_first, long_last, work, partner, slot_of],
        [pltpu.VMEM((levels, cols), F32)],
    )
    heat_pieces = exchanged(heat_cuts)
    (evolved,) = call(add_body, [shaped((slab, tile), F32)], [me, closed, *heat_pieces])
    return evolved


def solution(mesh):
    return jax.shard_map(
        per_device,
        mesh=mesh,
        in_specs=(
            P("group", "tile"),
            P(None, "group", "tile"),
            P(None, "tile"),
            P(None, "tile"),
            P("group", "tile", None),
            P("group", "tile"),
            P("group", "tile", None),
            *([P()] * 10),
        ),
        out_specs=P("group", "tile"),
        check_vma=False,
    )
```

```python
import functools
import math

import jax
import jax.numpy as jnp
from jax import lax
from jax.experimental import pallas as pl
from jax.experimental.pallas import tpu as pltpu
from jax.sharding import PartitionSpec as P

HW = 256
LANES = 128
SUBS = 8
STEP_LEVELS = SUBS // 2

depth_scale = 0.1
heat_scale = 12.0
LOG2E = 1.4426950408889634
LN2 = 0.6931471805599453
SAFE = 120.0

F32 = jnp.float32
BF16 = jnp.bfloat16
VMEM = pl.BlockSpec(memory_space=pltpu.VMEM)
ANY = pl.BlockSpec(memory_space=pl.ANY)
HBM = pl.BlockSpec(memory_space=pltpu.HBM)
SMEM = pl.BlockSpec(memory_space=pltpu.SMEM)
PARAMS = pltpu.CompilerParams(vmem_limit_bytes=48 * 1024 * 1024)


def call(body, outs, ins, scratch=(), flops=0, trans=0, after=None, where=VMEM):
    in_specs = [SMEM if a.size == 1 else where for a in ins]
    if after is not None:
        whole, ins = body, [after, *ins]
        in_specs = [ANY, *in_specs]

        def body(_, *refs):
            whole(*refs)

    return pl.pallas_call(
        body,
        out_shape=outs,
        in_specs=in_specs,
        out_specs=[VMEM for _ in outs],
        scratch_shapes=list(scratch),
        compiler_params=PARAMS,
        cost_estimate=pl.CostEstimate(
            flops=flops,
            transcendentals=trans,
            bytes_accessed=sum(a.size * a.dtype.itemsize for a in list(ins) + list(outs)),
        ),
    )(*ins)


def shaped(shape, dtype):
    return jax.ShapeDtypeStruct(shape, dtype)


def iota(shape, dim):
    return lax.broadcasted_iota(jnp.int32, shape, dim)


def mm(a, b):
    return jnp.dot(a, b, preferred_element_type=F32)


def far_first(n):
    return [0, *range(n - 1, 0, -1)]


def partners(me, pieces):
    return [(me[0] ^ bit, piece) for bit, piece in zip(far_first(len(pieces)), pieces)]


def lane_take(x, idx):
    return jnp.take_along_axis(x, idx, axis=1, mode="promise_in_bounds")


def diffused(src, src_at, table, weight, within, at):
    reach = HW // LANES
    wide = 2 * reach + 1
    rows = src.shape[0]
    groups = range(0, rows, SUBS)
    base = at - src_at
    middle = [src[r : r + SUBS, base : base + LANES] for r in groups]
    total = [jnp.zeros_like(m) for m in middle]
    for k in range(table.shape[0]):
        place = jnp.broadcast_to(table[k : k + 1, within : within + LANES], (SUBS, LANES)) - within
        lane = place & (LANES - 1)
        which = place >> (LANES.bit_length() - 1)
        factor = jnp.broadcast_to(weight[k : k + 1, within : within + LANES], (SUBS, LANES))
        tests = [which == w for w in range(1, wide)]
        for n, r in enumerate(groups):
            near = None
            for w in range(wide):
                lo = base + (w - reach) * LANES
                got = lane_take(src[r : r + SUBS, lo : lo + LANES], lane)
                near = got if w == 0 else jnp.where(tests[w - 1], got, near)
            total[n] = total[n] + factor * (near - middle[n])
    return [(r, m, m + t) for r, m, t in zip(groups, middle, total)]


def pack_body(me, own, table, weight, species, out, *rest):
    pieces, (table_here, weight_here, sems) = rest[:-3], rest[-3:]
    slab = own.shape[0]
    near = table.shape[0]
    cols = pieces[0].shape[2]
    moves = [
        pltpu.make_async_copy(own, out.at[0:slab], sems.at[0]),
        pltpu.make_async_copy(table, table_here, sems.at[1]),
        pltpu.make_async_copy(weight, weight_here, sems.at[2]),
    ]
    for source, piece in partners(me, pieces):
        at = pl.ds(pl.multiple_of(source * cols, LANES), cols)
        moves.append(pltpu.make_async_copy(species.at[:, :, at], piece, sems.at[len(moves)]))
    for move in moves:
        move.start()
    for move in moves:
        move.wait()
    out[slab : slab + near, :] = table_here[...].astype(F32)
    out[slab + near :, :] = weight_here[...]


def sections_body(
    me, place, outer, inner, own, table, weight, third_out, *rest
):
    pieces, (frame, first, second, tables, weights) = rest[:-5], rest[-5:]
    slab, tile = own.shape
    near = table.shape[0]
    cols = tile // len(pieces)
    odd = place[0] & 1
    for side, packed in ((odd, outer), (1 - odd, inner)):
        at = pl.ds(pl.multiple_of(side * (2 * tile), LANES), tile)
        frame[:, at] = packed[0:slab, :]
        tables[side * 2] = packed[slab : slab + near, :].astype(jnp.int32)
        weights[side * 2] = packed[slab + near : slab + 2 * near, :]
    frame[:, tile : 2 * tile] = own[...]
    tables[1] = table[...]
    weights[1] = weight[...]

    def run(src, src_at, halo, put):
        for at in range(tile - halo, 2 * tile + halo, LANES):
            t = at // tile
            for r, _, value in diffused(src, src_at, tables.at[t], weights.at[t], at - t * tile, at):
                put(r, at, value)

    def put_first(r, at, value):
        first[r : r + SUBS, at : at + LANES] = value

    def put_second(r, at, value):
        start = frame[r : r + SUBS, at : at + LANES]
        second[r : r + SUBS, at : at + LANES] = 0.75 * start + 0.25 * value

    def put_third(r, at, value):
        start = frame[r : r + SUBS, at : at + LANES]
        lo = at - tile + HW
        third_out[r : r + SUBS, lo : lo + LANES] = start / 3.0 + (2.0 / 3.0) * value

    run(frame, 0, 3 * HW, put_first)
    run(first, 0, 2 * HW, put_second)
    run(second, 0, HW, put_third)
    for goal, out in partners(me, pieces):
        lo = pl.multiple_of(HW + goal * cols, LANES)
        out[...] = third_out[:, pl.ds(lo, cols)].astype(BF16)


def closing_body(third, table, weight, out):
    tile = out.shape[1]
    for at in range(0, tile, LANES):
        for r, _, value in diffused(third, -HW, table, weight, at, at):
            out[r : r + SUBS, at : at + LANES] = value


def turned_over(matrix):
    return matrix.astype(F32).T


def head_parts(weight, out, at):
    hid, gpts = weight.shape
    scaled = LOG2E * turned_over(weight[...])
    high = scaled.astype(BF16)
    out[at : at + gpts, 0:hid] = high
    out[at : at + gpts, hid:] = (scaled - high.astype(F32)).astype(BF16)


def reach_of(heads):
    rows, depth = heads.shape
    sums = mm(jnp.abs(heads[...]), jnp.ones((depth, LANES), BF16))
    return jnp.max(sums.reshape(rows // SUBS, SUBS, LANES), axis=0)


def prepare_body(
    count, listing, zenith, w1, b1, w2, wd, wf, v1, c1, v2, vd, flux,
    kept_out, sent_out, kept_cos, sent_cos, slot_of,
    w1_out, b1_out, w2_out, heads_out, plain_out, reach_out, v1_out, c1_out, v2_out, vd_out, vreach_out, flux_out,
):
    for weight, out in ((w1, w1_out), (w2, w2_out), (v1, v1_out), (v2, v2_out)):
        out[...] = (0.5 * turned_over(weight[...])).astype(BF16)
    head_parts(wd, heads_out, 0)
    head_parts(wf, heads_out, wd.shape[1])
    head_parts(vd, vd_out, 0)
    gpts = wd.shape[1]
    plain_out[0:gpts, :] = turned_over(wd[...]).astype(BF16)
    plain_out[gpts:, :] = turned_over(wf[...]).astype(BF16)
    reach_out[...] = reach_of(heads_out)
    vreach_out[...] = reach_of(vd_out)
    for row, out, scale in ((b1, b1_out, 0.5), (c1, c1_out, 0.5), (flux, flux_out, 1.0)):
        out[...] = scale * jnp.broadcast_to(row[...], (LANES, row.shape[1])).T
    cols = listing.shape[-1]
    half = cols // 2
    sunlit = count[0, 0]
    label = iota((cols, half), 0)
    slot = iota((cols, half), 1)
    first = jnp.broadcast_to(listing[0, :, 0:half], (cols, half)) == label
    last = jnp.broadcast_to(listing[0, :, half:cols], (cols, half)) == label
    kept = jnp.where(first & (slot < sunlit), 1.0, 0.0).astype(BF16)
    sent = jnp.where(last & (slot + half < sunlit), 1.0, 0.0).astype(BF16)
    kept_out[...] = kept
    sent_out[...] = sent
    cosine = jnp.broadcast_to(zenith[0].astype(F32), (2 * SUBS, cols)).astype(BF16)
    sent_cos[...] = mm(cosine, sent).astype(BF16)
    kept_cos[...] = mm(cosine, kept)[0:SUBS]
    hits = jnp.where(jnp.concatenate([first, last], axis=1), 1.0, 0.0).astype(BF16)
    numbers = iota((2 * SUBS, cols), 1).astype(F32).astype(BF16)
    found = lax.dot_general(numbers, hits, (((1,), (1,)), ((), ())), preferred_element_type=F32)
    slot_of[...] = found[0:SUBS].astype(jnp.int32)


def join_body(n_group, me, *rest):
    gases, warms = rest[:n_group], rest[n_group : 2 * n_group]
    kept, sent, sent_cos, packed, outgoing, kept_x, spread = rest[2 * n_group :]
    slab = warms[0].shape[0]
    for (source, gas), warm in zip(partners(me, gases), warms):
        for h in range(packed.shape[0]):
            at = slice(h * LANES, (h + 1) * LANES)
            spread[0:slab, :] = warm[:, at].astype(F32)
            for f in range(gas.shape[0]):
                spread[(f + 1) * slab : (f + 2) * slab, :] = gas[f, :, at].astype(F32)
            for l in range(slab):
                row = pl.multiple_of((source * slab + l) * SUBS, SUBS)
                packed[h, pl.ds(row, SUBS), :] = spread[pl.ds(l, SUBS, stride=slab), :]
    cells = packed.shape[1]
    first, last = packed[0].astype(BF16), packed[1].astype(BF16)
    outgoing[0:cells, :] = (mm(first, sent[0:LANES]) + mm(last, sent[LANES:])).astype(BF16)
    outgoing[cells:, :] = sent_cos[...]
    kept_x[...] = mm(first, kept[0:LANES]) + mm(last, kept[LANES:])


def softplus(z, guarded, form):
    if form == 2:
        if not guarded:
            return jnp.log(1.0 + jnp.exp(z))
        return jnp.maximum(z, jnp.log(1.0 + jnp.exp(jnp.minimum(z, SAFE * LN2))))
    if not guarded:
        if form == 1:
            return jnp.log(1.0 + jnp.exp2(z.astype(BF16)).astype(F32))
        return jnp.log(1.0 + jnp.exp2(z))
    return jnp.maximum(z * LN2, jnp.log(1.0 + jnp.exp2(jnp.minimum(z, SAFE))))


def silu_of_half(v):
    half = v.astype(BF16)
    return half + half * jnp.tanh(half)


def sweep(x, first, bias, second, heads, reach, start, gpts, rate, both, buffers, form):
    one_a, one_b, hid_a, hid_b, z_a, z_b, trans, parts, peak = buffers
    levels = x.shape[0] // SUBS
    steps = levels // STEP_LEVELS
    wide = STEP_LEVELS * LANES
    rows = heads.shape[0]
    col_cut = wide // 2
    chunk = 2 * SUBS if form == 1 else SUBS
    units = first.shape[0]
    unit_cut = units // 2

    def first_tasks(t, out):
        def task(r):
            row = jnp.minimum(t, steps - 1) * (STEP_LEVELS * SUBS)
            tiles = [
                x[pl.ds(pl.multiple_of(row + i * SUBS, SUBS), SUBS), :] for i in range(STEP_LEVELS)
            ]
            v = mm(first[r : r + unit_cut, :], jnp.concatenate(tiles, axis=1).astype(BF16))
            v = v + jnp.concatenate([bias[r : r + unit_cut, :]] * STEP_LEVELS, axis=1)
            out[r : r + unit_cut, :] = silu_of_half(v)

        return [functools.partial(task, r) for r in range(0, units, unit_cut)]

    def second_tasks(one, out):
        def task(r):
            v = mm(second[r : r + unit_cut, :], one[...])
            value = silu_of_half(v)
            out[r : r + unit_cut, :] = value
            if form != 2:
                out[units + r : units + r + unit_cut, :] = value
            most = peak[...]
            for i in range(0, unit_cut, 2 * SUBS):
                for at in range(0, wide, LANES):
                    most = jnp.maximum(most, value[i : i + 2 * SUBS, at : at + LANES])
            peak[...] = most

        return [functools.partial(task, r) for r in range(0, units, unit_cut)]

    def optics_tasks(hid, out):
        def task(lo):
            at = slice(lo, lo + col_cut)
            out[:, at] = mm(heads[...], hid[0 : heads.shape[1], at])

        return [functools.partial(task, lo) for lo in range(0, wide, col_cut)]

    def consume_tasks(z, total, guarded):
        def product(lo):
            return z[lo : lo + chunk, :]

        def task(lo):
            carry = trans[lo : lo + chunk, :]
            depth = product(lo)
            share = product(gpts + lo) if both else None
            for i in range(STEP_LEVELS):
                at = slice(i * LANES, (i + 1) * LANES)
                following = carry * jnp.exp2(softplus(depth[:, at], guarded, form) * rate)
                term = following
                if both:
                    term = (carry - following) * softplus(share[:, at], guarded, form)
                for r in range(0, chunk, SUBS):
                    part = term[r : r + SUBS]
                    total[i] = part if total[i] is None else total[i] + part
                carry = following
            trans[lo : lo + chunk, :] = carry

        return [functools.partial(task, lo) for lo in range(0, gpts, chunk)]

    def woven(main, side):
        done = 0
        for n, task in enumerate(main):
            while done < len(side) and done * len(main) <= n * len(side):
                side[done]()
                done += 1
            task()
        for task in side[done:]:
            task()

    def plain(tasks):
        for task in tasks:
            task()

    def run(guarded):
        trans[...] = start
        if not both:
            parts[0:SUBS, :] = jnp.sum(start.reshape(gpts // SUBS, SUBS, LANES), axis=0)

        def step(t, z, z_next, hid_next, hid_later, one_later, one_last):
            total = [None] * STEP_LEVELS
            side = second_tasks(one_later, hid_later) + first_tasks(t + 3, one_last)
            woven(consume_tasks(z, total, guarded), optics_tasks(hid_next, z_next) + side)
            for i in range(STEP_LEVELS):
                at = pl.multiple_of((t * STEP_LEVELS + i + 1) * SUBS, SUBS)
                parts[pl.ds(at, SUBS), :] = total[i]

        def two(i, _):
            step(2 * i, z_a, z_b, hid_b, hid_a, one_a, one_b)
            step(2 * i + 1, z_b, z_a, hid_a, hid_b, one_b, one_a)
            return 0

        plain(first_tasks(0, one_a))
        plain(second_tasks(one_a, hid_a))
        plain(first_tasks(1, one_b))
        plain(optics_tasks(hid_a, z_a))
        plain(second_tasks(one_b, hid_b))
        plain(first_tasks(2, one_a))
        lax.fori_loop(0, steps // 2, two, 0)

    peak[...] = jnp.ones_like(peak)
    run(False)

    @pl.when(jnp.max(peak[...].astype(F32)) * jnp.max(reach[...]) > SAFE)
    def _():
        run(True)

    emitted = None
    for s in range(SUBS):
        part = parts[pl.ds(s + SUBS, levels, stride=SUBS), :]
        if not both:
            part = parts[pl.ds(s, levels, stride=SUBS), :] - part
        emitted = part if emitted is None else emitted + part
    return emitted


def sweep_scratch(hid, rows, gpts, levels):
    wide = STEP_LEVELS * LANES
    return [
        pltpu.VMEM((hid, wide), BF16),
        pltpu.VMEM((hid, wide), BF16),
        pltpu.VMEM((2 * hid, wide), BF16),
        pltpu.VMEM((2 * hid, wide), BF16),
        pltpu.VMEM((rows, wide), F32),
        pltpu.VMEM((rows, wide), F32),
        pltpu.VMEM((gpts, LANES), F32),
        pltpu.VMEM(((levels + 1) * SUBS, LANES), F32),
        pltpu.VMEM((2 * SUBS, LANES), BF16),
    ]


def longwave_body(which, packed, first, bias, second, heads, reach, out, *buffers):
    gpts = heads.shape[0] // 2
    levels = out.shape[0]
    x = packed.at[which]
    emitted = sweep(
        x, first, bias, second, heads, reach, jnp.ones((gpts, LANES), F32), gpts,
        -depth_scale * LOG2E, True, buffers, 1 + which,
    )
    planck = jnp.exp(0.25 * x[pl.ds(0, levels, stride=SUBS), :])
    out[...] = -(heat_scale / gpts) * planck * emitted


def shortwave_body(
    count, kept_x, kept_cos, in_x, first, bias, second, heads, reach, flux, out, work_x, *buffers
):
    cells, half = kept_x.shape
    gpts = heads.shape[0]
    slot = iota((half, half), 1) - count[0, 0]
    placed = jnp.where(slot == iota((half, half), 0), 1.0, 0.0).astype(BF16)
    work_x[...] = kept_x[...] + mm(in_x[0:cells, :], placed)
    cosine = kept_cos[...] + mm(in_x[cells:, :], placed)[0:SUBS]
    cosine = jnp.where(cosine > 0.0, cosine, 1.0)
    emitted = sweep(
        work_x, first, bias, second, heads, reach, flux[...], gpts,
        (-depth_scale * LOG2E) / cosine, False, buffers, 0,
    )
    out[...] = (heat_scale / gpts) * cosine[0:1] * emitted


def finish_body(me, count, long_first, long_last, work, partner, slot_of, *rest):
    pieces, heat = rest[:-1], rest[-1]
    levels, cols = heat.shape
    half = cols // 2
    slab = pieces[0].shape[0]
    sunlit = count[0, 0]
    for lo, long in ((0, long_first), (half, long_last)):
        slot = slot_of[:, lo : lo + half]
        here = slot < half
        place = jnp.where(here, slot, slot + half - sunlit) & (half - 1)
        lit = slot < sunlit
        for r in range(0, levels, SUBS):
            near = lane_take(work[r : r + SUBS, :], place)
            far = lane_take(partner[r : r + SUBS, :], place)
            short = jnp.where(lit, jnp.where(here, near, far), 0.0)
            heat[r : r + SUBS, lo : lo + half] = long[r : r + SUBS, :] + short
    for goal, out in partners(me, pieces):
        out[...] = heat[pl.ds(pl.multiple_of(goal * slab, SUBS), slab), :]


def add_body(me, closed, *rest):
    pieces, out = rest[:-1], rest[-1]
    cols = pieces[0].shape[1]
    for source, piece in partners(me, pieces):
        at = pl.ds(pl.multiple_of(source * cols, LANES), cols)
        out[:, at] = closed[:, at] + piece[...]


def per_device(
    potential, species, diffusion, neighbours, listing, day_count, zenith,
    lw_first, lw_bias, lw_second, lw_depth, lw_fraction,
    sw_first, sw_bias, sw_second, sw_depth, solar_flux,
):
    n_group = lax.axis_size("group")
    n_tile = lax.axis_size("tile")
    assert n_group & (n_group - 1) == 0 and n_tile % 2 == 0
    me = lax.axis_index("group").astype(jnp.int32).reshape(1)
    place = lax.axis_index("tile").astype(jnp.int32).reshape(1)
    slab, tile = potential.shape
    gases = species.shape[0]
    cols = tile // n_group
    half = cols // 2
    levels = slab * n_group
    hid = lw_first.shape[1]
    lw_gpts = lw_depth.shape[1]
    sw_gpts = sw_depth.shape[1]

    def outward(value):
        across = [(i, (i + 1 if i % 2 else i - 1) % n_tile) for i in range(n_tile)]
        return lax.ppermute(value, "tile", across)

    def paired(value):
        return lax.ppermute(value, "tile", [(i, i ^ 1) for i in range(n_tile)])

    def swapped(value, bit):
        return lax.ppermute(value, "group", [(i, i ^ bit) for i in range(n_group)])

    def exchanged(pieces):
        return [swapped(p, bit) if bit else p for bit, p in zip(far_first(n_group), pieces)]

    near = neighbours.shape[0]
    raw = (potential, neighbours, diffusion, species)
    framing, *gas_cuts = call(
        pack_body,
        [shaped((slab + 2 * near, tile), F32)] + [shaped((gases, slab, cols), BF16)] * n_group,
        [me, *(pltpu.with_memory_space_constraint(a, pltpu.HBM) for a in raw)],
        [
            pltpu.VMEM(neighbours.shape, jnp.int32),
            pltpu.VMEM(diffusion.shape, F32),
            pltpu.SemaphoreType.DMA((3 + n_group,)),
        ],
        where=HBM,
    )
    inner = paired(framing)
    outer = outward(framing)
    gas_pieces = exchanged(gas_cuts)

    (
        kept, sent, kept_cos, sent_cos, slot_of,
        lw_one, lw_shift, lw_two, lw_heads, lw_plain, lw_reach,
        sw_one, sw_shift, sw_two, sw_heads, sw_reach, flux,
    ) = call(
        prepare_body,
        [
            shaped((cols, half), BF16),
            shaped((cols, half), BF16),
            shaped((SUBS, half), F32),
            shaped((2 * SUBS, half), BF16),
            shaped((SUBS, cols), jnp.int32),
            shaped(lw_first.shape[::-1], BF16),
            shaped((hid, LANES), F32),
            shaped(lw_second.shape[::-1], BF16),
            shaped((2 * lw_gpts, 2 * hid), BF16),
            shaped((2 * lw_gpts, hid), BF16),
            shaped((SUBS, LANES), F32),
            shaped(sw_first.shape[::-1], BF16),
            shaped((hid, LANES), F32),
            shaped(sw_second.shape[::-1], BF16),
            shaped((sw_gpts, 2 * hid), BF16),
            shaped((SUBS, LANES), F32),
            shaped((sw_gpts, LANES), F32),
        ],
        [
            day_count, listing, zenith,
            lw_first, lw_bias[None], lw_second, lw_depth, lw_fraction,
            sw_first, sw_bias[None], sw_second, sw_depth, solar_flux[None],
        ],
        after=framing,
    )

    third, *warm_cuts = call(
        sections_body,
        [shaped((slab, tile + 2 * HW), F32)] + [shaped((slab, cols), BF16)] * n_group,
        [me, place, outer, inner, potential, neighbours, diffusion],
        [pltpu.VMEM((slab, 3 * tile), F32)] * 3
        + [pltpu.VMEM((3, *neighbours.shape), jnp.int32), pltpu.VMEM((3, *diffusion.shape), F32)],
        flops=10_000_000,
    )
    warm_pieces = exchanged(warm_cuts)
    (closed,) = call(
        closing_body, [shaped((slab, tile), F32)], [third, neighbours, diffusion], flops=2_000_000
    )

    cells = levels * SUBS
    packed, out_x, kept_x = call(
        functools.partial(join_body, n_group),
        [
            shaped((cols // LANES, cells, LANES), F32),
            shaped((cells + 2 * SUBS, half), BF16),
            shaped((cells, half), F32),
        ],
        [me, *gas_pieces, *warm_pieces, kept, sent, sent_cos],
        [pltpu.VMEM((SUBS * slab, LANES), F32)],
    )
    in_x = paired(out_x)

    def longwave(which):
        (heat,) = call(
            functools.partial(longwave_body, which),
            [shaped((levels, half), F32)],
            [packed, lw_one, lw_shift, lw_two, lw_plain if which else lw_heads, lw_reach],
            sweep_scratch(hid, 2 * lw_gpts, lw_gpts, levels),
            flops=4 * levels * half * hid * lw_gpts,
            trans=5 * levels * half * lw_gpts,
            after=work if which else None,
        )
        return heat

    long_first = longwave(0)
    (work,) = call(
        shortwave_body,
        [shaped((levels, half), F32)],
        [day_count, kept_x, kept_cos, in_x, sw_one, sw_shift, sw_two, sw_heads, sw_reach, flux],
        [pltpu.VMEM((cells, half), F32)] + sweep_scratch(hid, sw_gpts, sw_gpts, levels),
        flops=2 * levels * half * hid * sw_gpts,
        trans=3 * levels * half * sw_gpts,
        after=long_first,
    )
    partner = paired(work)
    long_last = longwave(1)
    heat_cuts = call(
        finish_body,
        [shaped((slab, cols), F32)] * n_group,
        [me, day_count, long_first, long_last, work, partner, slot_of],
        [pltpu.VMEM((levels, cols), F32)],
    )
    heat_pieces = exchanged(heat_cuts)
    (evolved,) = call(add_body, [shaped((slab, tile), F32)], [me, closed, *heat_pieces])
    return evolved


def solution(mesh):
    return jax.shard_map(
        per_device,
        mesh=mesh,
        in_specs=(
            P("group", "tile"),
            P(None, "group", "tile"),
            P(None, "tile"),
            P(None, "tile"),
            P("group", "tile", None),
            P("group", "tile"),
            P("group", "tile", None),
            *([P()] * 10),
        ),
        out_specs=P("group", "tile"),
        check_vma=False,
    )
```

```python
import functools
import math

import jax
import jax.numpy as jnp
from jax import lax
from jax.experimental import pallas as pl
from jax.experimental.pallas import tpu as pltpu
from jax.sharding import PartitionSpec as P

HW = 256
LANES = 128
SUBS = 8

depth_scale = 0.1
heat_scale = 12.0
LOG2E = 1.4426950408889634
LN2 = 0.6931471805599453
SAFE = 120.0

F32 = jnp.float32
BF16 = jnp.bfloat16
VMEM = pl.BlockSpec(memory_space=pltpu.VMEM)
ANY = pl.BlockSpec(memory_space=pl.ANY)
HBM = pl.BlockSpec(memory_space=pltpu.HBM)
SMEM = pl.BlockSpec(memory_space=pltpu.SMEM)
PARAMS = pltpu.CompilerParams(vmem_limit_bytes=48 * 1024 * 1024)


def call(body, outs, ins, scratch=(), flops=0, trans=0, after=None, where=VMEM):
    in_specs = [SMEM if a.size == 1 else where for a in ins]
    if after is not None:
        whole, ins = body, [after, *ins]
        in_specs = [ANY, *in_specs]

        def body(_, *refs):
            whole(*refs)

    return pl.pallas_call(
        body,
        out_shape=outs,
        in_specs=in_specs,
        out_specs=[VMEM for _ in outs],
        scratch_shapes=list(scratch),
        compiler_params=PARAMS,
        cost_estimate=pl.CostEstimate(
            flops=flops,
            transcendentals=trans,
            bytes_accessed=sum(a.size * a.dtype.itemsize for a in list(ins) + list(outs)),
        ),
    )(*ins)


def shaped(shape, dtype):
    return jax.ShapeDtypeStruct(shape, dtype)


def iota(shape, dim):
    return lax.broadcasted_iota(jnp.int32, shape, dim)


def mm(a, b):
    return jnp.dot(a, b, preferred_element_type=F32)


def far_first(n):
    return [0, *range(n - 1, 0, -1)]


def partners(me, pieces):
    return [(me[0] ^ bit, piece) for bit, piece in zip(far_first(len(pieces)), pieces)]


def lane_take(x, idx):
    return jnp.take_along_axis(x, idx, axis=1, mode="promise_in_bounds")


def diffused(src, src_at, table, weight, within, at):
    reach = HW // LANES
    wide = 2 * reach + 1
    rows = src.shape[0]
    groups = range(0, rows, SUBS)
    base = at - src_at
    middle = [src[r : r + SUBS, base : base + LANES] for r in groups]
    total = [jnp.zeros_like(m) for m in middle]
    for k in range(table.shape[0]):
        place = jnp.broadcast_to(table[k : k + 1, within : within + LANES], (SUBS, LANES)) - within
        lane = place & (LANES - 1)
        which = place >> (LANES.bit_length() - 1)
        factor = jnp.broadcast_to(weight[k : k + 1, within : within + LANES], (SUBS, LANES))
        tests = [which == w for w in range(1, wide)]
        for n, r in enumerate(groups):
            near = None
            for w in range(wide):
                lo = base + (w - reach) * LANES
                got = lane_take(src[r : r + SUBS, lo : lo + LANES], lane)
                near = got if w == 0 else jnp.where(tests[w - 1], got, near)
            total[n] = total[n] + factor * (near - middle[n])
    return [(r, m, m + t) for r, m, t in zip(groups, middle, total)]


def pack_body(me, own, table, weight, species, out, *rest):
    pieces, (table_here, weight_here, sems) = rest[:-3], rest[-3:]
    slab = own.shape[0]
    near = table.shape[0]
    cols = pieces[0].shape[2]
    moves = [
        pltpu.make_async_copy(own, out.at[0:slab], sems.at[0]),
        pltpu.make_async_copy(table, table_here, sems.at[1]),
        pltpu.make_async_copy(weight, weight_here, sems.at[2]),
    ]
    for source, piece in partners(me, pieces):
        at = pl.ds(pl.multiple_of(source * cols, LANES), cols)
        moves.append(pltpu.make_async_copy(species.at[:, :, at], piece, sems.at[len(moves)]))
    for move in moves:
        move.start()
    for move in moves:
        move.wait()
    out[slab : slab + near, :] = table_here[...].astype(F32)
    out[slab + near :, :] = weight_here[...]


def sections_body(
    me, place, outer, inner, own, table, weight, third_out, *rest
):
    pieces, (frame, first, second, tables, weights) = rest[:-5], rest[-5:]
    slab, tile = own.shape
    near = table.shape[0]
    cols = tile // len(pieces)
    odd = place[0] & 1
    for side, packed in ((odd, outer), (1 - odd, inner)):
        at = pl.ds(pl.multiple_of(side * (2 * tile), LANES), tile)
        frame[:, at] = packed[0:slab, :]
        tables[side * 2] = packed[slab : slab + near, :].astype(jnp.int32)
        weights[side * 2] = packed[slab + near : slab + 2 * near, :]
    frame[:, tile : 2 * tile] = own[...]
    tables[1] = table[...]
    weights[1] = weight[...]

    def run(src, src_at, halo, put):
        for at in range(tile - halo, 2 * tile + halo, LANES):
            t = at // tile
            for r, _, value in diffused(src, src_at, tables.at[t], weights.at[t], at - t * tile, at):
                put(r, at, value)

    def put_first(r, at, value):
        first[r : r + SUBS, at : at + LANES] = value

    def put_second(r, at, value):
        start = frame[r : r + SUBS, at : at + LANES]
        second[r : r + SUBS, at : at + LANES] = 0.75 * start + 0.25 * value

    def put_third(r, at, value):
        start = frame[r : r + SUBS, at : at + LANES]
        lo = at - tile + HW
        third_out[r : r + SUBS, lo : lo + LANES] = start / 3.0 + (2.0 / 3.0) * value

    run(frame, 0, 3 * HW, put_first)
    run(first, 0, 2 * HW, put_second)
    run(second, 0, HW, put_third)
    for goal, out in partners(me, pieces):
        lo = pl.multiple_of(HW + goal * cols, LANES)
        out[...] = third_out[:, pl.ds(lo, cols)].astype(BF16)


def closing_body(third, table, weight, out):
    tile = out.shape[1]
    for at in range(0, tile, LANES):
        for r, _, value in diffused(third, -HW, table, weight, at, at):
            out[r : r + SUBS, at : at + LANES] = value


def turned_over(matrix):
    return matrix.astype(F32).T


def head_parts(weight, out, at):
    hid, gpts = weight.shape
    scaled = LOG2E * turned_over(weight[...])
    high = scaled.astype(BF16)
    out[at : at + gpts, 0:hid] = high
    out[at : at + gpts, hid:] = (scaled - high.astype(F32)).astype(BF16)


def reach_of(heads):
    rows, depth = heads.shape
    sums = mm(jnp.abs(heads[...]), jnp.ones((depth, LANES), BF16))
    return jnp.max(sums.reshape(rows // SUBS, SUBS, LANES), axis=0)


def prepare_body(
    count, listing, zenith, w1, b1, w2, wd, wf, v1, c1, v2, vd, flux,
    kept_out, sent_out, kept_cos, sent_cos, slot_of,
    w1_out, b1_out, w2_out, heads_out, reach_out, v1_out, c1_out, v2_out, vd_out, vreach_out, flux_out,
):
    for weight, out in ((w1, w1_out), (w2, w2_out), (v1, v1_out), (v2, v2_out)):
        out[...] = (0.5 * turned_over(weight[...])).astype(BF16)
    head_parts(wd, heads_out, 0)
    head_parts(wf, heads_out, wd.shape[1])
    head_parts(vd, vd_out, 0)
    reach_out[...] = reach_of(heads_out)
    vreach_out[...] = reach_of(vd_out)
    for row, out, scale in ((b1, b1_out, 0.5), (c1, c1_out, 0.5), (flux, flux_out, 1.0)):
        out[...] = scale * jnp.broadcast_to(row[...], (LANES, row.shape[1])).T
    cols = listing.shape[-1]
    half = cols // 2
    sunlit = count[0, 0]
    label = iota((cols, half), 0)
    slot = iota((cols, half), 1)
    first = jnp.broadcast_to(listing[0, :, 0:half], (cols, half)) == label
    last = jnp.broadcast_to(listing[0, :, half:cols], (cols, half)) == label
    kept = jnp.where(first & (slot < sunlit), 1.0, 0.0).astype(BF16)
    sent = jnp.where(last & (slot + half < sunlit), 1.0, 0.0).astype(BF16)
    kept_out[...] = kept
    sent_out[...] = sent
    cosine = jnp.broadcast_to(zenith[0].astype(F32), (2 * SUBS, cols)).astype(BF16)
    sent_cos[...] = mm(cosine, sent).astype(BF16)
    kept_cos[...] = mm(cosine, kept)[0:SUBS]
    hits = jnp.where(jnp.concatenate([first, last], axis=1), 1.0, 0.0).astype(BF16)
    numbers = iota((2 * SUBS, cols), 1).astype(F32).astype(BF16)
    found = lax.dot_general(numbers, hits, (((1,), (1,)), ((), ())), preferred_element_type=F32)
    slot_of[...] = found[0:SUBS].astype(jnp.int32)


def join_body(n_group, me, *rest):
    gases, warms = rest[:n_group], rest[n_group : 2 * n_group]
    kept, sent, sent_cos, packed, outgoing, kept_x, spread = rest[2 * n_group :]
    slab = warms[0].shape[0]
    for (source, gas), warm in zip(partners(me, gases), warms):
        for h in range(packed.shape[0]):
            at = slice(h * LANES, (h + 1) * LANES)
            spread[0:slab, :] = warm[:, at].astype(F32)
            for f in range(gas.shape[0]):
                spread[(f + 1) * slab : (f + 2) * slab, :] = gas[f, :, at].astype(F32)
            for l in range(slab):
                row = pl.multiple_of((source * slab + l) * SUBS, SUBS)
                packed[h, pl.ds(row, SUBS), :] = spread[pl.ds(l, SUBS, stride=slab), :]
    cells = packed.shape[1]
    first, last = packed[0].astype(BF16), packed[1].astype(BF16)
    outgoing[0:cells, :] = (mm(first, sent[0:LANES]) + mm(last, sent[LANES:])).astype(BF16)
    outgoing[cells:, :] = sent_cos[...]
    kept_x[...] = mm(first, kept[0:LANES]) + mm(last, kept[LANES:])


def softplus(z, guarded):
    if not guarded:
        return jnp.log(1.0 + jnp.exp2(z))
    return jnp.maximum(z * LN2, jnp.log(1.0 + jnp.exp2(jnp.minimum(z, SAFE))))


def silu_of_half(v):
    half = v.astype(BF16)
    return half + half * jnp.tanh(half)


def sweep(x, first, bias, second, heads, reach, start, gpts, rate, both, buffers, form):
    ones, hids, zs, trans, parts, peak = buffers
    step_levels = zs.shape[2] // LANES
    one_a, one_b = ones.at[0], ones.at[1]
    hid_a, hid_b = hids.at[0], hids.at[1]
    z_a, z_b = zs.at[0], zs.at[1]
    levels = x.shape[0] // SUBS
    steps = levels // step_levels
    wide = step_levels * LANES
    rows = heads.shape[0]
    col_cut = 2 * LANES
    chunk = SUBS
    units = first.shape[0]
    unit_cut = units // 2

    def first_tasks(t, out):
        def task(r):
            row = jnp.minimum(t, steps - 1) * (step_levels * SUBS)
            tiles = [
                x[pl.ds(pl.multiple_of(row + i * SUBS, SUBS), SUBS), :] for i in range(step_levels)
            ]
            v = mm(first[r : r + unit_cut, :], jnp.concatenate(tiles, axis=1).astype(BF16))
            v = v + jnp.concatenate([bias[r : r + unit_cut, :]] * step_levels, axis=1)
            out[r : r + unit_cut, :] = silu_of_half(v)

        return [functools.partial(task, r) for r in range(0, units, unit_cut)]

    def second_tasks(one, out):
        def task(r):
            v = mm(second[r : r + unit_cut, :], one[...])
            value = silu_of_half(v)
            out[r : r + unit_cut, :] = value
            out[units + r : units + r + unit_cut, :] = value
            most = peak[...]
            for i in range(0, unit_cut, 2 * SUBS):
                for at in range(0, wide, LANES):
                    most = jnp.maximum(most, value[i : i + 2 * SUBS, at : at + LANES])
            peak[...] = most

        return [functools.partial(task, r) for r in range(0, units, unit_cut)]

    def optics_tasks(hid, out):
        def task(lo):
            at = slice(lo, lo + col_cut)
            out[:, at] = mm(heads[...], hid[:, at])

        return [functools.partial(task, lo) for lo in range(0, wide, col_cut)]

    def consume_tasks(z, total, guarded):
        def product(lo):
            return z[lo : lo + chunk, :]

        def task(lo):
            carry = trans[lo : lo + chunk, :]
            depth = product(lo)
            share = product(gpts + lo) if both else None
            for i in range(step_levels):
                at = slice(i * LANES, (i + 1) * LANES)
                following = carry * jnp.exp2(softplus(depth[:, at], guarded) * rate)
                term = following
                if both:
                    term = (carry - following) * softplus(share[:, at], guarded)
                for r in range(0, chunk, SUBS):
                    part = term[r : r + SUBS]
                    total[i] = part if total[i] is None else total[i] + part
                carry = following
            trans[lo : lo + chunk, :] = carry

        return [functools.partial(task, lo) for lo in range(0, gpts, chunk)]

    def woven(main, side):
        done = 0
        for n, task in enumerate(main):
            while done < len(side) and done * len(main) <= n * len(side):
                side[done]()
                done += 1
            task()
        for task in side[done:]:
            task()

    def plain(tasks):
        for task in tasks:
            task()

    def run(guarded):
        trans[...] = start
        if not both:
            parts[0:SUBS, :] = jnp.sum(start.reshape(gpts // SUBS, SUBS, LANES), axis=0)

        def step(t, z, z_next, hid_next, hid_later, one_later, one_last):
            total = [None] * step_levels
            side = second_tasks(one_later, hid_later) + first_tasks(t + 3, one_last)
            woven(consume_tasks(z, total, guarded), optics_tasks(hid_next, z_next) + side)
            for i in range(step_levels):
                at = pl.multiple_of((t * step_levels + i + 1) * SUBS, SUBS)
                parts[pl.ds(at, SUBS), :] = total[i]

        def one(t, _):
            now = t & 1
            then = 1 - now
            step(
                t, zs.at[now], zs.at[then], hids.at[then], hids.at[now], ones.at[now], ones.at[then]
            )
            return 0

        def two(i, _):
            step(2 * i, z_a, z_b, hid_b, hid_a, one_a, one_b)
            step(2 * i + 1, z_b, z_a, hid_a, hid_b, one_b, one_a)
            return 0

        plain(first_tasks(0, one_a))
        plain(second_tasks(one_a, hid_a))
        plain(first_tasks(1, one_b))
        plain(optics_tasks(hid_a, z_a))
        plain(second_tasks(one_b, hid_b))
        plain(first_tasks(2, one_a))
        if form == 2:
            lax.fori_loop(0, steps, one, 0)
        else:
            lax.fori_loop(0, steps // 2, two, 0)

    peak[...] = jnp.ones_like(peak)
    run(False)

    @pl.when(jnp.max(peak[...].astype(F32)) * jnp.max(reach[...]) > SAFE)
    def _():
        run(True)

    emitted = None
    for s in range(SUBS):
        part = parts[pl.ds(s + SUBS, levels, stride=SUBS), :]
        if not both:
            part = parts[pl.ds(s, levels, stride=SUBS), :] - part
        emitted = part if emitted is None else emitted + part
    return emitted


def sweep_scratch(hid, rows, gpts, levels, step_levels):
    wide = step_levels * LANES
    return [
        pltpu.VMEM((2, hid, wide), BF16),
        pltpu.VMEM((2, 2 * hid, wide), BF16),
        pltpu.VMEM((2, rows, wide), F32),
        pltpu.VMEM((gpts, LANES), F32),
        pltpu.VMEM(((levels + 1) * SUBS, LANES), F32),
        pltpu.VMEM((2 * SUBS, LANES), BF16),
    ]


def longwave_body(which, packed, first, bias, second, heads, reach, out, *buffers):
    gpts = heads.shape[0] // 2
    levels = out.shape[0]
    x = packed.at[which]
    emitted = sweep(
        x, first, bias, second, heads, reach, jnp.ones((gpts, LANES), F32), gpts,
        -depth_scale * LOG2E, True, buffers, 1 + which,
    )
    planck = jnp.exp(0.25 * x[pl.ds(0, levels, stride=SUBS), :])
    out[...] = -(heat_scale / gpts) * planck * emitted


def shortwave_body(
    count, kept_x, kept_cos, in_x, first, bias, second, heads, reach, flux, out, work_x, *buffers
):
    cells, half = kept_x.shape
    gpts = heads.shape[0]
    slot = iota((half, half), 1) - count[0, 0]
    placed = jnp.where(slot == iota((half, half), 0), 1.0, 0.0).astype(BF16)
    work_x[...] = kept_x[...] + mm(in_x[0:cells, :], placed)
    cosine = kept_cos[...] + mm(in_x[cells:, :], placed)[0:SUBS]
    cosine = jnp.where(cosine > 0.0, cosine, 1.0)
    emitted = sweep(
        work_x, first, bias, second, heads, reach, flux[...], gpts,
        (-depth_scale * LOG2E) / cosine, False, buffers, 0,
    )
    out[...] = (heat_scale / gpts) * cosine[0:1] * emitted


def finish_body(me, count, long_first, long_last, work, partner, slot_of, *rest):
    pieces, heat = rest[:-1], rest[-1]
    levels, cols = heat.shape
    half = cols // 2
    slab = pieces[0].shape[0]
    sunlit = count[0, 0]
    for lo, long in ((0, long_first), (half, long_last)):
        slot = slot_of[:, lo : lo + half]
        here = slot < half
        place = jnp.where(here, slot, slot + half - sunlit) & (half - 1)
        lit = slot < sunlit
        for r in range(0, levels, SUBS):
            near = lane_take(work[r : r + SUBS, :], place)
            far = lane_take(partner[r : r + SUBS, :], place)
            short = jnp.where(lit, jnp.where(here, near, far), 0.0)
            heat[r : r + SUBS, lo : lo + half] = long[r : r + SUBS, :] + short
    for goal, out in partners(me, pieces):
        out[...] = heat[pl.ds(pl.multiple_of(goal * slab, SUBS), slab), :]


def add_body(me, closed, *rest):
    pieces, out = rest[:-1], rest[-1]
    cols = pieces[0].shape[1]
    for source, piece in partners(me, pieces):
        at = pl.ds(pl.multiple_of(source * cols, LANES), cols)
        out[:, at] = closed[:, at] + piece[...]


def per_device(
    potential, species, diffusion, neighbours, listing, day_count, zenith,
    lw_first, lw_bias, lw_second, lw_depth, lw_fraction,
    sw_first, sw_bias, sw_second, sw_depth, solar_flux,
):
    n_group = lax.axis_size("group")
    n_tile = lax.axis_size("tile")
    assert n_group & (n_group - 1) == 0 and n_tile % 2 == 0
    me = lax.axis_index("group").astype(jnp.int32).reshape(1)
    place = lax.axis_index("tile").astype(jnp.int32).reshape(1)
    slab, tile = potential.shape
    gases = species.shape[0]
    cols = tile // n_group
    half = cols // 2
    levels = slab * n_group
    hid = lw_first.shape[1]
    lw_gpts = lw_depth.shape[1]
    sw_gpts = sw_depth.shape[1]

    def outward(value):
        across = [(i, (i + 1 if i % 2 else i - 1) % n_tile) for i in range(n_tile)]
        return lax.ppermute(value, "tile", across)

    def paired(value):
        return lax.ppermute(value, "tile", [(i, i ^ 1) for i in range(n_tile)])

    def swapped(value, bit):
        return lax.ppermute(value, "group", [(i, i ^ bit) for i in range(n_group)])

    def exchanged(pieces):
        return [swapped(p, bit) if bit else p for bit, p in zip(far_first(n_group), pieces)]

    near = neighbours.shape[0]
    raw = (potential, neighbours, diffusion, species)
    framing, *gas_cuts = call(
        pack_body,
        [shaped((slab + 2 * near, tile), F32)] + [shaped((gases, slab, cols), BF16)] * n_group,
        [me, *(pltpu.with_memory_space_constraint(a, pltpu.HBM) for a in raw)],
        [
            pltpu.VMEM(neighbours.shape, jnp.int32),
            pltpu.VMEM(diffusion.shape, F32),
            pltpu.SemaphoreType.DMA((3 + n_group,)),
        ],
        where=HBM,
    )
    inner = paired(framing)
    outer = outward(framing)
    gas_pieces = exchanged(gas_cuts)

    (
        kept, sent, kept_cos, sent_cos, slot_of,
        lw_one, lw_shift, lw_two, lw_heads, lw_reach,
        sw_one, sw_shift, sw_two, sw_heads, sw_reach, flux,
    ) = call(
        prepare_body,
        [
            shaped((cols, half), BF16),
            shaped((cols, half), BF16),
            shaped((SUBS, half), F32),
            shaped((2 * SUBS, half), BF16),
            shaped((SUBS, cols), jnp.int32),
            shaped(lw_first.shape[::-1], BF16),
            shaped((hid, LANES), F32),
            shaped(lw_second.shape[::-1], BF16),
            shaped((2 * lw_gpts, 2 * hid), BF16),
            shaped((SUBS, LANES), F32),
            shaped(sw_first.shape[::-1], BF16),
            shaped((hid, LANES), F32),
            shaped(sw_second.shape[::-1], BF16),
            shaped((sw_gpts, 2 * hid), BF16),
            shaped((SUBS, LANES), F32),
            shaped((sw_gpts, LANES), F32),
        ],
        [
            day_count, listing, zenith,
            lw_first, lw_bias[None], lw_second, lw_depth, lw_fraction,
            sw_first, sw_bias[None], sw_second, sw_depth, solar_flux[None],
        ],
        after=framing,
    )

    third, *warm_cuts = call(
        sections_body,
        [shaped((slab, tile + 2 * HW), F32)] + [shaped((slab, cols), BF16)] * n_group,
        [me, place, outer, inner, potential, neighbours, diffusion],
        [pltpu.VMEM((slab, 3 * tile), F32)] * 3
        + [pltpu.VMEM((3, *neighbours.shape), jnp.int32), pltpu.VMEM((3, *diffusion.shape), F32)],
        flops=10_000_000,
    )
    warm_pieces = exchanged(warm_cuts)
    (closed,) = call(
        closing_body, [shaped((slab, tile), F32)], [third, neighbours, diffusion], flops=2_000_000
    )

    cells = levels * SUBS
    packed, out_x, kept_x = call(
        functools.partial(join_body, n_group),
        [
            shaped((cols // LANES, cells, LANES), F32),
            shaped((cells + 2 * SUBS, half), BF16),
            shaped((cells, half), F32),
        ],
        [me, *gas_pieces, *warm_pieces, kept, sent, sent_cos],
        [pltpu.VMEM((SUBS * slab, LANES), F32)],
    )
    in_x = paired(out_x)

    def longwave(which):
        (heat,) = call(
            functools.partial(longwave_body, which),
            [shaped((levels, half), F32)],
            [packed, lw_one, lw_shift, lw_two, lw_heads, lw_reach],
            sweep_scratch(hid, 2 * lw_gpts, lw_gpts, levels, 4 if which else 2),
            flops=4 * levels * half * hid * lw_gpts,
            trans=5 * levels * half * lw_gpts,
            after=work if which else None,
        )
        return heat

    long_first = longwave(0)
    (work,) = call(
        shortwave_body,
        [shaped((levels, half), F32)],
        [day_count, kept_x, kept_cos, in_x, sw_one, sw_shift, sw_two, sw_heads, sw_reach, flux],
        [pltpu.VMEM((cells, half), F32)] + sweep_scratch(hid, sw_gpts, sw_gpts, levels, 4),
        flops=2 * levels * half * hid * sw_gpts,
        trans=3 * levels * half * sw_gpts,
        after=long_first,
    )
    partner = paired(work)
    long_last = longwave(1)
    heat_cuts = call(
        finish_body,
        [shaped((slab, cols), F32)] * n_group,
        [me, day_count, long_first, long_last, work, partner, slot_of],
        [pltpu.VMEM((levels, cols), F32)],
    )
    heat_pieces = exchanged(heat_cuts)
    (evolved,) = call(add_body, [shaped((slab, tile), F32)], [me, closed, *heat_pieces])
    return evolved


def solution(mesh):
    return jax.shard_map(
        per_device,
        mesh=mesh,
        in_specs=(
            P("group", "tile"),
            P(None, "group", "tile"),
            P(None, "tile"),
            P(None, "tile"),
            P("group", "tile", None),
            P("group", "tile"),
            P("group", "tile", None),
            *([P()] * 10),
        ),
        out_specs=P("group", "tile"),
        check_vma=False,
    )
```

```python
import functools
import math

import jax
import jax.numpy as jnp
from jax import lax
from jax.experimental import pallas as pl
from jax.experimental.pallas import tpu as pltpu
from jax.sharding import PartitionSpec as P

HW = 256
LANES = 128
SUBS = 8
STEP_LEVELS = 4

depth_scale = 0.1
heat_scale = 12.0
LOG2E = 1.4426950408889634
LN2 = 0.6931471805599453
SAFE = 120.0

F32 = jnp.float32
BF16 = jnp.bfloat16
VMEM = pl.BlockSpec(memory_space=pltpu.VMEM)
ANY = pl.BlockSpec(memory_space=pl.ANY)
HBM = pl.BlockSpec(memory_space=pltpu.HBM)
SMEM = pl.BlockSpec(memory_space=pltpu.SMEM)
PARAMS = pltpu.CompilerParams(vmem_limit_bytes=48 * 1024 * 1024)


def call(body, outs, ins, scratch=(), flops=0, trans=0, after=None, where=VMEM):
    in_specs = [SMEM if a.size == 1 else where for a in ins]
    if after is not None:
        whole, ins = body, [after, *ins]
        in_specs = [ANY, *in_specs]

        def body(_, *refs):
            whole(*refs)

    return pl.pallas_call(
        body,
        out_shape=outs,
        in_specs=in_specs,
        out_specs=[SMEM if a.size == 1 else VMEM for a in outs],
        scratch_shapes=list(scratch),
        compiler_params=PARAMS,
        cost_estimate=pl.CostEstimate(
            flops=flops,
            transcendentals=trans,
            bytes_accessed=sum(a.size * a.dtype.itemsize for a in list(ins) + list(outs)),
        ),
    )(*ins)


def shaped(shape, dtype):
    return jax.ShapeDtypeStruct(shape, dtype)


def iota(shape, dim):
    return lax.broadcasted_iota(jnp.int32, shape, dim)


def mm(a, b):
    return jnp.dot(a, b, preferred_element_type=F32)


def far_first(n):
    return [0, *range(n - 1, 0, -1)]


def partners(me, pieces):
    return [(me[0] ^ bit, piece) for bit, piece in zip(far_first(len(pieces)), pieces)]


def lane_take(x, idx):
    return jnp.take_along_axis(x, idx, axis=1, mode="promise_in_bounds")


def diffused(src, src_at, table, weight, within, at):
    reach = HW // LANES
    wide = 2 * reach + 1
    rows = src.shape[0]
    groups = range(0, rows, SUBS)
    base = at - src_at
    middle = [src[r : r + SUBS, base : base + LANES] for r in groups]
    total = [jnp.zeros_like(m) for m in middle]
    for k in range(table.shape[0]):
        place = jnp.broadcast_to(table[k : k + 1, within : within + LANES], (SUBS, LANES)) - within
        lane = place & (LANES - 1)
        which = place >> (LANES.bit_length() - 1)
        factor = jnp.broadcast_to(weight[k : k + 1, within : within + LANES], (SUBS, LANES))
        tests = [which == w for w in range(1, wide)]
        for n, r in enumerate(groups):
            near = None
            for w in range(wide):
                lo = base + (w - reach) * LANES
                got = lane_take(src[r : r + SUBS, lo : lo + LANES], lane)
                near = got if w == 0 else jnp.where(tests[w - 1], got, near)
            total[n] = total[n] + factor * (near - middle[n])
    return [(r, m, m + t) for r, m, t in zip(groups, middle, total)]


def pack_body(me, own, table, weight, species, out, *rest):
    pieces, (table_here, weight_here, sems) = rest[:-3], rest[-3:]
    slab = own.shape[0]
    near = table.shape[0]
    cols = pieces[0].shape[2]
    moves = [
        pltpu.make_async_copy(own, out.at[0:slab], sems.at[0]),
        pltpu.make_async_copy(table, table_here, sems.at[1]),
        pltpu.make_async_copy(weight, weight_here, sems.at[2]),
    ]
    for source, piece in partners(me, pieces):
        at = pl.ds(pl.multiple_of(source * cols, LANES), cols)
        moves.append(pltpu.make_async_copy(species.at[:, :, at], piece, sems.at[len(moves)]))
    for move in moves:
        move.start()
    for move in moves:
        move.wait()
    out[slab : slab + near, :] = table_here[...].astype(F32)
    out[slab + near :, :] = weight_here[...]


def sections_body(
    me, place, outer, inner, own, table, weight, third_out, *rest
):
    pieces, (frame, first, second, tables, weights) = rest[:-5], rest[-5:]
    slab, tile = own.shape
    near = table.shape[0]
    cols = tile // len(pieces)
    odd = place[0] & 1
    for side, packed in ((odd, outer), (1 - odd, inner)):
        at = pl.ds(pl.multiple_of(side * (2 * tile), LANES), tile)
        frame[:, at] = packed[0:slab, :]
        tables[side * 2] = packed[slab : slab + near, :].astype(jnp.int32)
        weights[side * 2] = packed[slab + near : slab + 2 * near, :]
    frame[:, tile : 2 * tile] = own[...]
    tables[1] = table[...]
    weights[1] = weight[...]

    def run(src, src_at, halo, put):
        for at in range(tile - halo, 2 * tile + halo, LANES):
            t = at // tile
            for r, _, value in diffused(src, src_at, tables.at[t], weights.at[t], at - t * tile, at):
                put(r, at, value)

    def put_first(r, at, value):
        first[r : r + SUBS, at : at + LANES] = value

    def put_second(r, at, value):
        start = frame[r : r + SUBS, at : at + LANES]
        second[r : r + SUBS, at : at + LANES] = 0.75 * start + 0.25 * value

    def put_third(r, at, value):
        start = frame[r : r + SUBS, at : at + LANES]
        lo = at - tile + HW
        third_out[r : r + SUBS, lo : lo + LANES] = start / 3.0 + (2.0 / 3.0) * value

    run(frame, 0, 3 * HW, put_first)
    run(first, 0, 2 * HW, put_second)
    run(second, 0, HW, put_third)
    for goal, out in partners(me, pieces):
        lo = pl.multiple_of(HW + goal * cols, LANES)
        out[...] = third_out[:, pl.ds(lo, cols)].astype(BF16)


def closing_body(third, table, weight, out):
    tile = out.shape[1]
    for at in range(0, tile, LANES):
        for r, _, value in diffused(third, -HW, table, weight, at, at):
            out[r : r + SUBS, at : at + LANES] = value


def turned_over(matrix):
    return matrix.astype(F32).T


def head_parts(weight, out, at):
    hid, gpts = weight.shape
    scaled = LOG2E * turned_over(weight[...])
    high = scaled.astype(BF16)
    out[at : at + gpts, 0:hid] = high
    out[at : at + gpts, hid:] = (scaled - high.astype(F32)).astype(BF16)


def limit_of(heads):
    sums = mm(jnp.abs(heads[...]), jnp.ones((heads.shape[1], LANES), BF16))
    return SAFE / jnp.maximum(jnp.max(sums), 1e-30)


def prepare_body(
    count, listing, zenith, w1, b1, w2, wd, wf, v1, c1, v2, vd, flux,
    kept_out, sent_out, kept_cos, sent_cos, slot_of,
    w1_out, b1_out, w2_out, heads_out, limit_out, v1_out, c1_out, v2_out, vd_out, vlimit_out, flux_out,
):
    for weight, out in ((w1, w1_out), (w2, w2_out), (v1, v1_out), (v2, v2_out)):
        out[...] = (0.5 * turned_over(weight[...])).astype(BF16)
    head_parts(wd, heads_out, 0)
    head_parts(wf, heads_out, wd.shape[1])
    head_parts(vd, vd_out, 0)
    limit_out[0, 0] = limit_of(heads_out)
    vlimit_out[0, 0] = limit_of(vd_out)
    for row, out, scale in ((b1, b1_out, 0.5), (c1, c1_out, 0.5), (flux, flux_out, 1.0)):
        out[...] = scale * jnp.broadcast_to(row[...], (LANES, row.shape[1])).T
    cols = listing.shape[-1]
    half = cols // 2
    sunlit = count[0, 0]
    label = iota((cols, half), 0)
    slot = iota((cols, half), 1)
    first = jnp.broadcast_to(listing[0, :, 0:half], (cols, half)) == label
    last = jnp.broadcast_to(listing[0, :, half:cols], (cols, half)) == label
    kept = jnp.where(first & (slot < sunlit), 1.0, 0.0).astype(BF16)
    sent = jnp.where(last & (slot + half < sunlit), 1.0, 0.0).astype(BF16)
    kept_out[...] = kept
    sent_out[...] = sent
    cosine = jnp.broadcast_to(zenith[0].astype(F32), (2 * SUBS, cols)).astype(BF16)
    sent_cos[...] = mm(cosine, sent).astype(BF16)
    kept_cos[...] = mm(cosine, kept)[0:SUBS]
    hits = jnp.where(jnp.concatenate([first, last], axis=1), 1.0, 0.0).astype(BF16)
    numbers = iota((2 * SUBS, cols), 1).astype(F32).astype(BF16)
    found = lax.dot_general(numbers, hits, (((1,), (1,)), ((), ())), preferred_element_type=F32)
    slot_of[...] = found[0:SUBS].astype(jnp.int32)


def join_body(n_group, me, *rest):
    gases, warms = rest[:n_group], rest[n_group : 2 * n_group]
    kept, sent, sent_cos, packed, outgoing, kept_x, spread = rest[2 * n_group :]
    slab = warms[0].shape[0]
    for (source, gas), warm in zip(partners(me, gases), warms):
        for h in range(packed.shape[0]):
            at = slice(h * LANES, (h + 1) * LANES)
            spread[0:slab, :] = warm[:, at].astype(F32)
            for f in range(gas.shape[0]):
                spread[(f + 1) * slab : (f + 2) * slab, :] = gas[f, :, at].astype(F32)
            for l in range(slab):
                row = pl.multiple_of((source * slab + l) * SUBS, SUBS)
                packed[h, pl.ds(row, SUBS), :] = spread[pl.ds(l, SUBS, stride=slab), :]
    cells = packed.shape[1]
    first, last = packed[0].astype(BF16), packed[1].astype(BF16)
    outgoing[0:cells, :] = (mm(first, sent[0:LANES]) + mm(last, sent[LANES:])).astype(BF16)
    outgoing[cells:, :] = sent_cos[...]
    kept_x[...] = mm(first, kept[0:LANES]) + mm(last, kept[LANES:])


def softplus(z):
    return jnp.log(1.0 + jnp.exp2(z))


def softplus_guarded(z):
    return jnp.maximum(z * LN2, softplus(jnp.minimum(z, SAFE)))


def silu_of_half(v):
    half = v.astype(BF16)
    return half + half * jnp.tanh(half)


def sweep(x, first, bias, second, heads, limit, start, gpts, rate, both, buffers):
    ones, hids, zs, trans, parts, peak = buffers
    one_a, one_b = ones.at[0], ones.at[1]
    hid_a, hid_b = hids.at[0], hids.at[1]
    z_a, z_b = zs.at[0], zs.at[1]
    levels = x.shape[0] // SUBS
    steps = levels // STEP_LEVELS
    wide = STEP_LEVELS * LANES
    rows = heads.shape[0]
    col_cut = 2 * LANES
    chunk = SUBS
    units = first.shape[0]
    unit_cut = units // 2

    def first_tasks(t, out):
        def task(r):
            row = jnp.minimum(t, steps - 1) * (STEP_LEVELS * SUBS)
            tiles = [
                x[pl.ds(pl.multiple_of(row + i * SUBS, SUBS), SUBS), :] for i in range(STEP_LEVELS)
            ]
            v = mm(first[r : r + unit_cut, :], jnp.concatenate(tiles, axis=1).astype(BF16))
            v = v + jnp.concatenate([bias[r : r + unit_cut, :]] * STEP_LEVELS, axis=1)
            out[r : r + unit_cut, :] = silu_of_half(v)

        return [functools.partial(task, r) for r in range(0, units, unit_cut)]

    def second_tasks(one, out):
        def task(r):
            v = mm(second[r : r + unit_cut, :], one[...])
            value = silu_of_half(v)
            out[r : r + unit_cut, :] = value
            out[units + r : units + r + unit_cut, :] = value
            most = peak[...]
            for i in range(0, unit_cut, 2 * SUBS):
                for at in range(0, wide, LANES):
                    most = jnp.maximum(most, value[i : i + 2 * SUBS, at : at + LANES])
            peak[...] = most

        return [functools.partial(task, r) for r in range(0, units, unit_cut)]

    def optics_tasks(hid, out):
        def task(lo):
            at = slice(lo, lo + col_cut)
            out[:, at] = mm(heads[...], hid[:, at])

        return [functools.partial(task, lo) for lo in range(0, wide, col_cut)]

    def consume_tasks(z, total):
        def product(lo):
            return z[lo : lo + chunk, :]

        def task(lo):
            carry = trans[lo : lo + chunk, :]
            depth = product(lo)
            share = product(gpts + lo) if both else None
            for i in range(STEP_LEVELS):
                at = slice(i * LANES, (i + 1) * LANES)
                following = carry * jnp.exp2(softplus(depth[:, at]) * rate)
                term = following
                if both:
                    term = (carry - following) * softplus(share[:, at])
                for r in range(0, chunk, SUBS):
                    part = term[r : r + SUBS]
                    total[i] = part if total[i] is None else total[i] + part
                carry = following
            trans[lo : lo + chunk, :] = carry

        return [functools.partial(task, lo) for lo in range(0, gpts, chunk)]

    def woven(main, side):
        done = 0
        for n, task in enumerate(main):
            while done < len(side) and done * len(main) <= n * len(side):
                side[done]()
                done += 1
            task()
        for task in side[done:]:
            task()

    def plain(tasks):
        for task in tasks:
            task()

    def run():
        trans[...] = start
        if not both:
            parts[0:SUBS, :] = jnp.sum(start.reshape(gpts // SUBS, SUBS, LANES), axis=0)

        def step(t, z, z_next, hid_next, hid_later, one_later, one_last):
            total = [None] * STEP_LEVELS
            side = second_tasks(one_later, hid_later) + first_tasks(t + 3, one_last)
            woven(consume_tasks(z, total), optics_tasks(hid_next, z_next) + side)
            for i in range(STEP_LEVELS):
                at = pl.multiple_of((t * STEP_LEVELS + i + 1) * SUBS, SUBS)
                parts[pl.ds(at, SUBS), :] = total[i]

        def two(i, _):
            step(2 * i, z_a, z_b, hid_b, hid_a, one_a, one_b)
            step(2 * i + 1, z_b, z_a, hid_a, hid_b, one_b, one_a)
            return 0

        plain(first_tasks(0, one_a))
        plain(second_tasks(one_a, hid_a))
        plain(first_tasks(1, one_b))
        plain(optics_tasks(hid_a, z_a))
        plain(second_tasks(one_b, hid_b))
        plain(first_tasks(2, one_a))
        lax.fori_loop(0, steps // 2, two, 0)

    def run_guarded():
        trans[...] = start
        at = slice(0, LANES)

        def level(l, _):
            tile = x[pl.ds(pl.multiple_of(l * SUBS, SUBS), SUBS), :].astype(BF16)
            hidden = silu_of_half(mm(first[...], tile) + bias[...])
            hidden = silu_of_half(mm(second[...], hidden))
            z_a[:, at] = mm(heads[...], jnp.concatenate([hidden, hidden], axis=0))

            def piece(c, total):
                lo = pl.multiple_of(c * SUBS, SUBS)
                carry = trans[pl.ds(lo, SUBS), :]
                depth = softplus_guarded(z_a[pl.ds(lo, SUBS), at])
                following = carry * jnp.exp2(depth * rate)
                trans[pl.ds(lo, SUBS), :] = following
                if not both:
                    return total + following
                share = softplus_guarded(z_a[pl.ds(pl.multiple_of(gpts + lo, SUBS), SUBS), at])
                return total + (carry - following) * share

            total = lax.fori_loop(0, gpts // SUBS, piece, jnp.zeros((SUBS, LANES), F32))
            parts[pl.ds(pl.multiple_of((l + 1) * SUBS, SUBS), SUBS), :] = total
            return 0

        lax.fori_loop(0, levels, level, 0)

    peak[...] = jnp.ones_like(peak)
    run()
    pl.when(jnp.max(peak[...].astype(F32)) > limit[0, 0])(run_guarded)
    emitted = None
    for s in range(SUBS):
        part = parts[pl.ds(s + SUBS, levels, stride=SUBS), :]
        if not both:
            part = parts[pl.ds(s, levels, stride=SUBS), :] - part
        emitted = part if emitted is None else emitted + part
    return emitted


def sweep_scratch(hid, rows, gpts, levels):
    wide = STEP_LEVELS * LANES
    return [
        pltpu.VMEM((2, hid, wide), BF16),
        pltpu.VMEM((2, 2 * hid, wide), BF16),
        pltpu.VMEM((2, rows, wide), F32),
        pltpu.VMEM((gpts, LANES), F32),
        pltpu.VMEM(((levels + 1) * SUBS, LANES), F32),
        pltpu.VMEM((2 * SUBS, LANES), BF16),
    ]


def longwave_body(which, packed, first, bias, second, heads, limit, out, *buffers):
    gpts = heads.shape[0] // 2
    levels = out.shape[0]
    x = packed.at[which]
    emitted = sweep(
        x, first, bias, second, heads, limit, jnp.ones((gpts, LANES), F32), gpts,
        -depth_scale * LOG2E, True, buffers,
    )
    planck = jnp.exp(0.25 * x[pl.ds(0, levels, stride=SUBS), :])
    out[...] = -(heat_scale / gpts) * planck * emitted


def shortwave_body(
    count, kept_x, kept_cos, in_x, first, bias, second, heads, limit, flux, out, work_x, *buffers
):
    cells, half = kept_x.shape
    gpts = heads.shape[0]
    slot = iota((half, half), 1) - count[0, 0]
    placed = jnp.where(slot == iota((half, half), 0), 1.0, 0.0).astype(BF16)
    work_x[...] = kept_x[...] + mm(in_x[0:cells, :], placed)
    cosine = kept_cos[...] + mm(in_x[cells:, :], placed)[0:SUBS]
    cosine = jnp.where(cosine > 0.0, cosine, 1.0)
    emitted = sweep(
        work_x, first, bias, second, heads, limit, flux[...], gpts,
        (-depth_scale * LOG2E) / cosine, False, buffers,
    )
    out[...] = (heat_scale / gpts) * cosine[0:1] * emitted


def finish_body(me, count, long_first, long_last, work, partner, slot_of, *rest):
    pieces, heat = rest[:-1], rest[-1]
    levels, cols = heat.shape
    half = cols // 2
    slab = pieces[0].shape[0]
    sunlit = count[0, 0]
    for lo, long in ((0, long_first), (half, long_last)):
        slot = slot_of[:, lo : lo + half]
        here = slot < half
        place = jnp.where(here, slot, slot + half - sunlit) & (half - 1)
        lit = slot < sunlit
        for r in range(0, levels, SUBS):
            near = lane_take(work[r : r + SUBS, :], place)
            far = lane_take(partner[r : r + SUBS, :], place)
            short = jnp.where(lit, jnp.where(here, near, far), 0.0)
            heat[r : r + SUBS, lo : lo + half] = long[r : r + SUBS, :] + short
    for goal, out in partners(me, pieces):
        out[...] = heat[pl.ds(pl.multiple_of(goal * slab, SUBS), slab), :]


def add_body(me, closed, *rest):
    pieces, out = rest[:-1], rest[-1]
    cols = pieces[0].shape[1]
    for source, piece in partners(me, pieces):
        at = pl.ds(pl.multiple_of(source * cols, LANES), cols)
        out[:, at] = closed[:, at] + piece[...]


def per_device(
    potential, species, diffusion, neighbours, listing, day_count, zenith,
    lw_first, lw_bias, lw_second, lw_depth, lw_fraction,
    sw_first, sw_bias, sw_second, sw_depth, solar_flux,
):
    n_group = lax.axis_size("group")
    n_tile = lax.axis_size("tile")
    assert n_group & (n_group - 1) == 0 and n_tile % 2 == 0
    me = lax.axis_index("group").astype(jnp.int32).reshape(1)
    place = lax.axis_index("tile").astype(jnp.int32).reshape(1)
    slab, tile = potential.shape
    gases = species.shape[0]
    cols = tile // n_group
    half = cols // 2
    levels = slab * n_group
    hid = lw_first.shape[1]
    lw_gpts = lw_depth.shape[1]
    sw_gpts = sw_depth.shape[1]

    def outward(value):
        across = [(i, (i + 1 if i % 2 else i - 1) % n_tile) for i in range(n_tile)]
        return lax.ppermute(value, "tile", across)

    def paired(value):
        return lax.ppermute(value, "tile", [(i, i ^ 1) for i in range(n_tile)])

    def swapped(value, bit):
        return lax.ppermute(value, "group", [(i, i ^ bit) for i in range(n_group)])

    def exchanged(pieces):
        return [swapped(p, bit) if bit else p for bit, p in zip(far_first(n_group), pieces)]

    near = neighbours.shape[0]
    raw = (potential, neighbours, diffusion, species)
    framing, *gas_cuts = call(
        pack_body,
        [shaped((slab + 2 * near, tile), F32)] + [shaped((gases, slab, cols), BF16)] * n_group,
        [me, *(pltpu.with_memory_space_constraint(a, pltpu.HBM) for a in raw)],
        [
            pltpu.VMEM(neighbours.shape, jnp.int32),
            pltpu.VMEM(diffusion.shape, F32),
            pltpu.SemaphoreType.DMA((3 + n_group,)),
        ],
        where=HBM,
    )
    inner = paired(framing)
    outer = outward(framing)
    gas_pieces = exchanged(gas_cuts)

    (
        kept, sent, kept_cos, sent_cos, slot_of,
        lw_one, lw_shift, lw_two, lw_heads, lw_limit,
        sw_one, sw_shift, sw_two, sw_heads, sw_limit, flux,
    ) = call(
        prepare_body,
        [
            shaped((cols, half), BF16),
            shaped((cols, half), BF16),
            shaped((SUBS, half), F32),
            shaped((2 * SUBS, half), BF16),
            shaped((SUBS, cols), jnp.int32),
            shaped(lw_first.shape[::-1], BF16),
            shaped((hid, LANES), F32),
            shaped(lw_second.shape[::-1], BF16),
            shaped((2 * lw_gpts, 2 * hid), BF16),
            shaped((1, 1), F32),
            shaped(sw_first.shape[::-1], BF16),
            shaped((hid, LANES), F32),
            shaped(sw_second.shape[::-1], BF16),
            shaped((sw_gpts, 2 * hid), BF16),
            shaped((1, 1), F32),
            shaped((sw_gpts, LANES), F32),
        ],
        [
            day_count, listing, zenith,
            lw_first, lw_bias[None], lw_second, lw_depth, lw_fraction,
            sw_first, sw_bias[None], sw_second, sw_depth, solar_flux[None],
        ],
        after=framing,
    )

    third, *warm_cuts = call(
        sections_body,
        [shaped((slab, tile + 2 * HW), F32)] + [shaped((slab, cols), BF16)] * n_group,
        [me, place, outer, inner, potential, neighbours, diffusion],
        [pltpu.VMEM((slab, 3 * tile), F32)] * 3
        + [pltpu.VMEM((3, *neighbours.shape), jnp.int32), pltpu.VMEM((3, *diffusion.shape), F32)],
        flops=10_000_000,
    )
    warm_pieces = exchanged(warm_cuts)
    (closed,) = call(
        closing_body, [shaped((slab, tile), F32)], [third, neighbours, diffusion], flops=2_000_000
    )

    cells = levels * SUBS
    packed, out_x, kept_x = call(
        functools.partial(join_body, n_group),
        [
            shaped((cols // LANES, cells, LANES), F32),
            shaped((cells + 2 * SUBS, half), BF16),
            shaped((cells, half), F32),
        ],
        [me, *gas_pieces, *warm_pieces, kept, sent, sent_cos],
        [pltpu.VMEM((SUBS * slab, LANES), F32)],
    )
    in_x = paired(out_x)

    def longwave(which):
        (heat,) = call(
            functools.partial(longwave_body, which),
            [shaped((levels, half), F32)],
            [packed, lw_one, lw_shift, lw_two, lw_heads, lw_limit],
            sweep_scratch(hid, 2 * lw_gpts, lw_gpts, levels),
            flops=4 * levels * half * hid * lw_gpts,
            trans=5 * levels * half * lw_gpts,
            after=work if which else None,
        )
        return heat

    long_first = longwave(0)
    (work,) = call(
        shortwave_body,
        [shaped((levels, half), F32)],
        [day_count, kept_x, kept_cos, in_x, sw_one, sw_shift, sw_two, sw_heads, sw_limit, flux],
        [pltpu.VMEM((cells, half), F32)] + sweep_scratch(hid, sw_gpts, sw_gpts, levels),
        flops=2 * levels * half * hid * sw_gpts,
        trans=3 * levels * half * sw_gpts,
        after=long_first,
    )
    partner = paired(work)
    long_last = longwave(1)
    heat_cuts = call(
        finish_body,
        [shaped((slab, cols), F32)] * n_group,
        [me, day_count, long_first, long_last, work, partner, slot_of],
        [pltpu.VMEM((levels, cols), F32)],
    )
    heat_pieces = exchanged(heat_cuts)
    (evolved,) = call(add_body, [shaped((slab, tile), F32)], [me, closed, *heat_pieces])
    return evolved


def solution(mesh):
    return jax.shard_map(
        per_device,
        mesh=mesh,
        in_specs=(
            P("group", "tile"),
            P(None, "group", "tile"),
            P(None, "tile"),
            P(None, "tile"),
            P("group", "tile", None),
            P("group", "tile"),
            P("group", "tile", None),
            *([P()] * 10),
        ),
        out_specs=P("group", "tile"),
        check_vma=False,
    )
```

```python
import functools
import math

import jax
import jax.numpy as jnp
from jax import lax
from jax.experimental import pallas as pl
from jax.experimental.pallas import tpu as pltpu
from jax.sharding import PartitionSpec as P

HW = 256
LANES = 128
SUBS = 8

depth_scale = 0.1
heat_scale = 12.0
LOG2E = 1.4426950408889634
LN2 = 0.6931471805599453
SAFE = 120.0

F32 = jnp.float32
BF16 = jnp.bfloat16
VMEM = pl.BlockSpec(memory_space=pltpu.VMEM)
ANY = pl.BlockSpec(memory_space=pl.ANY)
HBM = pl.BlockSpec(memory_space=pltpu.HBM)
SMEM = pl.BlockSpec(memory_space=pltpu.SMEM)
PARAMS = pltpu.CompilerParams(vmem_limit_bytes=48 * 1024 * 1024)


def call(body, outs, ins, scratch=(), flops=0, trans=0, after=None, where=VMEM):
    in_specs = [SMEM if a.size == 1 else where for a in ins]
    if after is not None:
        whole, ins = body, [after, *ins]
        in_specs = [ANY, *in_specs]

        def body(_, *refs):
            whole(*refs)

    return pl.pallas_call(
        body,
        out_shape=outs,
        in_specs=in_specs,
        out_specs=[VMEM for _ in outs],
        scratch_shapes=list(scratch),
        compiler_params=PARAMS,
        cost_estimate=pl.CostEstimate(
            flops=flops,
            transcendentals=trans,
            bytes_accessed=sum(a.size * a.dtype.itemsize for a in list(ins) + list(outs)),
        ),
    )(*ins)


def shaped(shape, dtype):
    return jax.ShapeDtypeStruct(shape, dtype)


def iota(shape, dim):
    return lax.broadcasted_iota(jnp.int32, shape, dim)


def mm(a, b):
    return jnp.dot(a, b, preferred_element_type=F32)


def far_first(n):
    return [0, *range(n - 1, 0, -1)]


def partners(me, pieces):
    return [(me[0] ^ bit, piece) for bit, piece in zip(far_first(len(pieces)), pieces)]


def lane_take(x, idx):
    return jnp.take_along_axis(x, idx, axis=1, mode="promise_in_bounds")


def diffused(src, src_at, table, weight, within, at):
    reach = HW // LANES
    wide = 2 * reach + 1
    rows = src.shape[0]
    groups = range(0, rows, SUBS)
    base = at - src_at
    middle = [src[r : r + SUBS, base : base + LANES] for r in groups]
    total = [jnp.zeros_like(m) for m in middle]
    for k in range(table.shape[0]):
        place = jnp.broadcast_to(table[k : k + 1, within : within + LANES], (SUBS, LANES)) - within
        lane = place & (LANES - 1)
        which = place >> (LANES.bit_length() - 1)
        factor = jnp.broadcast_to(weight[k : k + 1, within : within + LANES], (SUBS, LANES))
        tests = [which == w for w in range(1, wide)]
        for n, r in enumerate(groups):
            near = None
            for w in range(wide):
                lo = base + (w - reach) * LANES
                got = lane_take(src[r : r + SUBS, lo : lo + LANES], lane)
                near = got if w == 0 else jnp.where(tests[w - 1], got, near)
            total[n] = total[n] + factor * (near - middle[n])
    return [(r, m, m + t) for r, m, t in zip(groups, middle, total)]


def pack_body(me, own, table, weight, species, out, *rest):
    pieces, (table_here, weight_here, sems) = rest[:-3], rest[-3:]
    slab = own.shape[0]
    near = table.shape[0]
    cols = pieces[0].shape[2]
    moves = [
        pltpu.make_async_copy(own, out.at[0:slab], sems.at[0]),
        pltpu.make_async_copy(table, table_here, sems.at[1]),
        pltpu.make_async_copy(weight, weight_here, sems.at[2]),
    ]
    for source, piece in partners(me, pieces):
        at = pl.ds(pl.multiple_of(source * cols, LANES), cols)
        moves.append(pltpu.make_async_copy(species.at[:, :, at], piece, sems.at[len(moves)]))
    for move in moves:
        move.start()
    for move in moves:
        move.wait()
    out[slab : slab + near, :] = table_here[...].astype(F32)
    out[slab + near :, :] = weight_here[...]


def sections_body(
    me, place, outer, inner, own, table, weight, third_out, *rest
):
    pieces, (frame, first, second, tables, weights) = rest[:-5], rest[-5:]
    slab, tile = own.shape
    near = table.shape[0]
    cols = tile // len(pieces)
    odd = place[0] & 1
    for side, packed in ((odd, outer), (1 - odd, inner)):
        at = pl.ds(pl.multiple_of(side * (2 * tile), LANES), tile)
        frame[:, at] = packed[0:slab, :]
        tables[side * 2] = packed[slab : slab + near, :].astype(jnp.int32)
        weights[side * 2] = packed[slab + near : slab + 2 * near, :]
    frame[:, tile : 2 * tile] = own[...]
    tables[1] = table[...]
    weights[1] = weight[...]

    def run(src, src_at, halo, put):
        for at in range(tile - halo, 2 * tile + halo, LANES):
            t = at // tile
            for r, _, value in diffused(src, src_at, tables.at[t], weights.at[t], at - t * tile, at):
                put(r, at, value)

    def put_first(r, at, value):
        first[r : r + SUBS, at : at + LANES] = value

    def put_second(r, at, value):
        start = frame[r : r + SUBS, at : at + LANES]
        second[r : r + SUBS, at : at + LANES] = 0.75 * start + 0.25 * value

    def put_third(r, at, value):
        start = frame[r : r + SUBS, at : at + LANES]
        lo = at - tile + HW
        third_out[r : r + SUBS, lo : lo + LANES] = start / 3.0 + (2.0 / 3.0) * value

    run(frame, 0, 3 * HW, put_first)
    run(first, 0, 2 * HW, put_second)
    run(second, 0, HW, put_third)
    for goal, out in partners(me, pieces):
        lo = pl.multiple_of(HW + goal * cols, LANES)
        out[...] = third_out[:, pl.ds(lo, cols)].astype(BF16)


def closing_body(third, table, weight, out):
    tile = out.shape[1]
    for at in range(0, tile, LANES):
        for r, _, value in diffused(third, -HW, table, weight, at, at):
            out[r : r + SUBS, at : at + LANES] = value


def turned_over(matrix):
    return matrix.astype(F32).T


def head_parts(weight, out, at):
    hid, gpts = weight.shape
    scaled = LOG2E * turned_over(weight[...])
    high = scaled.astype(BF16)
    out[at : at + gpts, 0:hid] = high
    out[at : at + gpts, hid:] = (scaled - high.astype(F32)).astype(BF16)


def reach_of(heads):
    sums = mm(jnp.abs(heads[...]), jnp.ones((heads.shape[1], LANES), BF16))
    return jnp.broadcast_to(jnp.max(sums, axis=0, keepdims=True), (2 * SUBS, LANES))


def prepare_body(
    count, listing, zenith, w1, b1, w2, wd, wf, v1, c1, v2, vd, flux,
    kept_out, sent_out, kept_cos, sent_cos, slot_of,
    w1_out, b1_out, w2_out, heads_out, plain_out, reach_out, v1_out, c1_out, v2_out, vd_out, vreach_out, flux_out,
):
    for weight, out in ((w1, w1_out), (w2, w2_out), (v1, v1_out), (v2, v2_out)):
        out[...] = (0.5 * turned_over(weight[...])).astype(BF16)
    head_parts(wd, heads_out, 0)
    head_parts(wf, heads_out, wd.shape[1])
    head_parts(vd, vd_out, 0)
    gpts = wd.shape[1]
    plain_out[0:gpts, :] = turned_over(wd[...]).astype(BF16)
    plain_out[gpts:, :] = turned_over(wf[...]).astype(BF16)
    reach_out[...] = reach_of(heads_out)
    vreach_out[...] = reach_of(vd_out)
    for row, out, scale in ((b1, b1_out, 0.5), (c1, c1_out, 0.5), (flux, flux_out, 1.0)):
        out[...] = scale * jnp.broadcast_to(row[...], (LANES, row.shape[1])).T
    cols = listing.shape[-1]
    half = cols // 2
    sunlit = count[0, 0]
    label = iota((cols, half), 0)
    slot = iota((cols, half), 1)
    first = jnp.broadcast_to(listing[0, :, 0:half], (cols, half)) == label
    last = jnp.broadcast_to(listing[0, :, half:cols], (cols, half)) == label
    kept = jnp.where(first & (slot < sunlit), 1.0, 0.0).astype(BF16)
    sent = jnp.where(last & (slot + half < sunlit), 1.0, 0.0).astype(BF16)
    kept_out[...] = kept
    sent_out[...] = sent
    cosine = jnp.broadcast_to(zenith[0].astype(F32), (2 * SUBS, cols)).astype(BF16)
    sent_cos[...] = mm(cosine, sent).astype(BF16)
    kept_cos[...] = mm(cosine, kept)[0:SUBS]
    hits = jnp.where(jnp.concatenate([first, last], axis=1), 1.0, 0.0).astype(BF16)
    numbers = iota((2 * SUBS, cols), 1).astype(F32).astype(BF16)
    found = lax.dot_general(numbers, hits, (((1,), (1,)), ((), ())), preferred_element_type=F32)
    slot_of[...] = found[0:SUBS].astype(jnp.int32)


def join_body(n_group, me, *rest):
    gases, warms = rest[:n_group], rest[n_group : 2 * n_group]
    kept, sent, sent_cos, packed, outgoing, kept_x, spread = rest[2 * n_group :]
    slab = warms[0].shape[0]
    for (source, gas), warm in zip(partners(me, gases), warms):
        for h in range(packed.shape[0]):
            at = slice(h * LANES, (h + 1) * LANES)
            spread[0:slab, :] = warm[:, at].astype(F32)
            for f in range(gas.shape[0]):
                spread[(f + 1) * slab : (f + 2) * slab, :] = gas[f, :, at].astype(F32)
            for l in range(slab):
                row = pl.multiple_of((source * slab + l) * SUBS, SUBS)
                packed[h, pl.ds(row, SUBS), :] = spread[pl.ds(l, SUBS, stride=slab), :]
    cells = packed.shape[1]
    first, last = packed[0].astype(BF16), packed[1].astype(BF16)
    outgoing[0:cells, :] = (mm(first, sent[0:LANES]) + mm(last, sent[LANES:])).astype(BF16)
    outgoing[cells:, :] = sent_cos[...]
    kept_x[...] = mm(first, kept[0:LANES]) + mm(last, kept[LANES:])


def softplus(z, plain):
    if plain:
        return jnp.log(1.0 + jnp.exp(z.astype(BF16)).astype(F32))
    return jnp.log(1.0 + jnp.exp2(z))


def softplus_guarded(z, plain):
    if plain:
        return jnp.maximum(z, jnp.log(1.0 + jnp.exp(jnp.minimum(z, SAFE * LN2))))
    return jnp.maximum(z * LN2, jnp.log(1.0 + jnp.exp2(jnp.minimum(z, SAFE))))


def silu_of_half(v):
    half = v.astype(BF16)
    return half + half * jnp.tanh(half)


def sweep(x, first, bias, second, heads, reach, start, gpts, rate, both, buffers):
    ones, hids, zs, trans, parts, peak = buffers
    step_levels = zs.shape[2] // LANES
    plain_heads = heads.shape[1] == first.shape[0]
    one_a, one_b = ones.at[0], ones.at[1]
    hid_a, hid_b = hids.at[0], hids.at[1]
    z_a, z_b = zs.at[0], zs.at[1]
    levels = x.shape[0] // SUBS
    steps = levels // step_levels
    wide = step_levels * LANES
    rows = heads.shape[0]
    col_cut = 2 * LANES
    chunk = 2 * SUBS if plain_heads else SUBS
    units = first.shape[0]
    unit_cut = units // 2

    def first_tasks(t, out):
        def task(r):
            row = jnp.minimum(t, steps - 1) * (step_levels * SUBS)
            tiles = [
                x[pl.ds(pl.multiple_of(row + i * SUBS, SUBS), SUBS), :] for i in range(step_levels)
            ]
            v = mm(first[r : r + unit_cut, :], jnp.concatenate(tiles, axis=1).astype(BF16))
            v = v + jnp.concatenate([bias[r : r + unit_cut, :]] * step_levels, axis=1)
            out[r : r + unit_cut, :] = silu_of_half(v)

        return [functools.partial(task, r) for r in range(0, units, unit_cut)]

    def second_tasks(one, out):
        def task(r):
            v = mm(second[r : r + unit_cut, :], one[...])
            value = silu_of_half(v)
            out[r : r + unit_cut, :] = value
            if not plain_heads:
                out[units + r : units + r + unit_cut, :] = value
            most = peak[...]
            for i in range(0, unit_cut, 2 * SUBS):
                for at in range(0, wide, LANES):
                    most = jnp.maximum(most, value[i : i + 2 * SUBS, at : at + LANES])
            peak[...] = most

        return [functools.partial(task, r) for r in range(0, units, unit_cut)]

    def optics_tasks(hid, out):
        def task(lo):
            at = slice(lo, lo + col_cut)
            out[:, at] = mm(heads[...], hid[0 : heads.shape[1], at])

        return [functools.partial(task, lo) for lo in range(0, wide, col_cut)]

    def consume_tasks(z, total):
        def product(lo):
            return z[lo : lo + chunk, :]

        def task(lo):
            carry = trans[lo : lo + chunk, :]
            depth = product(lo)
            share = product(gpts + lo) if both else None
            for i in range(step_levels):
                at = slice(i * LANES, (i + 1) * LANES)
                following = carry * jnp.exp2(softplus(depth[:, at], plain_heads) * rate)
                term = following
                if both:
                    term = (carry - following) * softplus(share[:, at], plain_heads)
                for r in range(0, chunk, SUBS):
                    part = term[r : r + SUBS]
                    total[i] = part if total[i] is None else total[i] + part
                carry = following
            trans[lo : lo + chunk, :] = carry

        return [functools.partial(task, lo) for lo in range(0, gpts, chunk)]

    def woven(main, side):
        done = 0
        for n, task in enumerate(main):
            while done < len(side) and done * len(main) <= n * len(side):
                side[done]()
                done += 1
            task()
        for task in side[done:]:
            task()

    def plain(tasks):
        for task in tasks:
            task()

    def run():
        trans[...] = start
        if not both:
            parts[0:SUBS, :] = jnp.sum(start.reshape(gpts // SUBS, SUBS, LANES), axis=0)

        def step(t, z, z_next, hid_next, hid_later, one_later, one_last):
            total = [None] * step_levels
            side = second_tasks(one_later, hid_later) + first_tasks(t + 3, one_last)
            woven(consume_tasks(z, total), optics_tasks(hid_next, z_next) + side)
            for i in range(step_levels):
                at = pl.multiple_of((t * step_levels + i + 1) * SUBS, SUBS)
                parts[pl.ds(at, SUBS), :] = total[i]

        def two(i, _):
            most = jnp.max(peak[...].astype(F32) * reach[...])
            step(2 * i, z_a, z_b, hid_b, hid_a, one_a, one_b)
            step(2 * i + 1, z_b, z_a, hid_a, hid_b, one_b, one_a)
            return most

        plain(first_tasks(0, one_a))
        plain(second_tasks(one_a, hid_a))
        plain(first_tasks(1, one_b))
        plain(optics_tasks(hid_a, z_a))
        plain(second_tasks(one_b, hid_b))
        plain(first_tasks(2, one_a))
        return lax.fori_loop(0, steps // 2, two, jnp.float32(0.0))

    def run_guarded():
        trans[...] = start
        at = slice(0, LANES)

        def level(l, _):
            tile = x[pl.ds(pl.multiple_of(l * SUBS, SUBS), SUBS), :].astype(BF16)
            hidden = silu_of_half(mm(first[...], tile) + bias[...])
            hidden = silu_of_half(mm(second[...], hidden))
            z_a[:, at] = mm(heads[...], jnp.concatenate([hidden] * (heads.shape[1] // units), axis=0))

            def piece(c, total):
                lo = pl.multiple_of(c * SUBS, SUBS)
                carry = trans[pl.ds(lo, SUBS), :]
                depth = softplus_guarded(z_a[pl.ds(lo, SUBS), at], plain_heads)
                following = carry * jnp.exp2(depth * rate)
                trans[pl.ds(lo, SUBS), :] = following
                if not both:
                    return total + following
                share = softplus_guarded(
                    z_a[pl.ds(pl.multiple_of(gpts + lo, SUBS), SUBS), at], plain_heads
                )
                return total + (carry - following) * share

            total = lax.fori_loop(0, gpts // SUBS, piece, jnp.zeros((SUBS, LANES), F32))
            parts[pl.ds(pl.multiple_of((l + 1) * SUBS, SUBS), SUBS), :] = total
            return 0

        lax.fori_loop(0, levels, level, 0)

    peak[...] = jnp.ones_like(peak)
    most = run()
    pl.when(most > SAFE)(run_guarded)
    emitted = None
    for s in range(SUBS):
        part = parts[pl.ds(s + SUBS, levels, stride=SUBS), :]
        if not both:
            part = parts[pl.ds(s, levels, stride=SUBS), :] - part
        emitted = part if emitted is None else emitted + part
    return emitted


def sweep_scratch(hid, rows, gpts, levels, step_levels=4):
    wide = step_levels * LANES
    return [
        pltpu.VMEM((2, hid, wide), BF16),
        pltpu.VMEM((2, 2 * hid, wide), BF16),
        pltpu.VMEM((2, rows, wide), F32),
        pltpu.VMEM((gpts, LANES), F32),
        pltpu.VMEM(((levels + 1) * SUBS, LANES), F32),
        pltpu.VMEM((2 * SUBS, LANES), BF16),
    ]


def longwave_body(which, packed, first, bias, second, heads, reach, out, *buffers):
    gpts = heads.shape[0] // 2
    levels = out.shape[0]
    x = packed.at[which]
    emitted = sweep(
        x, first, bias, second, heads, reach, jnp.ones((gpts, LANES), F32), gpts,
        -depth_scale * LOG2E, True, buffers,
    )
    planck = jnp.exp(0.25 * x[pl.ds(0, levels, stride=SUBS), :])
    out[...] = -(heat_scale / gpts) * planck * emitted


def shortwave_body(
    count, kept_x, kept_cos, in_x, first, bias, second, heads, reach, flux, out, work_x, *buffers
):
    cells, half = kept_x.shape
    gpts = heads.shape[0]
    slot = iota((half, half), 1) - count[0, 0]
    placed = jnp.where(slot == iota((half, half), 0), 1.0, 0.0).astype(BF16)
    work_x[...] = kept_x[...] + mm(in_x[0:cells, :], placed)
    cosine = kept_cos[...] + mm(in_x[cells:, :], placed)[0:SUBS]
    cosine = jnp.where(cosine > 0.0, cosine, 1.0)
    emitted = sweep(
        work_x, first, bias, second, heads, reach, flux[...], gpts,
        (-depth_scale * LOG2E) / cosine, False, buffers,
    )
    out[...] = (heat_scale / gpts) * cosine[0:1] * emitted


def finish_body(me, count, long_first, long_last, work, partner, slot_of, *rest):
    pieces, heat = rest[:-1], rest[-1]
    levels, cols = heat.shape
    half = cols // 2
    slab = pieces[0].shape[0]
    sunlit = count[0, 0]
    for lo, long in ((0, long_first), (half, long_last)):
        slot = slot_of[:, lo : lo + half]
        here = slot < half
        place = jnp.where(here, slot, slot + half - sunlit) & (half - 1)
        lit = slot < sunlit
        for r in range(0, levels, SUBS):
            near = lane_take(work[r : r + SUBS, :], place)
            far = lane_take(partner[r : r + SUBS, :], place)
            short = jnp.where(lit, jnp.where(here, near, far), 0.0)
            heat[r : r + SUBS, lo : lo + half] = long[r : r + SUBS, :] + short
    for goal, out in partners(me, pieces):
        out[...] = heat[pl.ds(pl.multiple_of(goal * slab, SUBS), slab), :]


def add_body(me, closed, *rest):
    pieces, out = rest[:-1], rest[-1]
    cols = pieces[0].shape[1]
    for source, piece in partners(me, pieces):
        at = pl.ds(pl.multiple_of(source * cols, LANES), cols)
        out[:, at] = closed[:, at] + piece[...]


def per_device(
    potential, species, diffusion, neighbours, listing, day_count, zenith,
    lw_first, lw_bias, lw_second, lw_depth, lw_fraction,
    sw_first, sw_bias, sw_second, sw_depth, solar_flux,
):
    n_group = lax.axis_size("group")
    n_tile = lax.axis_size("tile")
    assert n_group & (n_group - 1) == 0 and n_tile % 2 == 0
    me = lax.axis_index("group").astype(jnp.int32).reshape(1)
    place = lax.axis_index("tile").astype(jnp.int32).reshape(1)
    slab, tile = potential.shape
    gases = species.shape[0]
    cols = tile // n_group
    half = cols // 2
    levels = slab * n_group
    hid = lw_first.shape[1]
    lw_gpts = lw_depth.shape[1]
    sw_gpts = sw_depth.shape[1]

    def outward(value):
        across = [(i, (i + 1 if i % 2 else i - 1) % n_tile) for i in range(n_tile)]
        return lax.ppermute(value, "tile", across)

    def paired(value):
        return lax.ppermute(value, "tile", [(i, i ^ 1) for i in range(n_tile)])

    def swapped(value, bit):
        return lax.ppermute(value, "group", [(i, i ^ bit) for i in range(n_group)])

    def exchanged(pieces):
        return [swapped(p, bit) if bit else p for bit, p in zip(far_first(n_group), pieces)]

    near = neighbours.shape[0]
    raw = (potential, neighbours, diffusion, species)
    framing, *gas_cuts = call(
        pack_body,
        [shaped((slab + 2 * near, tile), F32)] + [shaped((gases, slab, cols), BF16)] * n_group,
        [me, *(pltpu.with_memory_space_constraint(a, pltpu.HBM) for a in raw)],
        [
            pltpu.VMEM(neighbours.shape, jnp.int32),
            pltpu.VMEM(diffusion.shape, F32),
            pltpu.SemaphoreType.DMA((3 + n_group,)),
        ],
        where=HBM,
    )
    inner = paired(framing)
    outer = outward(framing)
    gas_pieces = exchanged(gas_cuts)

    (
        kept, sent, kept_cos, sent_cos, slot_of,
        lw_one, lw_shift, lw_two, lw_heads, lw_plain, lw_reach,
        sw_one, sw_shift, sw_two, sw_heads, sw_reach, flux,
    ) = call(
        prepare_body,
        [
            shaped((cols, half), BF16),
            shaped((cols, half), BF16),
            shaped((SUBS, half), F32),
            shaped((2 * SUBS, half), BF16),
            shaped((SUBS, cols), jnp.int32),
            shaped(lw_first.shape[::-1], BF16),
            shaped((hid, LANES), F32),
            shaped(lw_second.shape[::-1], BF16),
            shaped((2 * lw_gpts, 2 * hid), BF16),
            shaped((2 * lw_gpts, hid), BF16),
            shaped((2 * SUBS, LANES), F32),
            shaped(sw_first.shape[::-1], BF16),
            shaped((hid, LANES), F32),
            shaped(sw_second.shape[::-1], BF16),
            shaped((sw_gpts, 2 * hid), BF16),
            shaped((2 * SUBS, LANES), F32),
            shaped((sw_gpts, LANES), F32),
        ],
        [
            day_count, listing, zenith,
            lw_first, lw_bias[None], lw_second, lw_depth, lw_fraction,
            sw_first, sw_bias[None], sw_second, sw_depth, solar_flux[None],
        ],
        after=framing,
    )

    third, *warm_cuts = call(
        sections_body,
        [shaped((slab, tile + 2 * HW), F32)] + [shaped((slab, cols), BF16)] * n_group,
        [me, place, outer, inner, potential, neighbours, diffusion],
        [pltpu.VMEM((slab, 3 * tile), F32)] * 3
        + [pltpu.VMEM((3, *neighbours.shape), jnp.int32), pltpu.VMEM((3, *diffusion.shape), F32)],
        flops=10_000_000,
    )
    warm_pieces = exchanged(warm_cuts)
    (closed,) = call(
        closing_body, [shaped((slab, tile), F32)], [third, neighbours, diffusion], flops=2_000_000
    )

    cells = levels * SUBS
    packed, out_x, kept_x = call(
        functools.partial(join_body, n_group),
        [
            shaped((cols // LANES, cells, LANES), F32),
            shaped((cells + 2 * SUBS, half), BF16),
            shaped((cells, half), F32),
        ],
        [me, *gas_pieces, *warm_pieces, kept, sent, sent_cos],
        [pltpu.VMEM((SUBS * slab, LANES), F32)],
    )
    in_x = paired(out_x)

    def longwave(which):
        (heat,) = call(
            functools.partial(longwave_body, which),
            [shaped((levels, half), F32)],
            [packed, lw_one, lw_shift, lw_two, lw_heads if which else lw_plain, lw_reach],
            sweep_scratch(hid, 2 * lw_gpts, lw_gpts, levels, 8 if which else 4),
            flops=4 * levels * half * hid * lw_gpts,
            trans=5 * levels * half * lw_gpts,
            after=work if which else None,
        )
        return heat

    long_first = longwave(0)
    (work,) = call(
        shortwave_body,
        [shaped((levels, half), F32)],
        [day_count, kept_x, kept_cos, in_x, sw_one, sw_shift, sw_two, sw_heads, sw_reach, flux],
        [pltpu.VMEM((cells, half), F32)] + sweep_scratch(hid, sw_gpts, sw_gpts, levels),
        flops=2 * levels * half * hid * sw_gpts,
        trans=3 * levels * half * sw_gpts,
        after=long_first,
    )
    partner = paired(work)
    long_last = longwave(1)
    heat_cuts = call(
        finish_body,
        [shaped((slab, cols), F32)] * n_group,
        [me, day_count, long_first, long_last, work, partner, slot_of],
        [pltpu.VMEM((levels, cols), F32)],
    )
    heat_pieces = exchanged(heat_cuts)
    (evolved,) = call(add_body, [shaped((slab, tile), F32)], [me, closed, *heat_pieces])
    return evolved


def solution(mesh):
    return jax.shard_map(
        per_device,
        mesh=mesh,
        in_specs=(
            P("group", "tile"),
            P(None, "group", "tile"),
            P(None, "tile"),
            P(None, "tile"),
            P("group", "tile", None),
            P("group", "tile"),
            P("group", "tile", None),
            *([P()] * 10),
        ),
        out_specs=P("group", "tile"),
        check_vma=False,
    )
```

```python
import functools
import math

import jax
import jax.numpy as jnp
from jax import lax
from jax.experimental import pallas as pl
from jax.experimental.pallas import tpu as pltpu
from jax.sharding import PartitionSpec as P

HW = 256
LANES = 128
SUBS = 8

depth_scale = 0.1
heat_scale = 12.0
LOG2E = 1.4426950408889634
LN2 = 0.6931471805599453
SAFE = 120.0

F32 = jnp.float32
BF16 = jnp.bfloat16
VMEM = pl.BlockSpec(memory_space=pltpu.VMEM)
ANY = pl.BlockSpec(memory_space=pl.ANY)
HBM = pl.BlockSpec(memory_space=pltpu.HBM)
SMEM = pl.BlockSpec(memory_space=pltpu.SMEM)
PARAMS = pltpu.CompilerParams(vmem_limit_bytes=48 * 1024 * 1024)


def call(body, outs, ins, scratch=(), flops=0, trans=0, after=None, where=VMEM):
    in_specs = [SMEM if a.size == 1 else where for a in ins]
    if after is not None:
        whole, ins = body, [after, *ins]
        in_specs = [ANY, *in_specs]

        def body(_, *refs):
            whole(*refs)

    return pl.pallas_call(
        body,
        out_shape=outs,
        in_specs=in_specs,
        out_specs=[VMEM for _ in outs],
        scratch_shapes=list(scratch),
        compiler_params=PARAMS,
        cost_estimate=pl.CostEstimate(
            flops=flops,
            transcendentals=trans,
            bytes_accessed=sum(a.size * a.dtype.itemsize for a in list(ins) + list(outs)),
        ),
    )(*ins)


def shaped(shape, dtype):
    return jax.ShapeDtypeStruct(shape, dtype)


def iota(shape, dim):
    return lax.broadcasted_iota(jnp.int32, shape, dim)


def mm(a, b):
    return jnp.dot(a, b, preferred_element_type=F32)


def far_first(n):
    return [0, *range(n - 1, 0, -1)]


def partners(me, pieces):
    return [(me[0] ^ bit, piece) for bit, piece in zip(far_first(len(pieces)), pieces)]


def lane_take(x, idx):
    return jnp.take_along_axis(x, idx, axis=1, mode="promise_in_bounds")


def diffused(src, src_at, table, weight, within, at):
    reach = HW // LANES
    wide = 2 * reach + 1
    rows = src.shape[0]
    groups = range(0, rows, SUBS)
    base = at - src_at
    middle = [src[r : r + SUBS, base : base + LANES] for r in groups]
    total = [jnp.zeros_like(m) for m in middle]
    for k in range(table.shape[0]):
        place = jnp.broadcast_to(table[k : k + 1, within : within + LANES], (SUBS, LANES)) - within
        lane = place & (LANES - 1)
        which = place >> (LANES.bit_length() - 1)
        factor = jnp.broadcast_to(weight[k : k + 1, within : within + LANES], (SUBS, LANES))
        tests = [which == w for w in range(1, wide)]
        for n, r in enumerate(groups):
            near = None
            for w in range(wide):
                lo = base + (w - reach) * LANES
                got = lane_take(src[r : r + SUBS, lo : lo + LANES], lane)
                near = got if w == 0 else jnp.where(tests[w - 1], got, near)
            total[n] = total[n] + factor * (near - middle[n])
    return [(r, m, m + t) for r, m, t in zip(groups, middle, total)]


def pack_body(me, own, table, weight, species, out, *rest):
    pieces, (table_here, weight_here, sems) = rest[:-3], rest[-3:]
    slab = own.shape[0]
    near = table.shape[0]
    cols = pieces[0].shape[2]
    moves = [
        pltpu.make_async_copy(own, out.at[0:slab], sems.at[0]),
        pltpu.make_async_copy(table, table_here, sems.at[1]),
        pltpu.make_async_copy(weight, weight_here, sems.at[2]),
    ]
    for source, piece in partners(me, pieces):
        at = pl.ds(pl.multiple_of(source * cols, LANES), cols)
        moves.append(pltpu.make_async_copy(species.at[:, :, at], piece, sems.at[len(moves)]))
    for move in moves:
        move.start()
    for move in moves:
        move.wait()
    out[slab : slab + near, :] = table_here[...].astype(F32)
    out[slab + near :, :] = weight_here[...]


def sections_body(
    me, place, outer, inner, own, table, weight, third_out, *rest
):
    pieces, (frame, first, second, tables, weights) = rest[:-5], rest[-5:]
    slab, tile = own.shape
    near = table.shape[0]
    cols = tile // len(pieces)
    odd = place[0] & 1
    for side, packed in ((odd, outer), (1 - odd, inner)):
        at = pl.ds(pl.multiple_of(side * (2 * tile), LANES), tile)
        frame[:, at] = packed[0:slab, :]
        tables[side * 2] = packed[slab : slab + near, :].astype(jnp.int32)
        weights[side * 2] = packed[slab + near : slab + 2 * near, :]
    frame[:, tile : 2 * tile] = own[...]
    tables[1] = table[...]
    weights[1] = weight[...]

    def run(src, src_at, halo, put):
        for at in range(tile - halo, 2 * tile + halo, LANES):
            t = at // tile
            for r, _, value in diffused(src, src_at, tables.at[t], weights.at[t], at - t * tile, at):
                put(r, at, value)

    def put_first(r, at, value):
        first[r : r + SUBS, at : at + LANES] = value

    def put_second(r, at, value):
        start = frame[r : r + SUBS, at : at + LANES]
        second[r : r + SUBS, at : at + LANES] = 0.75 * start + 0.25 * value

    def put_third(r, at, value):
        start = frame[r : r + SUBS, at : at + LANES]
        lo = at - tile + HW
        third_out[r : r + SUBS, lo : lo + LANES] = start / 3.0 + (2.0 / 3.0) * value

    run(frame, 0, 3 * HW, put_first)
    run(first, 0, 2 * HW, put_second)
    run(second, 0, HW, put_third)
    for goal, out in partners(me, pieces):
        lo = pl.multiple_of(HW + goal * cols, LANES)
        out[...] = third_out[:, pl.ds(lo, cols)].astype(BF16)


def closing_body(third, table, weight, out):
    tile = out.shape[1]
    for at in range(0, tile, LANES):
        for r, _, value in diffused(third, -HW, table, weight, at, at):
            out[r : r + SUBS, at : at + LANES] = value


def turned_over(matrix):
    return matrix.astype(F32).T


def head_parts(weight, out, at):
    hid, gpts = weight.shape
    scaled = LOG2E * turned_over(weight[...])
    high = scaled.astype(BF16)
    out[at : at + gpts, 0:hid] = high
    out[at : at + gpts, hid:] = (scaled - high.astype(F32)).astype(BF16)


def reach_of(heads):
    sums = mm(jnp.abs(heads[...]), jnp.ones((heads.shape[1], LANES), BF16))
    return jnp.broadcast_to(jnp.max(sums, axis=0, keepdims=True), (2 * SUBS, LANES))


def prepare_body(
    count, listing, zenith, w1, b1, w2, wd, wf, v1, c1, v2, vd, flux,
    kept_out, sent_out, kept_cos, sent_cos, slot_of,
    w1_out, b1_out, w2_out, heads_out, reach_out, v1_out, c1_out, v2_out, vd_out, vreach_out, flux_out,
):
    for weight, out in ((w1, w1_out), (w2, w2_out), (v1, v1_out), (v2, v2_out)):
        out[...] = (0.5 * turned_over(weight[...])).astype(BF16)
    head_parts(wd, heads_out, 0)
    head_parts(wf, heads_out, wd.shape[1])
    head_parts(vd, vd_out, 0)
    reach_out[...] = reach_of(heads_out)
    vreach_out[...] = reach_of(vd_out)
    for row, out, scale in ((b1, b1_out, 0.5), (c1, c1_out, 0.5), (flux, flux_out, 1.0)):
        out[...] = scale * jnp.broadcast_to(row[...], (LANES, row.shape[1])).T
    cols = listing.shape[-1]
    half = cols // 2
    sunlit = count[0, 0]
    label = iota((cols, half), 0)
    slot = iota((cols, half), 1)
    first = jnp.broadcast_to(listing[0, :, 0:half], (cols, half)) == label
    last = jnp.broadcast_to(listing[0, :, half:cols], (cols, half)) == label
    kept = jnp.where(first & (slot < sunlit), 1.0, 0.0).astype(BF16)
    sent = jnp.where(last & (slot + half < sunlit), 1.0, 0.0).astype(BF16)
    kept_out[...] = kept
    sent_out[...] = sent
    cosine = jnp.broadcast_to(zenith[0].astype(F32), (2 * SUBS, cols)).astype(BF16)
    sent_cos[...] = mm(cosine, sent).astype(BF16)
    kept_cos[...] = mm(cosine, kept)[0:SUBS]
    hits = jnp.where(jnp.concatenate([first, last], axis=1), 1.0, 0.0).astype(BF16)
    numbers = iota((2 * SUBS, cols), 1).astype(F32).astype(BF16)
    found = lax.dot_general(numbers, hits, (((1,), (1,)), ((), ())), preferred_element_type=F32)
    slot_of[...] = found[0:SUBS].astype(jnp.int32)


def join_body(n_group, me, *rest):
    gases, warms = rest[:n_group], rest[n_group : 2 * n_group]
    kept, sent, sent_cos, packed, outgoing, kept_x, spread = rest[2 * n_group :]
    slab = warms[0].shape[0]
    for (source, gas), warm in zip(partners(me, gases), warms):
        for h in range(packed.shape[0]):
            at = slice(h * LANES, (h + 1) * LANES)
            spread[0:slab, :] = warm[:, at].astype(F32)
            for f in range(gas.shape[0]):
                spread[(f + 1) * slab : (f + 2) * slab, :] = gas[f, :, at].astype(F32)
            for l in range(slab):
                row = pl.multiple_of((source * slab + l) * SUBS, SUBS)
                packed[h, pl.ds(row, SUBS), :] = spread[pl.ds(l, SUBS, stride=slab), :]
    cells = packed.shape[1]
    first, last = packed[0].astype(BF16), packed[1].astype(BF16)
    outgoing[0:cells, :] = (mm(first, sent[0:LANES]) + mm(last, sent[LANES:])).astype(BF16)
    outgoing[cells:, :] = sent_cos[...]
    kept_x[...] = mm(first, kept[0:LANES]) + mm(last, kept[LANES:])


def softplus2(z):
    return lax.log2(1.0 + jnp.exp2(z))


def softplus2_guarded(z):
    return jnp.maximum(z, softplus2(jnp.minimum(z, SAFE)))


def silu_of_half(v):
    half = v.astype(BF16)
    return half + half * jnp.tanh(half)


def sweep(x, first, bias, second, heads, reach, start, gpts, rate, both, buffers, chunk_rows):
    ones, hids, zs, trans, parts, peak = buffers
    step_levels = zs.shape[2] // LANES
    one_a, one_b = ones.at[0], ones.at[1]
    hid_a, hid_b = hids.at[0], hids.at[1]
    z_a, z_b = zs.at[0], zs.at[1]
    levels = x.shape[0] // SUBS
    steps = levels // step_levels
    wide = step_levels * LANES
    rows = heads.shape[0]
    col_cut = 2 * LANES
    chunk = chunk_rows
    units = first.shape[0]
    unit_cut = units // 2

    def first_tasks(t, out):
        def task(r):
            row = jnp.minimum(t, steps - 1) * (step_levels * SUBS)
            tiles = [
                x[pl.ds(pl.multiple_of(row + i * SUBS, SUBS), SUBS), :] for i in range(step_levels)
            ]
            v = mm(first[r : r + unit_cut, :], jnp.concatenate(tiles, axis=1).astype(BF16))
            v = v + jnp.concatenate([bias[r : r + unit_cut, :]] * step_levels, axis=1)
            out[r : r + unit_cut, :] = silu_of_half(v)

        return [functools.partial(task, r) for r in range(0, units, unit_cut)]

    def second_tasks(one, out):
        def task(r):
            v = mm(second[r : r + unit_cut, :], one[...])
            value = silu_of_half(v)
            out[r : r + unit_cut, :] = value
            out[units + r : units + r + unit_cut, :] = value
            most = peak[...]
            for i in range(0, unit_cut, 2 * SUBS):
                for at in range(0, wide, LANES):
                    most = jnp.maximum(most, value[i : i + 2 * SUBS, at : at + LANES])
            peak[...] = most

        return [functools.partial(task, r) for r in range(0, units, unit_cut)]

    def optics_tasks(hid, out):
        def task(lo):
            at = slice(lo, lo + col_cut)
            out[:, at] = mm(heads[...], hid[:, at])

        return [functools.partial(task, lo) for lo in range(0, wide, col_cut)]

    def consume_tasks(z, total):
        def product(lo):
            return z[lo : lo + chunk, :]

        def task(lo):
            carry = trans[lo : lo + chunk, :]
            depth = product(lo)
            share = product(gpts + lo) if both else None
            for i in range(step_levels):
                at = slice(i * LANES, (i + 1) * LANES)
                following = carry * jnp.exp2(softplus2(depth[:, at]) * rate)
                term = following
                if both:
                    term = (carry - following) * softplus2(share[:, at])
                for r in range(0, chunk, SUBS):
                    part = term[r : r + SUBS]
                    total[i] = part if total[i] is None else total[i] + part
                carry = following
            trans[lo : lo + chunk, :] = carry

        return [functools.partial(task, lo) for lo in range(0, gpts, chunk)]

    def woven(main, side):
        done = 0
        for n, task in enumerate(main):
            while done < len(side) and done * len(main) <= n * len(side):
                side[done]()
                done += 1
            task()
        for task in side[done:]:
            task()

    def plain(tasks):
        for task in tasks:
            task()

    def run():
        trans[...] = start
        if not both:
            parts[0:SUBS, :] = jnp.sum(start.reshape(gpts // SUBS, SUBS, LANES), axis=0)

        def step(t, z, z_next, hid_next, hid_later, one_later, one_last):
            total = [None] * step_levels
            side = second_tasks(one_later, hid_later) + first_tasks(t + 3, one_last)
            woven(consume_tasks(z, total), optics_tasks(hid_next, z_next) + side)
            for i in range(step_levels):
                at = pl.multiple_of((t * step_levels + i + 1) * SUBS, SUBS)
                parts[pl.ds(at, SUBS), :] = total[i]

        def two(i, _):
            most = jnp.max(peak[...].astype(F32) * reach[...])
            step(2 * i, z_a, z_b, hid_b, hid_a, one_a, one_b)
            step(2 * i + 1, z_b, z_a, hid_a, hid_b, one_b, one_a)
            return most

        plain(first_tasks(0, one_a))
        plain(second_tasks(one_a, hid_a))
        plain(first_tasks(1, one_b))
        plain(optics_tasks(hid_a, z_a))
        plain(second_tasks(one_b, hid_b))
        plain(first_tasks(2, one_a))
        return lax.fori_loop(0, steps // 2, two, jnp.float32(0.0))

    def run_guarded():
        trans[...] = start
        at = slice(0, LANES)

        def level(l, _):
            tile = x[pl.ds(pl.multiple_of(l * SUBS, SUBS), SUBS), :].astype(BF16)
            hidden = silu_of_half(mm(first[...], tile) + bias[...])
            hidden = silu_of_half(mm(second[...], hidden))
            z_a[:, at] = mm(heads[...], jnp.concatenate([hidden, hidden], axis=0))

            def piece(c, total):
                lo = pl.multiple_of(c * SUBS, SUBS)
                carry = trans[pl.ds(lo, SUBS), :]
                depth = softplus2_guarded(z_a[pl.ds(lo, SUBS), at])
                following = carry * jnp.exp2(depth * rate)
                trans[pl.ds(lo, SUBS), :] = following
                if not both:
                    return total + following
                share = softplus2_guarded(z_a[pl.ds(pl.multiple_of(gpts + lo, SUBS), SUBS), at])
                return total + (carry - following) * share

            total = lax.fori_loop(0, gpts // SUBS, piece, jnp.zeros((SUBS, LANES), F32))
            parts[pl.ds(pl.multiple_of((l + 1) * SUBS, SUBS), SUBS), :] = total
            return 0

        lax.fori_loop(0, levels, level, 0)

    peak[...] = jnp.ones_like(peak)
    most = run()
    pl.when(most > SAFE)(run_guarded)
    emitted = None
    for s in range(SUBS):
        part = parts[pl.ds(s + SUBS, levels, stride=SUBS), :]
        if not both:
            part = parts[pl.ds(s, levels, stride=SUBS), :] - part
        emitted = part if emitted is None else emitted + part
    return emitted


def sweep_scratch(hid, rows, gpts, levels, step_levels=4):
    wide = step_levels * LANES
    return [
        pltpu.VMEM((2, hid, wide), BF16),
        pltpu.VMEM((2, 2 * hid, wide), BF16),
        pltpu.VMEM((2, rows, wide), F32),
        pltpu.VMEM((gpts, LANES), F32),
        pltpu.VMEM(((levels + 1) * SUBS, LANES), F32),
        pltpu.VMEM((2 * SUBS, LANES), BF16),
    ]


def longwave_body(which, packed, first, bias, second, heads, reach, out, *buffers):
    gpts = heads.shape[0] // 2
    levels = out.shape[0]
    x = packed.at[which]
    emitted = sweep(
        x, first, bias, second, heads, reach, jnp.ones((gpts, LANES), F32), gpts,
        -depth_scale, True, buffers, 2 * SUBS if which else SUBS,
    )
    planck = jnp.exp(0.25 * x[pl.ds(0, levels, stride=SUBS), :])
    out[...] = -(heat_scale * LN2 / gpts) * planck * emitted


def shortwave_body(
    count, kept_x, kept_cos, in_x, first, bias, second, heads, reach, flux, out, work_x, *buffers
):
    cells, half = kept_x.shape
    gpts = heads.shape[0]
    slot = iota((half, half), 1) - count[0, 0]
    placed = jnp.where(slot == iota((half, half), 0), 1.0, 0.0).astype(BF16)
    work_x[...] = kept_x[...] + mm(in_x[0:cells, :], placed)
    cosine = kept_cos[...] + mm(in_x[cells:, :], placed)[0:SUBS]
    cosine = jnp.where(cosine > 0.0, cosine, 1.0)
    emitted = sweep(
        work_x, first, bias, second, heads, reach, flux[...], gpts,
        -depth_scale / cosine, False, buffers, SUBS,
    )
    out[...] = (heat_scale / gpts) * cosine[0:1] * emitted


def finish_body(me, count, long_first, long_last, work, partner, slot_of, *rest):
    pieces, heat = rest[:-1], rest[-1]
    levels, cols = heat.shape
    half = cols // 2
    slab = pieces[0].shape[0]
    sunlit = count[0, 0]
    for lo, long in ((0, long_first), (half, long_last)):
        slot = slot_of[:, lo : lo + half]
        here = slot < half
        place = jnp.where(here, slot, slot + half - sunlit) & (half - 1)
        lit = slot < sunlit
        for r in range(0, levels, SUBS):
            near = lane_take(work[r : r + SUBS, :], place)
            far = lane_take(partner[r : r + SUBS, :], place)
            short = jnp.where(lit, jnp.where(here, near, far), 0.0)
            heat[r : r + SUBS, lo : lo + half] = long[r : r + SUBS, :] + short
    for goal, out in partners(me, pieces):
        out[...] = heat[pl.ds(pl.multiple_of(goal * slab, SUBS), slab), :]


def add_body(me, closed, *rest):
    pieces, out = rest[:-1], rest[-1]
    cols = pieces[0].shape[1]
    for source, piece in partners(me, pieces):
        at = pl.ds(pl.multiple_of(source * cols, LANES), cols)
        out[:, at] = closed[:, at] + piece[...]


def per_device(
    potential, species, diffusion, neighbours, listing, day_count, zenith,
    lw_first, lw_bias, lw_second, lw_depth, lw_fraction,
    sw_first, sw_bias, sw_second, sw_depth, solar_flux,
):
    n_group = lax.axis_size("group")
    n_tile = lax.axis_size("tile")
    assert n_group & (n_group - 1) == 0 and n_tile % 2 == 0
    me = lax.axis_index("group").astype(jnp.int32).reshape(1)
    place = lax.axis_index("tile").astype(jnp.int32).reshape(1)
    slab, tile = potential.shape
    gases = species.shape[0]
    cols = tile // n_group
    half = cols // 2
    levels = slab * n_group
    hid = lw_first.shape[1]
    lw_gpts = lw_depth.shape[1]
    sw_gpts = sw_depth.shape[1]

    def outward(value):
        across = [(i, (i + 1 if i % 2 else i - 1) % n_tile) for i in range(n_tile)]
        return lax.ppermute(value, "tile", across)

    def paired(value):
        return lax.ppermute(value, "tile", [(i, i ^ 1) for i in range(n_tile)])

    def swapped(value, bit):
        return lax.ppermute(value, "group", [(i, i ^ bit) for i in range(n_group)])

    def exchanged(pieces):
        return [swapped(p, bit) if bit else p for bit, p in zip(far_first(n_group), pieces)]

    near = neighbours.shape[0]
    raw = (potential, neighbours, diffusion, species)
    framing, *gas_cuts = call(
        pack_body,
        [shaped((slab + 2 * near, tile), F32)] + [shaped((gases, slab, cols), BF16)] * n_group,
        [me, *(pltpu.with_memory_space_constraint(a, pltpu.HBM) for a in raw)],
        [
            pltpu.VMEM(neighbours.shape, jnp.int32),
            pltpu.VMEM(diffusion.shape, F32),
            pltpu.SemaphoreType.DMA((3 + n_group,)),
        ],
        where=HBM,
    )
    inner = paired(framing)
    outer = outward(framing)
    gas_pieces = exchanged(gas_cuts)

    (
        kept, sent, kept_cos, sent_cos, slot_of,
        lw_one, lw_shift, lw_two, lw_heads, lw_reach,
        sw_one, sw_shift, sw_two, sw_heads, sw_reach, flux,
    ) = call(
        prepare_body,
        [
            shaped((cols, half), BF16),
            shaped((cols, half), BF16),
            shaped((SUBS, half), F32),
            shaped((2 * SUBS, half), BF16),
            shaped((SUBS, cols), jnp.int32),
            shaped(lw_first.shape[::-1], BF16),
            shaped((hid, LANES), F32),
            shaped(lw_second.shape[::-1], BF16),
            shaped((2 * lw_gpts, 2 * hid), BF16),
            shaped((2 * SUBS, LANES), F32),
            shaped(sw_first.shape[::-1], BF16),
            shaped((hid, LANES), F32),
            shaped(sw_second.shape[::-1], BF16),
            shaped((sw_gpts, 2 * hid), BF16),
            shaped((2 * SUBS, LANES), F32),
            shaped((sw_gpts, LANES), F32),
        ],
        [
            day_count, listing, zenith,
            lw_first, lw_bias[None], lw_second, lw_depth, lw_fraction,
            sw_first, sw_bias[None], sw_second, sw_depth, solar_flux[None],
        ],
        after=framing,
    )

    third, *warm_cuts = call(
        sections_body,
        [shaped((slab, tile + 2 * HW), F32)] + [shaped((slab, cols), BF16)] * n_group,
        [me, place, outer, inner, potential, neighbours, diffusion],
        [pltpu.VMEM((slab, 3 * tile), F32)] * 3
        + [pltpu.VMEM((3, *neighbours.shape), jnp.int32), pltpu.VMEM((3, *diffusion.shape), F32)],
        flops=10_000_000,
    )
    warm_pieces = exchanged(warm_cuts)
    (closed,) = call(
        closing_body, [shaped((slab, tile), F32)], [third, neighbours, diffusion], flops=2_000_000
    )

    cells = levels * SUBS
    packed, out_x, kept_x = call(
        functools.partial(join_body, n_group),
        [
            shaped((cols // LANES, cells, LANES), F32),
            shaped((cells + 2 * SUBS, half), BF16),
            shaped((cells, half), F32),
        ],
        [me, *gas_pieces, *warm_pieces, kept, sent, sent_cos],
        [pltpu.VMEM((SUBS * slab, LANES), F32)],
    )
    in_x = paired(out_x)

    def longwave(which):
        (heat,) = call(
            functools.partial(longwave_body, which),
            [shaped((levels, half), F32)],
            [packed, lw_one, lw_shift, lw_two, lw_heads, lw_reach],
            sweep_scratch(hid, 2 * lw_gpts, lw_gpts, levels, 8),
            flops=4 * levels * half * hid * lw_gpts,
            trans=5 * levels * half * lw_gpts,
            after=work if which else None,
        )
        return heat

    long_first = longwave(0)
    (work,) = call(
        shortwave_body,
        [shaped((levels, half), F32)],
        [day_count, kept_x, kept_cos, in_x, sw_one, sw_shift, sw_two, sw_heads, sw_reach, flux],
        [pltpu.VMEM((cells, half), F32)] + sweep_scratch(hid, sw_gpts, sw_gpts, levels),
        flops=2 * levels * half * hid * sw_gpts,
        trans=3 * levels * half * sw_gpts,
        after=long_first,
    )
    partner = paired(work)
    long_last = longwave(1)
    heat_cuts = call(
        finish_body,
        [shaped((slab, cols), F32)] * n_group,
        [me, day_count, long_first, long_last, work, partner, slot_of],
        [pltpu.VMEM((levels, cols), F32)],
    )
    heat_pieces = exchanged(heat_cuts)
    (evolved,) = call(add_body, [shaped((slab, tile), F32)], [me, closed, *heat_pieces])
    return evolved


def solution(mesh):
    return jax.shard_map(
        per_device,
        mesh=mesh,
        in_specs=(
            P("group", "tile"),
            P(None, "group", "tile"),
            P(None, "tile"),
            P(None, "tile"),
            P("group", "tile", None),
            P("group", "tile"),
            P("group", "tile", None),
            *([P()] * 10),
        ),
        out_specs=P("group", "tile"),
        check_vma=False,
    )
```

```python
import functools
import math

import jax
import jax.numpy as jnp
from jax import lax
from jax.experimental import pallas as pl
from jax.experimental.pallas import tpu as pltpu
from jax.sharding import PartitionSpec as P

HW = 256
LANES = 128
SUBS = 8

depth_scale = 0.1
heat_scale = 12.0
LOG2E = 1.4426950408889634
LN2 = 0.6931471805599453
SAFE = 120.0

F32 = jnp.float32
BF16 = jnp.bfloat16
VMEM = pl.BlockSpec(memory_space=pltpu.VMEM)
ANY = pl.BlockSpec(memory_space=pl.ANY)
HBM = pl.BlockSpec(memory_space=pltpu.HBM)
SMEM = pl.BlockSpec(memory_space=pltpu.SMEM)
PARAMS = pltpu.CompilerParams(vmem_limit_bytes=48 * 1024 * 1024)


def call(body, outs, ins, scratch=(), flops=0, trans=0, after=None, where=VMEM):
    in_specs = [SMEM if a.size == 1 else where for a in ins]
    if after is not None:
        whole, ins = body, [after, *ins]
        in_specs = [ANY, *in_specs]

        def body(_, *refs):
            whole(*refs)

    return pl.pallas_call(
        body,
        out_shape=outs,
        in_specs=in_specs,
        out_specs=[VMEM for _ in outs],
        scratch_shapes=list(scratch),
        compiler_params=PARAMS,
        cost_estimate=pl.CostEstimate(
            flops=flops,
            transcendentals=trans,
            bytes_accessed=sum(a.size * a.dtype.itemsize for a in list(ins) + list(outs)),
        ),
    )(*ins)


def shaped(shape, dtype):
    return jax.ShapeDtypeStruct(shape, dtype)


def iota(shape, dim):
    return lax.broadcasted_iota(jnp.int32, shape, dim)


def mm(a, b):
    return jnp.dot(a, b, preferred_element_type=F32)


def rounds(n):
    if n == 4:
        return [
            {1: 2, 2: 1},
            {2: 0, 1: 3},
            {0: 3, 3: 0},
            {3: 2, 0: 1},
            {3: 1, 1: 0, 0: 2, 2: 3},
        ]
    return [{i: (i + by) % n for i in range(n)} for by in range(1, n)]


def looked_up(me, table, n):
    value = jnp.int32(-1)
    for i in range(n):
        value = jnp.where(me == i, jnp.int32(table.get(i, -1)), value)
    return value


def goals(me, n):
    found = [looked_up(me[0], table, n) for table in rounds(n)]
    return [me[0], *(jnp.where(f < 0, me[0], f) for f in found)]


def origins(me, n):
    return [me[0], *(looked_up(me[0], {g: s for s, g in t.items()}, n) for t in rounds(n))]


def lane_take(x, idx):
    return jnp.take_along_axis(x, idx, axis=1, mode="promise_in_bounds")


def diffused(src, src_at, table, weight, within, at):
    reach = HW // LANES
    wide = 2 * reach + 1
    rows = src.shape[0]
    groups = range(0, rows, SUBS)
    base = at - src_at
    middle = [src[r : r + SUBS, base : base + LANES] for r in groups]
    total = [jnp.zeros_like(m) for m in middle]
    for k in range(table.shape[0]):
        place = jnp.broadcast_to(table[k : k + 1, within : within + LANES], (SUBS, LANES)) - within
        lane = place & (LANES - 1)
        which = place >> (LANES.bit_length() - 1)
        factor = jnp.broadcast_to(weight[k : k + 1, within : within + LANES], (SUBS, LANES))
        tests = [which == w for w in range(1, wide)]
        for n, r in enumerate(groups):
            near = None
            for w in range(wide):
                lo = base + (w - reach) * LANES
                got = lane_take(src[r : r + SUBS, lo : lo + LANES], lane)
                near = got if w == 0 else jnp.where(tests[w - 1], got, near)
            total[n] = total[n] + factor * (near - middle[n])
    return [(r, m, m + t) for r, m, t in zip(groups, middle, total)]


def pack_body(n_group, me, own, table, weight, species, out, *rest):
    pieces, (table_here, weight_here, sems) = rest[:-3], rest[-3:]
    slab = own.shape[0]
    near = table.shape[0]
    cols = pieces[0].shape[2]
    moves = [
        pltpu.make_async_copy(own, out.at[0:slab], sems.at[0]),
        pltpu.make_async_copy(table, table_here, sems.at[1]),
        pltpu.make_async_copy(weight, weight_here, sems.at[2]),
    ]
    for goal, piece in zip(goals(me, n_group), pieces):
        at = pl.ds(pl.multiple_of(goal * cols, LANES), cols)
        moves.append(pltpu.make_async_copy(species.at[:, :, at], piece, sems.at[len(moves)]))
    for move in moves:
        move.start()
    for move in moves:
        move.wait()
    out[slab : slab + near, :] = table_here[...].astype(F32)
    out[slab + near :, :] = weight_here[...]


def sections_body(
    n_group, me, place, outer, inner, own, table, weight, third_out, *rest
):
    pieces, (frame, first, second, tables, weights) = rest[:-5], rest[-5:]
    slab, tile = own.shape
    near = table.shape[0]
    cols = tile // n_group
    odd = place[0] & 1
    for side, packed in ((odd, outer), (1 - odd, inner)):
        at = pl.ds(pl.multiple_of(side * (2 * tile), LANES), tile)
        frame[:, at] = packed[0:slab, :]
        tables[side * 2] = packed[slab : slab + near, :].astype(jnp.int32)
        weights[side * 2] = packed[slab + near : slab + 2 * near, :]
    frame[:, tile : 2 * tile] = own[...]
    tables[1] = table[...]
    weights[1] = weight[...]

    def run(src, src_at, halo, put):
        for at in range(tile - halo, 2 * tile + halo, LANES):
            t = at // tile
            for r, _, value in diffused(src, src_at, tables.at[t], weights.at[t], at - t * tile, at):
                put(r, at, value)

    def put_first(r, at, value):
        first[r : r + SUBS, at : at + LANES] = value

    def put_second(r, at, value):
        start = frame[r : r + SUBS, at : at + LANES]
        second[r : r + SUBS, at : at + LANES] = 0.75 * start + 0.25 * value

    def put_third(r, at, value):
        start = frame[r : r + SUBS, at : at + LANES]
        lo = at - tile + HW
        third_out[r : r + SUBS, lo : lo + LANES] = start / 3.0 + (2.0 / 3.0) * value

    run(frame, 0, 3 * HW, put_first)
    run(first, 0, 2 * HW, put_second)
    run(second, 0, HW, put_third)
    for goal, out in zip(goals(me, n_group), pieces):
        lo = pl.multiple_of(HW + goal * cols, LANES)
        out[...] = third_out[:, pl.ds(lo, cols)].astype(BF16)


def closing_body(third, table, weight, out):
    tile = out.shape[1]
    for at in range(0, tile, LANES):
        for r, _, value in diffused(third, -HW, table, weight, at, at):
            out[r : r + SUBS, at : at + LANES] = value


def turned_over(matrix):
    return matrix.astype(F32).T


def head_parts(weight, out, at):
    hid, gpts = weight.shape
    scaled = LOG2E * turned_over(weight[...])
    high = scaled.astype(BF16)
    out[at : at + gpts, 0:hid] = high
    out[at : at + gpts, hid:] = (scaled - high.astype(F32)).astype(BF16)


def reach_of(heads):
    sums = mm(jnp.abs(heads[...]), jnp.ones((heads.shape[1], LANES), BF16))
    return jnp.broadcast_to(jnp.max(sums, axis=0, keepdims=True), (2 * SUBS, LANES))


def prepare_body(
    count, listing, zenith, w1, b1, w2, wd, wf, v1, c1, v2, vd, flux,
    kept_out, sent_out, kept_cos, sent_cos, slot_of,
    w1_out, b1_out, w2_out, heads_out, reach_out, v1_out, c1_out, v2_out, vd_out, vreach_out, flux_out,
):
    for weight, out in ((w1, w1_out), (w2, w2_out), (v1, v1_out), (v2, v2_out)):
        out[...] = (0.5 * turned_over(weight[...])).astype(BF16)
    head_parts(wd, heads_out, 0)
    head_parts(wf, heads_out, wd.shape[1])
    head_parts(vd, vd_out, 0)
    reach_out[...] = reach_of(heads_out)
    vreach_out[...] = reach_of(vd_out)
    for row, out, scale in ((b1, b1_out, 0.5), (c1, c1_out, 0.5), (flux, flux_out, 1.0)):
        out[...] = scale * jnp.broadcast_to(row[...], (LANES, row.shape[1])).T
    cols = listing.shape[-1]
    half = cols // 2
    sunlit = count[0, 0]
    label = iota((cols, half), 0)
    slot = iota((cols, half), 1)
    first = jnp.broadcast_to(listing[0, :, 0:half], (cols, half)) == label
    last = jnp.broadcast_to(listing[0, :, half:cols], (cols, half)) == label
    kept = jnp.where(first & (slot < sunlit), 1.0, 0.0).astype(BF16)
    sent = jnp.where(last & (slot + half < sunlit), 1.0, 0.0).astype(BF16)
    kept_out[...] = kept
    sent_out[...] = sent
    cosine = jnp.broadcast_to(zenith[0].astype(F32), (2 * SUBS, cols)).astype(BF16)
    sent_cos[...] = mm(cosine, sent).astype(BF16)
    kept_cos[...] = mm(cosine, kept)[0:SUBS]
    hits = jnp.where(jnp.concatenate([first, last], axis=1), 1.0, 0.0).astype(BF16)
    numbers = iota((2 * SUBS, cols), 1).astype(F32).astype(BF16)
    found = lax.dot_general(numbers, hits, (((1,), (1,)), ((), ())), preferred_element_type=F32)
    slot_of[...] = found[0:SUBS].astype(jnp.int32)


def join_body(n_group, me, *rest):
    kept, sent, sent_cos, packed, outgoing, kept_x, spread = rest[-7:]
    count = (len(rest) - 7) // 2
    gases, warms = rest[:count], rest[count : 2 * count]
    slab = warms[0].shape[0]
    def place(source, gas, warm):
        for h in range(packed.shape[0]):
            at = slice(h * LANES, (h + 1) * LANES)
            spread[0:slab, :] = warm[:, at].astype(F32)
            for f in range(gas.shape[0]):
                spread[(f + 1) * slab : (f + 2) * slab, :] = gas[f, :, at].astype(F32)
            for l in range(slab):
                row = pl.multiple_of((source * slab + l) * SUBS, SUBS)
                packed[h, pl.ds(row, SUBS), :] = spread[pl.ds(l, SUBS, stride=slab), :]

    for source, gas, warm in zip(origins(me, n_group), gases, warms):
        pl.when(source >= 0)(functools.partial(place, jnp.maximum(source, 0), gas, warm))
    cells = packed.shape[1]
    first, last = packed[0].astype(BF16), packed[1].astype(BF16)
    outgoing[0:cells, :] = (mm(first, sent[0:LANES]) + mm(last, sent[LANES:])).astype(BF16)
    outgoing[cells:, :] = sent_cos[...]
    kept_x[...] = mm(first, kept[0:LANES]) + mm(last, kept[LANES:])


def softplus2(z):
    return lax.log2(1.0 + jnp.exp2(z))


def softplus2_guarded(z):
    return jnp.maximum(z, softplus2(jnp.minimum(z, SAFE)))


def power(y):
    value = 1.0
    terms = [LN2**k / math.factorial(k) for k in range(7)]
    value = terms[6]
    for term in terms[5::-1]:
        value = value * y + term
    for _ in range(4):
        value = value * value
    return value


def silu_of_half(v):
    half = v.astype(BF16)
    return half + half * jnp.tanh(half)


def sweep(x, first, bias, second, heads, reach, start, gpts, rate, both, buffers, form):
    ones, hids, zs, trans, parts, peak = buffers
    step_levels = zs.shape[2] // LANES
    one_a, one_b = ones.at[0], ones.at[1]
    hid_a, hid_b = hids.at[0], hids.at[1]
    z_a, z_b = zs.at[0], zs.at[1]
    levels = x.shape[0] // SUBS
    steps = levels // step_levels
    wide = step_levels * LANES
    rows = heads.shape[0]
    col_cut = 2 * LANES
    chunk = SUBS
    units = first.shape[0]
    unit_cut = units

    def first_tasks(t, out):
        def task(r):
            row = jnp.minimum(t, steps - 1) * (step_levels * SUBS)
            tiles = [
                x[pl.ds(pl.multiple_of(row + i * SUBS, SUBS), SUBS), :] for i in range(step_levels)
            ]
            v = mm(first[r : r + unit_cut, :], jnp.concatenate(tiles, axis=1).astype(BF16))
            v = v + jnp.concatenate([bias[r : r + unit_cut, :]] * step_levels, axis=1)
            out[r : r + unit_cut, :] = silu_of_half(v)

        return [functools.partial(task, r) for r in range(0, units, unit_cut)]

    def second_tasks(one, out):
        def task(r):
            v = mm(second[r : r + unit_cut, :], one[...])
            value = silu_of_half(v)
            out[r : r + unit_cut, :] = value
            out[units + r : units + r + unit_cut, :] = value
            most = peak[...]
            for i in range(0, unit_cut, 2 * SUBS):
                for at in range(0, wide, LANES):
                    most = jnp.maximum(most, value[i : i + 2 * SUBS, at : at + LANES])
            peak[...] = most

        return [functools.partial(task, r) for r in range(0, units, unit_cut)]

    def optics_tasks(hid, out):
        def task(lo):
            at = slice(lo, lo + col_cut)
            out[:, at] = mm(heads[...], hid[:, at])

        return [functools.partial(task, lo) for lo in range(0, wide, col_cut)]

    def consume_tasks(z, total):
        def product(lo):
            return z[lo : lo + chunk, :]

        def task(lo):
            carry = trans[lo : lo + chunk, :]
            depth = product(lo)
            share = product(gpts + lo) if both else None
            for i in range(step_levels):
                at = slice(i * LANES, (i + 1) * LANES)
                depths = softplus2(depth[:, at])
                if form == 1:
                    following = carry * power(depths * (rate / 16.0))
                else:
                    following = carry * jnp.exp2(depths * rate)
                term = following
                if both:
                    term = (carry - following) * softplus2(share[:, at])
                for r in range(0, chunk, SUBS):
                    part = term[r : r + SUBS]
                    total[i] = part if total[i] is None else total[i] + part
                carry = following
            trans[lo : lo + chunk, :] = carry

        return [functools.partial(task, lo) for lo in range(0, gpts, chunk)]

    def woven(main, side):
        done = 0
        for n, task in enumerate(main):
            while done < len(side) and done * len(main) <= n * len(side):
                side[done]()
                done += 1
            task()
        for task in side[done:]:
            task()

    def plain(tasks):
        for task in tasks:
            task()

    def run():
        trans[...] = start
        if not both:
            parts[0:SUBS, :] = jnp.sum(start.reshape(gpts // SUBS, SUBS, LANES), axis=0)

        def step(t, z, z_next, hid_next, hid_later, one_later, one_last):
            total = [None] * step_levels
            side = second_tasks(one_later, hid_later) + first_tasks(t + 3, one_last)
            woven(consume_tasks(z, total), optics_tasks(hid_next, z_next) + side)
            for i in range(step_levels):
                at = pl.multiple_of((t * step_levels + i + 1) * SUBS, SUBS)
                parts[pl.ds(at, SUBS), :] = total[i]

        def two(i, _):
            most = jnp.max(peak[...].astype(F32) * reach[...])
            step(2 * i, z_a, z_b, hid_b, hid_a, one_a, one_b)
            step(2 * i + 1, z_b, z_a, hid_a, hid_b, one_b, one_a)
            return most

        plain(first_tasks(0, one_a))
        plain(second_tasks(one_a, hid_a))
        plain(first_tasks(1, one_b))
        plain(optics_tasks(hid_a, z_a))
        plain(second_tasks(one_b, hid_b))
        plain(first_tasks(2, one_a))
        return lax.fori_loop(0, steps // 2, two, jnp.float32(0.0))

    def run_guarded():
        trans[...] = start
        at = slice(0, LANES)

        def level(l, _):
            tile = x[pl.ds(pl.multiple_of(l * SUBS, SUBS), SUBS), :].astype(BF16)
            hidden = silu_of_half(mm(first[...], tile) + bias[...])
            hidden = silu_of_half(mm(second[...], hidden))
            z_a[:, at] = mm(heads[...], jnp.concatenate([hidden, hidden], axis=0))

            def piece(c, total):
                lo = pl.multiple_of(c * SUBS, SUBS)
                carry = trans[pl.ds(lo, SUBS), :]
                depth = softplus2_guarded(z_a[pl.ds(lo, SUBS), at])
                following = carry * jnp.exp2(depth * rate)
                trans[pl.ds(lo, SUBS), :] = following
                if not both:
                    return total + following
                share = softplus2_guarded(z_a[pl.ds(pl.multiple_of(gpts + lo, SUBS), SUBS), at])
                return total + (carry - following) * share

            total = lax.fori_loop(0, gpts // SUBS, piece, jnp.zeros((SUBS, LANES), F32))
            parts[pl.ds(pl.multiple_of((l + 1) * SUBS, SUBS), SUBS), :] = total
            return 0

        lax.fori_loop(0, levels, level, 0)

    peak[...] = jnp.ones_like(peak)
    most = run()
    pl.when(most > SAFE)(run_guarded)
    emitted = None
    for s in range(SUBS):
        part = parts[pl.ds(s + SUBS, levels, stride=SUBS), :]
        if not both:
            part = parts[pl.ds(s, levels, stride=SUBS), :] - part
        emitted = part if emitted is None else emitted + part
    return emitted


def sweep_scratch(hid, rows, gpts, levels, step_levels=4):
    wide = step_levels * LANES
    return [
        pltpu.VMEM((2, hid, wide), BF16),
        pltpu.VMEM((2, 2 * hid, wide), BF16),
        pltpu.VMEM((2, rows, wide), F32),
        pltpu.VMEM((gpts, LANES), F32),
        pltpu.VMEM(((levels + 1) * SUBS, LANES), F32),
        pltpu.VMEM((2 * SUBS, LANES), BF16),
    ]


def longwave_body(which, packed, first, bias, second, heads, reach, out, *buffers):
    gpts = heads.shape[0] // 2
    levels = out.shape[0]
    x = packed.at[which]
    emitted = sweep(
        x, first, bias, second, heads, reach, jnp.ones((gpts, LANES), F32), gpts,
        -depth_scale, True, buffers, 1 - which,
    )
    planck = jnp.exp(0.25 * x[pl.ds(0, levels, stride=SUBS), :])
    out[...] = -(heat_scale * LN2 / gpts) * planck * emitted


def shortwave_body(
    count, kept_x, kept_cos, in_x, first, bias, second, heads, reach, flux, out, work_x, *buffers
):
    cells, half = kept_x.shape
    gpts = heads.shape[0]
    slot = iota((half, half), 1) - count[0, 0]
    placed = jnp.where(slot == iota((half, half), 0), 1.0, 0.0).astype(BF16)
    work_x[...] = kept_x[...] + mm(in_x[0:cells, :], placed)
    cosine = kept_cos[...] + mm(in_x[cells:, :], placed)[0:SUBS]
    cosine = jnp.where(cosine > 0.0, cosine, 1.0)
    emitted = sweep(
        work_x, first, bias, second, heads, reach, flux[...], gpts,
        -depth_scale / cosine, False, buffers, 0,
    )
    out[...] = (heat_scale / gpts) * cosine[0:1] * emitted


def finish_body(n_group, me, count, long_first, long_last, work, partner, slot_of, *rest):
    pieces, heat = rest[:-1], rest[-1]
    levels, cols = heat.shape
    half = cols // 2
    slab = pieces[0].shape[0]
    sunlit = count[0, 0]
    for lo, long in ((0, long_first), (half, long_last)):
        slot = slot_of[:, lo : lo + half]
        here = slot < half
        place = jnp.where(here, slot, slot + half - sunlit) & (half - 1)
        lit = slot < sunlit
        for r in range(0, levels, SUBS):
            near = lane_take(work[r : r + SUBS, :], place)
            far = lane_take(partner[r : r + SUBS, :], place)
            short = jnp.where(lit, jnp.where(here, near, far), 0.0)
            heat[r : r + SUBS, lo : lo + half] = long[r : r + SUBS, :] + short
    for goal, out in zip(goals(me, n_group), pieces):
        out[...] = heat[pl.ds(pl.multiple_of(goal * slab, SUBS), slab), :]


def add_body(n_group, me, closed, *rest):
    pieces, out = rest[:-1], rest[-1]
    cols = pieces[0].shape[1]

    def place(source, piece):
        at = pl.ds(pl.multiple_of(source * cols, LANES), cols)
        out[:, at] = closed[:, at] + piece[...]

    for source, piece in zip(origins(me, n_group), pieces):
        pl.when(source >= 0)(functools.partial(place, jnp.maximum(source, 0), piece))


def per_device(
    potential, species, diffusion, neighbours, listing, day_count, zenith,
    lw_first, lw_bias, lw_second, lw_depth, lw_fraction,
    sw_first, sw_bias, sw_second, sw_depth, solar_flux,
):
    n_group = lax.axis_size("group")
    n_tile = lax.axis_size("tile")
    assert n_tile % 2 == 0
    n_pieces = 1 + len(rounds(n_group))
    me = lax.axis_index("group").astype(jnp.int32).reshape(1)
    place = lax.axis_index("tile").astype(jnp.int32).reshape(1)
    slab, tile = potential.shape
    gases = species.shape[0]
    cols = tile // n_group
    half = cols // 2
    levels = slab * n_group
    hid = lw_first.shape[1]
    lw_gpts = lw_depth.shape[1]
    sw_gpts = sw_depth.shape[1]

    def outward(value):
        across = [(i, (i + 1 if i % 2 else i - 1) % n_tile) for i in range(n_tile)]
        return lax.ppermute(value, "tile", across)

    def paired(value):
        return lax.ppermute(value, "tile", [(i, i ^ 1) for i in range(n_tile)])

    def exchanged(pieces):
        moved = [lax.ppermute(p, "group", list(t.items())) for p, t in zip(pieces[1:], rounds(n_group))]
        return [pieces[0], *moved]

    near = neighbours.shape[0]
    raw = (potential, neighbours, diffusion, species)
    framing, *gas_cuts = call(
        functools.partial(pack_body, n_group),
        [shaped((slab + 2 * near, tile), F32)] + [shaped((gases, slab, cols), BF16)] * n_pieces,
        [me, *(pltpu.with_memory_space_constraint(a, pltpu.HBM) for a in raw)],
        [
            pltpu.VMEM(neighbours.shape, jnp.int32),
            pltpu.VMEM(diffusion.shape, F32),
            pltpu.SemaphoreType.DMA((3 + n_pieces,)),
        ],
        where=HBM,
    )
    inner = paired(framing)
    outer = outward(framing)
    gas_pieces = exchanged(gas_cuts)

    (
        kept, sent, kept_cos, sent_cos, slot_of,
        lw_one, lw_shift, lw_two, lw_heads, lw_reach,
        sw_one, sw_shift, sw_two, sw_heads, sw_reach, flux,
    ) = call(
        prepare_body,
        [
            shaped((cols, half), BF16),
            shaped((cols, half), BF16),
            shaped((SUBS, half), F32),
            shaped((2 * SUBS, half), BF16),
            shaped((SUBS, cols), jnp.int32),
            shaped(lw_first.shape[::-1], BF16),
            shaped((hid, LANES), F32),
            shaped(lw_second.shape[::-1], BF16),
            shaped((2 * lw_gpts, 2 * hid), BF16),
            shaped((2 * SUBS, LANES), F32),
            shaped(sw_first.shape[::-1], BF16),
            shaped((hid, LANES), F32),
            shaped(sw_second.shape[::-1], BF16),
            shaped((sw_gpts, 2 * hid), BF16),
            shaped((2 * SUBS, LANES), F32),
            shaped((sw_gpts, LANES), F32),
        ],
        [
            day_count, listing, zenith,
            lw_first, lw_bias[None], lw_second, lw_depth, lw_fraction,
            sw_first, sw_bias[None], sw_second, sw_depth, solar_flux[None],
        ],
        after=framing,
    )

    third, *warm_cuts = call(
        functools.partial(sections_body, n_group),
        [shaped((slab, tile + 2 * HW), F32)] + [shaped((slab, cols), BF16)] * n_pieces,
        [me, place, outer, inner, potential, neighbours, diffusion],
        [pltpu.VMEM((slab, 3 * tile), F32)] * 3
        + [pltpu.VMEM((3, *neighbours.shape), jnp.int32), pltpu.VMEM((3, *diffusion.shape), F32)],
        flops=10_000_000,
    )
    warm_pieces = exchanged(warm_cuts)
    (closed,) = call(
        closing_body, [shaped((slab, tile), F32)], [third, neighbours, diffusion], flops=2_000_000
    )

    cells = levels * SUBS
    packed, out_x, kept_x = call(
        functools.partial(join_body, n_group),
        [
            shaped((cols // LANES, cells, LANES), F32),
            shaped((cells + 2 * SUBS, half), BF16),
            shaped((cells, half), F32),
        ],
        [me, *gas_pieces, *warm_pieces, kept, sent, sent_cos],
        [pltpu.VMEM((SUBS * slab, LANES), F32)],
    )
    in_x = paired(out_x)

    def longwave(which):
        (heat,) = call(
            functools.partial(longwave_body, which),
            [shaped((levels, half), F32)],
            [packed, lw_one, lw_shift, lw_two, lw_heads, lw_reach],
            sweep_scratch(hid, 2 * lw_gpts, lw_gpts, levels, 8),
            flops=4 * levels * half * hid * lw_gpts,
            trans=5 * levels * half * lw_gpts,
            after=work if which else None,
        )
        return heat

    long_first = longwave(0)
    (work,) = call(
        shortwave_body,
        [shaped((levels, half), F32)],
        [day_count, kept_x, kept_cos, in_x, sw_one, sw_shift, sw_two, sw_heads, sw_reach, flux],
        [pltpu.VMEM((cells, half), F32)] + sweep_scratch(hid, sw_gpts, sw_gpts, levels),
        flops=2 * levels * half * hid * sw_gpts,
        trans=3 * levels * half * sw_gpts,
        after=long_first,
    )
    partner = paired(work)
    long_last = longwave(1)
    heat_cuts = call(
        functools.partial(finish_body, n_group),
        [shaped((slab, cols), F32)] * n_pieces,
        [me, day_count, long_first, long_last, work, partner, slot_of],
        [pltpu.VMEM((levels, cols), F32)],
    )
    heat_pieces = exchanged(heat_cuts)
    (evolved,) = call(
        functools.partial(add_body, n_group), [shaped((slab, tile), F32)], [me, closed, *heat_pieces]
    )
    return evolved


def solution(mesh):
    return jax.shard_map(
        per_device,
        mesh=mesh,
        in_specs=(
            P("group", "tile"),
            P(None, "group", "tile"),
            P(None, "tile"),
            P(None, "tile"),
            P("group", "tile", None),
            P("group", "tile"),
            P("group", "tile", None),
            *([P()] * 10),
        ),
        out_specs=P("group", "tile"),
        check_vma=False,
    )
```

```python
import functools
import math

import jax
import jax.numpy as jnp
from jax import lax
from jax.experimental import pallas as pl
from jax.experimental.pallas import tpu as pltpu
from jax.sharding import PartitionSpec as P

HW = 256
LANES = 128
SUBS = 8

depth_scale = 0.1
heat_scale = 12.0
LOG2E = 1.4426950408889634
LN2 = 0.6931471805599453
SAFE = 120.0

F32 = jnp.float32
BF16 = jnp.bfloat16
VMEM = pl.BlockSpec(memory_space=pltpu.VMEM)
ANY = pl.BlockSpec(memory_space=pl.ANY)
HBM = pl.BlockSpec(memory_space=pltpu.HBM)
SMEM = pl.BlockSpec(memory_space=pltpu.SMEM)
PARAMS = pltpu.CompilerParams(vmem_limit_bytes=48 * 1024 * 1024)


def call(body, outs, ins, scratch=(), flops=0, trans=0, after=None, where=VMEM):
    in_specs = [SMEM if a.size == 1 else where for a in ins]
    if after is not None:
        whole, ins = body, [after, *ins]
        in_specs = [ANY, *in_specs]

        def body(_, *refs):
            whole(*refs)

    return pl.pallas_call(
        body,
        out_shape=outs,
        in_specs=in_specs,
        out_specs=[VMEM for _ in outs],
        scratch_shapes=list(scratch),
        compiler_params=PARAMS,
        cost_estimate=pl.CostEstimate(
            flops=flops,
            transcendentals=trans,
            bytes_accessed=sum(a.size * a.dtype.itemsize for a in list(ins) + list(outs)),
        ),
    )(*ins)


def shaped(shape, dtype):
    return jax.ShapeDtypeStruct(shape, dtype)


def iota(shape, dim):
    return lax.broadcasted_iota(jnp.int32, shape, dim)


def mm(a, b):
    return jnp.dot(a, b, preferred_element_type=F32)


def far_first(n):
    return [0, *range(n - 1, 0, -1)]


def partners(me, pieces):
    return [(me[0] ^ bit, piece) for bit, piece in zip(far_first(len(pieces)), pieces)]


def lane_take(x, idx):
    return jnp.take_along_axis(x, idx, axis=1, mode="promise_in_bounds")


def diffused(src, src_at, table, weight, within, at):
    reach = HW // LANES
    wide = 2 * reach + 1
    rows = src.shape[0]
    groups = range(0, rows, SUBS)
    base = at - src_at
    middle = [src[r : r + SUBS, base : base + LANES] for r in groups]
    total = [jnp.zeros_like(m) for m in middle]
    for k in range(table.shape[0]):
        place = jnp.broadcast_to(table[k : k + 1, within : within + LANES], (SUBS, LANES)) - within
        lane = place & (LANES - 1)
        which = place >> (LANES.bit_length() - 1)
        factor = jnp.broadcast_to(weight[k : k + 1, within : within + LANES], (SUBS, LANES))
        tests = [which == w for w in range(1, wide)]
        for n, r in enumerate(groups):
            near = None
            for w in range(wide):
                lo = base + (w - reach) * LANES
                got = lane_take(src[r : r + SUBS, lo : lo + LANES], lane)
                near = got if w == 0 else jnp.where(tests[w - 1], got, near)
            total[n] = total[n] + factor * (near - middle[n])
    return [(r, m, m + t) for r, m, t in zip(groups, middle, total)]


def pack_body(me, own, table, weight, species, out, *rest):
    pieces, (table_here, weight_here, sems) = rest[:-3], rest[-3:]
    slab = own.shape[0]
    near = table.shape[0]
    cols = pieces[0].shape[2]
    moves = [
        pltpu.make_async_copy(own, out.at[0:slab], sems.at[0]),
        pltpu.make_async_copy(table, table_here, sems.at[1]),
        pltpu.make_async_copy(weight, weight_here, sems.at[2]),
    ]
    for source, piece in partners(me, pieces):
        at = pl.ds(pl.multiple_of(source * cols, LANES), cols)
        moves.append(pltpu.make_async_copy(species.at[:, :, at], piece, sems.at[len(moves)]))
    for move in moves:
        move.start()
    for move in moves:
        move.wait()
    out[slab : slab + near, :] = table_here[...].astype(F32)
    out[slab + near :, :] = weight_here[...]


def sections_body(
    me, place, outer, inner, own, table, weight, third_out, *rest
):
    pieces, (frame, first, second, tables, weights) = rest[:-5], rest[-5:]
    slab, tile = own.shape
    near = table.shape[0]
    cols = tile // len(pieces)
    odd = place[0] & 1
    for side, packed in ((odd, outer), (1 - odd, inner)):
        at = pl.ds(pl.multiple_of(side * (2 * tile), LANES), tile)
        frame[:, at] = packed[0:slab, :]
        tables[side * 2] = packed[slab : slab + near, :].astype(jnp.int32)
        weights[side * 2] = packed[slab + near : slab + 2 * near, :]
    frame[:, tile : 2 * tile] = own[...]
    tables[1] = table[...]
    weights[1] = weight[...]

    def run(src, src_at, halo, put):
        for at in range(tile - halo, 2 * tile + halo, LANES):
            t = at // tile
            for r, _, value in diffused(src, src_at, tables.at[t], weights.at[t], at - t * tile, at):
                put(r, at, value)

    def put_first(r, at, value):
        first[r : r + SUBS, at : at + LANES] = value

    def put_second(r, at, value):
        start = frame[r : r + SUBS, at : at + LANES]
        second[r : r + SUBS, at : at + LANES] = 0.75 * start + 0.25 * value

    def put_third(r, at, value):
        start = frame[r : r + SUBS, at : at + LANES]
        lo = at - tile + HW
        third_out[r : r + SUBS, lo : lo + LANES] = start / 3.0 + (2.0 / 3.0) * value

    run(frame, 0, 3 * HW, put_first)
    run(first, 0, 2 * HW, put_second)
    run(second, 0, HW, put_third)
    for goal, out in partners(me, pieces):
        lo = pl.multiple_of(HW + goal * cols, LANES)
        out[...] = third_out[:, pl.ds(lo, cols)].astype(BF16)


def closing_body(third, table, weight, out):
    tile = out.shape[1]
    for at in range(0, tile, LANES):
        for r, _, value in diffused(third, -HW, table, weight, at, at):
            out[r : r + SUBS, at : at + LANES] = value


def turned_over(matrix):
    return matrix.astype(F32).T


def head_parts(weight, out, at):
    hid, gpts = weight.shape
    scaled = LOG2E * turned_over(weight[...])
    high = scaled.astype(BF16)
    out[at : at + gpts, 0:hid] = high
    out[at : at + gpts, hid:] = (scaled - high.astype(F32)).astype(BF16)


def first_parts(weight, bias, out):
    fin = weight.shape[0]
    rows = [(0.5 * weight[...].astype(F32)).astype(BF16).astype(F32)]
    rest = 0.5 * bias[...]
    for _ in range(3):
        part = rest.astype(BF16).astype(F32)
        rows.append(part)
        rest = rest - part
    rows.append(jnp.zeros((fin - 3, weight.shape[1]), F32))
    out[...] = jnp.concatenate(rows, axis=0).T.astype(BF16)


def reach_of(heads):
    sums = mm(jnp.abs(heads[...]), jnp.ones((heads.shape[1], LANES), BF16))
    return jnp.broadcast_to(jnp.max(sums, axis=0, keepdims=True), (2 * SUBS, LANES))


def prepare_body(
    count, listing, zenith, w1, b1, w2, wd, wf, v1, c1, v2, vd, flux,
    kept_out, sent_out, kept_cos, sent_cos, slot_of,
    w1_out, w2_out, heads_out, reach_out, v1_out, v2_out, vd_out, vreach_out, flux_out,
):
    for weight, out in ((w2, w2_out), (v2, v2_out)):
        out[...] = (0.5 * turned_over(weight[...])).astype(BF16)
    first_parts(w1, b1, w1_out)
    first_parts(v1, c1, v1_out)
    head_parts(wd, heads_out, 0)
    head_parts(wf, heads_out, wd.shape[1])
    head_parts(vd, vd_out, 0)
    reach_out[...] = reach_of(heads_out)
    vreach_out[...] = reach_of(vd_out)
    flux_out[...] = jnp.broadcast_to(flux[...], (LANES, flux.shape[1])).T
    cols = listing.shape[-1]
    half = cols // 2
    sunlit = count[0, 0]
    label = iota((cols, half), 0)
    slot = iota((cols, half), 1)
    first = jnp.broadcast_to(listing[0, :, 0:half], (cols, half)) == label
    last = jnp.broadcast_to(listing[0, :, half:cols], (cols, half)) == label
    kept = jnp.where(first & (slot < sunlit), 1.0, 0.0).astype(BF16)
    sent = jnp.where(last & (slot + half < sunlit), 1.0, 0.0).astype(BF16)
    kept_out[...] = kept
    sent_out[...] = sent
    cosine = jnp.broadcast_to(zenith[0].astype(F32), (2 * SUBS, cols)).astype(BF16)
    sent_cos[...] = mm(cosine, sent).astype(BF16)
    kept_cos[...] = mm(cosine, kept)[0:SUBS]
    hits = jnp.where(jnp.concatenate([first, last], axis=1), 1.0, 0.0).astype(BF16)
    numbers = iota((2 * SUBS, cols), 1).astype(F32).astype(BF16)
    found = lax.dot_general(numbers, hits, (((1,), (1,)), ((), ())), preferred_element_type=F32)
    slot_of[...] = found[0:SUBS].astype(jnp.int32)


def join_body(n_group, me, *rest):
    gases, warms = rest[:n_group], rest[n_group : 2 * n_group]
    kept, sent, sent_cos, packed, outgoing, kept_x, spread = rest[2 * n_group :]
    slab = warms[0].shape[0]
    for (source, gas), warm in zip(partners(me, gases), warms):
        for h in range(packed.shape[0]):
            at = slice(h * LANES, (h + 1) * LANES)
            spread[0:slab, :] = warm[:, at].astype(F32)
            for f in range(gas.shape[0]):
                spread[(f + 1) * slab : (f + 2) * slab, :] = gas[f, :, at].astype(F32)
            for l in range(slab):
                row = pl.multiple_of((source * slab + l) * SUBS, SUBS)
                packed[h, pl.ds(row, SUBS), :] = spread[pl.ds(l, SUBS, stride=slab), :]
    cells = packed.shape[1]
    first, last = packed[0].astype(BF16), packed[1].astype(BF16)
    outgoing[0:cells, :] = (mm(first, sent[0:LANES]) + mm(last, sent[LANES:])).astype(BF16)
    outgoing[cells:, :] = sent_cos[...]
    kept_x[...] = mm(first, kept[0:LANES]) + mm(last, kept[LANES:])


def softplus2(z):
    return lax.log2(1.0 + jnp.exp2(z))


def softplus2_guarded(z):
    return jnp.maximum(z, softplus2(jnp.minimum(z, SAFE)))


def silu_of_half(v):
    half = v.astype(BF16)
    return half + half * jnp.tanh(half)


def sweep(x, first, second, heads, reach, start, gpts, rate, both, put, buffers):
    ones, hids, zs, (trans, last, peak) = buffers[0:2], buffers[2:4], buffers[4:-3], buffers[-3:]
    lead = len(zs) // 2
    wide = ones[0].shape[1]
    step_levels = wide // LANES
    levels = x.shape[0] // SUBS
    steps = levels // step_levels
    units = first.shape[0]
    sub = iota((SUBS, LANES), 0)

    def fed(tile):
        return jnp.concatenate([tile, jnp.ones_like(tile)], axis=0).astype(BF16)

    def first_tasks(t, out):
        def task():
            row = jnp.minimum(t, steps - 1) * (step_levels * SUBS)
            tiles = [
                x[pl.ds(pl.multiple_of(row + i * SUBS, SUBS), SUBS), :] for i in range(step_levels)
            ]
            out[...] = silu_of_half(mm(first[...], fed(jnp.concatenate(tiles, axis=1))))

        return [task]

    def second_tasks(one, out):
        def task():
            value = silu_of_half(mm(second[...], one[...]))
            out[0:units, :] = value
            out[units:, :] = value
            most = peak[...]
            for i in range(0, units, 2 * SUBS):
                for at in range(0, wide, LANES):
                    most = jnp.maximum(most, value[i : i + 2 * SUBS, at : at + LANES])
            peak[...] = most

        return [task]

    def optics_tasks(hid, out):
        def task():
            out[...] = mm(heads[...], hid[...])

        return [task]

    def consume_tasks(z, total):
        def task(lo):
            carry = trans[lo : lo + SUBS, :]
            for i in range(step_levels):
                at = slice(i * LANES, (i + 1) * LANES)
                following = carry * jnp.exp2(softplus2(z[lo : lo + SUBS, at]) * rate)
                term = following
                if both:
                    term = (carry - following) * softplus2(z[gpts + lo : gpts + lo + SUBS, at])
                total[i] = term if total[i] is None else total[i] + term
                carry = following
            trans[lo : lo + SUBS, :] = carry

        return [functools.partial(task, lo) for lo in range(0, gpts, SUBS)]

    def woven(main, side):
        done = 0
        for n, task in enumerate(main):
            while done < len(side) and done * len(main) <= n * len(side):
                side[done]()
                done += 1
            task()

    def begin():
        trans[...] = start
        if not both:
            sums = jnp.sum(start.reshape(gpts // SUBS, SUBS, LANES), axis=0)
            last[...] = jnp.broadcast_to(jnp.sum(sums, axis=0, keepdims=True), (SUBS, LANES))

    def entered(total, n, before, after):
        row = jnp.broadcast_to(jnp.sum(total, axis=0, keepdims=True), (SUBS, LANES))
        after = jnp.where(sub == n, row, after)
        before = jnp.where(sub == n + 1, row, before)
        return before, after, row

    def put_group(level, before, after, row):
        if both:
            put(level, after)
        else:
            put(level, jnp.where(sub == 0, last[...], before) - after)
            last[...] = row

    def run():
        begin()
        unroll = 2 * SUBS // step_levels

        def several(i, _):
            before = after = jnp.zeros((SUBS, LANES), F32)
            for k in range(unroll):
                t = k + lead
                total = [None] * step_levels
                if k == max(unroll - 1 - lead, 0):
                    most = jnp.max(peak[...].astype(F32) * reach[...])
                side = (
                    optics_tasks(hids[t % 2], zs[t % len(zs)])
                    + second_tasks(ones[(t + 1) % 2], hids[(t + 1) % 2])
                    + first_tasks(i * unroll + t + 2, ones[t % 2])
                )
                woven(consume_tasks(zs[k % len(zs)], total), side)
                for j in range(step_levels):
                    n = k * step_levels + j
                    before, after, row = entered(total[j], n % SUBS, before, after)
                    if n % SUBS == SUBS - 1:
                        level = pl.multiple_of(i * (unroll * step_levels) + n + 1 - SUBS, SUBS)
                        put_group(level, before, after, row)
            return most

        ahead = []
        for t in range(lead + 2):
            ahead += first_tasks(t, ones[t % 2])
            if t >= 1:
                ahead += second_tasks(ones[(t - 1) % 2], hids[(t - 1) % 2])
            if t >= 2:
                ahead += optics_tasks(hids[t % 2], zs[t - 2])
        for task in ahead:
            task()
        return lax.fori_loop(0, steps // unroll, several, jnp.float32(0.0))

    def run_guarded():
        begin()
        z = zs[0]
        at = slice(0, LANES)
        nothing = jnp.zeros((SUBS, LANES), F32)

        def group(i, _):
            def level(n, held):
                row = pl.multiple_of((i * SUBS + n) * SUBS, SUBS)
                hidden = silu_of_half(mm(first[...], fed(x[pl.ds(row, SUBS), :])))
                hidden = silu_of_half(mm(second[...], hidden))
                z[:, at] = mm(heads[...], jnp.concatenate([hidden, hidden], axis=0))

                def piece(c, total):
                    lo = pl.multiple_of(c * SUBS, SUBS)
                    carry = trans[pl.ds(lo, SUBS), :]
                    depth = softplus2_guarded(z[pl.ds(lo, SUBS), at])
                    following = carry * jnp.exp2(depth * rate)
                    trans[pl.ds(lo, SUBS), :] = following
                    if not both:
                        return total + following
                    share = softplus2_guarded(z[pl.ds(pl.multiple_of(gpts + lo, SUBS), SUBS), at])
                    return total + (carry - following) * share

                total = lax.fori_loop(0, gpts // SUBS, piece, nothing)
                return entered(total, n, *held[:2])

            held = lax.fori_loop(0, SUBS, level, (nothing, nothing, nothing))
            put_group(pl.multiple_of(i * SUBS, SUBS), *held)
            return 0

        lax.fori_loop(0, levels // SUBS, group, 0)

    peak[...] = jnp.ones_like(peak)
    most = run()
    pl.when(most > SAFE)(run_guarded)


def sweep_scratch(hid, rows, gpts, step_levels, lead):
    wide = step_levels * LANES
    return [
        pltpu.VMEM((hid, wide), BF16),
        pltpu.VMEM((hid, wide), BF16),
        pltpu.VMEM((2 * hid, wide), BF16),
        pltpu.VMEM((2 * hid, wide), BF16),
        *([pltpu.VMEM((rows, wide), F32)] * (2 * lead)),
        pltpu.VMEM((gpts, LANES), F32),
        pltpu.VMEM((SUBS, LANES), F32),
        pltpu.VMEM((2 * SUBS, LANES), BF16),
    ]


def longwave_body(which, packed, first, second, heads, reach, out, *buffers):
    gpts = heads.shape[0] // 2
    x = packed.at[which]

    def put(level, emitted):
        row = pl.multiple_of(level * SUBS, SUBS)
        planck = jnp.exp(0.25 * x[pl.ds(row, SUBS, stride=SUBS), :])
        out[pl.ds(level, SUBS), :] = -(heat_scale * LN2 / gpts) * planck * emitted

    sweep(
        x, first, second, heads, reach, jnp.ones((gpts, LANES), F32), gpts,
        -depth_scale, True, put, buffers,
    )


def shortwave_body(
    count, kept_x, kept_cos, in_x, first, second, heads, reach, flux, out, work_x, *buffers
):
    cells, half = kept_x.shape
    gpts = heads.shape[0]
    slot = iota((half, half), 1) - count[0, 0]
    placed = jnp.where(slot == iota((half, half), 0), 1.0, 0.0).astype(BF16)
    work_x[...] = kept_x[...] + mm(in_x[0:cells, :], placed)
    cosine = kept_cos[...] + mm(in_x[cells:, :], placed)[0:SUBS]
    cosine = jnp.where(cosine > 0.0, cosine, 1.0)

    def put(level, emitted):
        out[pl.ds(level, SUBS), :] = (heat_scale / gpts) * cosine * emitted

    sweep(
        work_x, first, second, heads, reach, flux[...], gpts,
        -depth_scale / cosine, False, put, buffers,
    )


def finish_body(me, count, long_first, long_last, work, partner, slot_of, *rest):
    pieces, heat = rest[:-1], rest[-1]
    levels, cols = heat.shape
    half = cols // 2
    slab = pieces[0].shape[0]
    sunlit = count[0, 0]
    for lo, long in ((0, long_first), (half, long_last)):
        slot = slot_of[:, lo : lo + half]
        here = slot < half
        place = jnp.where(here, slot, slot + half - sunlit) & (half - 1)
        lit = slot < sunlit
        for r in range(0, levels, SUBS):
            near = lane_take(work[r : r + SUBS, :], place)
            far = lane_take(partner[r : r + SUBS, :], place)
            short = jnp.where(lit, jnp.where(here, near, far), 0.0)
            heat[r : r + SUBS, lo : lo + half] = long[r : r + SUBS, :] + short
    for goal, out in partners(me, pieces):
        out[...] = heat[pl.ds(pl.multiple_of(goal * slab, SUBS), slab), :]


def add_body(me, closed, *rest):
    pieces, out = rest[:-1], rest[-1]
    cols = pieces[0].shape[1]
    for source, piece in partners(me, pieces):
        at = pl.ds(pl.multiple_of(source * cols, LANES), cols)
        out[:, at] = closed[:, at] + piece[...]


def per_device(
    potential, species, diffusion, neighbours, listing, day_count, zenith,
    lw_first, lw_bias, lw_second, lw_depth, lw_fraction,
    sw_first, sw_bias, sw_second, sw_depth, solar_flux,
):
    n_group = lax.axis_size("group")
    n_tile = lax.axis_size("tile")
    assert n_group & (n_group - 1) == 0 and n_tile % 2 == 0
    me = lax.axis_index("group").astype(jnp.int32).reshape(1)
    place = lax.axis_index("tile").astype(jnp.int32).reshape(1)
    slab, tile = potential.shape
    gases = species.shape[0]
    cols = tile // n_group
    half = cols // 2
    levels = slab * n_group
    hid = lw_first.shape[1]
    lw_gpts = lw_depth.shape[1]
    sw_gpts = sw_depth.shape[1]

    def outward(value):
        across = [(i, (i + 1 if i % 2 else i - 1) % n_tile) for i in range(n_tile)]
        return lax.ppermute(value, "tile", across)

    def paired(value):
        return lax.ppermute(value, "tile", [(i, i ^ 1) for i in range(n_tile)])

    def swapped(value, bit):
        return lax.ppermute(value, "group", [(i, i ^ bit) for i in range(n_group)])

    def exchanged(pieces):
        return [swapped(p, bit) if bit else p for bit, p in zip(far_first(n_group), pieces)]

    near = neighbours.shape[0]
    raw = (potential, neighbours, diffusion, species)
    framing, *gas_cuts = call(
        pack_body,
        [shaped((slab + 2 * near, tile), F32)] + [shaped((gases, slab, cols), BF16)] * n_group,
        [me, *(pltpu.with_memory_space_constraint(a, pltpu.HBM) for a in raw)],
        [
            pltpu.VMEM(neighbours.shape, jnp.int32),
            pltpu.VMEM(diffusion.shape, F32),
            pltpu.SemaphoreType.DMA((3 + n_group,)),
        ],
        where=HBM,
    )
    inner = paired(framing)
    outer = outward(framing)
    gas_pieces = exchanged(gas_cuts)

    (
        kept, sent, kept_cos, sent_cos, slot_of,
        lw_one, lw_two, lw_heads, lw_reach,
        sw_one, sw_two, sw_heads, sw_reach, flux,
    ) = call(
        prepare_body,
        [
            shaped((cols, half), BF16),
            shaped((cols, half), BF16),
            shaped((SUBS, half), F32),
            shaped((2 * SUBS, half), BF16),
            shaped((SUBS, cols), jnp.int32),
            shaped((hid, 2 * SUBS), BF16),
            shaped(lw_second.shape[::-1], BF16),
            shaped((2 * lw_gpts, 2 * hid), BF16),
            shaped((2 * SUBS, LANES), F32),
            shaped((hid, 2 * SUBS), BF16),
            shaped(sw_second.shape[::-1], BF16),
            shaped((sw_gpts, 2 * hid), BF16),
            shaped((2 * SUBS, LANES), F32),
            shaped((sw_gpts, LANES), F32),
        ],
        [
            day_count, listing, zenith,
            lw_first, lw_bias[None], lw_second, lw_depth, lw_fraction,
            sw_first, sw_bias[None], sw_second, sw_depth, solar_flux[None],
        ],
        after=framing,
    )

    third, *warm_cuts = call(
        sections_body,
        [shaped((slab, tile + 2 * HW), F32)] + [shaped((slab, cols), BF16)] * n_group,
        [me, place, outer, inner, potential, neighbours, diffusion],
        [pltpu.VMEM((slab, 3 * tile), F32)] * 3
        + [pltpu.VMEM((3, *neighbours.shape), jnp.int32), pltpu.VMEM((3, *diffusion.shape), F32)],
        flops=10_000_000,
    )
    warm_pieces = exchanged(warm_cuts)
    (closed,) = call(
        closing_body, [shaped((slab, tile), F32)], [third, neighbours, diffusion], flops=2_000_000
    )

    cells = levels * SUBS
    packed, out_x, kept_x = call(
        functools.partial(join_body, n_group),
        [
            shaped((cols // LANES, cells, LANES), F32),
            shaped((cells + 2 * SUBS, half), BF16),
            shaped((cells, half), F32),
        ],
        [me, *gas_pieces, *warm_pieces, kept, sent, sent_cos],
        [pltpu.VMEM((SUBS * slab, LANES), F32)],
    )
    in_x = paired(out_x)

    def longwave(which):
        (heat,) = call(
            functools.partial(longwave_body, which),
            [shaped((levels, half), F32)],
            [packed, lw_one, lw_two, lw_heads, lw_reach],
            sweep_scratch(hid, 2 * lw_gpts, lw_gpts, *((2, 2) if which else (4, 1))),
            flops=4 * levels * half * hid * lw_gpts,
            trans=5 * levels * half * lw_gpts,
            after=work if which else None,
        )
        return heat

    long_first = longwave(0)
    (work,) = call(
        shortwave_body,
        [shaped((levels, half), F32)],
        [day_count, kept_x, kept_cos, in_x, sw_one, sw_two, sw_heads, sw_reach, flux],
        [pltpu.VMEM((cells, half), F32)] + sweep_scratch(hid, sw_gpts, sw_gpts, 4, 1),
        flops=2 * levels * half * hid * sw_gpts,
        trans=3 * levels * half * sw_gpts,
        after=long_first,
    )
    partner = paired(work)
    long_last = longwave(1)
    heat_cuts = call(
        finish_body,
        [shaped((slab, cols), F32)] * n_group,
        [me, day_count, long_first, long_last, work, partner, slot_of],
        [pltpu.VMEM((levels, cols), F32)],
    )
    heat_pieces = exchanged(heat_cuts)
    (evolved,) = call(add_body, [shaped((slab, tile), F32)], [me, closed, *heat_pieces])
    return evolved


def solution(mesh):
    return jax.shard_map(
        per_device,
        mesh=mesh,
        in_specs=(
            P("group", "tile"),
            P(None, "group", "tile"),
            P(None, "tile"),
            P(None, "tile"),
            P("group", "tile", None),
            P("group", "tile"),
            P("group", "tile", None),
            *([P()] * 10),
        ),
        out_specs=P("group", "tile"),
        check_vma=False,
    )
```

```python
import functools
import math

import jax
import jax.numpy as jnp
from jax import lax
from jax.experimental import pallas as pl
from jax.experimental.pallas import tpu as pltpu
from jax.sharding import PartitionSpec as P

HW = 256
LANES = 128
SUBS = 8

depth_scale = 0.1
heat_scale = 12.0
LOG2E = 1.4426950408889634
LN2 = 0.6931471805599453
SAFE = 120.0

F32 = jnp.float32
BF16 = jnp.bfloat16
VMEM = pl.BlockSpec(memory_space=pltpu.VMEM)
ANY = pl.BlockSpec(memory_space=pl.ANY)
HBM = pl.BlockSpec(memory_space=pltpu.HBM)
SMEM = pl.BlockSpec(memory_space=pltpu.SMEM)
PARAMS = pltpu.CompilerParams(vmem_limit_bytes=48 * 1024 * 1024)


def call(body, outs, ins, scratch=(), flops=0, trans=0, after=None, where=VMEM):
    in_specs = [SMEM if a.size == 1 else where for a in ins]
    if after is not None:
        whole, ins = body, [after, *ins]
        in_specs = [ANY, *in_specs]

        def body(_, *refs):
            whole(*refs)

    return pl.pallas_call(
        body,
        out_shape=outs,
        in_specs=in_specs,
        out_specs=[VMEM for _ in outs],
        scratch_shapes=list(scratch),
        compiler_params=PARAMS,
        cost_estimate=pl.CostEstimate(
            flops=flops,
            transcendentals=trans,
            bytes_accessed=sum(a.size * a.dtype.itemsize for a in list(ins) + list(outs)),
        ),
    )(*ins)


def shaped(shape, dtype):
    return jax.ShapeDtypeStruct(shape, dtype)


def iota(shape, dim):
    return lax.broadcasted_iota(jnp.int32, shape, dim)


def mm(a, b):
    return jnp.dot(a, b, preferred_element_type=F32)


def far_first(n):
    return [0, *range(n - 1, 0, -1)]


def partners(me, pieces):
    return [(me[0] ^ bit, piece) for bit, piece in zip(far_first(len(pieces)), pieces)]


def lane_take(x, idx):
    return jnp.take_along_axis(x, idx, axis=1, mode="promise_in_bounds")


def diffused(src, src_at, table, weight, within, at):
    reach = HW // LANES
    wide = 2 * reach + 1
    rows = src.shape[0]
    groups = range(0, rows, SUBS)
    base = at - src_at
    middle = [src[r : r + SUBS, base : base + LANES] for r in groups]
    total = [jnp.zeros_like(m) for m in middle]
    for k in range(table.shape[0]):
        place = jnp.broadcast_to(table[k : k + 1, within : within + LANES], (SUBS, LANES)) - within
        lane = place & (LANES - 1)
        which = place >> (LANES.bit_length() - 1)
        factor = jnp.broadcast_to(weight[k : k + 1, within : within + LANES], (SUBS, LANES))
        tests = [which == w for w in range(1, wide)]
        for n, r in enumerate(groups):
            near = None
            for w in range(wide):
                lo = base + (w - reach) * LANES
                got = lane_take(src[r : r + SUBS, lo : lo + LANES], lane)
                near = got if w == 0 else jnp.where(tests[w - 1], got, near)
            total[n] = total[n] + factor * (near - middle[n])
    return [(r, m, m + t) for r, m, t in zip(groups, middle, total)]


def pack_body(me, own, table, weight, species, out, *rest):
    pieces, (table_here, weight_here, sems) = rest[:-3], rest[-3:]
    slab = own.shape[0]
    near = table.shape[0]
    cols = pieces[0].shape[2]
    moves = [
        pltpu.make_async_copy(own, out.at[0:slab], sems.at[0]),
        pltpu.make_async_copy(table, table_here, sems.at[1]),
        pltpu.make_async_copy(weight, weight_here, sems.at[2]),
    ]
    for source, piece in partners(me, pieces):
        at = pl.ds(pl.multiple_of(source * cols, LANES), cols)
        moves.append(pltpu.make_async_copy(species.at[:, :, at], piece, sems.at[len(moves)]))
    for move in moves:
        move.start()
    for move in moves:
        move.wait()
    out[slab : slab + near, :] = table_here[...].astype(F32)
    out[slab + near :, :] = weight_here[...]


def sections_body(
    me, place, outer, inner, own, table, weight, third_out, *rest
):
    pieces, (frame, first, second, tables, weights) = rest[:-5], rest[-5:]
    slab, tile = own.shape
    near = table.shape[0]
    cols = tile // pieces[0].shape[0]
    odd = place[0] & 1
    for side, packed in ((odd, outer), (1 - odd, inner)):
        at = pl.ds(pl.multiple_of(side * (2 * tile), LANES), tile)
        frame[:, at] = packed[0:slab, :]
        tables[side * 2] = packed[slab : slab + near, :].astype(jnp.int32)
        weights[side * 2] = packed[slab + near : slab + 2 * near, :]
    frame[:, tile : 2 * tile] = own[...]
    tables[1] = table[...]
    weights[1] = weight[...]

    def run(src, src_at, halo, put):
        for at in range(tile - halo, 2 * tile + halo, LANES):
            t = at // tile
            for r, _, value in diffused(src, src_at, tables.at[t], weights.at[t], at - t * tile, at):
                put(r, at, value)

    def put_first(r, at, value):
        first[r : r + SUBS, at : at + LANES] = value

    def put_second(r, at, value):
        start = frame[r : r + SUBS, at : at + LANES]
        second[r : r + SUBS, at : at + LANES] = 0.75 * start + 0.25 * value

    def put_third(r, at, value):
        start = frame[r : r + SUBS, at : at + LANES]
        lo = at - tile + HW
        third_out[r : r + SUBS, lo : lo + LANES] = start / 3.0 + (2.0 / 3.0) * value

    run(frame, 0, 3 * HW, put_first)
    run(first, 0, 2 * HW, put_second)
    run(second, 0, HW, put_third)
    for n in range(pieces[0].shape[0]):
        lo = HW + n * cols
        pieces[0][n] = third_out[:, lo : lo + cols]


def closing_body(third, table, weight, out):
    tile = out.shape[1]
    for at in range(0, tile, LANES):
        for r, _, value in diffused(third, -HW, table, weight, at, at):
            out[r : r + SUBS, at : at + LANES] = value


def turned_over(matrix):
    return matrix.astype(F32).T


def head_parts(weight, out, at):
    hid, gpts = weight.shape
    scaled = LOG2E * turned_over(weight[...])
    high = scaled.astype(BF16)
    out[at : at + gpts, 0:hid] = high
    out[at : at + gpts, hid:] = (scaled - high.astype(F32)).astype(BF16)


def first_parts(weight, bias, out):
    fin = weight.shape[0]
    rows = [(0.5 * weight[...].astype(F32)).astype(BF16).astype(F32)]
    rest = 0.5 * bias[...]
    for _ in range(3):
        part = rest.astype(BF16).astype(F32)
        rows.append(part)
        rest = rest - part
    rows.append(jnp.zeros((fin - 3, weight.shape[1]), F32))
    out[...] = jnp.concatenate(rows, axis=0).T.astype(BF16)


def reach_of(heads):
    sums = mm(jnp.abs(heads[...]), jnp.ones((heads.shape[1], LANES), BF16))
    return jnp.broadcast_to(jnp.max(sums, axis=0, keepdims=True), (2 * SUBS, LANES))


def prepare_body(
    count, listing, zenith, w1, b1, w2, wd, wf, v1, c1, v2, vd, flux,
    kept_out, sent_out, kept_cos, sent_cos, slot_of,
    w1_out, w2_out, heads_out, reach_out, v1_out, v2_out, vd_out, vreach_out, flux_out,
):
    for weight, out in ((w2, w2_out), (v2, v2_out)):
        out[...] = (0.5 * turned_over(weight[...])).astype(BF16)
    first_parts(w1, b1, w1_out)
    first_parts(v1, c1, v1_out)
    head_parts(wd, heads_out, 0)
    head_parts(wf, heads_out, wd.shape[1])
    head_parts(vd, vd_out, 0)
    reach_out[...] = reach_of(heads_out)
    vreach_out[...] = reach_of(vd_out)
    flux_out[...] = jnp.broadcast_to(flux[...], (LANES, flux.shape[1])).T
    cols = listing.shape[-1]
    half = cols // 2
    sunlit = count[0, 0]
    label = iota((cols, half), 0)
    slot = iota((cols, half), 1)
    first = jnp.broadcast_to(listing[0, :, 0:half], (cols, half)) == label
    last = jnp.broadcast_to(listing[0, :, half:cols], (cols, half)) == label
    kept = jnp.where(first & (slot < sunlit), 1.0, 0.0).astype(BF16)
    sent = jnp.where(last & (slot + half < sunlit), 1.0, 0.0).astype(BF16)
    kept_out[...] = kept
    sent_out[...] = sent
    cosine = jnp.broadcast_to(zenith[0].astype(F32), (2 * SUBS, cols)).astype(BF16)
    sent_cos[...] = mm(cosine, sent).astype(BF16)
    kept_cos[...] = mm(cosine, kept)[0:SUBS]
    hits = jnp.where(jnp.concatenate([first, last], axis=1), 1.0, 0.0).astype(BF16)
    numbers = iota((2 * SUBS, cols), 1).astype(F32).astype(BF16)
    found = lax.dot_general(numbers, hits, (((1,), (1,)), ((), ())), preferred_element_type=F32)
    slot_of[...] = found[0:SUBS].astype(jnp.int32)


def join_body(n_group, me, *rest):
    gases, warm = rest[:n_group], rest[n_group]
    kept, sent, sent_cos, packed, outgoing, kept_x, spread = rest[n_group + 1 :]
    slab = warm.shape[1]
    for source, gas in partners(me, gases):
        for h in range(packed.shape[0]):
            at = slice(h * LANES, (h + 1) * LANES)
            spread[0:slab, :] = warm[source, :, at].astype(BF16).astype(F32)
            for f in range(gas.shape[0]):
                spread[(f + 1) * slab : (f + 2) * slab, :] = gas[f, :, at].astype(F32)
            for l in range(slab):
                row = pl.multiple_of((source * slab + l) * SUBS, SUBS)
                packed[h, pl.ds(row, SUBS), :] = spread[pl.ds(l, SUBS, stride=slab), :]
    cells = packed.shape[1]
    first, last = packed[0].astype(BF16), packed[1].astype(BF16)
    outgoing[0:cells, :] = (mm(first, sent[0:LANES]) + mm(last, sent[LANES:])).astype(BF16)
    outgoing[cells:, :] = sent_cos[...]
    kept_x[...] = mm(first, kept[0:LANES]) + mm(last, kept[LANES:])


def softplus2(z):
    return lax.log2(1.0 + jnp.exp2(z))


def softplus2_guarded(z):
    return jnp.maximum(z, softplus2(jnp.minimum(z, SAFE)))


def silu_of_half(v):
    half = v.astype(BF16)
    return half + half * jnp.tanh(half)


def sweep(x, first, second, heads, reach, start, gpts, rate, both, put, buffers, span):
    ones, hids, zs, (trans, last, peak) = buffers[0:2], buffers[2:4], buffers[4:-3], buffers[-3:]
    lead = len(zs) // 2
    wide = ones[0].shape[1]
    step_levels = wide // LANES
    levels = x.shape[0] // SUBS
    steps = levels // step_levels
    units = first.shape[0]
    sub = iota((SUBS, LANES), 0)

    def fed(tile):
        return jnp.concatenate([tile, jnp.ones_like(tile)], axis=0).astype(BF16)

    def first_tasks(t, out):
        def task():
            row = jnp.minimum(t, steps - 1) * (step_levels * SUBS)
            tiles = [
                x[pl.ds(pl.multiple_of(row + i * SUBS, SUBS), SUBS), :] for i in range(step_levels)
            ]
            out[...] = silu_of_half(mm(first[...], fed(jnp.concatenate(tiles, axis=1))))

        return [task]

    def second_tasks(one, out):
        def task():
            value = silu_of_half(mm(second[...], one[...]))
            out[0:units, :] = value
            out[units:, :] = value
            most = peak[...]
            for i in range(0, units, 2 * SUBS):
                for at in range(0, wide, LANES):
                    most = jnp.maximum(most, value[i : i + 2 * SUBS, at : at + LANES])
            peak[...] = most

        return [task]

    def optics_tasks(hid, out):
        def task():
            out[...] = mm(heads[...], hid[...])

        return [task]

    def consume_tasks(z, total):
        def task(lo):
            carry = trans[lo : lo + SUBS, :]
            for i in range(step_levels):
                at = slice(i * LANES, (i + 1) * LANES)
                following = carry * jnp.exp2(softplus2(z[lo : lo + SUBS, at]) * rate)
                term = following
                if both:
                    term = (carry - following) * softplus2(z[gpts + lo : gpts + lo + SUBS, at])
                total[i] = term if total[i] is None else total[i] + term
                carry = following
            trans[lo : lo + SUBS, :] = carry

        return [functools.partial(task, lo) for lo in range(0, gpts, SUBS)]

    def woven(main, side):
        done = 0
        for n, task in enumerate(main):
            while done < len(side) and done * len(main) <= n * len(side):
                side[done]()
                done += 1
            task()

    def begin():
        trans[...] = start
        if not both:
            sums = jnp.sum(start.reshape(gpts // SUBS, SUBS, LANES), axis=0)
            last[...] = jnp.broadcast_to(jnp.sum(sums, axis=0, keepdims=True), (SUBS, LANES))

    def entered(total, n, before, after):
        row = jnp.broadcast_to(jnp.sum(total, axis=0, keepdims=True), (SUBS, LANES))
        after = jnp.where(sub == n, row, after)
        before = jnp.where(sub == n + 1, row, before)
        return before, after, row

    def put_group(level, before, after, row):
        if both:
            put(level, after)
        else:
            put(level, jnp.where(sub == 0, last[...], before) - after)
            last[...] = row

    def run():
        begin()
        unroll = span // step_levels

        def several(i, _):
            before = after = jnp.zeros((SUBS, LANES), F32)
            for k in range(unroll):
                t = k + lead
                total = [None] * step_levels
                if k == max(unroll - 1 - lead, 0):
                    most = jnp.max(peak[...].astype(F32) * reach[...])
                side = (
                    optics_tasks(hids[t % 2], zs[t % len(zs)])
                    + second_tasks(ones[(t + 1) % 2], hids[(t + 1) % 2])
                    + first_tasks(i * unroll + t + 2, ones[t % 2])
                )
                woven(consume_tasks(zs[k % len(zs)], total), side)
                for j in range(step_levels):
                    n = k * step_levels + j
                    before, after, row = entered(total[j], n % SUBS, before, after)
                    if n % SUBS == SUBS - 1:
                        level = pl.multiple_of(i * (unroll * step_levels) + n + 1 - SUBS, SUBS)
                        put_group(level, before, after, row)
            return most

        ahead = []
        for t in range(lead + 2):
            ahead += first_tasks(t, ones[t % 2])
            if t >= 1:
                ahead += second_tasks(ones[(t - 1) % 2], hids[(t - 1) % 2])
            if t >= 2:
                ahead += optics_tasks(hids[t % 2], zs[t - 2])
        for task in ahead:
            task()
        return lax.fori_loop(0, steps // unroll, several, jnp.float32(0.0))

    def run_guarded():
        begin()
        z = zs[0]
        at = slice(0, LANES)
        nothing = jnp.zeros((SUBS, LANES), F32)

        def group(i, _):
            def level(n, held):
                row = pl.multiple_of((i * SUBS + n) * SUBS, SUBS)
                hidden = silu_of_half(mm(first[...], fed(x[pl.ds(row, SUBS), :])))
                hidden = silu_of_half(mm(second[...], hidden))
                z[:, at] = mm(heads[...], jnp.concatenate([hidden, hidden], axis=0))

                def piece(c, total):
                    lo = pl.multiple_of(c * SUBS, SUBS)
                    carry = trans[pl.ds(lo, SUBS), :]
                    depth = softplus2_guarded(z[pl.ds(lo, SUBS), at])
                    following = carry * jnp.exp2(depth * rate)
                    trans[pl.ds(lo, SUBS), :] = following
                    if not both:
                        return total + following
                    share = softplus2_guarded(z[pl.ds(pl.multiple_of(gpts + lo, SUBS), SUBS), at])
                    return total + (carry - following) * share

                total = lax.fori_loop(0, gpts // SUBS, piece, nothing)
                return entered(total, n, *held[:2])

            held = lax.fori_loop(0, SUBS, level, (nothing, nothing, nothing))
            put_group(pl.multiple_of(i * SUBS, SUBS), *held)
            return 0

        lax.fori_loop(0, levels // SUBS, group, 0)

    peak[...] = jnp.ones_like(peak)
    most = run()
    pl.when(most > SAFE)(run_guarded)


def sweep_scratch(hid, rows, gpts, step_levels, lead):
    wide = step_levels * LANES
    return [
        pltpu.VMEM((hid, wide), BF16),
        pltpu.VMEM((hid, wide), BF16),
        pltpu.VMEM((2 * hid, wide), BF16),
        pltpu.VMEM((2 * hid, wide), BF16),
        *([pltpu.VMEM((rows, wide), F32)] * (2 * lead)),
        pltpu.VMEM((gpts, LANES), F32),
        pltpu.VMEM((SUBS, LANES), F32),
        pltpu.VMEM((2 * SUBS, LANES), BF16),
    ]


def longwave_body(which, packed, first, second, heads, reach, out, *buffers):
    gpts = heads.shape[0] // 2
    x = packed.at[which]

    def put(level, emitted):
        row = pl.multiple_of(level * SUBS, SUBS)
        planck = jnp.exp(0.25 * x[pl.ds(row, SUBS, stride=SUBS), :])
        out[pl.ds(level, SUBS), :] = -(heat_scale * LN2 / gpts) * planck * emitted

    sweep(
        x, first, second, heads, reach, jnp.ones((gpts, LANES), F32), gpts,
        -depth_scale, True, put, buffers, 4 * SUBS if which else 2 * SUBS,
    )


def shortwave_body(
    count, kept_x, kept_cos, in_x, first, second, heads, reach, flux, out, work_x, *buffers
):
    cells, half = kept_x.shape
    gpts = heads.shape[0]
    slot = iota((half, half), 1) - count[0, 0]
    placed = jnp.where(slot == iota((half, half), 0), 1.0, 0.0).astype(BF16)
    work_x[...] = kept_x[...] + mm(in_x[0:cells, :], placed)
    cosine = kept_cos[...] + mm(in_x[cells:, :], placed)[0:SUBS]
    cosine = jnp.where(cosine > 0.0, cosine, 1.0)

    def put(level, emitted):
        out[pl.ds(level, SUBS), :] = (heat_scale / gpts) * cosine * emitted

    sweep(
        work_x, first, second, heads, reach, flux[...], gpts,
        -depth_scale / cosine, False, put, buffers, 4 * SUBS,
    )


def finish_body(me, count, long_first, long_last, work, partner, slot_of, *rest):
    pieces, heat = rest[:-1], rest[-1]
    levels, cols = heat.shape
    half = cols // 2
    slab = pieces[0].shape[0]
    sunlit = count[0, 0]
    for lo, long in ((0, long_first), (half, long_last)):
        slot = slot_of[:, lo : lo + half]
        here = slot < half
        place = jnp.where(here, slot, slot + half - sunlit) & (half - 1)
        lit = slot < sunlit
        for r in range(0, levels, SUBS):
            near = lane_take(work[r : r + SUBS, :], place)
            far = lane_take(partner[r : r + SUBS, :], place)
            short = jnp.where(lit, jnp.where(here, near, far), 0.0)
            heat[r : r + SUBS, lo : lo + half] = long[r : r + SUBS, :] + short
    for goal, out in partners(me, pieces):
        out[...] = heat[pl.ds(pl.multiple_of(goal * slab, SUBS), slab), :]


def add_body(me, closed, *rest):
    pieces, out = rest[:-1], rest[-1]
    cols = pieces[0].shape[1]
    for source, piece in partners(me, pieces):
        at = pl.ds(pl.multiple_of(source * cols, LANES), cols)
        out[:, at] = closed[:, at] + piece[...]


def per_device(
    potential, species, diffusion, neighbours, listing, day_count, zenith,
    lw_first, lw_bias, lw_second, lw_depth, lw_fraction,
    sw_first, sw_bias, sw_second, sw_depth, solar_flux,
):
    n_group = lax.axis_size("group")
    n_tile = lax.axis_size("tile")
    assert n_group & (n_group - 1) == 0 and n_tile % 2 == 0
    me = lax.axis_index("group").astype(jnp.int32).reshape(1)
    place = lax.axis_index("tile").astype(jnp.int32).reshape(1)
    slab, tile = potential.shape
    gases = species.shape[0]
    cols = tile // n_group
    half = cols // 2
    levels = slab * n_group
    hid = lw_first.shape[1]
    lw_gpts = lw_depth.shape[1]
    sw_gpts = sw_depth.shape[1]

    def outward(value):
        across = [(i, (i + 1 if i % 2 else i - 1) % n_tile) for i in range(n_tile)]
        return lax.ppermute(value, "tile", across)

    def paired(value):
        return lax.ppermute(value, "tile", [(i, i ^ 1) for i in range(n_tile)])

    def swapped(value, bit):
        return lax.ppermute(value, "group", [(i, i ^ bit) for i in range(n_group)])

    def exchanged(pieces):
        return [swapped(p, bit) if bit else p for bit, p in zip(far_first(n_group), pieces)]

    near = neighbours.shape[0]
    raw = (potential, neighbours, diffusion, species)
    framing, *gas_cuts = call(
        pack_body,
        [shaped((slab + 2 * near, tile), F32)] + [shaped((gases, slab, cols), BF16)] * n_group,
        [me, *(pltpu.with_memory_space_constraint(a, pltpu.HBM) for a in raw)],
        [
            pltpu.VMEM(neighbours.shape, jnp.int32),
            pltpu.VMEM(diffusion.shape, F32),
            pltpu.SemaphoreType.DMA((3 + n_group,)),
        ],
        where=HBM,
    )
    inner = paired(framing)
    outer = outward(framing)
    gas_pieces = exchanged(gas_cuts)

    (
        kept, sent, kept_cos, sent_cos, slot_of,
        lw_one, lw_two, lw_heads, lw_reach,
        sw_one, sw_two, sw_heads, sw_reach, flux,
    ) = call(
        prepare_body,
        [
            shaped((cols, half), BF16),
            shaped((cols, half), BF16),
            shaped((SUBS, half), F32),
            shaped((2 * SUBS, half), BF16),
            shaped((SUBS, cols), jnp.int32),
            shaped((hid, 2 * SUBS), BF16),
            shaped(lw_second.shape[::-1], BF16),
            shaped((2 * lw_gpts, 2 * hid), BF16),
            shaped((2 * SUBS, LANES), F32),
            shaped((hid, 2 * SUBS), BF16),
            shaped(sw_second.shape[::-1], BF16),
            shaped((sw_gpts, 2 * hid), BF16),
            shaped((2 * SUBS, LANES), F32),
            shaped((sw_gpts, LANES), F32),
        ],
        [
            day_count, listing, zenith,
            lw_first, lw_bias[None], lw_second, lw_depth, lw_fraction,
            sw_first, sw_bias[None], sw_second, sw_depth, solar_flux[None],
        ],
        after=framing,
    )

    third, warm_cuts = call(
        sections_body,
        [shaped((slab, tile + 2 * HW), F32), shaped((n_group, slab, cols), F32)],
        [me, place, outer, inner, potential, neighbours, diffusion],
        [pltpu.VMEM((slab, 3 * tile), F32)] * 3
        + [pltpu.VMEM((3, *neighbours.shape), jnp.int32), pltpu.VMEM((3, *diffusion.shape), F32)],
        flops=10_000_000,
    )
    warm = lax.all_to_all(warm_cuts, "group", split_axis=0, concat_axis=0, tiled=True)
    (closed,) = call(
        closing_body, [shaped((slab, tile), F32)], [third, neighbours, diffusion], flops=2_000_000
    )

    cells = levels * SUBS
    packed, out_x, kept_x = call(
        functools.partial(join_body, n_group),
        [
            shaped((cols // LANES, cells, LANES), F32),
            shaped((cells + 2 * SUBS, half), BF16),
            shaped((cells, half), F32),
        ],
        [me, *gas_pieces, warm, kept, sent, sent_cos],
        [pltpu.VMEM((SUBS * slab, LANES), F32)],
    )
    in_x = paired(out_x)

    def longwave(which):
        (heat,) = call(
            functools.partial(longwave_body, which),
            [shaped((levels, half), F32)],
            [packed, lw_one, lw_two, lw_heads, lw_reach],
            sweep_scratch(hid, 2 * lw_gpts, lw_gpts, 2, 1),
            flops=4 * levels * half * hid * lw_gpts,
            trans=5 * levels * half * lw_gpts,
            after=work if which else None,
        )
        return heat

    long_first = longwave(0)
    (work,) = call(
        shortwave_body,
        [shaped((levels, half), F32)],
        [day_count, kept_x, kept_cos, in_x, sw_one, sw_two, sw_heads, sw_reach, flux],
        [pltpu.VMEM((cells, half), F32)] + sweep_scratch(hid, sw_gpts, sw_gpts, 4, 1),
        flops=2 * levels * half * hid * sw_gpts,
        trans=3 * levels * half * sw_gpts,
        after=long_first,
    )
    partner = paired(work)
    long_last = longwave(1)
    heat_cuts = call(
        finish_body,
        [shaped((slab, cols), F32)] * n_group,
        [me, day_count, long_first, long_last, work, partner, slot_of],
        [pltpu.VMEM((levels, cols), F32)],
    )
    heat_pieces = exchanged(heat_cuts)
    (evolved,) = call(add_body, [shaped((slab, tile), F32)], [me, closed, *heat_pieces])
    return evolved


def solution(mesh):
    return jax.shard_map(
        per_device,
        mesh=mesh,
        in_specs=(
            P("group", "tile"),
            P(None, "group", "tile"),
            P(None, "tile"),
            P(None, "tile"),
            P("group", "tile", None),
            P("group", "tile"),
            P("group", "tile", None),
            *([P()] * 10),
        ),
        out_specs=P("group", "tile"),
        check_vma=False,
    )
```

```python
import functools
import math

import jax
import jax.numpy as jnp
from jax import lax
from jax.experimental import pallas as pl
from jax.experimental.pallas import tpu as pltpu
from jax.sharding import PartitionSpec as P

HW = 256
LANES = 128
SUBS = 8

depth_scale = 0.1
heat_scale = 12.0
LOG2E = 1.4426950408889634
LN2 = 0.6931471805599453
SAFE = 120.0

F32 = jnp.float32
BF16 = jnp.bfloat16
VMEM = pl.BlockSpec(memory_space=pltpu.VMEM)
ANY = pl.BlockSpec(memory_space=pl.ANY)
HBM = pl.BlockSpec(memory_space=pltpu.HBM)
SMEM = pl.BlockSpec(memory_space=pltpu.SMEM)
PARAMS = pltpu.CompilerParams(vmem_limit_bytes=48 * 1024 * 1024)


def call(body, outs, ins, scratch=(), flops=0, trans=0, after=None, where=VMEM):
    in_specs = [SMEM if a.size == 1 else where for a in ins]
    if after is not None:
        whole, ins = body, [after, *ins]
        in_specs = [ANY, *in_specs]

        def body(_, *refs):
            whole(*refs)

    return pl.pallas_call(
        body,
        out_shape=outs,
        in_specs=in_specs,
        out_specs=[VMEM for _ in outs],
        scratch_shapes=list(scratch),
        compiler_params=PARAMS,
        cost_estimate=pl.CostEstimate(
            flops=flops,
            transcendentals=trans,
            bytes_accessed=sum(a.size * a.dtype.itemsize for a in list(ins) + list(outs)),
        ),
    )(*ins)


def shaped(shape, dtype):
    return jax.ShapeDtypeStruct(shape, dtype)


def iota(shape, dim):
    return lax.broadcasted_iota(jnp.int32, shape, dim)


def mm(a, b):
    return jnp.dot(a, b, preferred_element_type=F32)


def far_first(n):
    return [0, *range(n - 1, 0, -1)]


def partners(me, pieces):
    return [(me[0] ^ bit, piece) for bit, piece in zip(far_first(len(pieces)), pieces)]


def lane_take(x, idx):
    return jnp.take_along_axis(x, idx, axis=1, mode="promise_in_bounds")


def diffused(src, src_at, table, weight, within, at):
    reach = HW // LANES
    wide = 2 * reach + 1
    rows = src.shape[0]
    groups = range(0, rows, SUBS)
    base = at - src_at
    middle = [src[r : r + SUBS, base : base + LANES] for r in groups]
    total = [jnp.zeros_like(m) for m in middle]
    for k in range(table.shape[0]):
        place = jnp.broadcast_to(table[k : k + 1, within : within + LANES], (SUBS, LANES)) - within
        lane = place & (LANES - 1)
        which = place >> (LANES.bit_length() - 1)
        factor = jnp.broadcast_to(weight[k : k + 1, within : within + LANES], (SUBS, LANES))
        tests = [which == w for w in range(1, wide)]
        for n, r in enumerate(groups):
            near = None
            for w in range(wide):
                lo = base + (w - reach) * LANES
                got = lane_take(src[r : r + SUBS, lo : lo + LANES], lane)
                near = got if w == 0 else jnp.where(tests[w - 1], got, near)
            total[n] = total[n] + factor * (near - middle[n])
    return [(r, m, m + t) for r, m, t in zip(groups, middle, total)]


def pack_body(me, own, table, weight, species, out, *rest):
    pieces, (table_here, weight_here, sems) = rest[:-3], rest[-3:]
    slab = own.shape[0]
    near = table.shape[0]
    cols = pieces[0].shape[2]
    moves = [
        pltpu.make_async_copy(own, out.at[0:slab], sems.at[0]),
        pltpu.make_async_copy(table, table_here, sems.at[1]),
        pltpu.make_async_copy(weight, weight_here, sems.at[2]),
    ]
    for source, piece in partners(me, pieces):
        at = pl.ds(pl.multiple_of(source * cols, LANES), cols)
        moves.append(pltpu.make_async_copy(species.at[:, :, at], piece, sems.at[len(moves)]))
    for move in moves:
        move.start()
    for move in moves:
        move.wait()
    out[slab : slab + near, :] = table_here[...].astype(F32)
    out[slab + near :, :] = weight_here[...]


def staged(place, outer, inner, own, table, weight, frame, tables, weights):
    slab, tile = own.shape
    near = table.shape[0]
    odd = place[0] & 1
    for side, packed in ((odd, outer), (1 - odd, inner)):
        at = pl.ds(pl.multiple_of(side * (2 * tile), LANES), tile)
        frame[:, at] = packed[0:slab, :]
        tables[side * 2] = packed[slab : slab + near, :].astype(jnp.int32)
        weights[side * 2] = packed[slab + near : slab + 2 * near, :]
    frame[:, tile : 2 * tile] = own[...]
    tables[1] = table[...]
    weights[1] = weight[...]


class Sections:
    def __init__(self, frame, first, second, third, tables, weights):
        self.tile = frame.shape[1] // 3
        self.frame, self.first, self.second, self.third = frame, first, second, third
        self.tables, self.weights = tables, weights

    def run(self, src, columns, put):
        for at in columns:
            t = at // self.tile
            within = at - t * self.tile
            for r, _, value in diffused(src, 0, self.tables.at[t], self.weights.at[t], within, at):
                put(slice(r, r + SUBS), slice(at, at + LANES), value)

    def around(self, inside, halo):
        tile = self.tile
        return [*range(tile - halo, tile - inside, LANES), *range(2 * tile + inside, 2 * tile + halo, LANES)]

    def own(self, halo):
        return range(self.tile - halo, 2 * self.tile + halo, LANES)

    def do_first(self, columns):
        def put(rows, at, value):
            self.first[rows, at] = value

        self.run(self.frame, columns, put)

    def do_second(self, columns):
        def put(rows, at, value):
            self.second[rows, at] = 0.75 * self.frame[rows, at] + 0.25 * value

        self.run(self.first, columns, put)

    def do_third(self, columns):
        def put(rows, at, value):
            self.third[rows, at] = self.frame[rows, at] / 3.0 + (2.0 / 3.0) * value

        self.run(self.second, columns, put)


def sections_body(me, place, outer, inner, own, table, weight, first, second, third, *rest):
    pieces, (frame, tables, weights) = rest[:-3], rest[-3:]
    tile = own.shape[1]
    cols = tile // len(pieces)
    staged(place, outer, inner, own, table, weight, frame, tables, weights)
    sections = Sections(frame, first, second, third, tables, weights)
    sections.do_first(sections.own(2 * HW))
    sections.do_second(sections.own(HW))
    sections.do_third(sections.own(0))
    for goal, out in partners(me, pieces):
        lo = pl.multiple_of(tile + goal * cols, LANES)
        out[...] = third[:, pl.ds(lo, cols)].astype(BF16)


def closing_body(
    place, outer, inner, own, table, weight, first_in, second_in, third_in, out,
    frame, first, second, third, tables, weights,
):
    tile = own.shape[1]
    staged(place, outer, inner, own, table, weight, frame, tables, weights)
    for held, full, halo in ((first_in, first, 2 * HW), (second_in, second, HW), (third_in, third, 0)):
        at = slice(tile - halo, 2 * tile + halo)
        full[:, at] = held[:, at]
    sections = Sections(frame, first, second, third, tables, weights)
    sections.do_first(sections.around(2 * HW, 3 * HW))
    sections.do_second(sections.around(HW, 2 * HW))
    sections.do_third(sections.around(0, HW))

    def put(rows, at, value):
        out[rows, at.start - tile : at.stop - tile] = value

    sections.run(third, sections.own(0), put)


def turned_over(matrix):
    return matrix.astype(F32).T


def head_parts(weight, out, at):
    hid, gpts = weight.shape
    scaled = LOG2E * turned_over(weight[...])
    high = scaled.astype(BF16)
    out[at : at + gpts, 0:hid] = high
    out[at : at + gpts, hid:] = (scaled - high.astype(F32)).astype(BF16)


def first_parts(weight, bias, out):
    fin = weight.shape[0]
    rows = [(0.5 * weight[...].astype(F32)).astype(BF16).astype(F32)]
    rest = 0.5 * bias[...]
    for _ in range(3):
        part = rest.astype(BF16).astype(F32)
        rows.append(part)
        rest = rest - part
    rows.append(jnp.zeros((fin - 3, weight.shape[1]), F32))
    out[...] = jnp.concatenate(rows, axis=0).T.astype(BF16)


def reach_of(heads):
    sums = mm(jnp.abs(heads[...]), jnp.ones((heads.shape[1], LANES), BF16))
    return jnp.broadcast_to(jnp.max(sums, axis=0, keepdims=True), (2 * SUBS, LANES))


def prepare_body(
    count, listing, zenith, w1, b1, w2, wd, wf, v1, c1, v2, vd, flux,
    kept_out, sent_out, kept_cos, sent_cos, slot_of,
    w1_out, w2_out, heads_out, reach_out, v1_out, v2_out, vd_out, vreach_out, flux_out,
):
    for weight, out in ((w2, w2_out), (v2, v2_out)):
        out[...] = (0.5 * turned_over(weight[...])).astype(BF16)
    first_parts(w1, b1, w1_out)
    first_parts(v1, c1, v1_out)
    head_parts(wd, heads_out, 0)
    head_parts(wf, heads_out, wd.shape[1])
    head_parts(vd, vd_out, 0)
    reach_out[...] = reach_of(heads_out)
    vreach_out[...] = reach_of(vd_out)
    flux_out[...] = jnp.broadcast_to(flux[...], (LANES, flux.shape[1])).T
    cols = listing.shape[-1]
    half = cols // 2
    sunlit = count[0, 0]
    label = iota((cols, half), 0)
    slot = iota((cols, half), 1)
    first = jnp.broadcast_to(listing[0, :, 0:half], (cols, half)) == label
    last = jnp.broadcast_to(listing[0, :, half:cols], (cols, half)) == label
    kept = jnp.where(first & (slot < sunlit), 1.0, 0.0).astype(BF16)
    sent = jnp.where(last & (slot + half < sunlit), 1.0, 0.0).astype(BF16)
    kept_out[...] = kept
    sent_out[...] = sent
    cosine = jnp.broadcast_to(zenith[0].astype(F32), (2 * SUBS, cols)).astype(BF16)
    sent_cos[...] = mm(cosine, sent).astype(BF16)
    kept_cos[...] = mm(cosine, kept)[0:SUBS]
    hits = jnp.where(jnp.concatenate([first, last], axis=1), 1.0, 0.0).astype(BF16)
    numbers = iota((2 * SUBS, cols), 1).astype(F32).astype(BF16)
    found = lax.dot_general(numbers, hits, (((1,), (1,)), ((), ())), preferred_element_type=F32)
    slot_of[...] = found[0:SUBS].astype(jnp.int32)


def join_body(n_group, me, *rest):
    gases, warms = rest[:n_group], rest[n_group : 2 * n_group]
    kept, sent, sent_cos, packed, outgoing, kept_x, spread = rest[2 * n_group :]
    slab = warms[0].shape[0]
    for (source, gas), warm in zip(partners(me, gases), warms):
        for h in range(packed.shape[0]):
            at = slice(h * LANES, (h + 1) * LANES)
            spread[0:slab, :] = warm[:, at].astype(F32)
            for f in range(gas.shape[0]):
                spread[(f + 1) * slab : (f + 2) * slab, :] = gas[f, :, at].astype(F32)
            for l in range(slab):
                row = pl.multiple_of((source * slab + l) * SUBS, SUBS)
                packed[h, pl.ds(row, SUBS), :] = spread[pl.ds(l, SUBS, stride=slab), :]
    cells = packed.shape[1]
    first, last = packed[0].astype(BF16), packed[1].astype(BF16)
    outgoing[0:cells, :] = (mm(first, sent[0:LANES]) + mm(last, sent[LANES:])).astype(BF16)
    outgoing[cells:, :] = sent_cos[...]
    kept_x[...] = mm(first, kept[0:LANES]) + mm(last, kept[LANES:])


def softplus2(z):
    return lax.log2(1.0 + jnp.exp2(z))


def softplus2_guarded(z):
    return jnp.maximum(z, softplus2(jnp.minimum(z, SAFE)))


def silu_of_half(v):
    half = v.astype(BF16)
    return half + half * jnp.tanh(half)


def sweep(x, first, second, heads, reach, start, gpts, rate, both, put, buffers, span):
    ones, hids, zs, (trans, last, peak) = buffers[0:2], buffers[2:4], buffers[4:-3], buffers[-3:]
    lead = len(zs) // 2
    wide = ones[0].shape[1]
    step_levels = wide // LANES
    levels = x.shape[0] // SUBS
    steps = levels // step_levels
    units = first.shape[0]
    sub = iota((SUBS, LANES), 0)

    def rows_of(level):
        return pl.ds(level * SUBS if isinstance(level, int) else pl.multiple_of(level * SUBS, SUBS), SUBS)

    def fed(tile):
        return jnp.concatenate([tile, jnp.ones_like(tile)], axis=0).astype(BF16)

    def first_tasks(t, out):
        def task():
            row = (min(t, steps - 1) if isinstance(t, int) else jnp.minimum(t, steps - 1)) * step_levels
            tiles = [x[rows_of(row + i), :] for i in range(step_levels)]
            out[...] = silu_of_half(mm(first[...], fed(jnp.concatenate(tiles, axis=1))))

        return [task]

    def second_tasks(one, out):
        def task():
            value = silu_of_half(mm(second[...], one[...]))
            out[0:units, :] = value
            out[units:, :] = value
            most = peak[...]
            for i in range(0, units, 2 * SUBS):
                for at in range(0, wide, LANES):
                    most = jnp.maximum(most, value[i : i + 2 * SUBS, at : at + LANES])
            peak[...] = most

        return [task]

    def optics_tasks(hid, out):
        def task():
            out[...] = mm(heads[...], hid[...])

        return [task]

    def consume_tasks(z, total):
        def task(lo):
            carry = trans[lo : lo + SUBS, :]
            for i in range(step_levels):
                at = slice(i * LANES, (i + 1) * LANES)
                following = carry * jnp.exp2(softplus2(z[lo : lo + SUBS, at]) * rate)
                term = following
                if both:
                    term = (carry - following) * softplus2(z[gpts + lo : gpts + lo + SUBS, at])
                total[i] = term if total[i] is None else total[i] + term
                carry = following
            trans[lo : lo + SUBS, :] = carry

        return [functools.partial(task, lo) for lo in range(0, gpts, SUBS)]

    def woven(main, side):
        done = 0
        for n, task in enumerate(main):
            while done < len(side) and done * len(main) <= n * len(side):
                side[done]()
                done += 1
            task()

    def begin():
        trans[...] = start
        if not both:
            sums = jnp.sum(start.reshape(gpts // SUBS, SUBS, LANES), axis=0)
            last[...] = jnp.broadcast_to(jnp.sum(sums, axis=0, keepdims=True), (SUBS, LANES))

    def entered(total, n, before, after):
        row = jnp.broadcast_to(jnp.sum(total, axis=0, keepdims=True), (SUBS, LANES))
        after = jnp.where(sub == n, row, after)
        before = jnp.where(sub == n + 1, row, before)
        return before, after, row

    def put_group(level, before, after, row):
        if both:
            put(level, after)
        else:
            put(level, jnp.where(sub == 0, last[...], before) - after)
            last[...] = row

    def run():
        begin()
        unroll = span // step_levels
        looped = unroll < steps

        def several(i, _):
            before = after = jnp.zeros((SUBS, LANES), F32)
            for k in range(unroll):
                t = k + lead
                total = [None] * step_levels
                if k == max(unroll - 1 - lead, 0):
                    most = jnp.max(peak[...].astype(F32) * reach[...])
                side = []
                if looped or t < steps:
                    side += optics_tasks(hids[t % 2], zs[t % len(zs)])
                if looped or t + 1 < steps:
                    side += second_tasks(ones[(t + 1) % 2], hids[(t + 1) % 2])
                if looped or t + 2 < steps:
                    side += first_tasks(i * unroll + t + 2, ones[t % 2])
                woven(consume_tasks(zs[k % len(zs)], total), side)
                for j in range(step_levels):
                    n = k * step_levels + j
                    before, after, row = entered(total[j], n % SUBS, before, after)
                    if n % SUBS == SUBS - 1:
                        level = i * (unroll * step_levels) + n + 1 - SUBS
                        if looped:
                            level = pl.multiple_of(level, SUBS)
                        put_group(level, before, after, row)
            return most

        ahead = []
        for t in range(lead + 2):
            ahead += first_tasks(t, ones[t % 2])
            if t >= 1:
                ahead += second_tasks(ones[(t - 1) % 2], hids[(t - 1) % 2])
            if t >= 2:
                ahead += optics_tasks(hids[t % 2], zs[t - 2])
        for task in ahead:
            task()
        if not looped:
            return several(0, None)
        return lax.fori_loop(0, steps // unroll, several, jnp.float32(0.0))

    def run_guarded():
        begin()
        z = zs[0]
        at = slice(0, LANES)
        nothing = jnp.zeros((SUBS, LANES), F32)

        def group(i, _):
            def level(n, held):
                row = pl.multiple_of((i * SUBS + n) * SUBS, SUBS)
                hidden = silu_of_half(mm(first[...], fed(x[pl.ds(row, SUBS), :])))
                hidden = silu_of_half(mm(second[...], hidden))
                z[:, at] = mm(heads[...], jnp.concatenate([hidden, hidden], axis=0))

                def piece(c, total):
                    lo = pl.multiple_of(c * SUBS, SUBS)
                    carry = trans[pl.ds(lo, SUBS), :]
                    depth = softplus2_guarded(z[pl.ds(lo, SUBS), at])
                    following = carry * jnp.exp2(depth * rate)
                    trans[pl.ds(lo, SUBS), :] = following
                    if not both:
                        return total + following
                    share = softplus2_guarded(z[pl.ds(pl.multiple_of(gpts + lo, SUBS), SUBS), at])
                    return total + (carry - following) * share

                total = lax.fori_loop(0, gpts // SUBS, piece, nothing)
                return entered(total, n, *held[:2])

            held = lax.fori_loop(0, SUBS, level, (nothing, nothing, nothing))
            put_group(pl.multiple_of(i * SUBS, SUBS), *held)
            return 0

        lax.fori_loop(0, levels // SUBS, group, 0)

    peak[...] = jnp.ones_like(peak)
    most = run()
    pl.when(most > SAFE)(run_guarded)


def sweep_scratch(hid, rows, gpts, step_levels, lead):
    wide = step_levels * LANES
    return [
        pltpu.VMEM((hid, wide), BF16),
        pltpu.VMEM((hid, wide), BF16),
        pltpu.VMEM((2 * hid, wide), BF16),
        pltpu.VMEM((2 * hid, wide), BF16),
        *([pltpu.VMEM((rows, wide), F32)] * (2 * lead)),
        pltpu.VMEM((gpts, LANES), F32),
        pltpu.VMEM((SUBS, LANES), F32),
        pltpu.VMEM((2 * SUBS, LANES), BF16),
    ]


def longwave_body(which, packed, first, second, heads, reach, out, *buffers):
    gpts = heads.shape[0] // 2
    x = packed.at[which]
    levels = out.shape[0]

    def put(level, emitted):
        row = level * SUBS if isinstance(level, int) else pl.multiple_of(level * SUBS, SUBS)
        planck = jnp.exp(0.25 * x[pl.ds(row, SUBS, stride=SUBS), :])
        out[pl.ds(level, SUBS), :] = -(heat_scale * LN2 / gpts) * planck * emitted

    sweep(
        x, first, second, heads, reach, jnp.ones((gpts, LANES), F32), gpts,
        -depth_scale, True, put, buffers, levels,
    )


def shortwave_body(
    count, kept_x, kept_cos, in_x, first, second, heads, reach, flux, out, work_x, *buffers
):
    cells, half = kept_x.shape
    levels = out.shape[0]
    gpts = heads.shape[0]
    slot = iota((half, half), 1) - count[0, 0]
    placed = jnp.where(slot == iota((half, half), 0), 1.0, 0.0).astype(BF16)
    work_x[...] = kept_x[...] + mm(in_x[0:cells, :], placed)
    cosine = kept_cos[...] + mm(in_x[cells:, :], placed)[0:SUBS]
    cosine = jnp.where(cosine > 0.0, cosine, 1.0)

    def put(level, emitted):
        out[pl.ds(level, SUBS), :] = (heat_scale / gpts) * cosine * emitted

    sweep(
        work_x, first, second, heads, reach, flux[...], gpts,
        -depth_scale / cosine, False, put, buffers, levels,
    )


def finish_body(me, count, long_first, long_last, work, partner, slot_of, *rest):
    pieces, heat = rest[:-1], rest[-1]
    levels, cols = heat.shape
    half = cols // 2
    slab = pieces[0].shape[0]
    sunlit = count[0, 0]
    for lo, long in ((0, long_first), (half, long_last)):
        slot = slot_of[:, lo : lo + half]
        here = slot < half
        place = jnp.where(here, slot, slot + half - sunlit) & (half - 1)
        lit = slot < sunlit
        for r in range(0, levels, SUBS):
            near = lane_take(work[r : r + SUBS, :], place)
            far = lane_take(partner[r : r + SUBS, :], place)
            short = jnp.where(lit, jnp.where(here, near, far), 0.0)
            heat[r : r + SUBS, lo : lo + half] = long[r : r + SUBS, :] + short
    for goal, out in partners(me, pieces):
        out[...] = heat[pl.ds(pl.multiple_of(goal * slab, SUBS), slab), :]


def add_body(me, closed, *rest):
    pieces, out = rest[:-1], rest[-1]
    cols = pieces[0].shape[1]
    for source, piece in partners(me, pieces):
        at = pl.ds(pl.multiple_of(source * cols, LANES), cols)
        out[:, at] = closed[:, at] + piece[...]


def per_device(
    potential, species, diffusion, neighbours, listing, day_count, zenith,
    lw_first, lw_bias, lw_second, lw_depth, lw_fraction,
    sw_first, sw_bias, sw_second, sw_depth, solar_flux,
):
    n_group = lax.axis_size("group")
    n_tile = lax.axis_size("tile")
    assert n_group & (n_group - 1) == 0 and n_tile % 2 == 0
    me = lax.axis_index("group").astype(jnp.int32).reshape(1)
    place = lax.axis_index("tile").astype(jnp.int32).reshape(1)
    slab, tile = potential.shape
    gases = species.shape[0]
    cols = tile // n_group
    half = cols // 2
    levels = slab * n_group
    hid = lw_first.shape[1]
    lw_gpts = lw_depth.shape[1]
    sw_gpts = sw_depth.shape[1]

    def outward(value):
        across = [(i, (i + 1 if i % 2 else i - 1) % n_tile) for i in range(n_tile)]
        return lax.ppermute(value, "tile", across)

    def paired(value):
        return lax.ppermute(value, "tile", [(i, i ^ 1) for i in range(n_tile)])

    def swapped(value, bit):
        return lax.ppermute(value, "group", [(i, i ^ bit) for i in range(n_group)])

    def exchanged(pieces):
        return [swapped(p, bit) if bit else p for bit, p in zip(far_first(n_group), pieces)]

    near = neighbours.shape[0]
    raw = (potential, neighbours, diffusion, species)
    framing, *gas_cuts = call(
        pack_body,
        [shaped((slab + 2 * near, tile), F32)] + [shaped((gases, slab, cols), BF16)] * n_group,
        [me, *(pltpu.with_memory_space_constraint(a, pltpu.HBM) for a in raw)],
        [
            pltpu.VMEM(neighbours.shape, jnp.int32),
            pltpu.VMEM(diffusion.shape, F32),
            pltpu.SemaphoreType.DMA((3 + n_group,)),
        ],
        where=HBM,
    )
    inner = paired(framing)
    outer = outward(framing)
    gas_pieces = exchanged(gas_cuts)

    (
        kept, sent, kept_cos, sent_cos, slot_of,
        lw_one, lw_two, lw_heads, lw_reach,
        sw_one, sw_two, sw_heads, sw_reach, flux,
    ) = call(
        prepare_body,
        [
            shaped((cols, half), BF16),
            shaped((cols, half), BF16),
            shaped((SUBS, half), F32),
            shaped((2 * SUBS, half), BF16),
            shaped((SUBS, cols), jnp.int32),
            shaped((hid, 2 * SUBS), BF16),
            shaped(lw_second.shape[::-1], BF16),
            shaped((2 * lw_gpts, 2 * hid), BF16),
            shaped((2 * SUBS, LANES), F32),
            shaped((hid, 2 * SUBS), BF16),
            shaped(sw_second.shape[::-1], BF16),
            shaped((sw_gpts, 2 * hid), BF16),
            shaped((2 * SUBS, LANES), F32),
            shaped((sw_gpts, LANES), F32),
        ],
        [
            day_count, listing, zenith,
            lw_first, lw_bias[None], lw_second, lw_depth, lw_fraction,
            sw_first, sw_bias[None], sw_second, sw_depth, solar_flux[None],
        ],
        after=framing,
    )

    wide = shaped((slab, 3 * tile), F32)
    frame_scratch = pltpu.VMEM(wide.shape, F32)
    table_scratch = [
        pltpu.VMEM((3, *neighbours.shape), jnp.int32), pltpu.VMEM((3, *diffusion.shape), F32)
    ]
    around = [outer, inner, potential, neighbours, diffusion]
    first, second, third, *warm_cuts = call(
        sections_body,
        [wide, wide, wide] + [shaped((slab, cols), BF16)] * n_group,
        [me, place, *around],
        [frame_scratch, *table_scratch],
        flops=10_000_000,
    )
    warm_pieces = exchanged(warm_cuts)
    (closed,) = call(
        closing_body,
        [shaped((slab, tile), F32)],
        [place, *around, first, second, third],
        [frame_scratch] * 4 + table_scratch,
        flops=4_000_000,
    )

    cells = levels * SUBS
    packed, out_x, kept_x = call(
        functools.partial(join_body, n_group),
        [
            shaped((cols // LANES, cells, LANES), F32),
            shaped((cells + 2 * SUBS, half), BF16),
            shaped((cells, half), F32),
        ],
        [me, *gas_pieces, *warm_pieces, kept, sent, sent_cos],
        [pltpu.VMEM((SUBS * slab, LANES), F32)],
    )
    in_x = paired(out_x)

    def longwave(which):
        (heat,) = call(
            functools.partial(longwave_body, which),
            [shaped((levels, half), F32)],
            [packed, lw_one, lw_two, lw_heads, lw_reach],
            sweep_scratch(hid, 2 * lw_gpts, lw_gpts, 2, 1),
            flops=4 * levels * half * hid * lw_gpts,
            trans=5 * levels * half * lw_gpts,
            after=work if which else None,
        )
        return heat

    long_first = longwave(0)
    (work,) = call(
        shortwave_body,
        [shaped((levels, half), F32)],
        [day_count, kept_x, kept_cos, in_x, sw_one, sw_two, sw_heads, sw_reach, flux],
        [pltpu.VMEM((cells, half), F32)] + sweep_scratch(hid, sw_gpts, sw_gpts, 4, 1),
        flops=2 * levels * half * hid * sw_gpts,
        trans=3 * levels * half * sw_gpts,
        after=long_first,
    )
    partner = paired(work)
    long_last = longwave(1)
    heat_cuts = call(
        finish_body,
        [shaped((slab, cols), F32)] * n_group,
        [me, day_count, long_first, long_last, work, partner, slot_of],
        [pltpu.VMEM((levels, cols), F32)],
    )
    heat_pieces = exchanged(heat_cuts)
    (evolved,) = call(add_body, [shaped((slab, tile), F32)], [me, closed, *heat_pieces])
    return evolved


def solution(mesh):
    return jax.shard_map(
        per_device,
        mesh=mesh,
        in_specs=(
            P("group", "tile"),
            P(None, "group", "tile"),
            P(None, "tile"),
            P(None, "tile"),
            P("group", "tile", None),
            P("group", "tile"),
            P("group", "tile", None),
            *([P()] * 10),
        ),
        out_specs=P("group", "tile"),
        check_vma=False,
    )
```

```python
import functools
import math

import jax
import jax.numpy as jnp
from jax import lax
from jax.experimental import pallas as pl
from jax.experimental.pallas import tpu as pltpu
from jax.sharding import PartitionSpec as P

HW = 256
LANES = 128
SUBS = 8

depth_scale = 0.1
heat_scale = 12.0
LOG2E = 1.4426950408889634
LN2 = 0.6931471805599453
SAFE = 120.0

F32 = jnp.float32
BF16 = jnp.bfloat16
VMEM = pl.BlockSpec(memory_space=pltpu.VMEM)
ANY = pl.BlockSpec(memory_space=pl.ANY)
HBM = pl.BlockSpec(memory_space=pltpu.HBM)
SMEM = pl.BlockSpec(memory_space=pltpu.SMEM)
PARAMS = pltpu.CompilerParams(vmem_limit_bytes=48 * 1024 * 1024)


def call(body, outs, ins, scratch=(), flops=0, trans=0, after=None, where=VMEM):
    in_specs = [SMEM if a.size == 1 else where for a in ins]
    if after is not None:
        whole, ins = body, [after, *ins]
        in_specs = [ANY, *in_specs]

        def body(_, *refs):
            whole(*refs)

    return pl.pallas_call(
        body,
        out_shape=outs,
        in_specs=in_specs,
        out_specs=[VMEM for _ in outs],
        scratch_shapes=list(scratch),
        compiler_params=PARAMS,
        cost_estimate=pl.CostEstimate(
            flops=flops,
            transcendentals=trans,
            bytes_accessed=sum(a.size * a.dtype.itemsize for a in list(ins) + list(outs)),
        ),
    )(*ins)


def shaped(shape, dtype):
    return jax.ShapeDtypeStruct(shape, dtype)


def iota(shape, dim):
    return lax.broadcasted_iota(jnp.int32, shape, dim)


def mm(a, b):
    return jnp.dot(a, b, preferred_element_type=F32)


def far_first(n):
    return [0, *range(n - 1, 0, -1)]


def partners(me, pieces):
    return [(me[0] ^ bit, piece) for bit, piece in zip(far_first(len(pieces)), pieces)]


def lane_take(x, idx):
    return jnp.take_along_axis(x, idx, axis=1, mode="promise_in_bounds")


def diffused(src, src_at, table, weight, within, at):
    reach = HW // LANES
    wide = 2 * reach + 1
    rows = src.shape[0]
    groups = range(0, rows, SUBS)
    base = at - src_at
    middle = [src[r : r + SUBS, base : base + LANES] for r in groups]
    total = [jnp.zeros_like(m) for m in middle]
    for k in range(table.shape[0]):
        place = jnp.broadcast_to(table[k : k + 1, within : within + LANES], (SUBS, LANES)) - within
        lane = place & (LANES - 1)
        which = place >> (LANES.bit_length() - 1)
        factor = jnp.broadcast_to(weight[k : k + 1, within : within + LANES], (SUBS, LANES))
        tests = [which == w for w in range(1, wide)]
        for n, r in enumerate(groups):
            near = None
            for w in range(wide):
                lo = base + (w - reach) * LANES
                got = lane_take(src[r : r + SUBS, lo : lo + LANES], lane)
                near = got if w == 0 else jnp.where(tests[w - 1], got, near)
            total[n] = total[n] + factor * (near - middle[n])
    return [(r, m, m + t) for r, m, t in zip(groups, middle, total)]


def pack_body(me, own, table, weight, species, out, *rest):
    pieces, (table_here, weight_here, sems) = rest[:-3], rest[-3:]
    slab = own.shape[0]
    near = table.shape[0]
    cols = pieces[0].shape[2]
    moves = [
        pltpu.make_async_copy(own, out.at[0:slab], sems.at[0]),
        pltpu.make_async_copy(table, table_here, sems.at[1]),
        pltpu.make_async_copy(weight, weight_here, sems.at[2]),
    ]
    for source, piece in partners(me, pieces):
        at = pl.ds(pl.multiple_of(source * cols, LANES), cols)
        moves.append(pltpu.make_async_copy(species.at[:, :, at], piece, sems.at[len(moves)]))
    for move in moves:
        move.start()
    for move in moves:
        move.wait()
    out[slab : slab + near, :] = table_here[...].astype(F32)
    out[slab + near :, :] = weight_here[...]


def staged(place, outer, inner, own, table, weight, frame, tables, weights):
    slab, tile = own.shape
    near = table.shape[0]
    odd = place[0] & 1
    for side, packed in ((odd, outer), (1 - odd, inner)):
        at = pl.ds(pl.multiple_of(side * (2 * tile), LANES), tile)
        frame[:, at] = packed[0:slab, :]
        tables[side * 2] = packed[slab : slab + near, :].astype(jnp.int32)
        weights[side * 2] = packed[slab + near : slab + 2 * near, :]
    frame[:, tile : 2 * tile] = own[...]
    tables[1] = table[...]
    weights[1] = weight[...]


class Sections:
    def __init__(self, frame, first, second, third, tables, weights):
        self.tile = frame.shape[1] // 3
        self.frame, self.first, self.second, self.third = frame, first, second, third
        self.tables, self.weights = tables, weights

    def run(self, src, columns, put):
        for at in columns:
            t = at // self.tile
            within = at - t * self.tile
            for r, _, value in diffused(src, 0, self.tables.at[t], self.weights.at[t], within, at):
                put(slice(r, r + SUBS), slice(at, at + LANES), value)

    def around(self, inside, halo):
        tile = self.tile
        return [*range(tile - halo, tile - inside, LANES), *range(2 * tile + inside, 2 * tile + halo, LANES)]

    def own(self, halo):
        return range(self.tile - halo, 2 * self.tile + halo, LANES)

    def do_first(self, columns):
        def put(rows, at, value):
            self.first[rows, at] = value

        self.run(self.frame, columns, put)

    def do_second(self, columns):
        def put(rows, at, value):
            self.second[rows, at] = 0.75 * self.frame[rows, at] + 0.25 * value

        self.run(self.first, columns, put)

    def do_third(self, columns):
        def put(rows, at, value):
            self.third[rows, at] = self.frame[rows, at] / 3.0 + (2.0 / 3.0) * value

        self.run(self.second, columns, put)


def sections_body(me, place, outer, inner, own, table, weight, first, second, third, *rest):
    pieces, (frame, tables, weights) = rest[:-3], rest[-3:]
    tile = own.shape[1]
    cols = tile // len(pieces)
    staged(place, outer, inner, own, table, weight, frame, tables, weights)
    sections = Sections(frame, first, second, third, tables, weights)
    sections.do_first(sections.own(2 * HW))
    sections.do_second(sections.own(HW))
    sections.do_third(sections.own(0))
    for goal, out in partners(me, pieces):
        lo = pl.multiple_of(tile + goal * cols, LANES)
        out[...] = third[:, pl.ds(lo, cols)].astype(BF16)


def closing_body(
    place, outer, inner, own, table, weight, first_in, second_in, third_in, out,
    frame, first, second, third, tables, weights,
):
    tile = own.shape[1]
    staged(place, outer, inner, own, table, weight, frame, tables, weights)
    for held, full, halo in ((first_in, first, 2 * HW), (second_in, second, HW), (third_in, third, 0)):
        at = slice(tile - halo, 2 * tile + halo)
        full[:, at] = held[:, at]
    sections = Sections(frame, first, second, third, tables, weights)
    sections.do_first(sections.around(2 * HW, 3 * HW))
    sections.do_second(sections.around(HW, 2 * HW))
    sections.do_third(sections.around(0, HW))

    def put(rows, at, value):
        out[rows, at.start - tile : at.stop - tile] = value

    sections.run(third, sections.own(0), put)


def turned_over(matrix):
    return matrix.astype(F32).T


def head_parts(weight, out, at):
    hid, gpts = weight.shape
    scaled = LOG2E * turned_over(weight[...])
    high = scaled.astype(BF16)
    out[at : at + gpts, 0:hid] = high
    out[at : at + gpts, hid:] = (scaled - high.astype(F32)).astype(BF16)


def first_parts(weight, bias, out):
    fin = weight.shape[0]
    rows = [(0.5 * weight[...].astype(F32)).astype(BF16).astype(F32)]
    rest = 0.5 * bias[...]
    for _ in range(3):
        part = rest.astype(BF16).astype(F32)
        rows.append(part)
        rest = rest - part
    rows.append(jnp.zeros((fin - 3, weight.shape[1]), F32))
    out[...] = jnp.concatenate(rows, axis=0).T.astype(BF16)


def reach_of(heads):
    sums = mm(jnp.abs(heads[...]), jnp.ones((heads.shape[1], LANES), BF16))
    return jnp.broadcast_to(jnp.max(sums, axis=0, keepdims=True), (2 * SUBS, LANES))


def prepare_body(
    count, listing, zenith, w1, b1, w2, wd, wf, v1, c1, v2, vd, flux,
    kept_out, sent_out, kept_cos, sent_cos, slot_of,
    w1_out, w2_out, heads_out, reach_out, v1_out, v2_out, vd_out, vreach_out, flux_out,
):
    for weight, out in ((w2, w2_out), (v2, v2_out)):
        out[...] = (0.5 * turned_over(weight[...])).astype(BF16)
    first_parts(w1, b1, w1_out)
    first_parts(v1, c1, v1_out)
    head_parts(wd, heads_out, 0)
    head_parts(wf, heads_out, wd.shape[1])
    head_parts(vd, vd_out, 0)
    reach_out[...] = reach_of(heads_out)
    vreach_out[...] = reach_of(vd_out)
    flux_out[...] = jnp.broadcast_to(flux[...], (LANES, flux.shape[1])).T
    cols = listing.shape[-1]
    half = cols // 2
    sunlit = count[0, 0]
    label = iota((cols, half), 0)
    slot = iota((cols, half), 1)
    first = jnp.broadcast_to(listing[0, :, 0:half], (cols, half)) == label
    last = jnp.broadcast_to(listing[0, :, half:cols], (cols, half)) == label
    kept = jnp.where(first & (slot < sunlit), 1.0, 0.0).astype(BF16)
    sent = jnp.where(last & (slot + half < sunlit), 1.0, 0.0).astype(BF16)
    kept_out[...] = kept
    sent_out[...] = sent
    cosine = jnp.broadcast_to(zenith[0].astype(F32), (2 * SUBS, cols)).astype(BF16)
    sent_cos[...] = mm(cosine, sent).astype(BF16)
    kept_cos[...] = mm(cosine, kept)[0:SUBS]
    hits = jnp.where(jnp.concatenate([first, last], axis=1), 1.0, 0.0).astype(BF16)
    numbers = iota((2 * SUBS, cols), 1).astype(F32).astype(BF16)
    found = lax.dot_general(numbers, hits, (((1,), (1,)), ((), ())), preferred_element_type=F32)
    slot_of[...] = found[0:SUBS].astype(jnp.int32)


def join_body(n_group, me, *rest):
    gases, warms = rest[:n_group], rest[n_group : 2 * n_group]
    kept, sent, sent_cos, packed, outgoing, kept_x, spread = rest[2 * n_group :]
    slab = warms[0].shape[0]
    for (source, gas), warm in zip(partners(me, gases), warms):
        for h in range(packed.shape[0]):
            at = slice(h * LANES, (h + 1) * LANES)
            spread[0:slab, :] = warm[:, at].astype(F32)
            for f in range(gas.shape[0]):
                spread[(f + 1) * slab : (f + 2) * slab, :] = gas[f, :, at].astype(F32)
            for l in range(slab):
                row = pl.multiple_of((source * slab + l) * SUBS, SUBS)
                packed[h, pl.ds(row, SUBS), :] = spread[pl.ds(l, SUBS, stride=slab), :]
    cells = packed.shape[1]
    first, last = packed[0].astype(BF16), packed[1].astype(BF16)
    outgoing[0:cells, :] = (mm(first, sent[0:LANES]) + mm(last, sent[LANES:])).astype(BF16)
    outgoing[cells:, :] = sent_cos[...]
    kept_x[...] = mm(first, kept[0:LANES]) + mm(last, kept[LANES:])


def softplus2(z):
    return lax.log2(1.0 + jnp.exp2(z))


def softplus2_guarded(z):
    return jnp.maximum(z, softplus2(jnp.minimum(z, SAFE)))


def silu_of_half(v):
    return (v + v * jnp.tanh(v)).astype(BF16)


def sweep(x, first, second, heads, reach, start, gpts, rate, both, put, buffers, span):
    ones, hids, zs, (trans, last, peak) = buffers[0:2], buffers[2:4], buffers[4:-3], buffers[-3:]
    lead = len(zs) // 2
    wide = ones[0].shape[1]
    step_levels = wide // LANES
    levels = x.shape[0] // SUBS
    steps = levels // step_levels
    units = first.shape[0]
    sub = iota((SUBS, LANES), 0)

    def rows_of(level):
        return pl.ds(level * SUBS if isinstance(level, int) else pl.multiple_of(level * SUBS, SUBS), SUBS)

    def fed(tile):
        return jnp.concatenate([tile, jnp.ones_like(tile)], axis=0).astype(BF16)

    def first_tasks(t, out):
        def task():
            row = (min(t, steps - 1) if isinstance(t, int) else jnp.minimum(t, steps - 1)) * step_levels
            tiles = [x[rows_of(row + i), :] for i in range(step_levels)]
            out[...] = silu_of_half(mm(first[...], fed(jnp.concatenate(tiles, axis=1))))

        return [task]

    def second_tasks(one, out):
        def task():
            value = silu_of_half(mm(second[...], one[...]))
            out[0:units, :] = value
            out[units:, :] = value
            most = peak[...]
            for i in range(0, units, 2 * SUBS):
                for at in range(0, wide, LANES):
                    most = jnp.maximum(most, value[i : i + 2 * SUBS, at : at + LANES])
            peak[...] = most

        return [task]

    def optics_tasks(hid, out):
        def task():
            out[...] = mm(heads[...], hid[...])

        return [task]

    def consume_tasks(z, total):
        def task(lo):
            carry = trans[lo : lo + SUBS, :]
            for i in range(step_levels):
                at = slice(i * LANES, (i + 1) * LANES)
                following = carry * jnp.exp2(softplus2(z[lo : lo + SUBS, at]) * rate)
                term = following
                if both:
                    term = (carry - following) * softplus2(z[gpts + lo : gpts + lo + SUBS, at])
                total[i] = term if total[i] is None else total[i] + term
                carry = following
            trans[lo : lo + SUBS, :] = carry

        return [functools.partial(task, lo) for lo in range(0, gpts, SUBS)]

    def woven(main, side):
        done = 0
        for n, task in enumerate(main):
            while done < len(side) and done * len(main) <= n * len(side):
                side[done]()
                done += 1
            task()

    def begin():
        trans[...] = start
        if not both:
            sums = jnp.sum(start.reshape(gpts // SUBS, SUBS, LANES), axis=0)
            last[...] = jnp.broadcast_to(jnp.sum(sums, axis=0, keepdims=True), (SUBS, LANES))

    def entered(total, n, before, after):
        row = jnp.broadcast_to(jnp.sum(total, axis=0, keepdims=True), (SUBS, LANES))
        after = jnp.where(sub == n, row, after)
        before = jnp.where(sub == n + 1, row, before)
        return before, after, row

    def put_group(level, before, after, row):
        if both:
            put(level, after)
        else:
            put(level, jnp.where(sub == 0, last[...], before) - after)
            last[...] = row

    def run():
        begin()
        unroll = span // step_levels
        looped = unroll < steps

        def several(i, _):
            before = after = jnp.zeros((SUBS, LANES), F32)
            for k in range(unroll):
                t = k + lead
                total = [None] * step_levels
                if k == max(unroll - 1 - lead, 0):
                    most = jnp.max(peak[...].astype(F32) * reach[...])
                side = []
                if looped or t < steps:
                    side += optics_tasks(hids[t % 2], zs[t % len(zs)])
                if looped or t + 1 < steps:
                    side += second_tasks(ones[(t + 1) % 2], hids[(t + 1) % 2])
                if looped or t + 2 < steps:
                    side += first_tasks(i * unroll + t + 2, ones[t % 2])
                woven(consume_tasks(zs[k % len(zs)], total), side)
                for j in range(step_levels):
                    n = k * step_levels + j
                    before, after, row = entered(total[j], n % SUBS, before, after)
                    if n % SUBS == SUBS - 1:
                        level = i * (unroll * step_levels) + n + 1 - SUBS
                        if looped:
                            level = pl.multiple_of(level, SUBS)
                        put_group(level, before, after, row)
            return most

        ahead = []
        for t in range(lead + 2):
            ahead += first_tasks(t, ones[t % 2])
            if t >= 1:
                ahead += second_tasks(ones[(t - 1) % 2], hids[(t - 1) % 2])
            if t >= 2:
                ahead += optics_tasks(hids[t % 2], zs[t - 2])
        for task in ahead:
            task()
        if not looped:
            return several(0, None)
        return lax.fori_loop(0, steps // unroll, several, jnp.float32(0.0))

    def run_guarded():
        begin()
        z = zs[0]
        at = slice(0, LANES)
        nothing = jnp.zeros((SUBS, LANES), F32)

        def group(i, _):
            def level(n, held):
                row = pl.multiple_of((i * SUBS + n) * SUBS, SUBS)
                hidden = silu_of_half(mm(first[...], fed(x[pl.ds(row, SUBS), :])))
                hidden = silu_of_half(mm(second[...], hidden))
                z[:, at] = mm(heads[...], jnp.concatenate([hidden, hidden], axis=0))

                def piece(c, total):
                    lo = pl.multiple_of(c * SUBS, SUBS)
                    carry = trans[pl.ds(lo, SUBS), :]
                    depth = softplus2_guarded(z[pl.ds(lo, SUBS), at])
                    following = carry * jnp.exp2(depth * rate)
                    trans[pl.ds(lo, SUBS), :] = following
                    if not both:
                        return total + following
                    share = softplus2_guarded(z[pl.ds(pl.multiple_of(gpts + lo, SUBS), SUBS), at])
                    return total + (carry - following) * share

                total = lax.fori_loop(0, gpts // SUBS, piece, nothing)
                return entered(total, n, *held[:2])

            held = lax.fori_loop(0, SUBS, level, (nothing, nothing, nothing))
            put_group(pl.multiple_of(i * SUBS, SUBS), *held)
            return 0

        lax.fori_loop(0, levels // SUBS, group, 0)

    peak[...] = jnp.ones_like(peak)
    most = run()
    pl.when(most > SAFE)(run_guarded)


def sweep_scratch(hid, rows, gpts, step_levels, lead):
    wide = step_levels * LANES
    return [
        pltpu.VMEM((hid, wide), BF16),
        pltpu.VMEM((hid, wide), BF16),
        pltpu.VMEM((2 * hid, wide), BF16),
        pltpu.VMEM((2 * hid, wide), BF16),
        *([pltpu.VMEM((rows, wide), F32)] * (2 * lead)),
        pltpu.VMEM((gpts, LANES), F32),
        pltpu.VMEM((SUBS, LANES), F32),
        pltpu.VMEM((2 * SUBS, LANES), BF16),
    ]


def longwave_body(which, packed, first, second, heads, reach, out, *buffers):
    gpts = heads.shape[0] // 2
    x = packed.at[which]
    levels = out.shape[0]

    def put(level, emitted):
        row = level * SUBS if isinstance(level, int) else pl.multiple_of(level * SUBS, SUBS)
        planck = jnp.exp(0.25 * x[pl.ds(row, SUBS, stride=SUBS), :])
        out[pl.ds(level, SUBS), :] = -(heat_scale * LN2 / gpts) * planck * emitted

    sweep(
        x, first, second, heads, reach, jnp.ones((gpts, LANES), F32), gpts,
        -depth_scale, True, put, buffers, levels,
    )


def shortwave_body(
    count, kept_x, kept_cos, in_x, first, second, heads, reach, flux, out, work_x, *buffers
):
    cells, half = kept_x.shape
    levels = out.shape[0]
    gpts = heads.shape[0]
    slot = iota((half, half), 1) - count[0, 0]
    placed = jnp.where(slot == iota((half, half), 0), 1.0, 0.0).astype(BF16)
    work_x[...] = kept_x[...] + mm(in_x[0:cells, :], placed)
    cosine = kept_cos[...] + mm(in_x[cells:, :], placed)[0:SUBS]
    cosine = jnp.where(cosine > 0.0, cosine, 1.0)

    def put(level, emitted):
        out[pl.ds(level, SUBS), :] = (heat_scale / gpts) * cosine * emitted

    sweep(
        work_x, first, second, heads, reach, flux[...], gpts,
        -depth_scale / cosine, False, put, buffers, levels,
    )


def finish_body(me, count, long_first, long_last, work, partner, slot_of, *rest):
    pieces, heat = rest[:-1], rest[-1]
    levels, cols = heat.shape
    half = cols // 2
    slab = pieces[0].shape[0]
    sunlit = count[0, 0]
    for lo, long in ((0, long_first), (half, long_last)):
        slot = slot_of[:, lo : lo + half]
        here = slot < half
        place = jnp.where(here, slot, slot + half - sunlit) & (half - 1)
        lit = slot < sunlit
        for r in range(0, levels, SUBS):
            near = lane_take(work[r : r + SUBS, :], place)
            far = lane_take(partner[r : r + SUBS, :], place)
            short = jnp.where(lit, jnp.where(here, near, far), 0.0)
            heat[r : r + SUBS, lo : lo + half] = long[r : r + SUBS, :] + short
    for goal, out in partners(me, pieces):
        out[...] = heat[pl.ds(pl.multiple_of(goal * slab, SUBS), slab), :]


def add_body(me, closed, *rest):
    pieces, out = rest[:-1], rest[-1]
    cols = pieces[0].shape[1]
    for source, piece in partners(me, pieces):
        at = pl.ds(pl.multiple_of(source * cols, LANES), cols)
        out[:, at] = closed[:, at] + piece[...]


def per_device(
    potential, species, diffusion, neighbours, listing, day_count, zenith,
    lw_first, lw_bias, lw_second, lw_depth, lw_fraction,
    sw_first, sw_bias, sw_second, sw_depth, solar_flux,
):
    n_group = lax.axis_size("group")
    n_tile = lax.axis_size("tile")
    assert n_group & (n_group - 1) == 0 and n_tile % 2 == 0
    me = lax.axis_index("group").astype(jnp.int32).reshape(1)
    place = lax.axis_index("tile").astype(jnp.int32).reshape(1)
    slab, tile = potential.shape
    gases = species.shape[0]
    cols = tile // n_group
    half = cols // 2
    levels = slab * n_group
    hid = lw_first.shape[1]
    lw_gpts = lw_depth.shape[1]
    sw_gpts = sw_depth.shape[1]

    def outward(value):
        across = [(i, (i + 1 if i % 2 else i - 1) % n_tile) for i in range(n_tile)]
        return lax.ppermute(value, "tile", across)

    def paired(value):
        return lax.ppermute(value, "tile", [(i, i ^ 1) for i in range(n_tile)])

    def swapped(value, bit):
        return lax.ppermute(value, "group", [(i, i ^ bit) for i in range(n_group)])

    def exchanged(pieces):
        return [swapped(p, bit) if bit else p for bit, p in zip(far_first(n_group), pieces)]

    near = neighbours.shape[0]
    raw = (potential, neighbours, diffusion, species)
    framing, *gas_cuts = call(
        pack_body,
        [shaped((slab + 2 * near, tile), F32)] + [shaped((gases, slab, cols), BF16)] * n_group,
        [me, *(pltpu.with_memory_space_constraint(a, pltpu.HBM) for a in raw)],
        [
            pltpu.VMEM(neighbours.shape, jnp.int32),
            pltpu.VMEM(diffusion.shape, F32),
            pltpu.SemaphoreType.DMA((3 + n_group,)),
        ],
        where=HBM,
    )
    inner = paired(framing)
    outer = outward(framing)
    gas_pieces = exchanged(gas_cuts)

    (
        kept, sent, kept_cos, sent_cos, slot_of,
        lw_one, lw_two, lw_heads, lw_reach,
        sw_one, sw_two, sw_heads, sw_reach, flux,
    ) = call(
        prepare_body,
        [
            shaped((cols, half), BF16),
            shaped((cols, half), BF16),
            shaped((SUBS, half), F32),
            shaped((2 * SUBS, half), BF16),
            shaped((SUBS, cols), jnp.int32),
            shaped((hid, 2 * SUBS), BF16),
            shaped(lw_second.shape[::-1], BF16),
            shaped((2 * lw_gpts, 2 * hid), BF16),
            shaped((2 * SUBS, LANES), F32),
            shaped((hid, 2 * SUBS), BF16),
            shaped(sw_second.shape[::-1], BF16),
            shaped((sw_gpts, 2 * hid), BF16),
            shaped((2 * SUBS, LANES), F32),
            shaped((sw_gpts, LANES), F32),
        ],
        [
            day_count, listing, zenith,
            lw_first, lw_bias[None], lw_second, lw_depth, lw_fraction,
            sw_first, sw_bias[None], sw_second, sw_depth, solar_flux[None],
        ],
        after=framing,
    )

    wide = shaped((slab, 3 * tile), F32)
    frame_scratch = pltpu.VMEM(wide.shape, F32)
    table_scratch = [
        pltpu.VMEM((3, *neighbours.shape), jnp.int32), pltpu.VMEM((3, *diffusion.shape), F32)
    ]
    around = [outer, inner, potential, neighbours, diffusion]
    first, second, third, *warm_cuts = call(
        sections_body,
        [wide, wide, wide] + [shaped((slab, cols), BF16)] * n_group,
        [me, place, *around],
        [frame_scratch, *table_scratch],
        flops=10_000_000,
    )
    warm_pieces = exchanged(warm_cuts)
    (closed,) = call(
        closing_body,
        [shaped((slab, tile), F32)],
        [place, *around, first, second, third],
        [frame_scratch] * 4 + table_scratch,
        flops=4_000_000,
    )

    cells = levels * SUBS
    packed, out_x, kept_x = call(
        functools.partial(join_body, n_group),
        [
            shaped((cols // LANES, cells, LANES), F32),
            shaped((cells + 2 * SUBS, half), BF16),
            shaped((cells, half), F32),
        ],
        [me, *gas_pieces, *warm_pieces, kept, sent, sent_cos],
        [pltpu.VMEM(((SUBS + 1) * slab, LANES), F32)],
    )
    in_x = paired(out_x)

    def longwave(which):
        (heat,) = call(
            functools.partial(longwave_body, which),
            [shaped((levels, half), F32)],
            [packed, lw_one, lw_two, lw_heads, lw_reach],
            sweep_scratch(hid, 2 * lw_gpts, lw_gpts, 2, 1),
            flops=4 * levels * half * hid * lw_gpts,
            trans=5 * levels * half * lw_gpts,
            after=work if which else None,
        )
        return heat

    long_first = longwave(0)
    (work,) = call(
        shortwave_body,
        [shaped((levels, half), F32)],
        [day_count, kept_x, kept_cos, in_x, sw_one, sw_two, sw_heads, sw_reach, flux],
        [pltpu.VMEM((cells, half), F32)] + sweep_scratch(hid, sw_gpts, sw_gpts, 4, 1),
        flops=2 * levels * half * hid * sw_gpts,
        trans=3 * levels * half * sw_gpts,
        after=long_first,
    )
    partner = paired(work)
    long_last = longwave(1)
    heat_cuts = call(
        finish_body,
        [shaped((slab, cols), F32)] * n_group,
        [me, day_count, long_first, long_last, work, partner, slot_of],
        [pltpu.VMEM((levels, cols), F32)],
    )
    heat_pieces = exchanged(heat_cuts)
    (evolved,) = call(add_body, [shaped((slab, tile), F32)], [me, closed, *heat_pieces])
    return evolved


def solution(mesh):
    return jax.shard_map(
        per_device,
        mesh=mesh,
        in_specs=(
            P("group", "tile"),
            P(None, "group", "tile"),
            P(None, "tile"),
            P(None, "tile"),
            P("group", "tile", None),
            P("group", "tile"),
            P("group", "tile", None),
            *([P()] * 10),
        ),
        out_specs=P("group", "tile"),
        check_vma=False,
    )
```
